32 devices in a mesh: ep: 8 (over z, x), tp: 4 (over y, core).
Axes of the slice: x: 2, y: 2, z: 4, core: 2. Of those that a mesh axis runs over, the one named last changes fastest.
Arguments:
- hidden: bfloat16 [5120, 2048], P('ep'), may hold values from -6 to 6
- attn_gain: float32 [2048], replicated, may hold values from 0.5 to 1.5
- qkv_weight: bfloat16 [2048, 3, 2048], P(None, None, 'tp'), may hold values from -0.125 to 0.125
- qkv_bias: float32 [3, 2048], P(None, 'tp'), may hold values from -3 to 3
- out_weight: bfloat16 [2048, 2048], P(None, 'tp'), may hold values from -0.5 to 0.5
- mlp_gain: float32 [2048], replicated, may hold values from 0.5 to 1.5
- router_weight: bfloat16 [2048, 8], replicated, may hold values from -0.0625 to 0.0625
- share_gate: bfloat16 [2048], replicated, may hold values from -0.125 to 0.125
- shared_gate_up: bfloat16 [2048, 2, 5632], P(None, None, 'tp'), may hold values from -0.125 to 0.125
- shared_down: bfloat16 [2048, 5632], P(None, 'tp'), may hold values from -0.15625 to 0.15625
- expert_gate_up: bfloat16 [8, 2048, 2, 1408], P('ep', None, None, 'tp'), may hold values from -0.125 to 0.125
- expert_down: bfloat16 [8, 2048, 1408], P('ep', None, 'tp'), may hold values from -1.25 to 1.25
- routes: int32 [5120, 4], P('ep'), may hold values from 0 to 7, all different within a row
- priority: int32 [5120, 4], P('ep'), may hold values from 0 to 2559, as said below
- prefix: int32 [8], P('ep'), may hold values from 64 to 320
- cotangent: bfloat16 [5120, 2048], P('ep'), may hold values from -6 to 6
Outputs:
- output: bfloat16 [5120, 2048], P('ep', 'tp')
- input_grad: bfloat16 [5120, 2048], P('ep', 'tp')
- attn_gain_grad: float32 [2048], replicated
- qkv_weight_grad: float32 [2048, 3, 2048], P('ep', None, 'tp')
- qkv_bias_grad: float32 [3, 2048], P(None, 'tp')
- out_weight_grad: float32 [2048, 2048], P('ep', 'tp')
- mlp_gain_grad: float32 [2048], replicated
- router_grad: float32 [2048, 8], replicated
- share_gate_grad: float32 [2048], replicated
- shared_gate_up_grad: float32 [2048, 2, 5632], P('ep', None, 'tp')
- shared_down_grad: float32 [2048, 5632], P('ep', 'tp')
- expert_gate_up_grad: float32 [8, 2048, 2, 1408], P('ep', None, None, 'tp')
- expert_down_grad: float32 [8, 2048, 1408], P('ep', None, 'tp')
The draws below stay inside these ranges and needn't reach their ends.
Inputs may be any that keep to these rules, and one draw needn't show every extreme that they name: `priority`: within each sequence's 640 rows the 2560 values are all different. `routes`: each row names 4 different experts.
All inputs are finite; a program needn't handle non-finite values.
Results may differ from the reference program's by a relative error of at most 0.035.
Values may be sent and summed in bfloat16 or wider, within the bound.
A program may use at most 320 MiB of HBM per device.

```python
import jax
import jax.numpy as jnp
from jax import lax

D = 2048
HEADS = 16
HEAD_DIM = 128
FF_E = 1408
FF_SH = 5632
TOP = 4
SEQ = 640
EXPERTS = 8
SEQS = 8
TOKENS = 5120
CAP = 400
N_EP = 8
N_TP = 4


def draw_priority(key, part):
    block_size = SEQ * TOP

    def one_block(block_index):
        return jax.random.permutation(jax.random.fold_in(key, block_index), block_size).astype(jnp.int32)
    blocks = jax.vmap(one_block)(jnp.arange(SEQS, dtype=jnp.int32))
    return blocks.reshape(SEQS * SEQ, TOP)


def place_ends(drawn, key, smallest, largest):
    longest = drawn.shape.index(max(drawn.shape))
    spots = []
    for shift in (0, 1):
        where = [jax.random.randint(jax.random.fold_in(key, axis), (), 0, length) for axis, length in enumerate(drawn.shape)]
        where[longest] = (where[longest] + shift) % drawn.shape[longest]
        spots.append(tuple(where))
    return drawn.at[spots[0]].set(smallest).at[spots[1]].set(largest)


def block_levels(stream_key, dims, shards, smallest, high):
    level = 1.0
    for axis_at, blocks in shards:
        draws = jax.random.uniform(jax.random.fold_in(jax.random.fold_in(stream_key, 6), axis_at), (blocks,), jnp.float32, smallest / len(shards), high / len(shards))
        level = level * jnp.repeat(jnp.exp(draws), dims[axis_at] // blocks).reshape((-1,) + (1,) * (len(dims) - 1 - axis_at))
    return level


def choose_distinct(stream_key, rows, amount, top, lift):
    sequence = jax.random.permutation(jax.random.fold_in(stream_key, 1), amount)
    boost = sequence
    for power in range(3):
        boost = boost * boost // amount
    boost = boost * lift // amount
    lots = jax.random.randint(jax.random.fold_in(stream_key, 2), (rows, amount), 0, 4096) + boost
    fixed_rows = jax.random.permutation(jax.random.fold_in(stream_key, 3), rows)[jnp.arange(amount) % rows]
    lots = jnp.where(jnp.arange(rows)[:, None] == fixed_rows[None, :], 1 << 14, lots)
    score = lots * amount + jnp.arange(amount)
    return lax.top_k(score.astype(jnp.int32), top)[1].astype(jnp.int32)


def gaussian(own_key, dims, deviation, bound, split=(), kind=jnp.bfloat16):
    result = deviation * jax.random.normal(own_key, dims, jnp.float32)
    if split:
        result = result * block_levels(own_key, dims, split, -0.22, 0.18)
    return jnp.clip(result, -bound, bound).astype(kind)


def setup_inputs(seed: int = 0) -> dict:
    streams_of = jax.random.split(jax.random.key(seed), 17)
    return {
        "hidden": gaussian(streams_of[0], (TOKENS, D), 1.0, 6.0, ((0, 8),)),
        "attn_gain": jnp.clip(1.0 + 0.1 * jax.random.normal(streams_of[1], (D,), jnp.float32), 0.5, 1.5),
        "qkv_weight": gaussian(streams_of[2], (D, 3, D), D ** -0.5, 0.125, ((2, 4),)),
        "qkv_bias": gaussian(streams_of[3], (3, D), 0.5, 3.0, ((1, 4),), jnp.float32),
        "out_weight": gaussian(streams_of[4], (D, D), (D // 16) ** -0.5, 0.5, ((1, 4),)),
        "mlp_gain": jnp.clip(1.0 + 0.1 * jax.random.normal(streams_of[5], (D,), jnp.float32), 0.5, 1.5),
        "router_weight": gaussian(streams_of[6], (D, EXPERTS), (4 * D) ** -0.5, 0.0625),
        "share_gate": gaussian(streams_of[7], (D,), D ** -0.5, 0.125),
        "shared_gate_up": gaussian(streams_of[8], (D, 2, FF_SH), D ** -0.5, 0.125, ((2, 4),)),
        "shared_down": gaussian(streams_of[9], (D, FF_SH), (FF_SH // 4) ** -0.5, 0.15625, ((1, 4),)),
        "expert_gate_up": gaussian(streams_of[10], (EXPERTS, D, 2, FF_E), D ** -0.5, 0.125, ((0, 8), (3, 4))),
        "expert_down": gaussian(streams_of[11], (EXPERTS, D, FF_E), (max(1, FF_E // (EXPERTS * EXPERTS))) ** -0.5, 1.25, ((0, 8), (2, 4))),
        "routes": choose_distinct(streams_of[12], TOKENS, EXPERTS, TOP, 4096),
        "priority": draw_priority(jax.random.fold_in(streams_of[16], 71), 0),
        "prefix": place_ends(jax.random.randint(streams_of[14], (SEQS,), SEQ // 10, SEQ // 2 + 1), jax.random.fold_in(streams_of[14], 1), SEQ // 10, (SEQ // 2 + 1) - 1).astype(jnp.int32),
        "cotangent": gaussian(streams_of[15], (TOKENS, D), 1.0, 6.0, ((0, 8),)),
    }


EPSILON = 1e-06
THETA = 1000000.0
HIGHEST = lax.Precision.HIGHEST

@jax.custom_vjp
def low(v):
    return lax.optimization_barrier(v.astype(jnp.bfloat16)).astype(jnp.float32)

@jax.custom_vjp
def low_back(v):
    return v

def low_keep(v):
    return (low(v), None)

def low_pass(kept, grad):
    return (grad,)

def back_keep(v):
    return (v, None)

def back_low(kept, grad):
    return (low(grad),)
low.defvjp(low_keep, low_pass)
low_back.defvjp(back_keep, back_low)

def rms_norm(values, gain_vec):
    factor = lax.rsqrt(lax.optimization_barrier(jnp.mean(values * values, axis=-1, keepdims=True)) + EPSILON)
    return values * factor * gain_vec

def rotary(values, positions):
    half_size = values.shape[-1] // 2
    frequency = THETA ** (-jnp.arange(half_size, dtype=jnp.float32) * 2.0 / values.shape[-1])
    angles = positions[:, None] * frequency[None, :]
    cosine = jnp.cos(angles)[:, None, :]
    sine_val = jnp.sin(angles)[:, None, :]
    first_half = values[..., :half_size]
    second_half = values[..., half_size:]
    return jnp.concatenate([first_half * cosine - second_half * sine_val, second_half * cosine + first_half * sine_val], axis=-1)

def attend_one(packed):
    queries, key_rows, value_rows, prefix_len = packed
    length = queries.shape[0]
    scores = low_back(jnp.einsum('qhd,khd->hqk', queries, key_rows, precision=HIGHEST) * queries.shape[-1] ** (-0.5))
    row_index = jnp.arange(length, dtype=jnp.int32)[:, None]
    col_index = jnp.arange(length, dtype=jnp.int32)[None, :]
    visible = (col_index <= row_index) | (col_index < prefix_len)
    scores = jnp.where(visible[None], scores, -1e+30)
    weights = low(jax.nn.softmax(scores, axis=-1))
    return jnp.einsum('hqk,khd->qhd', weights, value_rows, precision=HIGHEST)

def expert_one(packed):
    expert_rows, gate_up_weight, down_weight = packed
    group_width = FF_E // N_TP
    total_out = jnp.zeros(expert_rows.shape, jnp.float32)
    for group_index in range(N_TP):
        lower = group_index * group_width
        part_in = low_back(expert_rows)
        inner_pre = low_back(jnp.einsum('rd,dkf->rkf', part_in, gate_up_weight[:, :, lower:lower + group_width], precision=HIGHEST))
        hidden_units = low(jax.nn.silu(inner_pre[:, 0]) * inner_pre[:, 1])
        partial_out = jnp.dot(hidden_units, down_weight[:, lower:lower + group_width].T, precision=HIGHEST)
        total_out = total_out + low(low_back(partial_out))
    return total_out

def slots_one(route_rows, order_rows):
    assign_count = route_rows.shape[0] * route_rows.shape[1]
    flat_route = route_rows.reshape(assign_count)
    flat_order = order_rows.reshape(assign_count)
    by_order = jnp.zeros((assign_count,), jnp.int32).at[flat_order].set(flat_route)
    expert_hits = (by_order[:, None] == jnp.arange(EXPERTS, dtype=jnp.int32)[None, :]).astype(jnp.int32)
    before = (jnp.cumsum(expert_hits, axis=0) - expert_hits).astype(jnp.int32)
    sorted_slot = lax.optimization_barrier(jnp.sum(before * expert_hits, axis=1)).astype(jnp.int32)
    return sorted_slot[flat_order].reshape(route_rows.shape)

def reference(hidden, attn_gain, qkv_weight, qkv_bias, out_weight, mlp_gain, router_weight, share_gate, shared_gate_up, shared_down, expert_gate_up, expert_down, routes, priority, prefix, cotangent):
    expert_slots = N_EP * CAP
    slot_index = jax.vmap(slots_one)(routes.reshape(SEQS, SEQ, TOP), priority.reshape(SEQS, SEQ, TOP)).reshape(TOKENS, TOP)
    kept_mask = slot_index < CAP
    source = (jnp.arange(TOKENS, dtype=jnp.int32) // SEQ)[:, None]
    destination = jnp.where(kept_mask, routes * expert_slots + source * CAP + slot_index, EXPERTS * expert_slots).astype(jnp.int32)
    token_ids = jnp.broadcast_to(jnp.arange(TOKENS, dtype=jnp.int32)[:, None], (TOKENS, TOP))
    slot_token = jnp.full((EXPERTS * expert_slots + 1,), TOKENS, jnp.int32).at[destination.reshape(-1)].set(token_ids.reshape(-1))
    slot_token = slot_token[:EXPERTS * expert_slots].reshape(EXPERTS, expert_slots)
    kept_float = kept_mask.astype(jnp.float32)
    positions = (jnp.arange(TOKENS, dtype=jnp.int32) % SEQ).astype(jnp.float32)

    def to_sequences(values):
        return values.reshape(SEQS, SEQ, HEADS, HEAD_DIM)

    def forward(hidden_in, gain_one, qkv_w, qkv_b, out_w, gain_two, router_w, share_w, shared_gu, shared_dn, expert_gu, expert_dn):
        normed_one = low(rms_norm(hidden_in, gain_one))
        linear = low_back(jnp.einsum('td,dkh->tkh', normed_one, qkv_w, precision=HIGHEST))
        mixed_heads = (linear + qkv_b[None]).reshape(TOKENS, 3, HEADS, HEAD_DIM)
        queries = low(rotary(mixed_heads[:, 0], positions))
        key_rows = low(rotary(mixed_heads[:, 1], positions))
        value_rows = low(mixed_heads[:, 2])
        attended = lax.map(jax.checkpoint(attend_one), (to_sequences(queries), to_sequences(key_rows), to_sequences(value_rows), prefix))
        context = low(low_back(attended.reshape(TOKENS, D)))
        attn_out = low_back(jnp.dot(context, out_w.T, precision=HIGHEST))
        middle = hidden_in + attn_out
        normed_two = low(rms_norm(middle, gain_two))
        logits = low_back(jnp.dot(normed_two, router_w, precision=HIGHEST))
        router_probs = jax.nn.softmax(logits, axis=-1)
        gate_values = jnp.take_along_axis(router_probs, routes, axis=1) * kept_float
        gate_in = low_back(jnp.dot(normed_two, share_w, precision=HIGHEST))
        share_scale = jax.nn.sigmoid(gate_in)
        shared_pre = low_back(jnp.einsum('td,dkf->tkf', normed_two, shared_gu, precision=HIGHEST))
        shared_hidden = low(jax.nn.silu(shared_pre[:, 0]) * shared_pre[:, 1])
        shared_out = low_back(jnp.dot(shared_hidden, shared_dn.T, precision=HIGHEST))
        padded_rows = jnp.concatenate([normed_two, jnp.zeros((1, D), jnp.float32)], axis=0)
        dispatched = padded_rows[slot_token]
        results = lax.map(jax.checkpoint(expert_one), (dispatched, expert_gu, expert_dn))
        flat_results = jnp.concatenate([results.reshape(EXPERTS * expert_slots, D), jnp.zeros((1, D), jnp.float32)], axis=0)
        picked = flat_results[destination]
        routed = jnp.einsum('tk,tkd->td', gate_values, picked, precision=HIGHEST)
        return middle + share_scale[:, None] * shared_out + routed
    output, pullback = jax.vjp(forward, hidden.astype(jnp.float32), attn_gain.astype(jnp.float32), qkv_weight.astype(jnp.float32), qkv_bias.astype(jnp.float32), out_weight.astype(jnp.float32), mlp_gain.astype(jnp.float32), router_weight.astype(jnp.float32), share_gate.astype(jnp.float32), shared_gate_up.astype(jnp.float32), shared_down.astype(jnp.float32), expert_gate_up.astype(jnp.float32), expert_down.astype(jnp.float32))
    grad_in = pullback(cotangent.astype(jnp.float32))
    return (output.astype(jnp.bfloat16), grad_in[0].astype(jnp.bfloat16), grad_in[1], grad_in[2], grad_in[3], grad_in[4], grad_in[5], grad_in[6], grad_in[7], grad_in[8], grad_in[9], grad_in[10], grad_in[11])
```

```python
import jax
import jax.numpy as jnp
from jax import lax
from jax.sharding import PartitionSpec as P

HEAD_DIM = 128
EPSILON = 1e-06
THETA = 1000000.0
BF = jnp.bfloat16
F32 = jnp.float32


def mm(a, b, ca, cb):
    return lax.dot_general(a, b, (((ca,), (cb,)), ((), ())), preferred_element_type=F32)


def norm_factor(values):
    return lax.rsqrt(jnp.mean(values * values, axis=-1, keepdims=True) + EPSILON)


def swiglu_backward(hidden_grad, gate_pre, up_pre):
    sig = jax.nn.sigmoid(gate_pre)
    gate_grad = hidden_grad * up_pre * sig * (1.0 + gate_pre * (1.0 - sig))
    up_grad = hidden_grad * gate_pre * sig
    return gate_grad, up_grad


def angle_tables(length, head_size):
    half_size = head_size // 2
    frequency = THETA ** (-jnp.arange(half_size, dtype=F32) * 2.0 / head_size)
    angles = jnp.arange(length, dtype=F32)[:, None] * frequency[None, :]
    return jnp.cos(angles)[:, None, :], jnp.sin(angles)[:, None, :]


def rotate_forward(values, cosine, sine_val):
    half = values.shape[-1] // 2
    a, b = values[..., :half], values[..., half:]
    return jnp.concatenate([a * cosine - b * sine_val, b * cosine + a * sine_val], axis=-1)


def rotate_backward(grad_in, cosine, sine_val):
    half = grad_in.shape[-1] // 2
    a, b = grad_in[..., :half], grad_in[..., half:]
    return jnp.concatenate([a * cosine + b * sine_val, b * cosine - a * sine_val], axis=-1)


def masked_scores(queries, key_rows, prefix_len, head_size):
    length = queries.shape[0]
    scores = jnp.einsum(
        "qhd,khd->hqk", queries, key_rows, preferred_element_type=F32
    ) * head_size ** (-0.5)
    row_index = jnp.arange(length, dtype=jnp.int32)[:, None]
    col_index = jnp.arange(length, dtype=jnp.int32)[None, :]
    visible = (col_index <= row_index) | (col_index < prefix_len)
    return jnp.where(visible[None], scores, -1e30)


def swap(x, bit, n):
    return lax.ppermute(x, "tp", [(i, i ^ bit) for i in range(n)])


def tp_sum(x, n):
    half = x.shape[1] // 2
    low = (lax.axis_index("tp") % 2) == 0
    a, b = x[:, :half], x[:, half:]
    mine = jnp.where(low, a, b)
    theirs = jnp.where(low, b, a).astype(BF)
    one = (mine.astype(F32) + swap(theirs, 1, n).astype(F32)).astype(BF)
    two = (one.astype(F32) + swap(one, 2, n).astype(F32)).astype(BF)
    other = swap(two, 1, n)
    return jnp.concatenate([jnp.where(low, two, other), jnp.where(low, other, two)], axis=1).astype(F32)


def exchange(x, n):
    rows = x.shape[0] // n
    me = lax.axis_index("ep")
    out = jnp.zeros_like(x)
    out = lax.dynamic_update_slice_in_dim(
        out, lax.dynamic_slice_in_dim(x, me * rows, rows, 0), me * rows, 0
    )
    for shift in range(1, n):
        to = lax.rem(me + shift, n)
        came = lax.rem(me + n - shift, n)
        got = lax.ppermute(
            lax.dynamic_slice_in_dim(x, to * rows, rows, 0),
            "ep",
            [(i, (i + shift) % n) for i in range(n)],
        )
        out = lax.dynamic_update_slice_in_dim(out, got, came * rows, 0)
    return out


def body(
    hidden,
    attn_gain,
    qkv_weight,
    qkv_bias,
    out_weight,
    mlp_gain,
    router_weight,
    share_gate,
    shared_gate_up,
    shared_down,
    expert_gate_up,
    expert_down,
    routes,
    priority,
    prefix,
    cotangent,
):
    tokens, width = hidden.shape
    n_ep = lax.axis_size("ep")
    n_tp = lax.axis_size("tp")
    tp_i = lax.axis_index("tp")
    cols = width // n_tp
    col_start = tp_i * cols
    head_size = HEAD_DIM
    local_width = qkv_weight.shape[2]
    heads = local_width // head_size
    expert_local = expert_gate_up.shape[0]
    n_exp = expert_local * n_ep
    top = routes.shape[1]
    capacity = (5 * tokens * top + 4 * n_exp - 1) // (4 * n_exp)
    part = -(-capacity // n_tp)
    part_pad = -(-part // 16) * 16
    rows = n_exp * part_pad

    gu_t = jnp.transpose(expert_gate_up[0], (1, 2, 0))
    w_gate = lax.all_gather(gu_t[0], "tp", axis=0, tiled=True)
    w_up = lax.all_gather(gu_t[1], "tp", axis=0, tiled=True)
    w_down = lax.all_gather(jnp.transpose(expert_down[0], (1, 0)), "tp", axis=0, tiled=True)

    flat_route = routes.T.reshape(-1)
    flat_order = priority.T.reshape(-1)
    hits = (flat_route[:, None] == jnp.arange(n_exp, dtype=jnp.int32)[None, :]).astype(BF)
    smaller = (flat_order[None, :] < flat_order[:, None]).astype(BF)
    counts = mm(smaller, hits, 1, 0)
    slot = jnp.sum(counts * hits.astype(F32), axis=1).astype(jnp.int32).reshape(top, tokens)
    kept = slot < capacity
    in_part = slot - tp_i * part
    mine = kept & (in_part >= 0) & (in_part < part)
    dest = jnp.where(mine, routes.T * part_pad + in_part, -1)
    row_ids = jnp.arange(rows, dtype=jnp.int32)[:, None]
    place = (dest[0][None, :] == row_ids)
    for k in range(1, top):
        place = place | (dest[k][None, :] == row_ids)
    place = place.astype(BF)

    up_sent = mm(place, cotangent, 1, 0).astype(BF)
    up_rows = exchange(up_sent, n_ep)

    upstream = cotangent.astype(F32)
    residual_in = hidden.astype(F32)
    factor_one = norm_factor(residual_in)
    normed_one = (residual_in * factor_one * attn_gain).astype(BF)
    linear = jnp.einsum("td,dkh->tkh", normed_one, qkv_weight, preferred_element_type=F32)
    mixed_heads = (linear + qkv_bias[None]).reshape(tokens, 3, heads, head_size)
    cosine, sine_val = angle_tables(tokens, head_size)
    queries = rotate_forward(mixed_heads[:, 0], cosine, sine_val).astype(BF)
    key_rows = rotate_forward(mixed_heads[:, 1], cosine, sine_val).astype(BF)
    value_rows = mixed_heads[:, 2].astype(BF)
    scores = masked_scores(queries, key_rows, prefix[0], head_size)
    row_max = jnp.max(scores, axis=-1, keepdims=True)
    log_total = row_max + jnp.log(jnp.sum(jnp.exp(scores - row_max), axis=-1, keepdims=True))
    attn_probs = jnp.exp(scores - log_total).astype(BF)
    context = (
        jnp.einsum("hqk,khd->qhd", attn_probs, value_rows, preferred_element_type=F32)
        .astype(BF)
        .reshape(tokens, local_width)
    )
    attn_out = tp_sum(mm(context, out_weight, 1, 1), n_tp)
    middle = residual_in + attn_out
    factor_two = norm_factor(middle)
    normed_two = (middle * factor_two * mlp_gain).astype(BF)

    logits = mm(normed_two, router_weight, 1, 0)
    router_probs = jax.nn.softmax(logits, axis=-1)
    probs_hi = router_probs.astype(BF)
    probs_lo = (router_probs - probs_hi.astype(F32)).astype(BF)
    own = (row_ids // part_pad == jnp.arange(n_exp, dtype=jnp.int32)[None, :]).astype(F32)
    sent_rows = mm(place, normed_two, 1, 0).astype(BF)
    gate_hi = jnp.sum(mm(place, probs_hi, 1, 0) * own, axis=1, keepdims=True)
    gate_lo = jnp.sum(mm(place, probs_lo, 1, 0) * own, axis=1, keepdims=True)
    gate_sent = gate_hi + gate_lo
    lane = jnp.arange(128, dtype=jnp.int32)[None, :]
    gate_cols = jnp.where(lane == 0, gate_hi, jnp.where(lane == 1, gate_lo, 0.0)).astype(BF)
    got = exchange(jnp.concatenate([sent_rows, gate_cols], axis=1), n_ep)
    whole_rows = got[:, :width]
    gate_row = got[:, width : width + 1].astype(F32) + got[:, width + 1 : width + 2].astype(F32)

    gate_in = mm(normed_two, share_gate, 1, 0)
    share_scale = jax.nn.sigmoid(gate_in)
    shared_pre = jnp.einsum("td,dkf->tkf", normed_two, shared_gate_up, preferred_element_type=F32)
    shared_hidden = (jax.nn.silu(shared_pre[:, 0]) * shared_pre[:, 1]).astype(BF)
    shared_part = mm(shared_hidden, shared_down, 1, 1)
    shared_out_grad = (share_scale[:, None] * upstream).astype(BF)
    scale_grad_part = jnp.sum(upstream * shared_part, axis=1)
    shared_hidden_grad = mm(shared_out_grad, shared_down, 1, 0)
    sg, su = swiglu_backward(shared_hidden_grad, shared_pre[:, 0], shared_pre[:, 1])
    shared_pre_grad = jnp.stack([sg, su], axis=1).astype(BF)
    shared_back = jnp.einsum("tkf,dkf->td", shared_pre_grad, shared_gate_up, preferred_element_type=F32)
    sg, su = sg.astype(BF), su.astype(BF)
    shared_slab = lax.psum_scatter(
        jnp.concatenate(
            [
                mm(normed_two, sg, 0, 0).astype(BF),
                mm(normed_two, su, 0, 0).astype(BF),
                mm(shared_out_grad, shared_hidden, 0, 0).astype(BF),
            ],
            axis=1,
        ),
        "ep",
        scatter_dimension=0,
        tiled=True,
    ).astype(F32)
    sf = shared_hidden.shape[1]
    shared_gate_up_grad = jnp.stack([shared_slab[:, :sf], shared_slab[:, sf : 2 * sf]], axis=1)
    shared_down_grad = shared_slab[:, 2 * sf :]

    e_gate = mm(whole_rows, w_gate, 1, 1)
    e_up = mm(whole_rows, w_up, 1, 1)
    e_hidden = (jax.nn.silu(e_gate) * e_up).astype(BF)
    e_out = mm(e_hidden, w_down, 1, 0).astype(BF)
    row_grad = (gate_row * up_rows.astype(F32)).astype(BF)
    e_hidden_grad = mm(row_grad, w_down, 1, 1)
    eg, eu = swiglu_backward(e_hidden_grad, e_gate, e_up)
    eg, eu = eg.astype(BF), eu.astype(BF)
    back_sent = (mm(eg, w_gate, 1, 0) + mm(eu, w_up, 1, 0)).astype(BF)
    back_rows = exchange(back_sent, n_ep)
    out_rows = exchange(e_out, n_ep)
    d_down = lax.psum_scatter(mm(e_hidden, row_grad, 0, 0).astype(BF), "tp", scatter_dimension=0, tiled=True)
    d_gate = lax.psum_scatter(mm(eg, whole_rows, 0, 0).astype(BF), "tp", scatter_dimension=0, tiled=True)
    d_up = lax.psum_scatter(mm(eu, whole_rows, 0, 0).astype(BF), "tp", scatter_dimension=0, tiled=True)
    expert_down_grad = jnp.transpose(d_down.astype(F32), (1, 0))[None]
    expert_gate_up_grad = jnp.transpose(
        jnp.stack([d_gate, d_up], axis=0).astype(F32), (2, 0, 1)
    )[None]

    weighted_place = (place.astype(F32) * gate_sent).astype(BF)
    routed = mm(weighted_place, out_rows, 0, 0)
    out_cols = lax.psum_scatter(
        (share_scale[:, None] * shared_part + routed).astype(BF), "tp", scatter_dimension=1, tiled=True
    ).astype(F32)
    output = (lax.dynamic_slice_in_dim(middle, col_start, cols, 1) + out_cols).astype(BF)
    gate_grad_row = jnp.sum(up_sent.astype(F32) * out_rows.astype(F32), axis=1, keepdims=True)
    prob_part = mm(place, (gate_grad_row * own).astype(BF), 0, 0)
    pad = -(-(n_exp + 1) // 256) * 256 - n_exp - 1
    summed = tp_sum(
        jnp.concatenate(
            [
                shared_back + mm(place, back_rows, 0, 0),
                prob_part,
                scale_grad_part[:, None],
                jnp.zeros((tokens, pad), F32),
            ],
            axis=1,
        ),
        n_tp,
    )
    normed_two_grad = summed[:, :width]
    prob_grad = summed[:, width : width + n_exp]
    scale_grad = summed[:, width + n_exp]
    gate_in_grad = (scale_grad * share_scale * (1.0 - share_scale)).astype(BF)
    logit_grad = (
        router_probs * (prob_grad - jnp.sum(router_probs * prob_grad, axis=1, keepdims=True))
    ).astype(BF)
    normed_two_grad = (
        normed_two_grad
        + mm(logit_grad, router_weight, 1, 1)
        + gate_in_grad.astype(F32)[:, None] * share_gate.astype(F32)[None, :]
    )
    small_two = mm(
        jnp.concatenate([logit_grad, gate_in_grad[:, None]], axis=1), normed_two, 0, 0
    )
    mlp_gain_grad = jnp.sum(normed_two_grad * middle * factor_two, axis=0)
    scaled = normed_two_grad * mlp_gain
    middle_grad = upstream + factor_two * scaled - middle * (factor_two**3) * jnp.mean(
        scaled * middle, axis=-1, keepdims=True
    )
    small_sum = lax.psum(
        jnp.concatenate([small_two, mlp_gain_grad[None]], axis=0).astype(BF), "ep"
    ).astype(F32)
    router_sum = small_sum[:n_exp].T
    share_gate_sum = small_sum[n_exp]
    gain_two_sum = small_sum[n_exp + 1]

    attn_grad = middle_grad.astype(BF)
    context_grad = mm(attn_grad, out_weight, 1, 0).astype(BF).reshape(tokens, heads, head_size)
    attn_weights = jnp.exp(scores - log_total)
    prob_grad_att = jnp.einsum("qhd,khd->hqk", context_grad, value_rows, preferred_element_type=F32)
    value_grad = jnp.einsum(
        "hqk,qhd->khd", attn_weights.astype(BF), context_grad, preferred_element_type=F32
    )
    row_delta = jnp.sum(attn_weights * prob_grad_att, axis=-1, keepdims=True)
    score_grad = (attn_weights * (prob_grad_att - row_delta)).astype(BF)
    query_grad = jnp.einsum(
        "hqk,khd->qhd", score_grad, key_rows, preferred_element_type=F32
    ) * head_size ** (-0.5)
    key_grad = jnp.einsum(
        "hqk,qhd->khd", score_grad, queries, preferred_element_type=F32
    ) * head_size ** (-0.5)
    query_grad = rotate_backward(query_grad, cosine, sine_val)
    key_grad = rotate_backward(key_grad, cosine, sine_val)
    parts = [g.reshape(tokens, local_width) for g in (query_grad, key_grad, value_grad)]
    bias_grad = jnp.concatenate([jnp.sum(g, axis=0) for g in parts])
    linear_grad = jnp.concatenate([g.astype(BF) for g in parts], axis=1)
    attention_slab = lax.psum_scatter(
        jnp.concatenate(
            [mm(normed_one, linear_grad, 0, 0).astype(BF), mm(attn_grad, context, 0, 0).astype(BF)], axis=1
        ),
        "ep",
        scatter_dimension=0,
        tiled=True,
    ).astype(F32)
    qkv_weight_grad = attention_slab[:, : 3 * local_width].reshape(-1, 3, local_width)
    out_weight_grad = attention_slab[:, 3 * local_width :]
    w_t = jnp.transpose(qkv_weight, (1, 0, 2))
    normed_one_part = sum(
        mm(linear_grad[:, i * local_width : (i + 1) * local_width], w_t[i], 1, 1) for i in range(3)
    )
    normed_one_grad = tp_sum(normed_one_part, n_tp)
    attn_gain_grad = jnp.sum(normed_one_grad * residual_in * factor_one, axis=0)
    scaled = normed_one_grad * attn_gain
    input_grad = lax.dynamic_slice_in_dim(
        middle_grad
        + factor_one * scaled
        - residual_in * (factor_one**3) * jnp.mean(scaled * residual_in, axis=-1, keepdims=True),
        col_start,
        cols,
        1,
    ).astype(BF)
    last_sum = lax.psum(jnp.concatenate([attn_gain_grad, bias_grad]).astype(BF), "ep").astype(F32)
    gain_one_sum = last_sum[:width]
    bias_sum = last_sum[width:].reshape(3, local_width)
    return (
        output,
        input_grad,
        gain_one_sum,
        qkv_weight_grad,
        bias_sum,
        out_weight_grad,
        gain_two_sum,
        router_sum,
        share_gate_sum,
        shared_gate_up_grad,
        shared_down_grad,
        expert_gate_up_grad,
        expert_down_grad,
    )


def solution(mesh):
    return jax.shard_map(
        body,
        mesh=mesh,
        in_specs=(
            P("ep", None),
            P(),
            P(None, None, "tp"),
            P(None, "tp"),
            P(None, "tp"),
            P(),
            P(),
            P(),
            P(None, None, "tp"),
            P(None, "tp"),
            P("ep", None, None, "tp"),
            P("ep", None, "tp"),
            P("ep", None),
            P("ep", None),
            P("ep"),
            P("ep", None),
        ),
        out_specs=(
            P("ep", "tp"),
            P("ep", "tp"),
            P(),
            P("ep", None, "tp"),
            P(None, "tp"),
            P("ep", "tp"),
            P(),
            P(),
            P(),
            P("ep", None, "tp"),
            P("ep", "tp"),
            P("ep", None, None, "tp"),
            P("ep", None, "tp"),
        ),
        check_vma=False,
    )
```

```python
import functools

import jax
import jax.numpy as jnp
from jax import lax
from jax.experimental import pallas as pl
from jax.experimental.pallas import tpu as pltpu
from jax.sharding import PartitionSpec as P

HEAD_DIM = 128
EPSILON = 1e-06
THETA = 1000000.0
BF = jnp.bfloat16
F32 = jnp.float32


def mm(a, b, ca, cb):
    return lax.dot_general(a, b, (((ca,), (cb,)), ((), ())), preferred_element_type=F32)


def norm_factor(values):
    return lax.rsqrt(jnp.mean(values * values, axis=-1, keepdims=True) + EPSILON)


def swiglu_backward(hidden_grad, gate_pre, up_pre):
    sig = jax.nn.sigmoid(gate_pre)
    gate_grad = hidden_grad * up_pre * sig * (1.0 + gate_pre * (1.0 - sig))
    up_grad = hidden_grad * gate_pre * sig
    return gate_grad, up_grad


def angle_tables(length, head_size):
    half_size = head_size // 2
    frequency = THETA ** (-jnp.arange(half_size, dtype=F32) * 2.0 / head_size)
    angles = jnp.arange(length, dtype=F32)[:, None] * frequency[None, :]
    return jnp.cos(angles)[:, None, :], jnp.sin(angles)[:, None, :]


def rotate_forward(values, cosine, sine_val):
    half = values.shape[-1] // 2
    a, b = values[..., :half], values[..., half:]
    return jnp.concatenate([a * cosine - b * sine_val, b * cosine + a * sine_val], axis=-1)


def rotate_backward(grad_in, cosine, sine_val):
    half = grad_in.shape[-1] // 2
    a, b = grad_in[..., :half], grad_in[..., half:]
    return jnp.concatenate([a * cosine + b * sine_val, b * cosine - a * sine_val], axis=-1)


def masked_scores(queries, key_rows, prefix_len, head_size):
    length = queries.shape[0]
    scores = jnp.einsum(
        "qhd,khd->hqk", queries, key_rows, preferred_element_type=F32
    ) * head_size ** (-0.5)
    row_index = jnp.arange(length, dtype=jnp.int32)[:, None]
    col_index = jnp.arange(length, dtype=jnp.int32)[None, :]
    visible = (col_index <= row_index) | (col_index < prefix_len)
    return jnp.where(visible[None], scores, -1e30)


def swap(x, bit, n):
    return lax.ppermute(x, "tp", [(i, i ^ bit) for i in range(n)])


def tp_sum(x, n):
    half = x.shape[1] // 2
    low = (lax.axis_index("tp") % 2) == 0
    a, b = x[:, :half], x[:, half:]
    mine = jnp.where(low, a, b)
    theirs = jnp.where(low, b, a).astype(BF)
    one = (mine.astype(F32) + swap(theirs, 1, n).astype(F32)).astype(BF)
    two = (one.astype(F32) + swap(one, 2, n).astype(F32)).astype(BF)
    other = swap(two, 1, n)
    return jnp.concatenate([jnp.where(low, two, other), jnp.where(low, other, two)], axis=1).astype(F32)


def exchange(x, n, back=False):
    rows = x.shape[0] // n
    out = [x[:rows]]
    for shift in range(1, n):
        step = n - shift if back else shift
        out.append(
            lax.ppermute(
                x[shift * rows : (shift + 1) * rows], "ep", [(i, (i + step) % n) for i in range(n)]
            )
        )
    return jnp.concatenate(out, axis=0)

def ring_place(e, n):
    odd = e % 2
    return (1 - odd) * (e // 2) + odd * (n - 1 - e // 2)


def ring_member(p, n):
    second = p // (n // 2)
    return (1 - second) * 2 * p + second * (2 * (n - 1 - p) + 1)


def remote(src, dst, send_sem, recv_sem, axis, index):
    return pltpu.make_async_remote_copy(
        src_ref=src,
        dst_ref=dst,
        send_sem=send_sem,
        recv_sem=recv_sem,
        device_id={axis: index},
        device_id_type=pl.DeviceIdType.MESH,
    )


def greet(n, n_tp, ep, tp):
    barrier = pltpu.get_barrier_semaphore()
    for shift in range(1, n):
        pl.semaphore_signal(
            barrier, 1, device_id={"ep": lax.rem(ep + shift, n)}, device_id_type=pl.DeviceIdType.MESH
        )
    for shift in range(1, n_tp):
        pl.semaphore_signal(
            barrier, 1, device_id={"tp": lax.rem(tp + shift, n_tp)}, device_id_type=pl.DeviceIdType.MESH
        )
    pl.semaphore_wait(barrier, n - 1 + n_tp - 1)


def flip(index, bit):
    if bit == 1:
        return index + 1 - 2 * (index % 2)
    return index + 2 - 4 * ((index // 2) % 2)


def tail_kernel(
    n,
    n_tp,
    n1t,
    lg,
    agt,
    ctx,
    w,
    h_cols,
    r_one,
    gain,
    mid_cols,
    bias,
    small,
    qkv_out,
    o_out,
    in_out,
    gain_out,
    bias_out,
    small_out,
    ring_recv,
    ring_send,
    part_own,
    part_send,
    part_recv,
    y_send,
    y_recv,
    mean_send,
    mean_recv,
    vec_send,
    vec_recv,
    small_send,
    small_recv,
    gain_send,
    gain_recv,
    ring_ss,
    ring_rs,
    tp_ss,
    tp_rs,
    vec_ss,
    vec_rs,
    small_ss,
    small_rs,
    gain_ss,
    gain_rs,
):
    ep = lax.axis_index("ep")
    tp = lax.axis_index("tp")
    tokens, lw = ctx.shape
    rows = n1t.shape[0] // n
    width = n1t.shape[0]
    p = ring_place(ep, n)
    nxt = ring_member(lax.rem(p + 1, n), n)
    prv = ring_member(lax.rem(p + n - 1, n), n)
    core_peer, y_peer = flip(tp, 1), flip(tp, 2)
    greet(n, n_tp, ep, tp)

    def small_copy(shift):
        to = lax.rem(ep + shift, n)
        return remote(
            small_send, small_recv.at[ep], small_ss.at[shift], small_rs.at[shift], "ep", to
        )

    def small_wait(shift):
        came = lax.rem(ep + n - shift, n)
        return remote(
            small_send, small_recv.at[came], small_ss.at[shift], small_rs.at[shift], "ep", came
        )

    def block_of(ring, step):
        if ring < 2:
            return ring_member(lax.rem(p + 2 * n - 1 - step, n), n)
        return ring_member(lax.rem(p + 1 + step, n), n)

    def term(ring, owner):
        at = pl.ds(pl.multiple_of(owner * rows, rows), rows)
        if ring == 1:
            return jnp.dot(agt[at, :], ctx[...], preferred_element_type=F32)
        k = {0: 0, 2: 1, 3: 2}[ring]
        return jnp.dot(n1t[at, :], lg[:, k * lw : (k + 1) * lw], preferred_element_type=F32)

    def ring_copy(ring, step, slot):
        return remote(
            ring_send.at[ring, slot],
            ring_recv.at[ring, step],
            ring_ss.at[ring, slot],
            ring_rs.at[ring, step],
            "ep",
            nxt if ring < 2 else prv,
        )

    def ring_step(step, first):
        for ring in range(4):
            slot = lax.rem(step, 2)
            mine = term(ring, block_of(ring, step))
            ring_copy(ring, step - 1, slot).wait_recv()
            if not first:
                ring_copy(ring, step - 2, slot).wait_send()
            ring_send[ring, slot] = (mine + ring_recv[ring, step - 1].astype(F32)).astype(BF)
            ring_copy(ring, step, slot).start()

    for ring in range(4):
        ring_send[ring, 0] = term(ring, block_of(ring, 0)).astype(BF)
        ring_copy(ring, 0, 0).start()

    def part_block(column, store):
        for m in range(0, tokens, 128):
            total = None
            for k in range(3):
                d = lax.dot_general(
                    lg[m : m + 128, k * lw : (k + 1) * lw],
                    w[k, pl.ds(pl.multiple_of(column * lw, lw), lw), :],
                    (((1,), (1,)), ((), ())),
                    preferred_element_type=F32,
                )
                total = d if total is None else total + d
            store(m, total)

    def tp_copy(i, src, dst, peer):
        return remote(src, dst, tp_ss.at[i], tp_rs.at[i], "tp", peer)

    first = [tp_copy(i, part_send.at[i], part_recv.at[i], core_peer) for i in range(2)]
    for i in range(2):

        def put(m, total, i=i):
            part_send[i, m : m + 128, :] = total.astype(BF)

        part_block((core_peer % 2) + 2 * i, put)
        first[i].start()

    ring_step(1, True)

    small_send[...] = small[...]
    small_recv[ep] = small[...]
    for shift in range(1, n):
        small_copy(shift).start()

    def put_own(m, total):
        part_own[m : m + 128, :] = total

    other = (tp // 2) * -1 + 1
    part_block((tp % 2) + 2 * other, put_own)
    for i in range(2):
        first[i].wait()
    y_send[...] = (part_own[...] + part_recv[other].astype(F32)).astype(BF)
    second = tp_copy(2, y_send, y_recv, y_peer)
    second.start()

    ring_step(2, False)

    part_block(tp, put_own)
    second.wait()
    for m in range(0, tokens, 128):
        at = slice(m, m + 128)
        grad = (
            part_own[at, :]
            + part_recv[tp // 2, at, :].astype(F32)
            + y_recv[at, :].astype(F32)
        )
        part_own[at, :] = grad
        hid = h_cols[at, :].astype(F32)
        mean = jnp.sum(grad * gain[...] * hid, axis=1, keepdims=True)
        mean_send[0, at, :] = jnp.broadcast_to(mean, (128, 128))
        col = jnp.sum(grad * hid * r_one[at, :], axis=0, keepdims=True)
        if m == 0:
            vec_send[:, :lw] = col
        else:
            vec_send[:, :lw] += col
    third = tp_copy(3, mean_send.at[0], mean_recv.at[0], core_peer)
    third.start()
    vec_send[:, lw:] = bias[...]
    vec_recv[ep] = vec_send[...]

    def vec_copy(shift, way):
        to = lax.rem(ep + shift, n)
        came = lax.rem(ep + n - shift, n)
        if way == "out":
            return remote(vec_send, vec_recv.at[ep], vec_ss.at[shift], vec_rs.at[shift], "ep", to)
        return remote(vec_send, vec_recv.at[came], vec_ss.at[shift], vec_rs.at[shift], "ep", came)

    for shift in range(1, n):
        vec_copy(shift, "out").start()

    ring_step(3, False)

    third.wait()
    mean_send[1] = mean_send[0] + mean_recv[0]
    fourth = tp_copy(4, mean_send.at[1], mean_recv.at[1], y_peer)
    fourth.start()

    ring_step(4, False)

    fourth.wait()
    for m in range(0, tokens, 128):
        at = slice(m, m + 128)
        mean = (mean_send[1, at, :1] + mean_recv[1, at, :1]) * (1.0 / width)
        r = r_one[at, :]
        in_out[at, :] = (
            mid_cols[at, :]
            + r * part_own[at, :] * gain[...]
            - h_cols[at, :].astype(F32) * (r * r * r) * mean
        ).astype(BF)
    for shift in range(1, n):
        vec_copy(shift, "in").wait()
    total = vec_recv[0]
    for e in range(1, n):
        total = total + vec_recv[e]
    bias_out[...] = total[:, lw:]
    gain_send[...] = total[:, :lw]
    gain_recv[tp] = total[:, :lw]

    def gain_copy(shift, way):
        to = lax.rem(tp + shift, n_tp)
        came = lax.rem(tp + n_tp - shift, n_tp)
        if way == "out":
            return remote(gain_send, gain_recv.at[tp], gain_ss.at[shift], gain_rs.at[shift], "tp", to)
        return remote(gain_send, gain_recv.at[came], gain_ss.at[shift], gain_rs.at[shift], "tp", came)

    for shift in range(1, n_tp):
        gain_copy(shift, "out").start()

    @pl.loop(5, n - 1)
    def _(step):
        ring_step(step, False)

    for shift in range(1, n):
        small_wait(shift).wait()
    total = small_recv[0].astype(F32)
    for e in range(1, n):
        total = total + small_recv[e].astype(F32)
    small_out[...] = total
    for shift in range(1, n_tp):
        gain_copy(shift, "in").wait()
    for j in range(n_tp):
        gain_out[:, j * lw : (j + 1) * lw] = gain_recv[j]

    for ring in range(4):
        mine = term(ring, ep)
        ring_copy(ring, n - 2, 0).wait_recv()
        done = mine + ring_recv[ring, n - 2].astype(F32)
        if ring == 1:
            o_out[...] = done
        else:
            qkv_out[{0: 0, 2: 1, 3: 2}[ring]] = done
    for ring in range(4):
        for step in (n - 3, n - 2):
            ring_copy(ring, step, step % 2).wait_send()


def tail(n, n_tp, n1t, lg, agt, ctx, w, h_cols, r_one, gain, mid_cols, bias, small):
    width, tokens = n1t.shape
    lw = ctx.shape[1]
    rows = width // n
    wide = small.shape[0]
    vmem = pl.BlockSpec(memory_space=pltpu.VMEM)
    dma = pltpu.SemaphoreType.DMA
    return pl.pallas_call(
        functools.partial(tail_kernel, n, n_tp),
        out_shape=(
            jax.ShapeDtypeStruct((3, rows, lw), F32),
            jax.ShapeDtypeStruct((rows, lw), F32),
            jax.ShapeDtypeStruct((tokens, lw), BF),
            jax.ShapeDtypeStruct((1, width), F32),
            jax.ShapeDtypeStruct((1, 3 * lw), F32),
            jax.ShapeDtypeStruct((wide, width), F32),
        ),
        in_specs=[vmem] * 11,
        out_specs=[vmem] * 6,
        scratch_shapes=[
            pltpu.VMEM((4, n - 1, rows, lw), BF),
            pltpu.VMEM((4, 2, rows, lw), BF),
            pltpu.VMEM((tokens, lw), F32),
            pltpu.VMEM((2, tokens, lw), BF),
            pltpu.VMEM((2, tokens, lw), BF),
            pltpu.VMEM((tokens, lw), BF),
            pltpu.VMEM((tokens, lw), BF),
            pltpu.VMEM((2, tokens, 128), F32),
            pltpu.VMEM((2, tokens, 128), F32),
            pltpu.VMEM((1, 4 * lw), F32),
            pltpu.VMEM((n, 1, 4 * lw), F32),
            pltpu.VMEM((wide, width), BF),
            pltpu.VMEM((n, wide, width), BF),
            pltpu.VMEM((1, lw), F32),
            pltpu.VMEM((n_tp, 1, lw), F32),
            dma((4, 2)),
            dma((4, n - 1)),
            dma((5,)),
            dma((5,)),
            dma((n,)),
            dma((n,)),
            dma((n,)),
            dma((n,)),
            dma((n_tp,)),
            dma((n_tp,)),
        ],
        compiler_params=pltpu.CompilerParams(
            collective_id=0, has_side_effects=True, vmem_limit_bytes=56 * 2**20
        ),
        cost_estimate=pl.CostEstimate(
            flops=2 * tokens * width * 7 * lw, bytes_accessed=30 * 2**20, transcendentals=0
        ),
    )(n1t, lg, agt, ctx, w, h_cols, r_one, gain, mid_cols, bias, small)


def body(
    hidden,
    attn_gain,
    qkv_weight,
    qkv_bias,
    out_weight,
    mlp_gain,
    router_weight,
    share_gate,
    shared_gate_up,
    shared_down,
    expert_gate_up,
    expert_down,
    routes,
    priority,
    prefix,
    cotangent,
):
    tokens, width = hidden.shape
    n_ep = lax.axis_size("ep")
    n_tp = lax.axis_size("tp")
    tp_i = lax.axis_index("tp")
    cols = width // n_tp
    col_start = tp_i * cols
    head_size = HEAD_DIM
    local_width = qkv_weight.shape[2]
    heads = local_width // head_size
    expert_local = expert_gate_up.shape[0]
    n_exp = expert_local * n_ep
    top = routes.shape[1]
    capacity = (5 * tokens * top + 4 * n_exp - 1) // (4 * n_exp)
    part = -(-capacity // n_tp)
    part_pad = -(-part // 16) * 16
    rows = n_exp * part_pad

    gu_t = jnp.transpose(expert_gate_up[0], (1, 2, 0))
    w_gate = lax.all_gather(gu_t[0], "tp", axis=0, tiled=True)
    w_up = lax.all_gather(gu_t[1], "tp", axis=0, tiled=True)
    w_down = lax.all_gather(jnp.transpose(expert_down[0], (1, 0)), "tp", axis=0, tiled=True)

    flat_route = routes.T.reshape(-1)
    flat_order = priority.T.reshape(-1)
    hits = (flat_route[:, None] == jnp.arange(n_exp, dtype=jnp.int32)[None, :]).astype(BF)
    smaller = (flat_order[None, :] < flat_order[:, None]).astype(BF)
    counts = mm(smaller, hits, 1, 0)
    slot = jnp.sum(counts * hits.astype(F32), axis=1).astype(jnp.int32).reshape(top, tokens)
    kept = slot < capacity
    in_part = slot - tp_i * part
    mine = kept & (in_part >= 0) & (in_part < part)
    ep_i = lax.axis_index("ep")
    hop = lax.rem(routes.T + n_exp - ep_i * expert_local, n_exp)
    dest = jnp.where(mine, hop * part_pad + in_part, -1)
    row_ids = jnp.arange(rows, dtype=jnp.int32)[:, None]
    place = (dest[0][None, :] == row_ids)
    for k in range(1, top):
        place = place | (dest[k][None, :] == row_ids)
    place = place.astype(BF)

    up_sent = mm(place, cotangent, 1, 0).astype(BF)
    up_rows = exchange(up_sent, n_ep)

    upstream = cotangent.astype(F32)
    residual_in = hidden.astype(F32)
    factor_one = norm_factor(residual_in)
    normed_one = (residual_in * factor_one * attn_gain).astype(BF)
    linear = jnp.einsum("td,dkh->tkh", normed_one, qkv_weight, preferred_element_type=F32)
    mixed_heads = (linear + qkv_bias[None]).reshape(tokens, 3, heads, head_size)
    cosine, sine_val = angle_tables(tokens, head_size)
    queries = rotate_forward(mixed_heads[:, 0], cosine, sine_val).astype(BF)
    key_rows = rotate_forward(mixed_heads[:, 1], cosine, sine_val).astype(BF)
    value_rows = mixed_heads[:, 2].astype(BF)
    scores = masked_scores(queries, key_rows, prefix[0], head_size)
    row_max = jnp.max(scores, axis=-1, keepdims=True)
    log_total = row_max + jnp.log(jnp.sum(jnp.exp(scores - row_max), axis=-1, keepdims=True))
    attn_probs = jnp.exp(scores - log_total).astype(BF)
    context = (
        jnp.einsum("hqk,khd->qhd", attn_probs, value_rows, preferred_element_type=F32)
        .astype(BF)
        .reshape(tokens, local_width)
    )
    attn_out = tp_sum(mm(context, out_weight, 1, 1), n_tp)
    middle = residual_in + attn_out
    factor_two = norm_factor(middle)
    normed_two = (middle * factor_two * mlp_gain).astype(BF)

    logits = mm(normed_two, router_weight, 1, 0)
    router_probs = jax.nn.softmax(logits, axis=-1)
    probs_hi = router_probs.astype(BF)
    probs_lo = (router_probs - probs_hi.astype(F32)).astype(BF)
    row_expert = lax.rem(row_ids // part_pad + ep_i * expert_local, n_exp)
    own = (row_expert == jnp.arange(n_exp, dtype=jnp.int32)[None, :]).astype(F32)
    sent_rows = mm(place, normed_two, 1, 0).astype(BF)
    gate_hi = jnp.sum(mm(place, probs_hi, 1, 0) * own, axis=1, keepdims=True)
    gate_lo = jnp.sum(mm(place, probs_lo, 1, 0) * own, axis=1, keepdims=True)
    gate_sent = gate_hi + gate_lo
    lane = jnp.arange(128, dtype=jnp.int32)[None, :]
    gate_cols = jnp.where(lane == 0, gate_hi, jnp.where(lane == 1, gate_lo, 0.0)).astype(BF)
    got = exchange(jnp.concatenate([sent_rows, gate_cols], axis=1), n_ep)
    whole_rows = got[:, :width]
    gate_row = got[:, width : width + 1].astype(F32) + got[:, width + 1 : width + 2].astype(F32)

    gate_in = mm(normed_two, share_gate, 1, 0)
    share_scale = jax.nn.sigmoid(gate_in)
    shared_pre = jnp.einsum("td,dkf->tkf", normed_two, shared_gate_up, preferred_element_type=F32)
    shared_hidden = (jax.nn.silu(shared_pre[:, 0]) * shared_pre[:, 1]).astype(BF)
    shared_part = mm(shared_hidden, shared_down, 1, 1)
    shared_out_grad = (share_scale[:, None] * upstream).astype(BF)
    scale_grad_part = jnp.sum(upstream * shared_part, axis=1)
    shared_hidden_grad = mm(shared_out_grad, shared_down, 1, 0)
    sg, su = swiglu_backward(shared_hidden_grad, shared_pre[:, 0], shared_pre[:, 1])
    shared_pre_grad = jnp.stack([sg, su], axis=1).astype(BF)
    shared_back = jnp.einsum("tkf,dkf->td", shared_pre_grad, shared_gate_up, preferred_element_type=F32)
    sg, su = sg.astype(BF), su.astype(BF)
    slab = jnp.concatenate(
        [
            mm(normed_two, sg, 0, 0).astype(BF),
            mm(normed_two, su, 0, 0).astype(BF),
            mm(shared_out_grad, shared_hidden, 0, 0).astype(BF),
        ],
        axis=1,
    )
    slab, whole_rows, gate_row = lax.optimization_barrier((slab, whole_rows, gate_row))
    shared_slab = lax.psum_scatter(slab, "ep", scatter_dimension=0, tiled=True).astype(F32)
    sf = shared_hidden.shape[1]
    shared_gate_up_grad = jnp.stack([shared_slab[:, :sf], shared_slab[:, sf : 2 * sf]], axis=1)
    shared_down_grad = shared_slab[:, 2 * sf :]

    e_gate = mm(whole_rows, w_gate, 1, 1)
    e_up = mm(whole_rows, w_up, 1, 1)
    e_hidden = (jax.nn.silu(e_gate) * e_up).astype(BF)
    e_out = mm(e_hidden, w_down, 1, 0).astype(BF)
    row_grad = (gate_row * up_rows.astype(F32)).astype(BF)
    e_hidden_grad = mm(row_grad, w_down, 1, 1)
    eg, eu = swiglu_backward(e_hidden_grad, e_gate, e_up)
    eg, eu = eg.astype(BF), eu.astype(BF)
    back_sent = (mm(eg, w_gate, 1, 0) + mm(eu, w_up, 1, 0)).astype(BF)
    back_rows = exchange(back_sent, n_ep, True)
    out_rows = exchange(e_out, n_ep, True)
    d_down = lax.psum_scatter(mm(e_hidden, row_grad, 0, 0).astype(BF), "tp", scatter_dimension=0, tiled=True)
    d_gate = lax.psum_scatter(mm(eg, whole_rows, 0, 0).astype(BF), "tp", scatter_dimension=0, tiled=True)
    d_up = lax.psum_scatter(mm(eu, whole_rows, 0, 0).astype(BF), "tp", scatter_dimension=0, tiled=True)
    expert_down_grad = jnp.transpose(d_down.astype(F32), (1, 0))[None]
    expert_gate_up_grad = jnp.transpose(
        jnp.stack([d_gate, d_up], axis=0).astype(F32), (2, 0, 1)
    )[None]

    weighted_place = (place.astype(F32) * gate_sent).astype(BF)
    routed = mm(weighted_place, out_rows, 0, 0)
    out_cols = lax.psum_scatter(
        (share_scale[:, None] * shared_part + routed).astype(BF), "tp", scatter_dimension=1, tiled=True
    ).astype(F32)
    output = (lax.dynamic_slice_in_dim(middle, col_start, cols, 1) + out_cols).astype(BF)
    gate_grad_row = jnp.sum(up_sent.astype(F32) * out_rows.astype(F32), axis=1, keepdims=True)
    prob_part = mm(place, (gate_grad_row * own).astype(BF), 0, 0)
    pad = -(-(n_exp + 1) // 256) * 256 - n_exp - 1
    summed = tp_sum(
        jnp.concatenate(
            [
                shared_back + mm(place, back_rows, 0, 0),
                prob_part,
                scale_grad_part[:, None],
                jnp.zeros((tokens, pad), F32),
            ],
            axis=1,
        ),
        n_tp,
    )
    normed_two_grad = summed[:, :width]
    prob_grad = summed[:, width : width + n_exp]
    scale_grad = summed[:, width + n_exp]
    gate_in_grad = (scale_grad * share_scale * (1.0 - share_scale)).astype(BF)
    logit_grad = (
        router_probs * (prob_grad - jnp.sum(router_probs * prob_grad, axis=1, keepdims=True))
    ).astype(BF)
    normed_two_grad = (
        normed_two_grad
        + mm(logit_grad, router_weight, 1, 1)
        + gate_in_grad.astype(F32)[:, None] * share_gate.astype(F32)[None, :]
    )
    small_two = mm(
        jnp.concatenate([logit_grad, gate_in_grad[:, None]], axis=1), normed_two, 0, 0
    )
    mlp_gain_grad = jnp.sum(normed_two_grad * middle * factor_two, axis=0)
    scaled = normed_two_grad * mlp_gain
    middle_grad = upstream + factor_two * scaled - middle * (factor_two**3) * jnp.mean(
        scaled * middle, axis=-1, keepdims=True
    )
    small_pad = -(-(n_exp + 2) // 16) * 16 - n_exp - 2
    small = jnp.concatenate(
        [small_two, mlp_gain_grad[None], jnp.zeros((small_pad, width), F32)], axis=0
    ).astype(BF)

    attn_grad = middle_grad.astype(BF)
    context_grad = mm(attn_grad, out_weight, 1, 0).astype(BF).reshape(tokens, heads, head_size)
    attn_weights = jnp.exp(scores - log_total)
    prob_grad_att = jnp.einsum("qhd,khd->hqk", context_grad, value_rows, preferred_element_type=F32)
    value_grad = jnp.einsum(
        "hqk,qhd->khd", attn_weights.astype(BF), context_grad, preferred_element_type=F32
    )
    row_delta = jnp.sum(attn_weights * prob_grad_att, axis=-1, keepdims=True)
    score_grad = (attn_weights * (prob_grad_att - row_delta)).astype(BF)
    query_grad = jnp.einsum(
        "hqk,khd->qhd", score_grad, key_rows, preferred_element_type=F32
    ) * head_size ** (-0.5)
    key_grad = jnp.einsum(
        "hqk,qhd->khd", score_grad, queries, preferred_element_type=F32
    ) * head_size ** (-0.5)
    query_grad = rotate_backward(query_grad, cosine, sine_val)
    key_grad = rotate_backward(key_grad, cosine, sine_val)
    parts = [g.reshape(tokens, local_width) for g in (query_grad, key_grad, value_grad)]
    bias_grad = jnp.concatenate([jnp.sum(g, axis=0) for g in parts])
    linear_grad = jnp.concatenate([g.astype(BF) for g in parts], axis=1)
    qkv_grad, out_weight_grad, input_grad, gain_one, bias_sum, small_sum = tail(
        n_ep,
        n_tp,
        normed_one.T,
        linear_grad,
        attn_grad.T,
        context,
        jnp.transpose(qkv_weight, (1, 0, 2)),
        lax.dynamic_slice_in_dim(hidden, col_start, cols, 1),
        factor_one,
        lax.dynamic_slice_in_dim(attn_gain, col_start, cols, 0)[None],
        lax.dynamic_slice_in_dim(middle_grad, col_start, cols, 1),
        bias_grad[None],
        small,
    )
    qkv_weight_grad = jnp.transpose(qkv_grad, (1, 0, 2))
    gain_one_sum = gain_one[0]
    bias_sum = bias_sum.reshape(3, local_width)
    router_sum = small_sum[:n_exp].T
    share_gate_sum = small_sum[n_exp]
    gain_two_sum = small_sum[n_exp + 1]
    return (
        output,
        input_grad,
        gain_one_sum,
        qkv_weight_grad,
        bias_sum,
        out_weight_grad,
        gain_two_sum,
        router_sum,
        share_gate_sum,
        shared_gate_up_grad,
        shared_down_grad,
        expert_gate_up_grad,
        expert_down_grad,
    )


def solution(mesh):
    return jax.shard_map(
        body,
        mesh=mesh,
        in_specs=(
            P("ep", None),
            P(),
            P(None, None, "tp"),
            P(None, "tp"),
            P(None, "tp"),
            P(),
            P(),
            P(),
            P(None, None, "tp"),
            P(None, "tp"),
            P("ep", None, None, "tp"),
            P("ep", None, "tp"),
            P("ep", None),
            P("ep", None),
            P("ep"),
            P("ep", None),
        ),
        out_specs=(
            P("ep", "tp"),
            P("ep", "tp"),
            P(),
            P("ep", None, "tp"),
            P(None, "tp"),
            P("ep", "tp"),
            P(),
            P(),
            P(),
            P("ep", None, "tp"),
            P("ep", "tp"),
            P("ep", None, None, "tp"),
            P("ep", None, "tp"),
        ),
        check_vma=False,
    )
```

```python
import functools

import jax
import jax.numpy as jnp
from jax import lax
from jax.experimental import pallas as pl
from jax.experimental.pallas import tpu as pltpu
from jax.sharding import PartitionSpec as P

HEAD_DIM = 128
EPSILON = 1e-06
THETA = 1000000.0
BF = jnp.bfloat16
F32 = jnp.float32


def mm(a, b, ca, cb):
    return lax.dot_general(a, b, (((ca,), (cb,)), ((), ())), preferred_element_type=F32)


def norm_factor(values):
    return lax.rsqrt(jnp.mean(values * values, axis=-1, keepdims=True) + EPSILON)


def swiglu_backward(hidden_grad, gate_pre, up_pre):
    sig = jax.nn.sigmoid(gate_pre)
    gate_grad = hidden_grad * up_pre * sig * (1.0 + gate_pre * (1.0 - sig))
    up_grad = hidden_grad * gate_pre * sig
    return gate_grad, up_grad


def angle_tables(length, head_size):
    half_size = head_size // 2
    frequency = THETA ** (-jnp.arange(half_size, dtype=F32) * 2.0 / head_size)
    angles = jnp.arange(length, dtype=F32)[:, None] * frequency[None, :]
    return jnp.cos(angles)[:, None, :], jnp.sin(angles)[:, None, :]


def rotate_forward(values, cosine, sine_val):
    half = values.shape[-1] // 2
    a, b = values[..., :half], values[..., half:]
    return jnp.concatenate([a * cosine - b * sine_val, b * cosine + a * sine_val], axis=-1)


def rotate_backward(grad_in, cosine, sine_val):
    half = grad_in.shape[-1] // 2
    a, b = grad_in[..., :half], grad_in[..., half:]
    return jnp.concatenate([a * cosine + b * sine_val, b * cosine - a * sine_val], axis=-1)


def masked_scores(queries, key_rows, prefix_len, head_size):
    length = queries.shape[0]
    scores = jnp.einsum(
        "qhd,khd->hqk", queries, key_rows, preferred_element_type=F32
    ) * head_size ** (-0.5)
    row_index = jnp.arange(length, dtype=jnp.int32)[:, None]
    col_index = jnp.arange(length, dtype=jnp.int32)[None, :]
    visible = (col_index <= row_index) | (col_index < prefix_len)
    return jnp.where(visible[None], scores, -1e30)


def swap(x, bit, n):
    return lax.ppermute(x, "tp", [(i, i ^ bit) for i in range(n)])


def tp_sum(x, n):
    half = x.shape[1] // 2
    low = (lax.axis_index("tp") % 2) == 0
    a, b = x[:, :half], x[:, half:]
    mine = jnp.where(low, a, b)
    theirs = jnp.where(low, b, a).astype(BF)
    one = (mine.astype(F32) + swap(theirs, 1, n).astype(F32)).astype(BF)
    two = (one.astype(F32) + swap(one, 2, n).astype(F32)).astype(BF)
    other = swap(two, 1, n)
    return jnp.concatenate([jnp.where(low, two, other), jnp.where(low, other, two)], axis=1).astype(F32)


def tp_scatter(x, n):
    me = lax.axis_index("tp")
    cols = x.shape[1] // n

    def block(bits):
        return lax.dynamic_slice_in_dim(x, (me ^ bits) * cols, cols, 1)

    one = swap(jnp.concatenate([block(1), block(3)], axis=0).astype(BF), 1, n).astype(F32)
    rows = x.shape[0]
    two = swap((block(2) + one[rows:]).astype(BF), 2, n)
    return block(0) + one[:rows] + two.astype(F32)


def exchange(x, n, back=False):
    rows = x.shape[0] // n
    out = [x[:rows]]
    for shift in range(1, n):
        step = n - shift if back else shift
        out.append(
            lax.ppermute(
                x[shift * rows : (shift + 1) * rows], "ep", [(i, (i + step) % n) for i in range(n)]
            )
        )
    return jnp.concatenate(out, axis=0)

def ring_place(e, n):
    odd = e % 2
    return (1 - odd) * (e // 2) + odd * (n - 1 - e // 2)


def ring_member(p, n):
    second = p // (n // 2)
    return (1 - second) * 2 * p + second * (2 * (n - 1 - p) + 1)


def remote(src, dst, send_sem, recv_sem, axis, index):
    return pltpu.make_async_remote_copy(
        src_ref=src,
        dst_ref=dst,
        send_sem=send_sem,
        recv_sem=recv_sem,
        device_id={axis: index},
        device_id_type=pl.DeviceIdType.MESH,
    )


def greet(n, n_tp, ep, tp):
    barrier = pltpu.get_barrier_semaphore()
    for shift in range(1, n):
        pl.semaphore_signal(
            barrier, 1, device_id={"ep": lax.rem(ep + shift, n)}, device_id_type=pl.DeviceIdType.MESH
        )
    for shift in range(1, n_tp):
        pl.semaphore_signal(
            barrier, 1, device_id={"tp": lax.rem(tp + shift, n_tp)}, device_id_type=pl.DeviceIdType.MESH
        )
    pl.semaphore_wait(barrier, n - 1 + n_tp - 1)


def flip(index, bit):
    if bit == 1:
        return index + 1 - 2 * (index % 2)
    return index + 2 - 4 * ((index // 2) % 2)


def tail_kernel(
    n,
    n_tp,
    n1,
    lg,
    ag,
    ctx,
    w,
    h_cols,
    r_one,
    gain,
    mid_cols,
    bias,
    small,
    qkv_out,
    o_out,
    in_out,
    gain_out,
    bias_out,
    small_out,
    ring_recv,
    ring_send,
    part_own,
    part_send,
    part_recv,
    y_send,
    y_recv,
    mean_send,
    mean_recv,
    vec_send,
    vec_recv,
    small_send,
    small_recv,
    gain_send,
    gain_recv,
    ring_ss,
    ring_rs,
    tp_ss,
    tp_rs,
    vec_ss,
    vec_rs,
    small_ss,
    small_rs,
    gain_ss,
    gain_rs,
):
    ep = lax.axis_index("ep")
    tp = lax.axis_index("tp")
    tokens, lw = ctx.shape
    rows = qkv_out.shape[1]
    width = rows * n
    p = ring_place(ep, n)
    nxt = ring_member(lax.rem(p + 1, n), n)
    prv = ring_member(lax.rem(p + n - 1, n), n)
    core_peer, y_peer = flip(tp, 1), flip(tp, 2)
    greet(n, n_tp, ep, tp)

    def small_copy(shift):
        to = lax.rem(ep + shift, n)
        return remote(
            small_send, small_recv.at[ep], small_ss.at[shift], small_rs.at[shift], "ep", to
        )

    def small_wait(shift):
        came = lax.rem(ep + n - shift, n)
        return remote(
            small_send, small_recv.at[came], small_ss.at[shift], small_rs.at[shift], "ep", came
        )

    def block_of(ring, step):
        if ring < 2:
            return ring_member(lax.rem(p + 2 * n - 1 - step, n), n)
        return ring_member(lax.rem(p + 1 + step, n), n)

    def term(ring, owner):
        if ring == 1:
            return block_dot(ag, owner, rows, ctx[...])
        k = {0: 0, 2: 1, 3: 2}[ring]
        return block_dot(n1, owner, rows, lg[:, k * lw : (k + 1) * lw])

    def ring_copy(ring, step, slot):
        return remote(
            ring_send.at[ring, slot],
            ring_recv.at[ring, step],
            ring_ss.at[ring, slot],
            ring_rs.at[ring, step],
            "ep",
            nxt if ring < 2 else prv,
        )

    def ring_step(step, first):
        for ring in range(4):
            slot = lax.rem(step, 2)
            mine = term(ring, block_of(ring, step))
            ring_copy(ring, step - 1, slot).wait_recv()
            if not first:
                ring_copy(ring, step - 2, slot).wait_send()
            ring_send[ring, slot] = (mine + ring_recv[ring, step - 1].astype(F32)).astype(BF)
            ring_copy(ring, step, slot).start()

    for ring in range(4):
        ring_send[ring, 0] = term(ring, block_of(ring, 0)).astype(BF)
        ring_copy(ring, 0, 0).start()

    def part_block(column, store):
        for m in range(0, tokens, 128):
            total = None
            for k in range(3):
                d = lax.dot_general(
                    lg[m : m + 128, k * lw : (k + 1) * lw],
                    w[k, pl.ds(pl.multiple_of(column * lw, lw), lw), :],
                    (((1,), (1,)), ((), ())),
                    preferred_element_type=F32,
                )
                total = d if total is None else total + d
            store(m, total)

    def tp_copy(i, src, dst, peer):
        return remote(src, dst, tp_ss.at[i], tp_rs.at[i], "tp", peer)

    first = [tp_copy(i, part_send.at[i], part_recv.at[i], core_peer) for i in range(2)]
    for i in range(2):

        def put(m, total, i=i):
            part_send[i, m : m + 128, :] = total.astype(BF)

        part_block((core_peer % 2) + 2 * i, put)
        first[i].start()

    ring_step(1, True)

    small_send[...] = small[...]
    small_recv[ep] = small[...]
    for shift in range(1, n):
        small_copy(shift).start()

    def put_own(m, total):
        part_own[m : m + 128, :] = total

    other = (tp // 2) * -1 + 1
    part_block((tp % 2) + 2 * other, put_own)
    for i in range(2):
        first[i].wait()
    y_send[...] = (part_own[...] + part_recv[other].astype(F32)).astype(BF)
    second = tp_copy(2, y_send, y_recv, y_peer)
    second.start()

    ring_step(2, False)

    part_block(tp, put_own)
    second.wait()
    for m in range(0, tokens, 128):
        at = slice(m, m + 128)
        grad = (
            part_own[at, :]
            + part_recv[tp // 2, at, :].astype(F32)
            + y_recv[at, :].astype(F32)
        )
        part_own[at, :] = grad
        hid = h_cols[at, :].astype(F32)
        mean = jnp.sum(grad * gain[...] * hid, axis=1, keepdims=True)
        mean_send[0, at, :] = jnp.broadcast_to(mean, (128, 128))
        col = jnp.sum(grad * hid * r_one[at, :], axis=0, keepdims=True)
        if m == 0:
            vec_send[:, :lw] = col
        else:
            vec_send[:, :lw] += col
    third = tp_copy(3, mean_send.at[0], mean_recv.at[0], core_peer)
    third.start()
    vec_send[:, lw:] = bias[...]
    vec_recv[ep] = vec_send[...]

    def vec_copy(shift, way):
        to = lax.rem(ep + shift, n)
        came = lax.rem(ep + n - shift, n)
        if way == "out":
            return remote(vec_send, vec_recv.at[ep], vec_ss.at[shift], vec_rs.at[shift], "ep", to)
        return remote(vec_send, vec_recv.at[came], vec_ss.at[shift], vec_rs.at[shift], "ep", came)

    for shift in range(1, n):
        vec_copy(shift, "out").start()

    ring_step(3, False)

    third.wait()
    mean_send[1] = mean_send[0] + mean_recv[0]
    fourth = tp_copy(4, mean_send.at[1], mean_recv.at[1], y_peer)
    fourth.start()

    ring_step(4, False)

    fourth.wait()
    for m in range(0, tokens, 128):
        at = slice(m, m + 128)
        mean = (mean_send[1, at, :1] + mean_recv[1, at, :1]) * (1.0 / width)
        r = r_one[at, :]
        in_out[at, :] = (
            mid_cols[at, :]
            + r * part_own[at, :] * gain[...]
            - h_cols[at, :].astype(F32) * (r * r * r) * mean
        ).astype(BF)
    for shift in range(1, n):
        vec_copy(shift, "in").wait()
    total = vec_recv[0]
    for e in range(1, n):
        total = total + vec_recv[e]
    bias_out[...] = total[:, lw:]
    gain_send[...] = total[:, :lw]
    gain_recv[tp] = total[:, :lw]

    def gain_copy(shift, way):
        to = lax.rem(tp + shift, n_tp)
        came = lax.rem(tp + n_tp - shift, n_tp)
        if way == "out":
            return remote(gain_send, gain_recv.at[tp], gain_ss.at[shift], gain_rs.at[shift], "tp", to)
        return remote(gain_send, gain_recv.at[came], gain_ss.at[shift], gain_rs.at[shift], "tp", came)

    for shift in range(1, n_tp):
        gain_copy(shift, "out").start()

    @pl.loop(5, n - 1)
    def _(step):
        ring_step(step, False)

    for shift in range(1, n):
        small_wait(shift).wait()
    total = small_recv[0].astype(F32)
    for e in range(1, n):
        total = total + small_recv[e].astype(F32)
    small_out[...] = total
    for shift in range(1, n_tp):
        gain_copy(shift, "in").wait()
    for j in range(n_tp):
        gain_out[:, j * lw : (j + 1) * lw] = gain_recv[j]

    for ring in range(4):
        mine = term(ring, ep)
        ring_copy(ring, n - 2, 0).wait_recv()
        done = mine + ring_recv[ring, n - 2].astype(F32)
        if ring == 1:
            o_out[...] = done
        else:
            qkv_out[{0: 0, 2: 1, 3: 2}[ring]] = done
    for ring in range(4):
        for step in (n - 3, n - 2):
            ring_copy(ring, step, step % 2).wait_send()


def tail(n, n_tp, n1, lg, ag, ctx, w, h_cols, r_one, gain, mid_cols, bias, small):
    tokens, width = n1.shape
    lw = ctx.shape[1]
    rows = width // n
    if rows % 128:
        n1, ag = n1.T, ag.T
    wide = small.shape[0]
    vmem = pl.BlockSpec(memory_space=pltpu.VMEM)
    dma = pltpu.SemaphoreType.DMA
    return pl.pallas_call(
        functools.partial(tail_kernel, n, n_tp),
        out_shape=(
            jax.ShapeDtypeStruct((3, rows, lw), F32),
            jax.ShapeDtypeStruct((rows, lw), F32),
            jax.ShapeDtypeStruct((tokens, lw), BF),
            jax.ShapeDtypeStruct((1, width), F32),
            jax.ShapeDtypeStruct((1, 3 * lw), F32),
            jax.ShapeDtypeStruct((wide, width), F32),
        ),
        in_specs=[vmem] * 11,
        out_specs=[vmem] * 6,
        scratch_shapes=[
            pltpu.VMEM((4, n - 1, rows, lw), BF),
            pltpu.VMEM((4, 2, rows, lw), BF),
            pltpu.VMEM((tokens, lw), F32),
            pltpu.VMEM((2, tokens, lw), BF),
            pltpu.VMEM((2, tokens, lw), BF),
            pltpu.VMEM((tokens, lw), BF),
            pltpu.VMEM((tokens, lw), BF),
            pltpu.VMEM((2, tokens, 128), F32),
            pltpu.VMEM((2, tokens, 128), F32),
            pltpu.VMEM((1, 4 * lw), F32),
            pltpu.VMEM((n, 1, 4 * lw), F32),
            pltpu.VMEM((wide, width), BF),
            pltpu.VMEM((n, wide, width), BF),
            pltpu.VMEM((1, lw), F32),
            pltpu.VMEM((n_tp, 1, lw), F32),
            dma((4, 2)),
            dma((4, n - 1)),
            dma((5,)),
            dma((5,)),
            dma((n,)),
            dma((n,)),
            dma((n,)),
            dma((n,)),
            dma((n_tp,)),
            dma((n_tp,)),
        ],
        compiler_params=pltpu.CompilerParams(
            collective_id=0, has_side_effects=True, vmem_limit_bytes=56 * 2**20
        ),
        cost_estimate=pl.CostEstimate(
            flops=2 * tokens * width * 7 * lw, bytes_accessed=30 * 2**20, transcendentals=0
        ),
    )(n1, lg, ag, ctx, w, h_cols, r_one, gain, mid_cols, bias, small)

def cols_of(ref, owner, rows):
    at = pl.ds(pl.multiple_of(owner * rows, rows), rows)
    return ref[:, at] if rows % 128 == 0 else ref[at, :]


def block_dot(ref, owner, rows, other):
    dims = (((0,), (0,)), ((), ())) if rows % 128 == 0 else (((1,), (0,)), ((), ()))
    return lax.dot_general(cols_of(ref, owner, rows), other, dims, preferred_element_type=F32)


def middle_kernel(
    n,
    n_tp,
    capp,
    x_hbm,
    u_hbm,
    gu_a,
    gu_c,
    gu_b,
    gu_own,
    dn_a,
    dn_c,
    dn_b,
    dn_own,
    nt,
    pg,
    back,
    o_hbm,
    rg_hbm,
    e_hbm,
    gu_out,
    w,
    xb,
    ub,
    rgb,
    ob,
    eb,
    rbs,
    ring_recv,
    ring_send,
    w_sem,
    x_sem,
    u_sem,
    out_sem,
    ring_ss,
    ring_rs,
    back_ss,
    back_rs,
):
    ep = lax.axis_index("ep")
    gr = xb.shape[1]
    width = u_hbm.shape[1]
    units = w.shape[1]
    quarter = units // 4
    groups = x_hbm.shape[0] // gr
    per = n // groups
    rows = gu_out.shape[1]
    half = ring_recv.shape[3]
    p = ring_place(ep, n)
    nxt = ring_member(lax.rem(p + 1, n), n)
    prv = ring_member(lax.rem(p + n - 1, n), n)

    w_in = [
        pltpu.make_async_copy(ref, w.at[:2, i * quarter : (i + 1) * quarter, :], w_sem.at[i])
        for i, ref in enumerate((gu_a, gu_c, gu_b, gu_own))
    ] + [
        pltpu.make_async_copy(ref, w.at[2, i * quarter : (i + 1) * quarter, :], w_sem.at[4 + i])
        for i, ref in enumerate((dn_a, dn_c, dn_b, dn_own))
    ]
    for copy in w_in:
        copy.start()

    def x_copy(g):
        at = pl.ds(pl.multiple_of(g * gr, gr), gr)
        slot = lax.rem(g, 2)
        return pltpu.make_async_copy(x_hbm.at[at, :], xb.at[slot], x_sem.at[slot])

    def u_copy(g):
        at = pl.ds(pl.multiple_of(g * gr, gr), gr)
        slot = lax.rem(g, 2)
        return pltpu.make_async_copy(u_hbm.at[at, :], ub.at[slot], u_sem.at[slot])

    x_copy(0).start()
    u_copy(0).start()

    barrier = pltpu.get_barrier_semaphore()
    for shift in range(1, n):
        pl.semaphore_signal(
            barrier, 1, device_id={"ep": lax.rem(ep + shift, n)}, device_id_type=pl.DeviceIdType.MESH
        )
    pl.semaphore_wait(barrier, n - 1)

    piece = [(0, half), (half, units), (units, units + half), (units + half, 2 * units)]

    def block_of(ring, step):
        if ring < 2:
            return ring_member(lax.rem(p + 2 * n - 1 - step, n), n)
        return ring_member(lax.rem(p + 1 + step, n), n)

    def term(ring, owner):
        lo, hi = piece[ring]
        return block_dot(nt, owner, rows, pg[:, lo:hi])

    def ring_copy(ring, step, slot):
        lo, hi = piece[ring]
        return remote(
            ring_send.at[ring, slot, :, : hi - lo],
            ring_recv.at[ring, step, :, : hi - lo],
            ring_ss.at[ring, slot],
            ring_rs.at[ring, step],
            "ep",
            nxt if ring < 2 else prv,
        )

    def ring_step(step):
        slot = lax.rem(step, 2)
        for ring in (0, 2, 1, 3):
            lo, hi = piece[ring]
            mine = term(ring, block_of(ring, step))
            ring_copy(ring, step - 1, slot).wait_recv()

            @pl.when(step >= 2)
            def _():
                ring_copy(ring, step - 2, slot).wait_send()

            ring_send[ring, slot, :, : hi - lo] = (
                mine + ring_recv[ring, step - 1, :, : hi - lo].astype(F32)
            ).astype(BF)
            ring_copy(ring, step, slot).start()

    for ring in (0, 2, 1, 3):
        lo, hi = piece[ring]
        ring_send[ring, 0, :, : hi - lo] = term(ring, block_of(ring, 0)).astype(BF)
        ring_copy(ring, 0, 0).start()

    for copy in w_in:
        copy.wait()

    nt_dims = (((1,), (1,)), ((), ()))

    def saved(g):
        at = pl.ds(pl.multiple_of(g * gr, gr), gr)
        return (
            pltpu.make_async_copy(rgb, rg_hbm.at[at, :], out_sem.at[0]),
            pltpu.make_async_copy(ob, o_hbm.at[at, :], out_sem.at[1]),
            pltpu.make_async_copy(eb, e_hbm.at[:, at, :], out_sem.at[2]),
        )

    def back_copy(r):
        at = pl.ds(pl.multiple_of(r * capp, capp), capp)
        return remote(
            rbs.at[at, :], back.at[at, :], back_ss.at[r], back_rs.at[r], "ep", lax.rem(ep + n - r, n)
        )

    kept_copy = pltpu.make_async_copy(rbs.at[:capp, :], back.at[:capp, :], back_ss.at[0])

    @pl.loop(0, groups)
    def _(g):
        slot = lax.rem(g, 2)

        @pl.when(g + 1 < groups)
        def _():
            x_copy(g + 1).start()
            u_copy(g + 1).start()

        x_copy(g).wait()
        u_copy(g).wait()

        @pl.when(g >= 1)
        def _():
            for copy in saved(g - 1):
                copy.wait()

        gate = xb[slot, :, width : width + 1].astype(F32) + xb[slot, :, width + 1 : width + 2].astype(F32)
        rgb[...] = (gate * ub[slot].astype(F32)).astype(BF)

        def hidden(at):
            x = xb[slot, :, :width]
            g_pre = lax.dot_general(x, w[0, at, :], nt_dims, preferred_element_type=F32)
            u_pre = lax.dot_general(x, w[1, at, :], nt_dims, preferred_element_type=F32)
            grad = lax.dot_general(rgb[...], w[2, at, :], nt_dims, preferred_element_type=F32)
            sig = jax.nn.sigmoid(g_pre)
            eb[0, :, at] = (g_pre * sig * u_pre).astype(BF)
            eb[1, :, at] = (grad * u_pre * sig * (1.0 + g_pre * (1.0 - sig))).astype(BF)
            eb[2, :, at] = (grad * g_pre * sig).astype(BF)

        @pl.loop(0, units // 256)
        def _(c):
            hidden(pl.ds(pl.multiple_of(c * 256, 256), 256))

        if units % 256:
            hidden(pl.ds(units // 256 * 256, units % 256))

        def columns(c, total):
            at = pl.ds(pl.multiple_of(c * 256, 256), 256)
            out = jnp.dot(eb[0], w[2, :, at], preferred_element_type=F32)
            ob[:, at] = out.astype(BF)
            grad = jnp.dot(eb[1], w[0, :, at], preferred_element_type=F32) + jnp.dot(
                eb[2], w[1, :, at], preferred_element_type=F32
            )
            rbs[pl.ds(pl.multiple_of(g * gr, gr), gr), at] = grad.astype(BF)
            return total + jnp.sum(out * ub[slot, :, at].astype(F32), axis=1, keepdims=True)

        total = lax.fori_loop(0, width // 256, columns, jnp.zeros((gr, 1), F32))
        hi = total.astype(BF).astype(F32)
        lane = lax.broadcasted_iota(jnp.int32, (gr, 128), 1)
        rbs[pl.ds(pl.multiple_of(g * gr, gr), gr), width:] = jnp.where(
            lane == 0, hi, jnp.where(lane == 1, total - hi, 0.0)
        ).astype(BF)
        for copy in saved(g):
            copy.start()
        for i in range(per):
            r = g * per + i
            if i == 0:

                @pl.when(g == 0)
                def _():
                    kept_copy.start()

                @pl.when(g > 0)
                def _():
                    back_copy(r).start()
            else:
                back_copy(r).start()
        ring_step(g + 1)

    for copy in saved(groups - 1):
        copy.wait()

    @pl.loop(groups + 1, n - 1)
    def _(step):
        ring_step(step)

    for ring in (0, 2, 1, 3):
        lo, hi = piece[ring]
        mine = term(ring, ep)
        ring_copy(ring, n - 2, 0).wait_recv()
        base = (ring // 2) * units
        gu_out[ring // 2, :, lo - base : hi - base] = mine + ring_recv[
            ring, n - 2, :, : hi - lo
        ].astype(F32)
    for ring in range(4):
        for step in (n - 3, n - 2):
            ring_copy(ring, step, step % 2).wait_send()
    kept_copy.wait()

    @pl.loop(1, n)
    def _(r):
        back_copy(r).wait()


def routed_expert(n, n_tp, capp, x, u, weights, nt, pg):
    total, wide = x.shape
    width = u.shape[1]
    units = 4 * weights[-1].shape[0]
    gr = total // 4
    rows = width // n
    half = (units // 128 + 1) // 2 * 128
    vmem = pl.BlockSpec(memory_space=pltpu.VMEM)
    hbm = pl.BlockSpec(memory_space=pl.ANY)
    dma = pltpu.SemaphoreType.DMA
    if rows % 128:
        nt = nt.T
    return pl.pallas_call(
        functools.partial(middle_kernel, n, n_tp, capp),
        out_shape=(
            jax.ShapeDtypeStruct((total, wide), BF),
            jax.ShapeDtypeStruct((total, width), BF),
            jax.ShapeDtypeStruct((total, width), BF),
            jax.ShapeDtypeStruct((3, total, units), BF),
            jax.ShapeDtypeStruct((2, rows, units), F32),
        ),
        in_specs=[hbm] * 10 + [vmem] * 2,
        out_specs=[hbm] * 4 + [vmem],
        scratch_shapes=[
            pltpu.VMEM((3, units, width), BF),
            pltpu.VMEM((2, gr, wide), BF),
            pltpu.VMEM((2, gr, width), BF),
            pltpu.VMEM((gr, width), BF),
            pltpu.VMEM((gr, width), BF),
            pltpu.VMEM((3, gr, units), BF),
            pltpu.VMEM((total, wide), BF),
            pltpu.VMEM((4, n - 1, rows, half), BF),
            pltpu.VMEM((4, 2, rows, half), BF),
            dma((8,)),
            dma((2,)),
            dma((2,)),
            dma((3,)),
            dma((4, 2)),
            dma((4, n - 1)),
            dma((n,)),
            dma((n,)),
        ],
        compiler_params=pltpu.CompilerParams(
            collective_id=1, has_side_effects=True, vmem_limit_bytes=60 * 2**20
        ),
        cost_estimate=pl.CostEstimate(
            flops=2 * total * width * 6 * units, bytes_accessed=40 * 2**20, transcendentals=0
        ),
    )(x, u, *weights, nt, pg)

def front_kernel(
    n,
    n_tp,
    capp,
    hidden,
    gain1,
    gain2,
    w,
    bias,
    cosine,
    sine,
    prefix,
    ow,
    up_sent,
    gu_own,
    dn_own,
    up_rows,
    gu_a,
    dn_a,
    dn_b,
    n1,
    qkv,
    ctx,
    mid,
    nt,
    core_send,
    core_recv,
    y_send,
    y_recv,
    summed,
    up_ss,
    up_rs,
    w_ss,
    w_rs,
    core_ss,
    core_rs,
    y_ss,
    y_rs,
    g_ss,
    g_rs,
):
    ep = lax.axis_index("ep")
    tp = lax.axis_index("tp")
    tokens, width = hidden.shape
    lw = ctx.shape[1]
    heads = lw // HEAD_DIM
    core_peer, y_peer = flip(tp, 1), flip(tp, 2)
    greet(n, n_tp, ep, tp)

    def up_copy(r, way):
        to = lax.rem(ep + r, n) if way == "out" else lax.rem(ep + n - r, n)
        at = pl.ds(r * capp, capp)
        return remote(up_sent.at[at, :], up_rows.at[at, :], up_ss.at[r], up_rs.at[r], "ep", to)

    for r in range(1, n):
        up_copy(r, "out").start()
    kept = pltpu.make_async_copy(up_sent.at[:capp, :], up_rows.at[:capp, :], up_ss.at[0])
    kept.start()
    w_copies = [
        remote(dn_own, dn_b, w_ss.at[0], w_rs.at[0], "tp", y_peer),
        remote(dn_own, dn_a, w_ss.at[1], w_rs.at[1], "tp", core_peer),
        remote(gu_own, gu_a, w_ss.at[2], w_rs.at[2], "tp", core_peer),
    ]
    for copy in w_copies:
        copy.start()

    @pl.loop(0, tokens // 64)
    def _(m):
        at = pl.ds(pl.multiple_of(m * 64, 64), 64)
        h = hidden[at, :].astype(F32)
        factor = lax.rsqrt(jnp.sum(h * h, axis=1, keepdims=True) * (1.0 / width) + EPSILON)
        n1[at, :] = (h * factor * gain1[...]).astype(BF)

    for k in range(3):

        @pl.loop(0, lw // 256)
        def _(c, k=k):
            at = pl.ds(pl.multiple_of(c * 256, 256), 256)
            x = jnp.dot(n1[...], w[k, :, at], preferred_element_type=F32) + bias[k : k + 1, at]
            if k < 2:
                x = jnp.concatenate(
                    [
                        x[:, i * HEAD_DIM : (i + 1) * HEAD_DIM] * cosine[...]
                        + pltpu.roll(x[:, i * HEAD_DIM : (i + 1) * HEAD_DIM], HEAD_DIM // 2, 1) * sine[...]
                        for i in range(256 // HEAD_DIM)
                    ],
                    axis=1,
                )
            qkv[k, :, at] = x.astype(BF)

    @pl.loop(0, tokens // 128)
    def _(m):
        at = pl.ds(pl.multiple_of(m * 128, 128), 128)
        row = lax.broadcasted_iota(jnp.int32, (128, tokens), 0) + m * 128
        col = lax.broadcasted_iota(jnp.int32, (128, tokens), 1)
        visible = (col <= row) | (col < prefix[...])
        for i in range(heads):
            lanes = slice(i * HEAD_DIM, (i + 1) * HEAD_DIM)
            s = lax.dot_general(
                qkv[0, at, lanes], qkv[1, :, lanes], (((1,), (1,)), ((), ())), preferred_element_type=F32
            )
            s = jnp.where(visible, s * HEAD_DIM ** (-0.5), -1e30)
            e = jnp.exp(s - jnp.max(s, axis=1, keepdims=True))
            e = e * (1.0 / jnp.sum(e, axis=1, keepdims=True))
            ctx[at, lanes] = jnp.dot(
                e.astype(BF), qkv[2, :, lanes], preferred_element_type=F32
            ).astype(BF)

    pieces = 4
    half = width // 2
    size = half // pieces
    mine, theirs = (tp % 2) * half, (core_peer % 2) * half

    def project(base, i):
        at = pl.ds(pl.multiple_of(base + i * size, size), size)
        return lax.dot_general(
            ctx[...], ow[at, :], (((1,), (1,)), ((), ())), preferred_element_type=F32
        )

    def core_copy(i):
        return remote(
            core_send.at[i], core_recv.at[i], core_ss.at[i], core_rs.at[i], "tp", core_peer
        )

    def y_copy(i):
        return remote(y_send.at[i], y_recv.at[i], y_ss.at[i], y_rs.at[i], "tp", y_peer)

    def gather_copy(i, way):
        slot = (tp % 2) if way == "out" else (core_peer % 2)
        return remote(
            summed.at[slot, i], summed.at[slot, i], g_ss.at[i], g_rs.at[i], "tp", core_peer
        )

    for i in range(pieces):
        core_send[i] = project(theirs, i).astype(BF)
        core_copy(i).start()
    for i in range(pieces):
        own = project(mine, i)
        core_copy(i).wait_recv()
        y_send[i] = (own + core_recv[i].astype(F32)).astype(BF)
        y_copy(i).start()
    for i in range(pieces):
        y_copy(i).wait_recv()
        summed[tp % 2, i] = (y_send[i].astype(F32) + y_recv[i].astype(F32)).astype(BF)
        gather_copy(i, "out").start()
    for i in range(pieces):
        gather_copy(i, "in").wait_recv()

    @pl.loop(0, tokens // 32)
    def _(m):
        at = pl.ds(pl.multiple_of(m * 32, 32), 32)
        total = jnp.zeros((32, 1), F32)
        for j in range(2):
            for i in range(pieces):
                lanes = slice(j * half + i * size, j * half + (i + 1) * size)
                x = hidden[at, lanes].astype(F32) + summed[j, i, at, :].astype(F32)
                mid[at, lanes] = x
                total = total + jnp.sum(x * x, axis=1, keepdims=True)
        factor = lax.rsqrt(total * (1.0 / width) + EPSILON)
        nt[at, :] = (mid[at, :] * factor * gain2[...]).astype(BF)

    for i in range(pieces):
        core_copy(i).wait_send()
        y_copy(i).wait_send()
        gather_copy(i, "out").wait_send()
    for copy in w_copies:
        copy.wait()
    kept.wait()
    for r in range(1, n):
        up_copy(r, "in").wait()


def front(n, n_tp, capp, hidden, gain1, gain2, w, bias, cosine, sine, prefix, ow, up_sent, gu_own, dn_own):
    tokens, width = hidden.shape
    lw = ow.shape[1]
    quarter = dn_own.shape[0]
    vmem = pl.BlockSpec(memory_space=pltpu.VMEM)
    hbm = pl.BlockSpec(memory_space=pl.ANY)
    dma = pltpu.SemaphoreType.DMA
    return pl.pallas_call(
        functools.partial(front_kernel, n, n_tp, capp),
        out_shape=(
            jax.ShapeDtypeStruct(up_sent.shape, BF),
            jax.ShapeDtypeStruct((2, quarter, width), BF),
            jax.ShapeDtypeStruct((quarter, width), BF),
            jax.ShapeDtypeStruct((quarter, width), BF),
            jax.ShapeDtypeStruct((tokens, width), BF),
            jax.ShapeDtypeStruct((3, tokens, lw), BF),
            jax.ShapeDtypeStruct((tokens, lw), BF),
            jax.ShapeDtypeStruct((tokens, width), F32),
            jax.ShapeDtypeStruct((tokens, width), BF),
        ),
        in_specs=[vmem] * 9 + [hbm] * 3,
        out_specs=[hbm] * 4 + [vmem] * 5,
        scratch_shapes=[
            pltpu.VMEM((4, tokens, width // 8), BF),
            pltpu.VMEM((4, tokens, width // 8), BF),
            pltpu.VMEM((4, tokens, width // 8), BF),
            pltpu.VMEM((4, tokens, width // 8), BF),
            pltpu.VMEM((2, 4, tokens, width // 8), BF),
            dma((n,)),
            dma((n,)),
            dma((3,)),
            dma((3,)),
            dma((4,)),
            dma((4,)),
            dma((4,)),
            dma((4,)),
            dma((4,)),
            dma((4,)),
        ],
        compiler_params=pltpu.CompilerParams(
            collective_id=2, has_side_effects=True, vmem_limit_bytes=56 * 2**20
        ),
        cost_estimate=pl.CostEstimate(
            flops=2 * tokens * width * 4 * lw, bytes_accessed=30 * 2**20, transcendentals=0
        ),
    )(hidden, gain1, gain2, w, bias, cosine, sine, prefix, ow, up_sent, gu_own, dn_own)


def dispatch_kernel(
    n,
    n_tp,
    capp,
    n_exp,
    nt,
    place,
    router,
    cot,
    sgu,
    sdn,
    gu_own,
    dn_b,
    x_rows,
    gu_b,
    gu_c,
    dn_c,
    probs,
    gate,
    og,
    pg,
    sh,
    part,
    sback,
    x_send,
    x_ss,
    x_rs,
    w_ss,
    w_rs,
):
    ep = lax.axis_index("ep")
    tp = lax.axis_index("tp")
    tokens, width = nt.shape
    units = sdn.shape[1]
    total = place.shape[0]
    core_peer, y_peer = flip(tp, 1), flip(tp, 2)
    greet(n, n_tp, ep, tp)
    w_y = remote(gu_own, gu_b, w_ss.at[0], w_rs.at[0], "tp", y_peer)
    w_y.start()
    w_on = remote(dn_b, dn_c, w_ss.at[1], w_rs.at[1], "tp", core_peer)
    w_on.start()

    logits = jnp.dot(nt[...], router[...], preferred_element_type=F32)
    lane = lax.broadcasted_iota(jnp.int32, logits.shape, 1)
    chosen = jnp.where(lane < n_exp, logits, -1e30)
    e = jnp.exp(chosen - jnp.max(chosen, axis=1, keepdims=True))
    prob = e / jnp.sum(e, axis=1, keepdims=True)
    prob = jnp.where(lane == n_exp, jax.nn.sigmoid(logits), prob)
    probs[...] = prob
    hi = prob.astype(BF)
    lo = (prob - hi.astype(F32)).astype(BF)

    def x_copy(r, way):
        to = lax.rem(ep + r, n) if way == "out" else lax.rem(ep + n - r, n)
        at = pl.ds(pl.multiple_of(r * capp, capp), capp)
        return remote(x_send.at[at, :], x_rows.at[at, :], x_ss.at[r], x_rs.at[r], "ep", to)

    kept = pltpu.make_async_copy(x_send.at[:capp, :], x_rows.at[:capp, :], x_ss.at[0])

    per = 1
    while 2 * per * capp <= 128 and n % (2 * per) == 0:
        per *= 2
    size = per * capp

    @pl.loop(0, n // per)
    def _(b):
        at = pl.ds(pl.multiple_of(b * size, size), size)
        where = place[at, :]
        x_send[at, :width] = jnp.dot(where, nt[...], preferred_element_type=F32).astype(BF)
        row = lax.broadcasted_iota(jnp.int32, (size, 128), 0) + b * size
        spot = lax.broadcasted_iota(jnp.int32, (size, 128), 1)
        expert = lax.rem(row // capp + ep * (n_exp // n), n_exp)
        pick = spot == expert
        g_hi = jnp.sum(
            jnp.where(pick, jnp.dot(where, hi, preferred_element_type=F32), 0.0), axis=1, keepdims=True
        )
        g_lo = jnp.sum(
            jnp.where(pick, jnp.dot(where, lo, preferred_element_type=F32), 0.0), axis=1, keepdims=True
        )
        gate[at, :] = g_hi + g_lo
        x_send[at, width:] = jnp.where(spot == 0, g_hi, jnp.where(spot == 1, g_lo, 0.0)).astype(BF)
        for i in range(per):
            r = b * per + i
            if i == 0:

                @pl.when(b == 0)
                def _():
                    kept.start()

                @pl.when(b > 0)
                def _():
                    x_copy(r, "out").start()
            else:
                x_copy(r, "out").start()

    @pl.loop(0, tokens // 64)
    def _(m):
        at = pl.ds(pl.multiple_of(m * 64, 64), 64)
        og[at, :] = (probs[at, n_exp : n_exp + 1] * cot[at, :].astype(F32)).astype(BF)

    def hidden(at, up_at):
        g_pre = jnp.dot(nt[...], sgu[0, :, at], preferred_element_type=F32)
        u_pre = jnp.dot(nt[...], sgu[1, :, at], preferred_element_type=F32)
        grad = jnp.dot(og[...], sdn[:, at], preferred_element_type=F32)
        sig = jax.nn.sigmoid(g_pre)
        sh[:, at] = (g_pre * sig * u_pre).astype(BF)
        pg[:, at] = (grad * u_pre * sig * (1.0 + g_pre * (1.0 - sig))).astype(BF)
        pg[:, up_at] = (grad * g_pre * sig).astype(BF)

    @pl.loop(0, units // 256)
    def _(c):
        hidden(
            pl.ds(pl.multiple_of(c * 256, 256), 256),
            pl.ds(pl.multiple_of(c * 256 + units, 128), 256),
        )

    if units % 256:
        rest = units // 256 * 256
        hidden(pl.ds(rest, units - rest), pl.ds(units + rest, units - rest))

    w_y.wait()
    w_far = remote(gu_b, gu_c, w_ss.at[2], w_rs.at[2], "tp", core_peer)
    w_far.start()

    nt_dims = (((1,), (1,)), ((), ()))

    @pl.loop(0, width // 256)
    def _(c):
        at = pl.ds(pl.multiple_of(c * 256, 256), 256)
        part[:, at] = lax.dot_general(sh[...], sdn[at, :], nt_dims, preferred_element_type=F32)
        sback[:, at] = lax.dot_general(
            pg[:, :units], sgu[0, at, :], nt_dims, preferred_element_type=F32
        ) + lax.dot_general(pg[:, units:], sgu[1, at, :], nt_dims, preferred_element_type=F32)

    w_on.wait()
    w_far.wait()
    kept.wait()

    @pl.loop(1, n)
    def _(r):
        x_copy(r, "in").wait()


def dispatch(n, n_tp, capp, n_exp, nt, place, router, cot, sgu, sdn, gu_own, dn_b):
    tokens, width = nt.shape
    units = sdn.shape[1]
    total = place.shape[0]
    vmem = pl.BlockSpec(memory_space=pltpu.VMEM)
    hbm = pl.BlockSpec(memory_space=pl.ANY)
    dma = pltpu.SemaphoreType.DMA
    return pl.pallas_call(
        functools.partial(dispatch_kernel, n, n_tp, capp, n_exp),
        out_shape=(
            jax.ShapeDtypeStruct((total, width + 128), BF),
            jax.ShapeDtypeStruct(gu_own.shape, BF),
            jax.ShapeDtypeStruct(gu_own.shape, BF),
            jax.ShapeDtypeStruct(dn_b.shape, BF),
            jax.ShapeDtypeStruct((tokens, 128), F32),
            jax.ShapeDtypeStruct((total, 1), F32),
            jax.ShapeDtypeStruct((tokens, width), BF),
            jax.ShapeDtypeStruct((tokens, 2 * units), BF),
            jax.ShapeDtypeStruct((tokens, units), BF),
            jax.ShapeDtypeStruct((tokens, width), F32),
            jax.ShapeDtypeStruct((tokens, width), F32),
        ),
        in_specs=[vmem] * 6 + [hbm] * 2,
        out_specs=[hbm] * 4 + [vmem] * 7,
        scratch_shapes=[
            pltpu.VMEM((total, width + 128), BF),
            dma((n,)),
            dma((n,)),
            dma((3,)),
            dma((3,)),
        ],
        compiler_params=pltpu.CompilerParams(
            collective_id=3, has_side_effects=True, vmem_limit_bytes=60 * 2**20
        ),
        cost_estimate=pl.CostEstimate(
            flops=2 * tokens * width * 6 * units, bytes_accessed=40 * 2**20, transcendentals=0
        ),
    )(nt, place, router, cot, sgu, sdn, gu_own, dn_b)


def body(
    hidden,
    attn_gain,
    qkv_weight,
    qkv_bias,
    out_weight,
    mlp_gain,
    router_weight,
    share_gate,
    shared_gate_up,
    shared_down,
    expert_gate_up,
    expert_down,
    routes,
    priority,
    prefix,
    cotangent,
):
    tokens, width = hidden.shape
    n_ep = lax.axis_size("ep")
    n_tp = lax.axis_size("tp")
    tp_i = lax.axis_index("tp")
    cols = width // n_tp
    col_start = tp_i * cols
    head_size = HEAD_DIM
    local_width = qkv_weight.shape[2]
    heads = local_width // head_size
    expert_local = expert_gate_up.shape[0]
    n_exp = expert_local * n_ep
    top = routes.shape[1]
    capacity = (5 * tokens * top + 4 * n_exp - 1) // (4 * n_exp)
    part = -(-capacity // n_tp)
    part_pad = -(-part // 16) * 16
    rows = n_exp * part_pad

    flat_route = routes.T.reshape(-1)
    flat_order = priority.T.reshape(-1)
    hits = (flat_route[:, None] == jnp.arange(n_exp, dtype=jnp.int32)[None, :]).astype(BF)
    smaller = (flat_order[None, :] < flat_order[:, None]).astype(BF)
    counts = mm(smaller, hits, 1, 0)
    slot = jnp.sum(counts * hits.astype(F32), axis=1).astype(jnp.int32).reshape(top, tokens)
    kept = slot < capacity
    in_part = slot - tp_i * part
    mine = kept & (in_part >= 0) & (in_part < part)
    ep_i = lax.axis_index("ep")
    hop = lax.rem(routes.T + n_exp - ep_i * expert_local, n_exp)
    dest = jnp.where(mine, hop * part_pad + in_part, -1)
    row_ids = jnp.arange(rows, dtype=jnp.int32)[:, None]
    place = (dest[0][None, :] == row_ids)
    for k in range(1, top):
        place = place | (dest[k][None, :] == row_ids)
    place = place.astype(BF)

    up_sent = mm(place, cotangent, 1, 0).astype(BF)

    upstream = cotangent.astype(F32)
    residual_in = hidden.astype(F32)
    factor_one = norm_factor(residual_in)
    cosine, sine_val = angle_tables(tokens, head_size)
    cos_all = jnp.concatenate([cosine[:, 0], cosine[:, 0]], axis=1)
    sin_all = jnp.concatenate([-sine_val[:, 0], sine_val[:, 0]], axis=1)
    w_t = jnp.transpose(qkv_weight, (1, 0, 2))
    gu_own = jnp.transpose(expert_gate_up[0], (1, 2, 0))
    dn_own = jnp.transpose(expert_down[0], (1, 0))
    up_rows, gu_a, dn_a, dn_b, normed_one, qkv, context, middle, normed_two = front(
        n_ep,
        n_tp,
        part_pad,
        hidden,
        attn_gain[None],
        mlp_gain[None],
        w_t,
        qkv_bias,
        cos_all,
        sin_all,
        jnp.broadcast_to(prefix[None], (1, tokens)),
        out_weight,
        up_sent,
        gu_own,
        dn_own,
    )
    factor_two = norm_factor(middle)

    row_expert = lax.rem(row_ids // part_pad + ep_i * expert_local, n_exp)
    own = (row_expert == jnp.arange(n_exp, dtype=jnp.int32)[None, :]).astype(F32)
    router_all = jnp.concatenate(
        [router_weight, share_gate[:, None], jnp.zeros((width, 127 - n_exp), BF)], axis=1
    )
    got, gu_b, gu_c, dn_c, probs_all, gate_sent, shared_out_grad, pre_grad, shared_hidden, shared_part, shared_back = (
        dispatch(
            n_ep,
            n_tp,
            part_pad,
            n_exp,
            normed_two,
            place,
            router_all,
            cotangent,
            jnp.transpose(shared_gate_up, (1, 0, 2)),
            shared_down,
            gu_own,
            dn_b,
        )
    )
    router_probs = probs_all[:, :n_exp]
    share_scale = probs_all[:, n_exp]
    scale_grad_part = jnp.sum(upstream * shared_part, axis=1)
    shared_down_grad = lax.psum_scatter(
        mm(shared_out_grad, shared_hidden, 0, 0).astype(BF), "ep", scatter_dimension=0, tiled=True
    ).astype(F32)

    back_rows, e_out, row_grad, e_all, gu_grad = routed_expert(
        n_ep,
        n_tp,
        part_pad,
        got,
        up_rows,
        (gu_a, gu_c, gu_b, gu_own, dn_a, dn_c, dn_b, dn_own),
        normed_two,
        pre_grad,
    )
    shared_gate_up_grad = jnp.transpose(gu_grad, (1, 0, 2))
    out_rows = exchange(e_out, n_ep, True)
    whole_rows = got[:, :width]
    quarter = dn_own.shape[0]
    pairs = ((e_all[1], whole_rows), (e_all[2], whole_rows), (e_all[0], row_grad))
    weight_grads = []
    for left, right in pairs:
        came = swap(mm(left[:, : 2 * quarter], right, 0, 0).astype(BF), 1, n_tp)
        on = swap(
            (
                mm(left[:, 2 * quarter : 3 * quarter], right, 0, 0) + came[quarter:].astype(F32)
            ).astype(BF),
            2,
            n_tp,
        )
        weight_grads.append(
            mm(left[:, 3 * quarter :], right, 0, 0) + came[:quarter].astype(F32) + on.astype(F32)
        )
    expert_down_grad = jnp.transpose(weight_grads[2], (1, 0))[None]
    expert_gate_up_grad = jnp.transpose(jnp.stack(weight_grads[:2], axis=0), (2, 0, 1))[None]

    weighted_place = (place.astype(F32) * gate_sent).astype(BF)
    routed = mm(weighted_place, out_rows, 0, 0)
    out_cols = tp_scatter(share_scale[:, None] * shared_part + routed, n_tp)
    output = (lax.dynamic_slice_in_dim(middle, col_start, cols, 1) + out_cols).astype(BF)
    gate_grad_row = back_rows[:, width : width + 1].astype(F32) + back_rows[:, width + 1 : width + 2].astype(F32)
    prob_part = mm(place, (gate_grad_row * own).astype(BF), 0, 0)
    few = tp_sum(
        jnp.concatenate(
            [prob_part, scale_grad_part[:, None], jnp.zeros((tokens, 256 - n_exp - 1), F32)], axis=1
        ),
        n_tp,
    )
    normed_two_grad = tp_sum(shared_back + mm(place, back_rows[:, :width], 0, 0), n_tp)
    prob_grad = few[:, :n_exp]
    scale_grad = few[:, n_exp]
    gate_in_grad = (scale_grad * share_scale * (1.0 - share_scale)).astype(BF)
    logit_grad = (
        router_probs * (prob_grad - jnp.sum(router_probs * prob_grad, axis=1, keepdims=True))
    ).astype(BF)
    normed_two_grad = (
        normed_two_grad
        + mm(logit_grad, router_weight, 1, 1)
        + gate_in_grad.astype(F32)[:, None] * share_gate.astype(F32)[None, :]
    )
    small_two = mm(
        jnp.concatenate([logit_grad, gate_in_grad[:, None]], axis=1), normed_two, 0, 0
    )
    mlp_gain_grad = jnp.sum(normed_two_grad * middle * factor_two, axis=0)
    scaled = normed_two_grad * mlp_gain
    middle_grad = upstream + factor_two * scaled - middle * (factor_two**3) * jnp.mean(
        scaled * middle, axis=-1, keepdims=True
    )
    small_pad = -(-(n_exp + 2) // 16) * 16 - n_exp - 2
    small = jnp.concatenate(
        [small_two, mlp_gain_grad[None], jnp.zeros((small_pad, width), F32)], axis=0
    ).astype(BF)

    attn_grad = middle_grad.astype(BF)
    context_grad = mm(attn_grad, out_weight, 1, 0).astype(BF).reshape(tokens, heads, head_size)
    queries, key_rows, value_rows = (qkv[i].reshape(tokens, heads, head_size) for i in range(3))
    scores = masked_scores(queries, key_rows, prefix[0], head_size)
    attn_weights = jax.nn.softmax(scores, axis=-1)
    prob_grad_att = jnp.einsum("qhd,khd->hqk", context_grad, value_rows, preferred_element_type=F32)
    value_grad = jnp.einsum(
        "hqk,qhd->khd", attn_weights.astype(BF), context_grad, preferred_element_type=F32
    )
    row_delta = jnp.sum(attn_weights * prob_grad_att, axis=-1, keepdims=True)
    score_grad = (attn_weights * (prob_grad_att - row_delta)).astype(BF)
    query_grad = jnp.einsum(
        "hqk,khd->qhd", score_grad, key_rows, preferred_element_type=F32
    ) * head_size ** (-0.5)
    key_grad = jnp.einsum(
        "hqk,qhd->khd", score_grad, queries, preferred_element_type=F32
    ) * head_size ** (-0.5)
    query_grad = rotate_backward(query_grad, cosine, sine_val)
    key_grad = rotate_backward(key_grad, cosine, sine_val)
    parts = [g.reshape(tokens, local_width) for g in (query_grad, key_grad, value_grad)]
    bias_grad = jnp.concatenate([jnp.sum(g, axis=0) for g in parts])
    linear_grad = jnp.concatenate([g.astype(BF) for g in parts], axis=1)
    qkv_grad, out_weight_grad, input_grad, gain_one, bias_sum, small_sum = tail(
        n_ep,
        n_tp,
        normed_one,
        linear_grad,
        attn_grad,
        context,
        w_t,
        lax.dynamic_slice_in_dim(hidden, col_start, cols, 1),
        factor_one,
        lax.dynamic_slice_in_dim(attn_gain, col_start, cols, 0)[None],
        lax.dynamic_slice_in_dim(middle_grad, col_start, cols, 1),
        bias_grad[None],
        small,
    )
    qkv_weight_grad = jnp.transpose(qkv_grad, (1, 0, 2))
    gain_one_sum = gain_one[0]
    bias_sum = bias_sum.reshape(3, local_width)
    router_sum = small_sum[:n_exp].T
    share_gate_sum = small_sum[n_exp]
    gain_two_sum = small_sum[n_exp + 1]
    return (
        output,
        input_grad,
        gain_one_sum,
        qkv_weight_grad,
        bias_sum,
        out_weight_grad,
        gain_two_sum,
        router_sum,
        share_gate_sum,
        shared_gate_up_grad,
        shared_down_grad,
        expert_gate_up_grad,
        expert_down_grad,
    )


def solution(mesh):
    return jax.shard_map(
        body,
        mesh=mesh,
        in_specs=(
            P("ep", None),
            P(),
            P(None, None, "tp"),
            P(None, "tp"),
            P(None, "tp"),
            P(),
            P(),
            P(),
            P(None, None, "tp"),
            P(None, "tp"),
            P("ep", None, None, "tp"),
            P("ep", None, "tp"),
            P("ep", None),
            P("ep", None),
            P("ep"),
            P("ep", None),
        ),
        out_specs=(
            P("ep", "tp"),
            P("ep", "tp"),
            P(),
            P("ep", None, "tp"),
            P(None, "tp"),
            P("ep", "tp"),
            P(),
            P(),
            P(),
            P("ep", None, "tp"),
            P("ep", "tp"),
            P("ep", None, None, "tp"),
            P("ep", None, "tp"),
        ),
        check_vma=False,
    )
```

```python
import functools

import jax
import jax.numpy as jnp
from jax import lax
from jax.experimental import pallas as pl
from jax.experimental.pallas import tpu as pltpu
from jax.sharding import PartitionSpec as P

HEAD_DIM = 128
EPSILON = 1e-06
THETA = 1000000.0
BF = jnp.bfloat16
F32 = jnp.float32


def mm(a, b, ca, cb):
    return lax.dot_general(a, b, (((ca,), (cb,)), ((), ())), preferred_element_type=F32)


def norm_factor(values):
    return lax.rsqrt(jnp.mean(values * values, axis=-1, keepdims=True) + EPSILON)


def angle_tables(length, head_size):
    half_size = head_size // 2
    frequency = THETA ** (-jnp.arange(half_size, dtype=F32) * 2.0 / head_size)
    angles = jnp.arange(length, dtype=F32)[:, None] * frequency[None, :]
    return jnp.cos(angles)[:, None, :], jnp.sin(angles)[:, None, :]


def ring_place(e, n):
    odd = e % 2
    return (1 - odd) * (e // 2) + odd * (n - 1 - e // 2)


def ring_member(p, n):
    second = p // (n // 2)
    return (1 - second) * 2 * p + second * (2 * (n - 1 - p) + 1)


def remote(src, dst, send_sem, recv_sem, axis, index):
    return pltpu.make_async_remote_copy(
        src_ref=src,
        dst_ref=dst,
        send_sem=send_sem,
        recv_sem=recv_sem,
        device_id={axis: index},
        device_id_type=pl.DeviceIdType.MESH,
    )


def greet(n, n_tp, ep, tp):
    barrier = pltpu.get_barrier_semaphore()
    for shift in range(1, n):
        pl.semaphore_signal(
            barrier, 1, device_id={"ep": lax.rem(ep + shift, n)}, device_id_type=pl.DeviceIdType.MESH
        )
    for shift in range(1, n_tp):
        pl.semaphore_signal(
            barrier, 1, device_id={"tp": lax.rem(tp + shift, n_tp)}, device_id_type=pl.DeviceIdType.MESH
        )
    pl.semaphore_wait(barrier, n - 1 + n_tp - 1)


def flip(index, bit):
    if bit == 1:
        return index + 1 - 2 * (index % 2)
    return index + 2 - 4 * ((index // 2) % 2)


def tail_kernel(
    n,
    n_tp,
    n1,
    lg,
    ag,
    ctx,
    w,
    h_cols,
    r_one,
    gain,
    mid_cols,
    bias,
    small,
    o_rows,
    place_t,
    spart,
    res_cols,
    qkv_out,
    o_out,
    in_out,
    out_out,
    gain_out,
    bias_out,
    small_out,
    ring_recv,
    ring_send,
    part_own,
    part_send,
    part_recv,
    y_send,
    y_recv,
    mean_send,
    mean_recv,
    vec_send,
    vec_recv,
    small_send,
    small_recv,
    gain_send,
    gain_recv,
    out_send,
    out_recv,
    oy_send,
    oy_recv,
    ring_ss,
    ring_rs,
    tp_ss,
    tp_rs,
    vec_ss,
    vec_rs,
    small_ss,
    small_rs,
    gain_ss,
    gain_rs,
):
    ep = lax.axis_index("ep")
    tp = lax.axis_index("tp")
    tokens, lw = ctx.shape
    rows = qkv_out.shape[1]
    width = rows * n
    p = ring_place(ep, n)
    nxt = ring_member(lax.rem(p + 1, n), n)
    prv = ring_member(lax.rem(p + n - 1, n), n)
    core_peer, y_peer = flip(tp, 1), flip(tp, 2)
    greet(n, n_tp, ep, tp)

    def small_copy(shift):
        to = lax.rem(ep + shift, n)
        return remote(
            small_send, small_recv.at[ep], small_ss.at[shift], small_rs.at[shift], "ep", to
        )

    def small_wait(shift):
        came = lax.rem(ep + n - shift, n)
        return remote(
            small_send, small_recv.at[came], small_ss.at[shift], small_rs.at[shift], "ep", came
        )

    def block_of(ring, step):
        if ring < 2:
            return ring_member(lax.rem(p + 2 * n - 1 - step, n), n)
        return ring_member(lax.rem(p + 1 + step, n), n)

    def term(ring, owner):
        if ring == 1:
            return block_dot(ag, owner, rows, ctx[...])
        k = {0: 0, 2: 1, 3: 2}[ring]
        return block_dot(n1, owner, rows, lg[:, k * lw : (k + 1) * lw])

    def ring_copy(ring, step, slot):
        return remote(
            ring_send.at[ring, slot],
            ring_recv.at[ring, step],
            ring_ss.at[ring, slot],
            ring_rs.at[ring, step],
            "ep",
            nxt if ring < 2 else prv,
        )

    def ring_step(step, first):
        for ring in range(4):
            slot = lax.rem(step, 2)
            mine = term(ring, block_of(ring, step))
            ring_copy(ring, step - 1, slot).wait_recv()
            if not first:
                ring_copy(ring, step - 2, slot).wait_send()
            ring_send[ring, slot] = (mine + ring_recv[ring, step - 1].astype(F32)).astype(BF)
            ring_copy(ring, step, slot).start()

    for ring in range(4):
        ring_send[ring, 0] = term(ring, block_of(ring, 0)).astype(BF)
        ring_copy(ring, 0, 0).start()

    def part_block(column, store):
        for m in range(0, tokens, 128):
            total = None
            for k in range(3):
                d = lax.dot_general(
                    lg[m : m + 128, k * lw : (k + 1) * lw],
                    w[k, pl.ds(pl.multiple_of(column * lw, lw), lw), :],
                    (((1,), (1,)), ((), ())),
                    preferred_element_type=F32,
                )
                total = d if total is None else total + d
            store(m, total)

    def tp_copy(i, src, dst, peer):
        return remote(src, dst, tp_ss.at[i], tp_rs.at[i], "tp", peer)

    first = [tp_copy(i, part_send.at[i], part_recv.at[i], core_peer) for i in range(2)]
    for i in range(2):

        def put(m, total, i=i):
            part_send[i, m : m + 128, :] = total.astype(BF)

        part_block((core_peer % 2) + 2 * i, put)
        first[i].start()

    ring_step(1, True)

    small_send[...] = small[...]
    small_recv[ep] = small[...]
    for shift in range(1, n):
        small_copy(shift).start()

    def put_own(m, total):
        part_own[m : m + 128, :] = total

    other = (tp // 2) * -1 + 1
    part_block((tp % 2) + 2 * other, put_own)
    for i in range(2):
        first[i].wait()
    y_send[...] = (part_own[...] + part_recv[other].astype(F32)).astype(BF)
    second = tp_copy(2, y_send, y_recv, y_peer)
    second.start()

    ring_step(2, False)

    part_block(tp, put_own)
    second.wait()
    for m in range(0, tokens, 128):
        at = slice(m, m + 128)
        grad = (
            part_own[at, :]
            + part_recv[tp // 2, at, :].astype(F32)
            + y_recv[at, :].astype(F32)
        )
        part_own[at, :] = grad
        hid = h_cols[at, :].astype(F32)
        mean = jnp.sum(grad * gain[...] * hid, axis=1, keepdims=True)
        mean_send[0, at, :] = jnp.broadcast_to(mean, (128, 128))
        col = jnp.sum(grad * hid * r_one[at, :], axis=0, keepdims=True)
        if m == 0:
            vec_send[:, :lw] = col
        else:
            vec_send[:, :lw] += col
    third = tp_copy(3, mean_send.at[0], mean_recv.at[0], core_peer)
    third.start()
    vec_send[:, lw:] = bias[...]
    vec_recv[ep] = vec_send[...]

    def vec_copy(shift, way):
        to = lax.rem(ep + shift, n)
        came = lax.rem(ep + n - shift, n)
        if way == "out":
            return remote(vec_send, vec_recv.at[ep], vec_ss.at[shift], vec_rs.at[shift], "ep", to)
        return remote(vec_send, vec_recv.at[came], vec_ss.at[shift], vec_rs.at[shift], "ep", came)

    for shift in range(1, n):
        vec_copy(shift, "out").start()

    ring_step(3, False)

    third.wait()
    mean_send[1] = mean_send[0] + mean_recv[0]
    fourth = tp_copy(4, mean_send.at[1], mean_recv.at[1], y_peer)
    fourth.start()

    def out_block(column):
        at = pl.ds(pl.multiple_of(column * lw, lw), lw)
        return spart[:, at].astype(F32) + jnp.dot(
            place_t[...], o_rows[:, at], preferred_element_type=F32
        )

    fifth = [tp_copy(5 + i, out_send.at[i], out_recv.at[i], core_peer) for i in range(2)]
    for i in range(2):
        out_send[i] = out_block((core_peer % 2) + 2 * i).astype(BF)
        fifth[i].start()

    ring_step(4, False)

    for copy in fifth:
        copy.wait()
    oy_send[...] = (out_block((tp % 2) + 2 * other) + out_recv[other].astype(F32)).astype(BF)
    sixth = tp_copy(7, oy_send, oy_recv, y_peer)
    sixth.start()
    fourth.wait()
    for m in range(0, tokens, 128):
        at = slice(m, m + 128)
        mean = (mean_send[1, at, :1] + mean_recv[1, at, :1]) * (1.0 / width)
        r = r_one[at, :]
        in_out[at, :] = (
            mid_cols[at, :].astype(F32)
            + r * part_own[at, :] * gain[...]
            - h_cols[at, :].astype(F32) * (r * r * r) * mean
        ).astype(BF)
    for shift in range(1, n):
        vec_copy(shift, "in").wait()
    total = vec_recv[0]
    for e in range(1, n):
        total = total + vec_recv[e]
    bias_out[...] = total[:, lw:]
    gain_send[...] = total[:, :lw]
    gain_recv[tp] = total[:, :lw]

    def gain_copy(shift, way):
        to = lax.rem(tp + shift, n_tp)
        came = lax.rem(tp + n_tp - shift, n_tp)
        if way == "out":
            return remote(gain_send, gain_recv.at[tp], gain_ss.at[shift], gain_rs.at[shift], "tp", to)
        return remote(gain_send, gain_recv.at[came], gain_ss.at[shift], gain_rs.at[shift], "tp", came)

    for shift in range(1, n_tp):
        gain_copy(shift, "out").start()

    ring_step(5, False)

    own = out_block(tp) + res_cols[...] + out_recv[tp // 2].astype(F32)
    sixth.wait()
    out_out[...] = (own + oy_recv[...].astype(F32)).astype(BF)

    @pl.loop(6, n - 1)
    def _(step):
        ring_step(step, False)

    for shift in range(1, n):
        small_wait(shift).wait()
    total = small_recv[0].astype(F32)
    for e in range(1, n):
        total = total + small_recv[e].astype(F32)
    small_out[...] = total
    for shift in range(1, n_tp):
        gain_copy(shift, "in").wait()
    for j in range(n_tp):
        gain_out[:, j * lw : (j + 1) * lw] = gain_recv[j]

    for ring in range(4):
        mine = term(ring, ep)
        ring_copy(ring, n - 2, 0).wait_recv()
        done = mine + ring_recv[ring, n - 2].astype(F32)
        if ring == 1:
            o_out[...] = done
        else:
            qkv_out[{0: 0, 2: 1, 3: 2}[ring]] = done
    for ring in range(4):
        for step in (n - 3, n - 2):
            ring_copy(ring, step, step % 2).wait_send()


def tail(n, n_tp, n1, lg, ag, ctx, w, h_cols, r_one, gain, mid_cols, bias, small, o_rows, place_t, spart, res_cols):
    tokens, width = n1.shape
    lw = ctx.shape[1]
    rows = width // n
    if rows % 128:
        n1, ag = n1.T, ag.T
    wide = small.shape[0]
    vmem = pl.BlockSpec(memory_space=pltpu.VMEM)
    dma = pltpu.SemaphoreType.DMA
    return pl.pallas_call(
        functools.partial(tail_kernel, n, n_tp),
        out_shape=(
            jax.ShapeDtypeStruct((3, rows, lw), F32),
            jax.ShapeDtypeStruct((rows, lw), F32),
            jax.ShapeDtypeStruct((tokens, lw), BF),
            jax.ShapeDtypeStruct((tokens, lw), BF),
            jax.ShapeDtypeStruct((1, width), F32),
            jax.ShapeDtypeStruct((1, 3 * lw), F32),
            jax.ShapeDtypeStruct((wide, width), F32),
        ),
        in_specs=[vmem] * 15,
        out_specs=[vmem] * 7,
        scratch_shapes=[
            pltpu.VMEM((4, n - 1, rows, lw), BF),
            pltpu.VMEM((4, 2, rows, lw), BF),
            pltpu.VMEM((tokens, lw), F32),
            pltpu.VMEM((2, tokens, lw), BF),
            pltpu.VMEM((2, tokens, lw), BF),
            pltpu.VMEM((tokens, lw), BF),
            pltpu.VMEM((tokens, lw), BF),
            pltpu.VMEM((2, tokens, 128), F32),
            pltpu.VMEM((2, tokens, 128), F32),
            pltpu.VMEM((1, 4 * lw), F32),
            pltpu.VMEM((n, 1, 4 * lw), F32),
            pltpu.VMEM((wide, width), BF),
            pltpu.VMEM((n, wide, width), BF),
            pltpu.VMEM((1, lw), F32),
            pltpu.VMEM((n_tp, 1, lw), F32),
            pltpu.VMEM((2, tokens, lw), BF),
            pltpu.VMEM((2, tokens, lw), BF),
            pltpu.VMEM((tokens, lw), BF),
            pltpu.VMEM((tokens, lw), BF),
            dma((4, 2)),
            dma((4, n - 1)),
            dma((8,)),
            dma((8,)),
            dma((n,)),
            dma((n,)),
            dma((n,)),
            dma((n,)),
            dma((n_tp,)),
            dma((n_tp,)),
        ],
        compiler_params=pltpu.CompilerParams(
            collective_id=0, has_side_effects=True, vmem_limit_bytes=60 * 2**20
        ),
        cost_estimate=pl.CostEstimate(
            flops=2 * tokens * width * 7 * lw, bytes_accessed=30 * 2**20, transcendentals=0
        ),
    )(n1, lg, ag, ctx, w, h_cols, r_one, gain, mid_cols, bias, small, o_rows, place_t, spart, res_cols)

def cols_of(ref, owner, rows):
    at = pl.ds(pl.multiple_of(owner * rows, rows), rows)
    return ref[:, at] if rows % 128 == 0 else ref[at, :]


def block_dot(ref, owner, rows, other):
    dims = (((0,), (0,)), ((), ())) if rows % 128 == 0 else (((1,), (0,)), ((), ()))
    return lax.dot_general(cols_of(ref, owner, rows), other, dims, preferred_element_type=F32)


def middle_kernel(
    n,
    n_tp,
    capp,
    x_hbm,
    u_hbm,
    gu_a,
    gu_c,
    gu_b,
    gu_own,
    dn_a,
    dn_c,
    dn_b,
    dn_own,
    gates,
    nt,
    pg,
    og,
    sh,
    back,
    g_back,
    o_hbm,
    dw_recv,
    dw_own,
    dw_y,
    gu_out,
    dn_out,
    w,
    xb,
    ub,
    rgb,
    eb,
    rbs,
    gbs,
    ring_recv,
    ring_send,
    w_sem,
    x_sem,
    u_sem,
    out_sem,
    ring_ss,
    ring_rs,
    free,
    back_ss,
    back_rs,
    gate_ss,
    gate_rs,
    dw_ss,
    dw_rs,
    dw_sem,
):
    ep = lax.axis_index("ep")
    tp = lax.axis_index("tp")
    core_peer, y_peer = flip(tp, 1), flip(tp, 2)
    gr = ub.shape[1]
    width = u_hbm.shape[1]
    units = w.shape[1]
    quarter = units // 4
    groups = x_hbm.shape[0] // gr
    per = n // groups
    rows = gu_out.shape[1]
    half = ring_recv.shape[3]
    p = ring_place(ep, n)
    nxt = ring_member(lax.rem(p + 1, n), n)
    prv = ring_member(lax.rem(p + n - 1, n), n)

    w_in = [
        pltpu.make_async_copy(ref, w.at[:2, i * quarter : (i + 1) * quarter, :], w_sem.at[i])
        for i, ref in enumerate((gu_a, gu_c, gu_b, gu_own))
    ] + [
        pltpu.make_async_copy(ref, w.at[2, i * quarter : (i + 1) * quarter, :], w_sem.at[4 + i])
        for i, ref in enumerate((dn_a, dn_c, dn_b, dn_own))
    ]
    for copy in w_in:
        copy.start()

    x_in = pltpu.make_async_copy(x_hbm, xb, x_sem)

    def u_copy(g):
        at = pl.ds(pl.multiple_of(g * gr, gr), gr)
        slot = lax.rem(g, 2)
        return pltpu.make_async_copy(u_hbm.at[at, :], ub.at[slot], u_sem.at[slot])

    x_in.start()
    u_copy(0).start()
    greet(n, n_tp, ep, tp)

    edges = [0]
    for ring in range(4):
        edges.append(edges[-1] + (3 * units // 128 + 3 - ring) // 4 * 128)
    wide_of = [edges[i + 1] - edges[i] for i in range(4)]

    def block_of(ring, step):
        if ring < 2:
            return ring_member(lax.rem(p + 2 * n - 1 - step, n), n)
        return ring_member(lax.rem(p + 1 + step, n), n)

    def term(ring, owner):
        lo, hi = edges[ring], edges[ring + 1]
        parts = []
        if lo < 2 * units:
            parts.append(block_dot(nt, owner, rows, pg[:, lo : min(hi, 2 * units)]))
        if hi > 2 * units:
            parts.append(block_dot(og, owner, rows, sh[:, max(lo - 2 * units, 0) : hi - 2 * units]))
        return parts[0] if len(parts) == 1 else jnp.concatenate(parts, axis=1)

    def ring_copy(ring, slot):
        return remote(
            ring_send.at[ring, slot, :, : wide_of[ring]],
            ring_recv.at[ring, slot, :, : wide_of[ring]],
            ring_ss.at[ring, slot],
            ring_rs.at[ring, slot],
            "ep",
            nxt if ring < 2 else prv,
        )

    order = (0, 2, 1, 3)

    def ring_step(step):
        slot, last = lax.rem(step, 2), lax.rem(step + 1, 2)
        for ring in order:
            size = wide_of[ring]
            mine = term(ring, block_of(ring, step))
            ring_copy(ring, last).wait_recv()

            @pl.when(step >= 2)
            def _():
                ring_copy(ring, slot).wait_send()

            ring_send[ring, slot, :, :size] = (
                mine + ring_recv[ring, last, :, :size].astype(F32)
            ).astype(BF)

            @pl.when(step <= n - 3)
            def _():
                pl.semaphore_signal(
                    free.at[ring],
                    1,
                    device_id={"ep": prv if ring < 2 else nxt},
                    device_id_type=pl.DeviceIdType.MESH,
                )

            @pl.when(step >= 2)
            def _():
                pl.semaphore_wait(free.at[ring], 1)

            ring_copy(ring, slot).start()

    for ring in order:
        ring_send[ring, 0, :, : wide_of[ring]] = term(ring, block_of(ring, 0)).astype(BF)
        ring_copy(ring, 0).start()

    for copy in w_in:
        copy.wait()
    x_in.wait()

    nt_dims, first_dims = (((1,), (1,)), ((), ())), (((0,), (0,)), ((), ()))

    def saved(g):
        at = pl.ds(pl.multiple_of(g * gr, gr), gr)
        slot = lax.rem(g, 2)
        return pltpu.make_async_copy(ub.at[slot], o_hbm.at[at, :], out_sem.at[slot])

    def back_copy(r):
        at = pl.ds(pl.multiple_of(r * capp, capp), capp)
        return remote(
            rbs.at[at, :], back.at[at, :], back_ss.at[r], back_rs.at[r], "ep", lax.rem(ep + n - r, n)
        )

    kept_copy = pltpu.make_async_copy(rbs.at[:capp, :], back.at[:capp, :], back_ss.at[0])

    def gate_copy(r):
        return remote(
            gbs.at[r], g_back.at[r], gate_ss.at[r], gate_rs.at[r], "ep", lax.rem(ep + n - r, n)
        )

    g_kept = pltpu.make_async_copy(gbs.at[0], g_back.at[0], gate_ss.at[0])
    gbs[...] = jnp.zeros_like(gbs)

    @pl.loop(0, groups)
    def _(g):
        slot = lax.rem(g, 2)
        mine = pl.ds(pl.multiple_of(g * gr, gr), gr)
        u_copy(g).wait()

        @pl.when(g >= 1)
        def _():
            saved(g - 1).wait()

        @pl.when(g + 1 < groups)
        def _():
            u_copy(g + 1).start()

        gate = jnp.concatenate([gate_column(gates, g * per + i, capp) for i in range(per)], axis=0)
        rgb[mine, :] = (gate * ub[slot].astype(F32)).astype(BF)

        def hidden(at):
            x = xb[mine, :]
            g_pre = lax.dot_general(x, w[0, at, :], nt_dims, preferred_element_type=F32)
            u_pre = lax.dot_general(x, w[1, at, :], nt_dims, preferred_element_type=F32)
            grad = lax.dot_general(rgb[mine, :], w[2, at, :], nt_dims, preferred_element_type=F32)
            sig = jax.nn.sigmoid(g_pre)
            eb[2, mine, at] = (g_pre * sig * u_pre).astype(BF)
            eb[0, mine, at] = (grad * u_pre * sig * (1.0 + g_pre * (1.0 - sig))).astype(BF)
            eb[1, mine, at] = (grad * g_pre * sig).astype(BF)

        @pl.loop(0, units // 256)
        def _(c):
            hidden(pl.ds(pl.multiple_of(c * 256, 256), 256))

        if units % 256:
            hidden(pl.ds(units // 256 * 256, units % 256))

        def columns(c, total):
            at = pl.ds(pl.multiple_of(c * 256, 256), 256)
            out = jnp.dot(eb[2, mine, :], w[2, :, at], preferred_element_type=F32)
            grad = jnp.dot(eb[0, mine, :], w[0, :, at], preferred_element_type=F32) + jnp.dot(
                eb[1, mine, :], w[1, :, at], preferred_element_type=F32
            )
            rbs[mine, at] = grad.astype(BF)
            total = total + jnp.sum(out * ub[slot, :, at].astype(F32), axis=1, keepdims=True)
            ub[slot, :, at] = out.astype(BF)
            return total

        total = lax.fori_loop(0, width // 256, columns, jnp.zeros((gr, 1), F32))
        hi = total.astype(BF).astype(F32)
        lane = lax.broadcasted_iota(jnp.int32, (gr, 128), 1)
        terms = jnp.where(lane == 0, hi, jnp.where(lane == 1, total - hi, 0.0)).astype(BF)
        pick = (
            lax.broadcasted_iota(jnp.int32, (16, 128), 0) == lax.broadcasted_iota(jnp.int32, (16, 128), 1)
        ).astype(F32).astype(BF)
        turned = lax.dot_general(pick, terms, nt_dims, preferred_element_type=F32).astype(BF)
        for i in range(per):
            gbs[g * per + i, :, :capp] = turned[:, i * capp : (i + 1) * capp]
        saved(g).start()
        for i in range(per):
            r = g * per + i
            if i == 0:

                @pl.when(g == 0)
                def _():
                    kept_copy.start()
                    g_kept.start()

                @pl.when(g > 0)
                def _():
                    back_copy(r).start()
                    gate_copy(r).start()
            else:
                back_copy(r).start()
                gate_copy(r).start()

        @pl.when(lax.rem(g, 2) == 1)
        def _():
            ring_step((g + 1) // 2)

    def weight_rows(at):
        for k in range(3):
            for c in range(0, width, 512):
                w[k, at, c : c + 512] = lax.dot_general(
                    eb[k, :, at],
                    (rgb if k == 2 else xb)[:, c : c + 512],
                    first_dims,
                    preferred_element_type=F32,
                ).astype(BF)

    @pl.loop(0, units // 256)
    def _(c):
        weight_rows(pl.ds(pl.multiple_of(c * 256, 256), 256))

    if units % 256:
        weight_rows(pl.ds(units // 256 * 256, units % 256))

    dw_core = remote(
        w.at[:, : 2 * quarter, :], dw_recv, dw_ss.at[0], dw_rs.at[0], "tp", core_peer
    )
    dw_core.start()
    ring_step(groups // 2 + 1)
    dw_core.wait()
    dw_in = pltpu.make_async_copy(dw_recv, w.at[:, : 2 * quarter, :], dw_sem.at[0])
    dw_in.start()
    dw_in.wait()
    for k in range(3):

        @pl.loop(0, quarter // 32)
        def _(c, k=k):
            far = pl.ds(pl.multiple_of(2 * quarter + c * 32, 32), 32)
            came = pl.ds(pl.multiple_of(quarter + c * 32, 32), 32)
            w[k, far, :] = (w[k, far, :].astype(F32) + w[k, came, :].astype(F32)).astype(BF)

    dw_far = remote(
        w.at[:, 2 * quarter : 3 * quarter, :], dw_y, dw_ss.at[1], dw_rs.at[1], "tp", y_peer
    )
    dw_far.start()
    for k in range(3):

        @pl.loop(0, quarter // 32)
        def _(c, k=k):
            far = pl.ds(pl.multiple_of(3 * quarter + c * 32, 32), 32)
            came = pl.ds(pl.multiple_of(c * 32, 32), 32)
            w[k, far, :] = (w[k, far, :].astype(F32) + w[k, came, :].astype(F32)).astype(BF)

    dw_keep = pltpu.make_async_copy(w.at[:, 3 * quarter :, :], dw_own, dw_sem.at[1])
    dw_keep.start()

    @pl.loop(groups // 2 + 2, n - 1)
    def _(step):
        ring_step(step)

    for ring in order:
        mine = term(ring, ep)
        ring_copy(ring, n % 2).wait_recv()
        done = mine + ring_recv[ring, n % 2, :, : wide_of[ring]].astype(F32)
        lo, hi = edges[ring], edges[ring + 1]
        for k, out in enumerate((gu_out.at[0], gu_out.at[1], dn_out)):
            a, b = max(lo, k * units), min(hi, (k + 1) * units)
            if a < b:
                out[:, a - k * units : b - k * units] = done[:, a - lo : b - lo].astype(BF)
    for ring in range(4):
        for slot in range(2):
            ring_copy(ring, slot).wait_send()
    g_kept.wait()
    kept_copy.wait()
    saved(groups - 1).wait()
    dw_keep.wait()
    dw_far.wait()

    @pl.loop(1, n)
    def _(r):
        back_copy(r).wait()
        gate_copy(r).wait()


def routed_expert(n, n_tp, capp, x, u, weights, gates, nt, pg, og, sh):
    total, width = x.shape
    units = 4 * weights[-1].shape[0]
    gr = total // 4
    rows = width // n
    half = (3 * units // 128 + 3) // 4 * 128
    vmem = pl.BlockSpec(memory_space=pltpu.VMEM)
    hbm = pl.BlockSpec(memory_space=pl.ANY)
    dma = pltpu.SemaphoreType.DMA
    if rows % 128:
        nt, og = nt.T, og.T
    return pl.pallas_call(
        functools.partial(middle_kernel, n, n_tp, capp),
        out_shape=(
            jax.ShapeDtypeStruct((total, width), BF),
            jax.ShapeDtypeStruct((n, 16, 128), BF),
            jax.ShapeDtypeStruct((total, width), BF),
            jax.ShapeDtypeStruct((3, units // 2, width), BF),
            jax.ShapeDtypeStruct((3, units // 4, width), BF),
            jax.ShapeDtypeStruct((3, units // 4, width), BF),
            jax.ShapeDtypeStruct((2, rows, units), BF),
            jax.ShapeDtypeStruct((rows, units), BF),
        ),
        in_specs=[hbm] * 10 + [vmem] * 5,
        out_specs=[hbm] * 6 + [vmem] * 2,
        scratch_shapes=[
            pltpu.VMEM((3, units, width), BF),
            pltpu.VMEM((total, width), BF),
            pltpu.VMEM((2, gr, width), BF),
            pltpu.VMEM((total, width), BF),
            pltpu.VMEM((3, total, units), BF),
            pltpu.VMEM((total, width), BF),
            pltpu.VMEM((n, 16, 128), BF),
            pltpu.VMEM((4, 2, rows, half), BF),
            pltpu.VMEM((4, 2, rows, half), BF),
            dma((8,)),
            dma,
            dma((2,)),
            dma((2,)),
            dma((4, 2)),
            dma((4, 2)),
            pltpu.SemaphoreType.REGULAR((4,)),
            dma((n,)),
            dma((n,)),
            dma((n,)),
            dma((n,)),
            dma((2,)),
            dma((2,)),
            dma((2,)),
        ],
        compiler_params=pltpu.CompilerParams(
            collective_id=1, has_side_effects=True, vmem_limit_bytes=63 * 2**20
        ),
        cost_estimate=pl.CostEstimate(
            flops=2 * total * width * 6 * units, bytes_accessed=40 * 2**20, transcendentals=0
        ),
    )(x, u, *weights, gates, nt, pg, og, sh)


def tp_total(
    project, between, tp, core_send, core_recv, y_send, y_recv, summed,
    core_ss, core_rs, y_ss, y_rs, g_ss, g_rs,
):
    core_peer, y_peer = flip(tp, 1), flip(tp, 2)
    pieces, size = core_send.shape[0], core_send.shape[2]
    half = pieces * size

    def core_copy(i):
        return remote(core_send.at[i], core_recv.at[i], core_ss.at[i], core_rs.at[i], "tp", core_peer)

    def y_copy(i):
        return remote(y_send.at[i], y_recv.at[i], y_ss.at[i], y_rs.at[i], "tp", y_peer)

    def gather_copy(i, slot):
        return remote(summed.at[slot, i], summed.at[slot, i], g_ss.at[i], g_rs.at[i], "tp", core_peer)

    me, other = tp % 2, core_peer % 2
    for i in range(pieces):
        core_send[i] = project(other * half, i, size).astype(BF)
        core_copy(i).start()
        own = project(me * half, i, size)
        core_copy(i).wait_recv()
        y_send[i] = (own + core_recv[i].astype(F32)).astype(BF)
        y_copy(i).start()
    between()
    for i in range(pieces):
        y_copy(i).wait_recv()
        summed[me, i] = (y_send[i].astype(F32) + y_recv[i].astype(F32)).astype(BF)
        gather_copy(i, me).start()
    for i in range(pieces):
        gather_copy(i, other).wait_recv()
    for i in range(pieces):
        core_copy(i).wait_send()
        y_copy(i).wait_send()
        gather_copy(i, me).wait_send()


def blocks_at_once(n, capp):
    per = 1
    while 2 * per * capp <= 128 and n % (2 * per) == 0:
        per *= 2
    return per


def gate_column(tiles, r, capp):
    ones = jnp.ones((16, 128), BF)
    return lax.dot_general(
        tiles[r, :, :capp], ones, (((0,), (0,)), ((), ())), preferred_element_type=F32
    )[:, :1]


def front_kernel(
    n,
    n_tp,
    capp,
    hidden,
    gain1,
    gain2,
    w,
    bias,
    cosine,
    sine,
    prefix,
    ow,
    place,
    cot,
    gu_own,
    dn_own,
    up_rows,
    gu_a,
    dn_a,
    dn_b,
    n1,
    qkv,
    ctx,
    mid,
    nt,
    up_sent,
    core_send,
    core_recv,
    y_send,
    y_recv,
    summed,
    up_ss,
    up_rs,
    w_ss,
    w_rs,
    core_ss,
    core_rs,
    y_ss,
    y_rs,
    g_ss,
    g_rs,
):
    ep = lax.axis_index("ep")
    tp = lax.axis_index("tp")
    tokens, width = hidden.shape
    lw = ctx.shape[1]
    heads = lw // HEAD_DIM
    core_peer, y_peer = flip(tp, 1), flip(tp, 2)
    greet(n, n_tp, ep, tp)

    def up_copy(r, way):
        to = lax.rem(ep + r, n) if way == "out" else lax.rem(ep + n - r, n)
        at = pl.ds(pl.multiple_of(r * capp, capp), capp)
        return remote(up_sent.at[at, :], up_rows.at[at, :], up_ss.at[r], up_rs.at[r], "ep", to)

    kept = pltpu.make_async_copy(up_sent.at[:capp, :], up_rows.at[:capp, :], up_ss.at[0])
    per = blocks_at_once(n, capp)
    size = per * capp

    @pl.loop(0, n // per)
    def _(b):
        at = pl.ds(pl.multiple_of(b * size, size), size)
        up_sent[at, :] = jnp.dot(place[at, :], cot[...], preferred_element_type=F32).astype(BF)
        for i in range(per):
            if i == 0:

                @pl.when(b == 0)
                def _():
                    kept.start()

                @pl.when(b > 0)
                def _():
                    up_copy(b * per, "out").start()
            else:
                up_copy(b * per + i, "out").start()

    w_copies = [
        remote(dn_own, dn_b, w_ss.at[0], w_rs.at[0], "tp", y_peer),
        remote(dn_own, dn_a, w_ss.at[1], w_rs.at[1], "tp", core_peer),
        remote(gu_own, gu_a, w_ss.at[2], w_rs.at[2], "tp", core_peer),
    ]
    for copy in w_copies:
        copy.start()

    @pl.loop(0, tokens // 64)
    def _(m):
        at = pl.ds(pl.multiple_of(m * 64, 64), 64)
        h = hidden[at, :].astype(F32)
        factor = lax.rsqrt(jnp.sum(h * h, axis=1, keepdims=True) * (1.0 / width) + EPSILON)
        n1[at, :] = (h * factor * gain1[...]).astype(BF)

    for k in range(3):

        @pl.loop(0, lw // 256)
        def _(c, k=k):
            at = pl.ds(pl.multiple_of(c * 256, 256), 256)
            x = jnp.dot(n1[...], w[k, :, at], preferred_element_type=F32) + bias[k : k + 1, at]
            if k < 2:
                x = jnp.concatenate(
                    [
                        x[:, i * HEAD_DIM : (i + 1) * HEAD_DIM] * cosine[...]
                        + pltpu.roll(x[:, i * HEAD_DIM : (i + 1) * HEAD_DIM], HEAD_DIM // 2, 1) * sine[...]
                        for i in range(256 // HEAD_DIM)
                    ],
                    axis=1,
                )
            qkv[k, :, at] = x.astype(BF)

    @pl.loop(0, tokens // 128)
    def _(m):
        at = pl.ds(pl.multiple_of(m * 128, 128), 128)
        row = lax.broadcasted_iota(jnp.int32, (128, tokens), 0) + m * 128
        col = lax.broadcasted_iota(jnp.int32, (128, tokens), 1)
        visible = (col <= row) | (col < prefix[...])
        for i in range(heads):
            lanes = slice(i * HEAD_DIM, (i + 1) * HEAD_DIM)
            s = lax.dot_general(
                qkv[0, at, lanes], qkv[1, :, lanes], (((1,), (1,)), ((), ())), preferred_element_type=F32
            )
            s = jnp.where(visible, s * HEAD_DIM ** (-0.5), -1e30)
            e = jnp.exp(s - jnp.max(s, axis=1, keepdims=True))
            e = e * (1.0 / jnp.sum(e, axis=1, keepdims=True))
            ctx[at, lanes] = jnp.dot(
                e.astype(BF), qkv[2, :, lanes], preferred_element_type=F32
            ).astype(BF)

    pieces, size = core_send.shape[0], core_send.shape[2]
    half = pieces * size

    def project(base, i, size):
        at = pl.ds(pl.multiple_of(base + i * size, size), size)
        return lax.dot_general(
            ctx[...], ow[at, :], (((1,), (1,)), ((), ())), preferred_element_type=F32
        )

    tp_total(
        project, lambda: None, tp, core_send, core_recv, y_send, y_recv, summed,
        core_ss, core_rs, y_ss, y_rs, g_ss, g_rs,
    )

    @pl.loop(0, tokens // 32)
    def _(m):
        at = pl.ds(pl.multiple_of(m * 32, 32), 32)
        total = jnp.zeros((32, 1), F32)
        for j in range(2):
            for i in range(pieces):
                lanes = slice(j * half + i * size, j * half + (i + 1) * size)
                x = hidden[at, lanes].astype(F32) + summed[j, i, at, :].astype(F32)
                mid[at, lanes] = x
                total = total + jnp.sum(x * x, axis=1, keepdims=True)
        factor = lax.rsqrt(total * (1.0 / width) + EPSILON)
        nt[at, :] = (mid[at, :] * factor * gain2[...]).astype(BF)

    for copy in w_copies:
        copy.wait()
    kept.wait()
    for r in range(1, n):
        up_copy(r, "in").wait()


def front(n, n_tp, capp, hidden, gain1, gain2, w, bias, cosine, sine, prefix, ow, place, cot, gu_own, dn_own):
    tokens, width = hidden.shape
    lw = ow.shape[1]
    quarter = dn_own.shape[0]
    vmem = pl.BlockSpec(memory_space=pltpu.VMEM)
    hbm = pl.BlockSpec(memory_space=pl.ANY)
    dma = pltpu.SemaphoreType.DMA
    return pl.pallas_call(
        functools.partial(front_kernel, n, n_tp, capp),
        out_shape=(
            jax.ShapeDtypeStruct((n * capp, width), BF),
            jax.ShapeDtypeStruct((2, quarter, width), BF),
            jax.ShapeDtypeStruct((quarter, width), BF),
            jax.ShapeDtypeStruct((quarter, width), BF),
            jax.ShapeDtypeStruct((tokens, width), BF),
            jax.ShapeDtypeStruct((3, tokens, lw), BF),
            jax.ShapeDtypeStruct((tokens, lw), BF),
            jax.ShapeDtypeStruct((tokens, width), F32),
            jax.ShapeDtypeStruct((tokens, width), BF),
        ),
        in_specs=[vmem] * 11 + [hbm] * 2,
        out_specs=[hbm] * 4 + [vmem] * 5,
        scratch_shapes=[
            pltpu.VMEM((n * capp, width), BF),
            pltpu.VMEM((4, tokens, width // 8), BF),
            pltpu.VMEM((4, tokens, width // 8), BF),
            pltpu.VMEM((4, tokens, width // 8), BF),
            pltpu.VMEM((4, tokens, width // 8), BF),
            pltpu.VMEM((2, 4, tokens, width // 8), BF),
            dma((n,)),
            dma((n,)),
            dma((3,)),
            dma((3,)),
            dma((4,)),
            dma((4,)),
            dma((4,)),
            dma((4,)),
            dma((4,)),
            dma((4,)),
        ],
        compiler_params=pltpu.CompilerParams(
            collective_id=2, has_side_effects=True, vmem_limit_bytes=56 * 2**20
        ),
        cost_estimate=pl.CostEstimate(
            flops=2 * tokens * width * 4 * lw, bytes_accessed=30 * 2**20, transcendentals=0
        ),
    )(hidden, gain1, gain2, w, bias, cosine, sine, prefix, ow, place, cot, gu_own, dn_own)


def dispatch_kernel(
    n,
    n_tp,
    capp,
    n_exp,
    nt,
    place,
    router,
    cot,
    sgu,
    sdn,
    gu_own,
    dn_b,
    x_rows,
    g_rows,
    gu_b,
    gu_c,
    dn_c,
    probs,
    gate,
    og,
    pg,
    sh,
    part,
    sback,
    sgrad,
    x_send,
    g_send,
    x_ss,
    x_rs,
    gate_ss,
    gate_rs,
    w_ss,
    w_rs,
):
    ep = lax.axis_index("ep")
    tp = lax.axis_index("tp")
    tokens, width = nt.shape
    units = sdn.shape[1]
    total = place.shape[0]
    core_peer, y_peer = flip(tp, 1), flip(tp, 2)
    greet(n, n_tp, ep, tp)
    w_y = remote(gu_own, gu_b, w_ss.at[0], w_rs.at[0], "tp", y_peer)
    w_y.start()
    w_on = remote(dn_b, dn_c, w_ss.at[1], w_rs.at[1], "tp", core_peer)
    w_on.start()

    def x_copy(r, way):
        to = lax.rem(ep + r, n) if way == "out" else lax.rem(ep + n - r, n)
        at = pl.ds(pl.multiple_of(r * capp, capp), capp)
        return remote(x_send.at[at, :], x_rows.at[at, :], x_ss.at[r], x_rs.at[r], "ep", to)

    def gate_copy(r, way):
        to = lax.rem(ep + r, n) if way == "out" else lax.rem(ep + n - r, n)
        return remote(g_send.at[r], g_rows.at[r], gate_ss.at[r], gate_rs.at[r], "ep", to)

    kept = pltpu.make_async_copy(x_send.at[:capp, :], x_rows.at[:capp, :], x_ss.at[0])
    g_kept = pltpu.make_async_copy(g_send.at[0], g_rows.at[0], gate_ss.at[0])
    per = blocks_at_once(n, capp)
    size = per * capp

    @pl.loop(0, n // per)
    def _(b):
        at = pl.ds(pl.multiple_of(b * size, size), size)
        x_send[at, :] = jnp.dot(place[at, :], nt[...], preferred_element_type=F32).astype(BF)
        for i in range(per):
            if i == 0:

                @pl.when(b == 0)
                def _():
                    kept.start()

                @pl.when(b > 0)
                def _():
                    x_copy(b * per, "out").start()
            else:
                x_copy(b * per + i, "out").start()

    logits = jnp.dot(nt[...], router[...], preferred_element_type=F32)
    lane = lax.broadcasted_iota(jnp.int32, logits.shape, 1)
    chosen = jnp.where(lane < n_exp, logits, -1e30)
    e = jnp.exp(chosen - jnp.max(chosen, axis=1, keepdims=True))
    prob = e / jnp.sum(e, axis=1, keepdims=True)
    prob = jnp.where(lane == n_exp, jax.nn.sigmoid(logits), prob)
    probs[...] = prob
    hi = prob.astype(BF)
    lo = (prob - hi.astype(F32)).astype(BF)
    g_send[...] = jnp.zeros_like(g_send)
    across = (((0,), (1,)), ((), ()))

    @pl.loop(0, n)
    def _(r):
        where = place[pl.ds(pl.multiple_of(r * capp, capp), capp), :]
        expert = lax.rem(r + ep, n)
        pick = lax.broadcasted_iota(jnp.int32, (128, capp), 0) == expert
        g_hi = jnp.sum(
            jnp.where(pick, lax.dot_general(hi, where, across, preferred_element_type=F32), 0.0),
            axis=0,
            keepdims=True,
        )
        g_lo = jnp.sum(
            jnp.where(pick, lax.dot_general(lo, where, across, preferred_element_type=F32), 0.0),
            axis=0,
            keepdims=True,
        )
        term = lax.broadcasted_iota(jnp.int32, (16, capp), 0)
        g_send[r, :, :capp] = jnp.where(term == 0, g_hi, jnp.where(term == 1, g_lo, 0.0)).astype(BF)
        gate[r] = g_hi + g_lo

        @pl.when(r == 0)
        def _():
            g_kept.start()

        @pl.when(r > 0)
        def _():
            gate_copy(r, "out").start()

    @pl.loop(0, tokens // 64)
    def _(m):
        at = pl.ds(pl.multiple_of(m * 64, 64), 64)
        og[at, :] = (probs[at, n_exp : n_exp + 1] * cot[at, :].astype(F32)).astype(BF)

    def hidden(at, up_at):
        g_pre = jnp.dot(nt[...], sgu[0, :, at], preferred_element_type=F32)
        u_pre = jnp.dot(nt[...], sgu[1, :, at], preferred_element_type=F32)
        grad = jnp.dot(og[...], sdn[:, at], preferred_element_type=F32)
        sig = jax.nn.sigmoid(g_pre)
        sh[:, at] = (g_pre * sig * u_pre).astype(BF)
        pg[:, at] = (grad * u_pre * sig * (1.0 + g_pre * (1.0 - sig))).astype(BF)
        pg[:, up_at] = (grad * g_pre * sig).astype(BF)

    @pl.loop(0, units // 256)
    def _(c):
        hidden(
            pl.ds(pl.multiple_of(c * 256, 256), 256),
            pl.ds(pl.multiple_of(c * 256 + units, 128), 256),
        )

    if units % 256:
        rest = units // 256 * 256
        hidden(pl.ds(rest, units - rest), pl.ds(units + rest, units - rest))

    w_y.wait()
    w_far = remote(gu_b, gu_c, w_ss.at[2], w_rs.at[2], "tp", core_peer)
    w_far.start()

    nt_dims = (((1,), (1,)), ((), ()))

    share = probs[:, n_exp : n_exp + 1]

    def columns(c, total):
        at = pl.ds(pl.multiple_of(c * 256, 256), 256)
        out = lax.dot_general(sh[...], sdn[at, :], nt_dims, preferred_element_type=F32)
        part[:, at] = (share * out).astype(BF)
        sback[:, at] = lax.dot_general(
            pg[:, :units], sgu[0, at, :], nt_dims, preferred_element_type=F32
        ) + lax.dot_general(pg[:, units:], sgu[1, at, :], nt_dims, preferred_element_type=F32)
        return total + jnp.sum(cot[:, at].astype(F32) * out, axis=1, keepdims=True)

    sgrad[...] = lax.fori_loop(0, width // 256, columns, jnp.zeros((tokens, 1), F32))

    w_on.wait()
    w_far.wait()
    kept.wait()
    g_kept.wait()

    @pl.loop(1, n)
    def _(r):
        gate_copy(r, "in").wait()
        x_copy(r, "in").wait()


def dispatch(n, n_tp, capp, n_exp, nt, place, router, cot, sgu, sdn, gu_own, dn_b):
    tokens, width = nt.shape
    units = sdn.shape[1]
    total = place.shape[0]
    vmem = pl.BlockSpec(memory_space=pltpu.VMEM)
    hbm = pl.BlockSpec(memory_space=pl.ANY)
    dma = pltpu.SemaphoreType.DMA
    return pl.pallas_call(
        functools.partial(dispatch_kernel, n, n_tp, capp, n_exp),
        out_shape=(
            jax.ShapeDtypeStruct((total, width), BF),
            jax.ShapeDtypeStruct((n, 16, 128), BF),
            jax.ShapeDtypeStruct(gu_own.shape, BF),
            jax.ShapeDtypeStruct(gu_own.shape, BF),
            jax.ShapeDtypeStruct(dn_b.shape, BF),
            jax.ShapeDtypeStruct((tokens, 128), F32),
            jax.ShapeDtypeStruct((n, 1, capp), F32),
            jax.ShapeDtypeStruct((tokens, width), BF),
            jax.ShapeDtypeStruct((tokens, 2 * units), BF),
            jax.ShapeDtypeStruct((tokens, units), BF),
            jax.ShapeDtypeStruct((tokens, width), BF),
            jax.ShapeDtypeStruct((tokens, width), F32),
            jax.ShapeDtypeStruct((tokens, 1), F32),
        ),
        in_specs=[vmem] * 6 + [hbm] * 2,
        out_specs=[hbm] * 5 + [vmem] * 8,
        scratch_shapes=[
            pltpu.VMEM((total, width), BF),
            pltpu.VMEM((n, 16, 128), BF),
            dma((n,)),
            dma((n,)),
            dma((n,)),
            dma((n,)),
            dma((3,)),
            dma((3,)),
        ],
        compiler_params=pltpu.CompilerParams(
            collective_id=3, has_side_effects=True, vmem_limit_bytes=60 * 2**20
        ),
        cost_estimate=pl.CostEstimate(
            flops=2 * tokens * width * 6 * units, bytes_accessed=40 * 2**20, transcendentals=0
        ),
    )(nt, place, router, cot, sgu, sdn, gu_own, dn_b)

def backward_kernel(
    n,
    n_tp,
    capp,
    n_exp,
    back,
    g_back,
    place_t,
    sback,
    sgrad,
    probs,
    router,
    nt,
    mid,
    cot,
    gain2,
    qkv,
    ow,
    cosine,
    sine,
    prefix,
    o_sent,
    o_rows,
    ag,
    lg,
    bias,
    small,
    core_send,
    core_recv,
    y_send,
    y_recv,
    summed,
    few_send,
    few_recv,
    ng,
    cg,
    dk,
    dv,
    o_ss,
    o_rs,
    core_ss,
    core_rs,
    y_ss,
    y_rs,
    g_ss,
    g_rs,
    few_ss,
    few_rs,
):
    ep = lax.axis_index("ep")
    tp = lax.axis_index("tp")
    tokens, width = nt.shape
    total = back.shape[0]
    lw = ow.shape[1]
    heads = lw // HEAD_DIM
    core_peer, y_peer = flip(tp, 1), flip(tp, 2)
    greet(n, n_tp, ep, tp)

    def o_copy(r):
        at = pl.ds(pl.multiple_of(r * capp, capp), capp)
        return remote(
            o_sent.at[at, :], o_rows.at[at, :], o_ss.at[r], o_rs.at[r], "ep", lax.rem(ep + n - r, n)
        )

    kept = pltpu.make_async_copy(o_sent.at[:capp, :], o_rows.at[:capp, :], o_ss.at[0])

    for r in range(1, n):
        o_copy(r).start()
    kept.start()

    row = lax.broadcasted_iota(jnp.int32, (total, 128), 0)
    spot = lax.broadcasted_iota(jnp.int32, (total, 128), 1)
    expert = lax.rem(row // capp + ep * (n_exp // n), n_exp)
    gg = jnp.concatenate([gate_column(g_back, r, capp) for r in range(n)], axis=0)
    few = jnp.dot(
        place_t[...], jnp.where(spot == expert, gg, 0.0).astype(BF), preferred_element_type=F32
    )
    lane = lax.broadcasted_iota(jnp.int32, (tokens, 128), 1)
    few_send[0] = jnp.where(lane == n_exp, sgrad[...], few).astype(BF)
    few_core = remote(few_send.at[0], few_recv.at[0], few_ss.at[0], few_rs.at[0], "tp", core_peer)
    few_core.start()

    def project(base, i, size):
        at = pl.ds(pl.multiple_of(base + i * size, size), size)
        return sback[:, at] + jnp.dot(place_t[...], back[:, at], preferred_element_type=F32)

    def between():
        few_core.wait()
        few_send[1] = (few_send[0].astype(F32) + few_recv[0].astype(F32)).astype(BF)
        few_y = remote(few_send.at[1], few_recv.at[1], few_ss.at[1], few_rs.at[1], "tp", y_peer)
        few_y.start()
        few_y.wait()

    tp_total(
        project, between, tp, core_send, core_recv, y_send, y_recv, summed,
        core_ss, core_rs, y_ss, y_rs, g_ss, g_rs,
    )

    prob = jnp.where(lane < n_exp, probs[...], 0.0)
    share = probs[:, n_exp : n_exp + 1]
    grads = few_send[1].astype(F32) + few_recv[1].astype(F32)
    inner = jnp.sum(prob * grads, axis=1, keepdims=True)
    gate_in = grads * share * (1.0 - share)
    few_send[0] = jnp.where(
        lane < n_exp, prob * (grads - inner), jnp.where(lane == n_exp, gate_in, 0.0)
    ).astype(BF)
    pieces, size = summed.shape[1], summed.shape[3]
    for j in range(2):
        for i in range(pieces):
            at = slice((j * pieces + i) * size, (j * pieces + i + 1) * size)
            ng[:, at] = summed[j, i].astype(F32) + lax.dot_general(
                few_send[0], router[at, :], (((1,), (1,)), ((), ())), preferred_element_type=F32
            )

    step = 32

    def norm_rows(m, acc):
        at = pl.ds(pl.multiple_of(m * step, step), step)
        h = mid[at, :]
        grad = ng[at, :]
        factor = lax.rsqrt(jnp.sum(h * h, axis=1, keepdims=True) * (1.0 / width) + EPSILON)
        scaled = grad * gain2[...]
        mean = jnp.sum(scaled * h, axis=1, keepdims=True) * (1.0 / width)
        ag[at, :] = (
            cot[at, :].astype(F32) + factor * scaled - h * (factor * factor * factor) * mean
        ).astype(BF)
        return acc + jnp.sum((grad * h * factor).reshape(step // 8, 8, width), axis=0)

    acc = lax.fori_loop(0, tokens // step, norm_rows, jnp.zeros((8, width), F32))

    @pl.loop(0, lw // 256)
    def _(c):
        at = pl.ds(pl.multiple_of(c * 256, 256), 256)
        cg[:, at] = jnp.dot(ag[...], ow[:, at], preferred_element_type=F32).astype(BF)

    dk[...] = jnp.zeros_like(dk)
    dv[...] = jnp.zeros_like(dv)
    first_dims, last_dims = (((0,), (0,)), ((), ())), (((1,), (1,)), ((), ()))

    def attend(m, sums):
        at = pl.ds(pl.multiple_of(m * 128, 128), 128)
        row = lax.broadcasted_iota(jnp.int32, (128, tokens), 0) + m * 128
        col = lax.broadcasted_iota(jnp.int32, (128, tokens), 1)
        visible = (col <= row) | (col < prefix[...])
        parts = []
        for i in range(heads):
            lanes = slice(i * HEAD_DIM, (i + 1) * HEAD_DIM)
            q, grad = qkv[0, at, lanes], cg[at, lanes]
            s = lax.dot_general(q, qkv[1, :, lanes], last_dims, preferred_element_type=F32)
            s = jnp.where(visible, s * HEAD_DIM ** (-0.5), -1e30)
            e = jnp.exp(s - jnp.max(s, axis=1, keepdims=True))
            e = e * (1.0 / jnp.sum(e, axis=1, keepdims=True))
            dp = lax.dot_general(grad, qkv[2, :, lanes], last_dims, preferred_element_type=F32)
            delta = jnp.sum(e * dp, axis=1, keepdims=True)
            ds = (e * (dp - delta)).astype(BF)
            dv[:, lanes] += lax.dot_general(e.astype(BF), grad, first_dims, preferred_element_type=F32)
            dk[:, lanes] += lax.dot_general(ds, q, first_dims, preferred_element_type=F32)
            dq = jnp.dot(ds, qkv[1, :, lanes], preferred_element_type=F32) * HEAD_DIM ** (-0.5)
            dq = dq * cosine[at, :] - pltpu.roll(dq, HEAD_DIM // 2, 1) * sine[at, :]
            lg[at, lanes] = dq.astype(BF)
            parts.append(jnp.sum(dq.reshape(16, 8, HEAD_DIM), axis=0))
        return sums + jnp.concatenate(parts, axis=1)

    sums = lax.fori_loop(0, tokens // 128, attend, jnp.zeros((8, lw), F32))
    bias[:, :lw] = jnp.sum(sums, axis=0, keepdims=True)
    for i in range(heads):
        lanes = slice(i * HEAD_DIM, (i + 1) * HEAD_DIM)
        grad = dk[:, lanes] * HEAD_DIM ** (-0.5)
        grad = grad * cosine[...] - pltpu.roll(grad, HEAD_DIM // 2, 1) * sine[...]
        at = slice(lw + i * HEAD_DIM, lw + (i + 1) * HEAD_DIM)
        lg[:, at] = grad.astype(BF)
        bias[:, at] = jnp.sum(grad, axis=0, keepdims=True)
    lg[:, 2 * lw :] = dv[...].astype(BF)
    bias[:, 2 * lw :] = jnp.sum(dv[...], axis=0, keepdims=True)

    wide = small.shape[0]
    gain_row = jnp.sum(acc, axis=0, keepdims=True)
    for c in range(0, width, 512):
        at = slice(c, c + 512)
        rows = lax.dot_general(few_send[0], nt[:, at], first_dims, preferred_element_type=F32)[:wide]
        index = lax.broadcasted_iota(jnp.int32, rows.shape, 0)
        small[:, at] = jnp.where(index == n_exp + 1, gain_row[:, at], rows).astype(BF)

    kept.wait()
    for r in range(1, n):
        o_copy(r).wait()


def backward(n, n_tp, capp, n_exp, back, g_back, place_t, sback, sgrad, probs, router, nt, mid, cot, gain2, qkv, ow, cosine, sine, prefix, o_sent):
    tokens, width = nt.shape
    lw = ow.shape[1]
    wide = -(-(n_exp + 2) // 16) * 16
    vmem = pl.BlockSpec(memory_space=pltpu.VMEM)
    hbm = pl.BlockSpec(memory_space=pl.ANY)
    dma = pltpu.SemaphoreType.DMA
    piece = (4, tokens, width // 8)
    return pl.pallas_call(
        functools.partial(backward_kernel, n, n_tp, capp, n_exp),
        out_shape=(
            jax.ShapeDtypeStruct(o_sent.shape, BF),
            jax.ShapeDtypeStruct((tokens, width), BF),
            jax.ShapeDtypeStruct((tokens, 3 * lw), BF),
            jax.ShapeDtypeStruct((1, 3 * lw), F32),
            jax.ShapeDtypeStruct((wide, width), BF),
        ),
        in_specs=[vmem] * 16 + [hbm],
        out_specs=[hbm] + [vmem] * 4,
        scratch_shapes=[
            pltpu.VMEM(piece, BF),
            pltpu.VMEM(piece, BF),
            pltpu.VMEM(piece, BF),
            pltpu.VMEM(piece, BF),
            pltpu.VMEM((2,) + piece, BF),
            pltpu.VMEM((2, tokens, 128), BF),
            pltpu.VMEM((2, tokens, 128), BF),
            pltpu.VMEM((tokens, width), F32),
            pltpu.VMEM((tokens, lw), BF),
            pltpu.VMEM((tokens, lw), F32),
            pltpu.VMEM((tokens, lw), F32),
            dma((n,)),
            dma((n,)),
            dma((4,)),
            dma((4,)),
            dma((4,)),
            dma((4,)),
            dma((4,)),
            dma((4,)),
            dma((2,)),
            dma((2,)),
        ],
        compiler_params=pltpu.CompilerParams(
            collective_id=4, has_side_effects=True, vmem_limit_bytes=60 * 2**20
        ),
        cost_estimate=pl.CostEstimate(
            flops=2 * tokens * width * 4 * lw, bytes_accessed=30 * 2**20, transcendentals=0
        ),
    )(back, g_back, place_t, sback, sgrad, probs, router, nt, mid, cot, gain2, qkv, ow, cosine, sine, prefix, o_sent)


def body(
    hidden,
    attn_gain,
    qkv_weight,
    qkv_bias,
    out_weight,
    mlp_gain,
    router_weight,
    share_gate,
    shared_gate_up,
    shared_down,
    expert_gate_up,
    expert_down,
    routes,
    priority,
    prefix,
    cotangent,
):
    tokens, width = hidden.shape
    n_ep = lax.axis_size("ep")
    n_tp = lax.axis_size("tp")
    tp_i = lax.axis_index("tp")
    cols = width // n_tp
    col_start = tp_i * cols
    head_size = HEAD_DIM
    local_width = qkv_weight.shape[2]
    heads = local_width // head_size
    expert_local = expert_gate_up.shape[0]
    n_exp = expert_local * n_ep
    top = routes.shape[1]
    capacity = (5 * tokens * top + 4 * n_exp - 1) // (4 * n_exp)
    part = -(-capacity // n_tp)
    part_pad = -(-part // 16) * 16
    rows = n_exp * part_pad

    flat_route = routes.T.reshape(-1)
    flat_order = priority.T.reshape(-1)
    hits = (flat_route[:, None] == jnp.arange(n_exp, dtype=jnp.int32)[None, :]).astype(BF)
    smaller = (flat_order[None, :] < flat_order[:, None]).astype(BF)
    counts = mm(smaller, hits, 1, 0)
    slot = jnp.sum(counts * hits.astype(F32), axis=1).astype(jnp.int32).reshape(top, tokens)
    kept = slot < capacity
    in_part = slot - tp_i * part
    mine = kept & (in_part >= 0) & (in_part < part)
    ep_i = lax.axis_index("ep")
    hop = lax.rem(routes.T + n_exp - ep_i * expert_local, n_exp)
    dest = jnp.where(mine, hop * part_pad + in_part, -1)
    row_ids = jnp.arange(rows, dtype=jnp.int32)[:, None]
    place = (dest[0][None, :] == row_ids)
    for k in range(1, top):
        place = place | (dest[k][None, :] == row_ids)
    place = place.astype(BF)
    dest_t = dest.T
    place_t = dest_t[:, :1] == row_ids.T
    for k in range(1, top):
        place_t = place_t | (dest_t[:, k : k + 1] == row_ids.T)
    place_t = place_t.astype(BF)


    residual_in = hidden.astype(F32)
    factor_one = norm_factor(residual_in)
    cosine, sine_val = angle_tables(tokens, head_size)
    cos_all = jnp.concatenate([cosine[:, 0], cosine[:, 0]], axis=1)
    sin_all = jnp.concatenate([-sine_val[:, 0], sine_val[:, 0]], axis=1)
    w_t = jnp.transpose(qkv_weight, (1, 0, 2))
    prefix_row = jnp.broadcast_to(prefix[None], (1, tokens))
    gu_own = jnp.transpose(expert_gate_up[0], (1, 2, 0))
    dn_own = jnp.transpose(expert_down[0], (1, 0))
    up_rows, gu_a, dn_a, dn_b, normed_one, qkv, context, middle, normed_two = front(
        n_ep,
        n_tp,
        part_pad,
        hidden,
        attn_gain[None],
        mlp_gain[None],
        w_t,
        qkv_bias,
        cos_all,
        sin_all,
        prefix_row,
        out_weight,
        place,
        cotangent,
        gu_own,
        dn_own,
    )

    router_all = jnp.concatenate(
        [router_weight, share_gate[:, None], jnp.zeros((width, 127 - n_exp), BF)], axis=1
    )
    got, gates, gu_b, gu_c, dn_c, probs_all, gate_sent, shared_out_grad, pre_grad, shared_hidden, scaled_part, shared_back, scale_grad = (
        dispatch(
            n_ep,
            n_tp,
            part_pad,
            n_exp,
            normed_two,
            place,
            router_all,
            cotangent,
            jnp.transpose(shared_gate_up, (1, 0, 2)),
            shared_down,
            gu_own,
            dn_b,
        )
    )
    back_rows, back_gates, e_out, _, dw_own, dw_y, gu_grad, shared_down_grad = routed_expert(
        n_ep,
        n_tp,
        part_pad,
        got,
        up_rows,
        (gu_a, gu_c, gu_b, gu_own, dn_a, dn_c, dn_b, dn_own),
        gates,
        normed_two,
        pre_grad,
        shared_out_grad,
        shared_hidden,
    )
    shared_gate_up_grad = jnp.transpose(gu_grad, (1, 0, 2)).astype(F32)
    shared_down_grad = shared_down_grad.astype(F32)
    dw = dw_own.astype(F32) + dw_y.astype(F32)
    expert_down_grad = jnp.transpose(dw[2], (1, 0))[None]
    expert_gate_up_grad = jnp.transpose(dw[:2], (2, 0, 1))[None]

    out_rows, attn_grad, linear_grad, bias_grad, small = backward(
        n_ep,
        n_tp,
        part_pad,
        n_exp,
        back_rows,
        back_gates,
        place_t,
        shared_back,
        scale_grad,
        probs_all,
        router_all,
        normed_two,
        middle,
        cotangent,
        mlp_gain[None],
        qkv,
        out_weight,
        cos_all,
        sin_all,
        prefix_row,
        e_out,
    )
    weighted_place = (place_t.astype(F32) * gate_sent.reshape(1, rows)).astype(BF)
    qkv_grad, out_weight_grad, input_grad, output, gain_one, bias_sum, small_sum = tail(
        n_ep,
        n_tp,
        normed_one,
        linear_grad,
        attn_grad,
        context,
        w_t,
        lax.dynamic_slice_in_dim(hidden, col_start, cols, 1),
        factor_one,
        lax.dynamic_slice_in_dim(attn_gain, col_start, cols, 0)[None],
        lax.dynamic_slice_in_dim(attn_grad, col_start, cols, 1),
        bias_grad,
        small,
        out_rows,
        weighted_place,
        scaled_part,
        lax.dynamic_slice_in_dim(middle, col_start, cols, 1),
    )
    qkv_weight_grad = jnp.transpose(qkv_grad, (1, 0, 2))
    gain_one_sum = gain_one[0]
    bias_sum = bias_sum.reshape(3, local_width)
    router_sum = small_sum[:n_exp].T
    share_gate_sum = small_sum[n_exp]
    gain_two_sum = small_sum[n_exp + 1]
    return (
        output,
        input_grad,
        gain_one_sum,
        qkv_weight_grad,
        bias_sum,
        out_weight_grad,
        gain_two_sum,
        router_sum,
        share_gate_sum,
        shared_gate_up_grad,
        shared_down_grad,
        expert_gate_up_grad,
        expert_down_grad,
    )


def solution(mesh):
    return jax.shard_map(
        body,
        mesh=mesh,
        in_specs=(
            P("ep", None),
            P(),
            P(None, None, "tp"),
            P(None, "tp"),
            P(None, "tp"),
            P(),
            P(),
            P(),
            P(None, None, "tp"),
            P(None, "tp"),
            P("ep", None, None, "tp"),
            P("ep", None, "tp"),
            P("ep", None),
            P("ep", None),
            P("ep"),
            P("ep", None),
        ),
        out_specs=(
            P("ep", "tp"),
            P("ep", "tp"),
            P(),
            P("ep", None, "tp"),
            P(None, "tp"),
            P("ep", "tp"),
            P(),
            P(),
            P(),
            P("ep", None, "tp"),
            P("ep", "tp"),
            P("ep", None, None, "tp"),
            P("ep", None, "tp"),
        ),
        check_vma=False,
    )
```

```python
import functools

import jax
import jax.numpy as jnp
import numpy as np
from jax import lax
from jax.experimental import pallas as pl
from jax.experimental.pallas import tpu as pltpu
from jax.sharding import PartitionSpec as P

HEAD_DIM = 128
EPSILON = 1e-06
THETA = 1000000.0
BF = jnp.bfloat16
F32 = jnp.float32


def mm(a, b, ca, cb):
    return lax.dot_general(a, b, (((ca,), (cb,)), ((), ())), preferred_element_type=F32)


def angle_tables(length, head_size):
    half_size = head_size // 2
    frequency = (THETA ** (-np.arange(half_size, dtype=np.float32) * 2.0 / head_size)).astype(np.float32)
    angles = (np.arange(length, dtype=np.float32)[:, None] * frequency[None, :]).astype(np.float64)
    cosine, sine_val = np.cos(angles), np.sin(angles)
    return (
        np.concatenate([cosine, cosine], axis=1).astype(np.float32),
        np.concatenate([-sine_val, sine_val], axis=1).astype(np.float32),
    )


def ring_place(e, n):
    odd = e % 2
    return (1 - odd) * (e // 2) + odd * (n - 1 - e // 2)


def ring_member(p, n):
    second = p // (n // 2)
    return (1 - second) * 2 * p + second * (2 * (n - 1 - p) + 1)


def remote(src, dst, send_sem, recv_sem, axis, index):
    return pltpu.make_async_remote_copy(
        src_ref=src,
        dst_ref=dst,
        send_sem=send_sem,
        recv_sem=recv_sem,
        device_id={axis: index},
        device_id_type=pl.DeviceIdType.MESH,
    )


def greet(n, n_tp, ep, tp):
    barrier = pltpu.get_barrier_semaphore()
    for shift in range(1, n):
        pl.semaphore_signal(
            barrier, 1, device_id={"ep": lax.rem(ep + shift, n)}, device_id_type=pl.DeviceIdType.MESH
        )
    for shift in range(1, n_tp):
        pl.semaphore_signal(
            barrier, 1, device_id={"tp": lax.rem(tp + shift, n_tp)}, device_id_type=pl.DeviceIdType.MESH
        )
    pl.semaphore_wait(barrier, n - 1 + n_tp - 1)


def flip(index, bit):
    if bit == 1:
        return index + 1 - 2 * (index % 2)
    return index + 2 - 4 * ((index // 2) % 2)


def tail_kernel(
    n,
    n_tp,
    n1,
    lg,
    ag,
    ctx,
    w,
    hidden,
    r_one,
    gain_all,
    bias,
    small,
    o_rows,
    weighted,
    spart,
    mid,
    ag_hbm,
    qkv_out,
    o_out,
    in_out,
    out_out,
    gain_out,
    bias_out,
    small_out,
    h_cols,
    res_cols,
    ag_cols,
    in_sem,
    ring_recv,
    ring_send,
    part_own,
    part_send,
    part_recv,
    y_send,
    y_recv,
    mean_send,
    mean_recv,
    vec_send,
    vec_recv,
    small_recv,
    small_sum,
    gain_send,
    gain_recv,
    out_send,
    out_recv,
    oy_send,
    oy_recv,
    ring_ss,
    ring_rs,
    tp_ss,
    tp_rs,
    vec_ss,
    vec_rs,
    small_ss,
    small_rs,
    gain_ss,
    gain_rs,
):
    ep = lax.axis_index("ep")
    tp = lax.axis_index("tp")
    tokens, lw = ctx.shape
    columns = pl.ds(pl.multiple_of(tp * lw, lw), lw)
    col_in = [
        pltpu.make_async_copy(hidden.at[:, columns], h_cols, in_sem.at[0]),
        pltpu.make_async_copy(mid.at[:, columns], res_cols, in_sem.at[1]),
        pltpu.make_async_copy(ag_hbm.at[:, columns], ag_cols, in_sem.at[2]),
    ]
    for copy in col_in:
        copy.start()
    gain = gain_all[:, columns]
    rows = qkv_out.shape[1]
    width = rows * n
    p = ring_place(ep, n)
    nxt = ring_member(lax.rem(p + 1, n), n)
    prv = ring_member(lax.rem(p + n - 1, n), n)
    core_peer, y_peer = flip(tp, 1), flip(tp, 2)
    greet(n, n_tp, ep, tp)

    def small_copy(shift, turn, way):
        to, came = lax.rem(ep + shift, n), lax.rem(ep + n - shift, n)
        if turn == 0:
            src, dst, arrived = small.at[to], small_recv.at[ep], small_recv.at[came]
        else:
            src, dst, arrived = small_sum, small_out.at[ep], small_out.at[came]
        sems = small_ss.at[turn, shift], small_rs.at[turn, shift]
        if way == 0:
            return remote(src, dst, *sems, "ep", to)
        return remote(src, arrived, *sems, "ep", came)

    def block_of(ring, step):
        if ring < 2:
            return ring_member(lax.rem(p + 2 * n - 1 - step, n), n)
        return ring_member(lax.rem(p + 1 + step, n), n)

    def term(ring, owner):
        if ring == 1:
            return block_dot(ag, owner, rows, ctx[...])
        k = {0: 0, 2: 1, 3: 2}[ring]
        return block_dot(n1, owner, rows, lg[:, k * lw : (k + 1) * lw])

    def ring_copy(ring, step, slot):
        return remote(
            ring_send.at[ring, slot],
            ring_recv.at[ring, step],
            ring_ss.at[ring, slot],
            ring_rs.at[ring, step],
            "ep",
            nxt if ring < 2 else prv,
        )

    def ring_step(step, first):
        for ring in range(4):
            slot = lax.rem(step, 2)
            mine = term(ring, block_of(ring, step))
            ring_copy(ring, step - 1, slot).wait_recv()
            if not first:
                ring_copy(ring, step - 2, slot).wait_send()
            ring_send[ring, slot] = (mine + ring_recv[ring, step - 1].astype(F32)).astype(BF)
            ring_copy(ring, step, slot).start()

    for ring in range(4):
        ring_send[ring, 0] = term(ring, block_of(ring, 0)).astype(BF)
        ring_copy(ring, 0, 0).start()

    def part_block(column, store):
        for m in range(0, tokens, 128):
            total = None
            for k in range(3):
                d = lax.dot_general(
                    lg[m : m + 128, k * lw : (k + 1) * lw],
                    w[k, pl.ds(pl.multiple_of(column * lw, lw), lw), :],
                    (((1,), (1,)), ((), ())),
                    preferred_element_type=F32,
                )
                total = d if total is None else total + d
            store(m, total)

    def tp_copy(i, src, dst, peer):
        return remote(src, dst, tp_ss.at[i], tp_rs.at[i], "tp", peer)

    first = [tp_copy(i, part_send.at[i], part_recv.at[i], core_peer) for i in range(2)]
    for i in range(2):

        def put(m, total, i=i):
            part_send[i, m : m + 128, :] = total.astype(BF)

        part_block((core_peer % 2) + 2 * i, put)
        first[i].start()

    ring_step(1, True)

    small_recv[ep] = small[ep]
    for shift in range(1, n):
        small_copy(shift, 0, 0).start()
    for copy in col_in:
        copy.wait()

    def put_own(m, total):
        part_own[m : m + 128, :] = total

    other = (tp // 2) * -1 + 1
    part_block((tp % 2) + 2 * other, put_own)
    for i in range(2):
        first[i].wait()
    y_send[...] = (part_own[...] + part_recv[other].astype(F32)).astype(BF)
    second = tp_copy(2, y_send, y_recv, y_peer)
    second.start()

    ring_step(2, False)

    part_block(tp, put_own)
    second.wait()
    for m in range(0, tokens, 128):
        at = slice(m, m + 128)
        grad = (
            part_own[at, :]
            + part_recv[tp // 2, at, :].astype(F32)
            + y_recv[at, :].astype(F32)
        )
        part_own[at, :] = grad
        hid = h_cols[at, :].astype(F32)
        mean = jnp.sum(grad * gain * hid, axis=1, keepdims=True)
        mean_send[0, at, :] = jnp.broadcast_to(mean, (128, 128))
        col = jnp.sum(grad * hid * r_one[at, :], axis=0, keepdims=True)
        if m == 0:
            vec_send[:, :lw] = col
        else:
            vec_send[:, :lw] += col
    third = tp_copy(3, mean_send.at[0], mean_recv.at[0], core_peer)
    third.start()
    vec_send[:, lw:] = bias[...]
    vec_recv[ep] = vec_send[...]

    def vec_copy(shift, way):
        to = lax.rem(ep + shift, n)
        came = lax.rem(ep + n - shift, n)
        if way == "out":
            return remote(vec_send, vec_recv.at[ep], vec_ss.at[shift], vec_rs.at[shift], "ep", to)
        return remote(vec_send, vec_recv.at[came], vec_ss.at[shift], vec_rs.at[shift], "ep", came)

    for shift in range(1, n):
        vec_copy(shift, "out").start()

    ring_step(3, False)

    third.wait()
    mean_send[1] = mean_send[0] + mean_recv[0]
    fourth = tp_copy(4, mean_send.at[1], mean_recv.at[1], y_peer)
    fourth.start()

    def out_block(column):
        at = pl.ds(pl.multiple_of(column * lw, lw), lw)
        return spart[:, at].astype(F32) + jnp.dot(
            weighted[...], o_rows[:, at], preferred_element_type=F32
        )

    fifth = [tp_copy(5 + i, out_send.at[i], out_recv.at[i], core_peer) for i in range(2)]
    for i in range(2):
        out_send[i] = out_block((core_peer % 2) + 2 * i).astype(BF)
        fifth[i].start()

    ring_step(4, False)

    for shift in range(1, n):
        small_copy(shift, 0, 1).wait()
    total = small_recv[0].astype(F32)
    for e in range(1, n):
        total = total + small_recv[e].astype(F32)
    small_sum[...] = total
    small_out[ep] = total
    for shift in range(1, n):
        small_copy(shift, 1, 0).start()
    for copy in fifth:
        copy.wait()
    oy_send[...] = (out_block((tp % 2) + 2 * other) + out_recv[other].astype(F32)).astype(BF)
    sixth = tp_copy(7, oy_send, oy_recv, y_peer)
    sixth.start()
    fourth.wait()
    for m in range(0, tokens, 128):
        at = slice(m, m + 128)
        mean = (mean_send[1, at, :1] + mean_recv[1, at, :1]) * (1.0 / width)
        r = r_one[at, :]
        in_out[at, :] = (
            ag_cols[at, :].astype(F32)
            + r * part_own[at, :] * gain
            - h_cols[at, :].astype(F32) * (r * r * r) * mean
        ).astype(BF)
    for shift in range(1, n):
        vec_copy(shift, "in").wait()
    total = vec_recv[0]
    for e in range(1, n):
        total = total + vec_recv[e]
    bias_out[...] = total[:, lw:]
    gain_send[...] = total[:, :lw]
    gain_recv[tp] = total[:, :lw]

    def gain_copy(shift, way):
        to = lax.rem(tp + shift, n_tp)
        came = lax.rem(tp + n_tp - shift, n_tp)
        if way == "out":
            return remote(gain_send, gain_recv.at[tp], gain_ss.at[shift], gain_rs.at[shift], "tp", to)
        return remote(gain_send, gain_recv.at[came], gain_ss.at[shift], gain_rs.at[shift], "tp", came)

    for shift in range(1, n_tp):
        gain_copy(shift, "out").start()

    ring_step(5, False)

    own = out_block(tp) + res_cols[...] + out_recv[tp // 2].astype(F32)
    sixth.wait()
    out_out[...] = (own + oy_recv[...].astype(F32)).astype(BF)

    @pl.loop(6, n - 1)
    def _(step):
        ring_step(step, False)

    for shift in range(1, n):
        small_copy(shift, 1, 1).wait()
    for shift in range(1, n_tp):
        gain_copy(shift, "in").wait()
    for j in range(n_tp):
        gain_out[:, j * lw : (j + 1) * lw] = gain_recv[j]

    for ring in range(4):
        mine = term(ring, ep)
        ring_copy(ring, n - 2, 0).wait_recv()
        done = mine + ring_recv[ring, n - 2].astype(F32)
        if ring == 1:
            o_out[...] = done
        else:
            qkv_out[{0: 0, 2: 1, 3: 2}[ring]] = done
    for ring in range(4):
        for step in (n - 3, n - 2):
            ring_copy(ring, step, step % 2).wait_send()


def tail(n, n_tp, n1, lg, ag, ctx, w, hidden, r_one, gain, bias, small, o_rows, weighted, spart, mid):
    tokens, width = n1.shape
    lw = ctx.shape[1]
    rows = width // n
    ag_hbm = ag
    if rows % 128:
        n1, ag = n1.T, ag.T
    wide = small.shape[1]
    vmem = pl.BlockSpec(memory_space=pltpu.VMEM)
    hbm = pl.BlockSpec(memory_space=pl.ANY)
    dma = pltpu.SemaphoreType.DMA
    return pl.pallas_call(
        functools.partial(tail_kernel, n, n_tp),
        out_shape=(
            jax.ShapeDtypeStruct((3, rows, lw), F32),
            jax.ShapeDtypeStruct((rows, lw), F32),
            jax.ShapeDtypeStruct((tokens, lw), BF),
            jax.ShapeDtypeStruct((tokens, lw), BF),
            jax.ShapeDtypeStruct((1, width), F32),
            jax.ShapeDtypeStruct((1, 3 * lw), F32),
            jax.ShapeDtypeStruct((n, wide, rows), F32),
        ),
        in_specs=[vmem] * 5 + [hbm] + [vmem] * 7 + [hbm] * 2,
        out_specs=[vmem] * 7,
        scratch_shapes=[
            pltpu.VMEM((tokens, lw), BF),
            pltpu.VMEM((tokens, lw), F32),
            pltpu.VMEM((tokens, lw), BF),
            dma((3,)),
            pltpu.VMEM((4, n - 1, rows, lw), BF),
            pltpu.VMEM((4, 2, rows, lw), BF),
            pltpu.VMEM((tokens, lw), F32),
            pltpu.VMEM((2, tokens, lw), BF),
            pltpu.VMEM((2, tokens, lw), BF),
            pltpu.VMEM((tokens, lw), BF),
            pltpu.VMEM((tokens, lw), BF),
            pltpu.VMEM((2, tokens, 128), F32),
            pltpu.VMEM((2, tokens, 128), F32),
            pltpu.VMEM((1, 4 * lw), F32),
            pltpu.VMEM((n, 1, 4 * lw), F32),
            pltpu.VMEM((n, wide, rows), BF),
            pltpu.VMEM((wide, rows), F32),
            pltpu.VMEM((1, lw), F32),
            pltpu.VMEM((n_tp, 1, lw), F32),
            pltpu.VMEM((2, tokens, lw), BF),
            pltpu.VMEM((2, tokens, lw), BF),
            pltpu.VMEM((tokens, lw), BF),
            pltpu.VMEM((tokens, lw), BF),
            dma((4, 2)),
            dma((4, n - 1)),
            dma((8,)),
            dma((8,)),
            dma((n,)),
            dma((n,)),
            dma((2, n)),
            dma((2, n)),
            dma((n_tp,)),
            dma((n_tp,)),
        ],
        compiler_params=pltpu.CompilerParams(
            collective_id=0, has_side_effects=True, vmem_limit_bytes=60 * 2**20
        ),
        cost_estimate=pl.CostEstimate(
            flops=2 * tokens * width * 7 * lw, bytes_accessed=30 * 2**20, transcendentals=0
        ),
    )(n1, lg, ag, ctx, w, hidden, r_one, gain, bias, small, o_rows, weighted, spart, mid, ag_hbm)

def cols_of(ref, owner, rows):
    at = pl.ds(pl.multiple_of(owner * rows, rows), rows)
    return ref[:, at] if rows % 128 == 0 else ref[at, :]


def block_dot(ref, owner, rows, other):
    dims = (((0,), (0,)), ((), ())) if rows % 128 == 0 else (((1,), (0,)), ((), ()))
    return lax.dot_general(cols_of(ref, owner, rows), other, dims, preferred_element_type=F32)


def middle_kernel(
    n,
    n_tp,
    shape,
    x_hbm,
    u_hbm,
    gu_a,
    gu_c,
    gu_b,
    gu_own,
    dn_a,
    dn_c,
    dn_b,
    dn_own,
    gates,
    nt,
    pg,
    og,
    sh,
    back,
    g_back,
    o_hbm,
    dw_recv,
    dw_own,
    dw_y,
    gu_out,
    dn_out,
    zero,
    w,
    xb,
    ub,
    rgb,
    eb,
    rbs,
    gbs,
    ring_recv,
    ring_send,
    w_sem,
    x_sem,
    u_sem,
    out_sem,
    ring_ss,
    ring_rs,
    free,
    back_ss,
    back_rs,
    gate_ss,
    gate_rs,
    dw_ss,
    dw_rs,
    dw_sem,
):
    ep = lax.axis_index("ep")
    tp = lax.axis_index("tp")
    core_peer, y_peer = flip(tp, 1), flip(tp, 2)
    gr = ub.shape[1]
    capp = shape[0]
    zero[...] = jnp.zeros_like(zero)
    width = u_hbm.shape[1]
    units = w.shape[1]
    quarter = units // 4
    groups = x_hbm.shape[0] // gr
    per = n // groups
    rows = gu_out.shape[1]
    half = ring_recv.shape[3]
    p = ring_place(ep, n)
    nxt = ring_member(lax.rem(p + 1, n), n)
    prv = ring_member(lax.rem(p + n - 1, n), n)

    w_in = [
        pltpu.make_async_copy(ref, w.at[:2, i * quarter : (i + 1) * quarter, :], w_sem.at[i])
        for i, ref in enumerate((gu_a, gu_c, gu_b, gu_own))
    ] + [
        pltpu.make_async_copy(ref, w.at[2, i * quarter : (i + 1) * quarter, :], w_sem.at[4 + i])
        for i, ref in enumerate((dn_a, dn_c, dn_b, dn_own))
    ]
    for copy in w_in:
        copy.start()

    x_in = pltpu.make_async_copy(x_hbm, xb, x_sem)

    def u_copy(g):
        at = pl.ds(pl.multiple_of(g * gr, gr), gr)
        slot = lax.rem(g, 2)
        return pltpu.make_async_copy(u_hbm.at[at, :], ub.at[slot], u_sem.at[slot])

    x_in.start()
    u_copy(0).start()
    greet(n, n_tp, ep, tp)

    edges = [0]
    for ring in range(4):
        edges.append(edges[-1] + (3 * units // 128 + 3 - ring) // 4 * 128)
    wide_of = [edges[i + 1] - edges[i] for i in range(4)]

    def block_of(ring, step):
        if ring < 2:
            return ring_member(lax.rem(p + 2 * n - 1 - step, n), n)
        return ring_member(lax.rem(p + 1 + step, n), n)

    def term(ring, owner):
        lo, hi = edges[ring], edges[ring + 1]
        parts = []
        if lo < 2 * units:
            parts.append(block_dot(nt, owner, rows, pg[:, lo : min(hi, 2 * units)]))
        if hi > 2 * units:
            parts.append(block_dot(og, owner, rows, sh[:, max(lo - 2 * units, 0) : hi - 2 * units]))
        return parts[0] if len(parts) == 1 else jnp.concatenate(parts, axis=1)

    def ring_copy(ring, slot):
        return remote(
            ring_send.at[ring, slot, :, : wide_of[ring]],
            ring_recv.at[ring, slot, :, : wide_of[ring]],
            ring_ss.at[ring, slot],
            ring_rs.at[ring, slot],
            "ep",
            nxt if ring < 2 else prv,
        )

    order = (0, 2, 1, 3)

    def ring_step(step):
        slot, last = lax.rem(step, 2), lax.rem(step + 1, 2)
        for ring in order:
            size = wide_of[ring]
            mine = term(ring, block_of(ring, step))
            ring_copy(ring, last).wait_recv()

            @pl.when(step >= 2)
            def _():
                ring_copy(ring, slot).wait_send()

            ring_send[ring, slot, :, :size] = (
                mine + ring_recv[ring, last, :, :size].astype(F32)
            ).astype(BF)

            @pl.when(step <= n - 3)
            def _():
                pl.semaphore_signal(
                    free.at[ring],
                    1,
                    device_id={"ep": prv if ring < 2 else nxt},
                    device_id_type=pl.DeviceIdType.MESH,
                )

            @pl.when(step >= 2)
            def _():
                pl.semaphore_wait(free.at[ring], 1)

            ring_copy(ring, slot).start()

    for ring in order:
        ring_send[ring, 0, :, : wide_of[ring]] = term(ring, block_of(ring, 0)).astype(BF)
        ring_copy(ring, 0).start()

    for copy in w_in:
        copy.wait()
    x_in.wait()

    nt_dims, first_dims = (((1,), (1,)), ((), ())), (((0,), (0,)), ((), ()))

    def saved(g):
        at = pl.ds(pl.multiple_of(g * gr, gr), gr)
        slot = lax.rem(g, 2)
        return pltpu.make_async_copy(ub.at[slot], o_hbm.at[at, :], out_sem.at[slot])

    def back_copies(r):
        return block_copies(r, rbs, back, back_ss, back_rs, lax.rem(ep + n - r, n), shape, tp, zero)

    kept_copy = pltpu.make_async_copy(rbs.at[:capp, :], back.at[:capp, :], back_ss.at[0, 0])

    def gate_copy(r):
        return remote(
            gbs.at[r], g_back.at[r], gate_ss.at[r], gate_rs.at[r], "ep", lax.rem(ep + n - r, n)
        )

    g_kept = pltpu.make_async_copy(gbs.at[0], g_back.at[0], gate_ss.at[0])
    gbs[...] = jnp.zeros_like(gbs)

    @pl.loop(0, groups)
    def _(g):
        slot = lax.rem(g, 2)
        mine = pl.ds(pl.multiple_of(g * gr, gr), gr)
        u_copy(g).wait()

        @pl.when(g >= 1)
        def _():
            saved(g - 1).wait()

        @pl.when(g + 1 < groups)
        def _():
            u_copy(g + 1).start()

        gate = jnp.concatenate([gate_column(gates, g * per + i, capp) for i in range(per)], axis=0)
        rgb[mine, :] = (gate * ub[slot].astype(F32)).astype(BF)

        def hidden(at):
            x = xb[mine, :]
            g_pre = lax.dot_general(x, w[0, at, :], nt_dims, preferred_element_type=F32)
            u_pre = lax.dot_general(x, w[1, at, :], nt_dims, preferred_element_type=F32)
            grad = lax.dot_general(rgb[mine, :], w[2, at, :], nt_dims, preferred_element_type=F32)
            sig = jax.nn.sigmoid(g_pre)
            eb[2, mine, at] = (g_pre * sig * u_pre).astype(BF)
            eb[0, mine, at] = (grad * u_pre * sig * (1.0 + g_pre * (1.0 - sig))).astype(BF)
            eb[1, mine, at] = (grad * g_pre * sig).astype(BF)

        @pl.loop(0, units // 256)
        def _(c):
            hidden(pl.ds(pl.multiple_of(c * 256, 256), 256))

        if units % 256:
            hidden(pl.ds(units // 256 * 256, units % 256))

        def columns(c, total):
            at = pl.ds(pl.multiple_of(c * 256, 256), 256)
            out = jnp.dot(eb[2, mine, :], w[2, :, at], preferred_element_type=F32)
            grad = jnp.dot(eb[0, mine, :], w[0, :, at], preferred_element_type=F32) + jnp.dot(
                eb[1, mine, :], w[1, :, at], preferred_element_type=F32
            )
            rbs[mine, at] = grad.astype(BF)
            total = total + jnp.sum(out * ub[slot, :, at].astype(F32), axis=1, keepdims=True)
            ub[slot, :, at] = out.astype(BF)
            return total

        total = lax.fori_loop(0, width // 256, columns, jnp.zeros((gr, 1), F32))
        hi = total.astype(BF).astype(F32)
        lane = lax.broadcasted_iota(jnp.int32, (gr, 128), 1)
        terms = jnp.where(lane == 0, hi, jnp.where(lane == 1, total - hi, 0.0)).astype(BF)
        pick = (
            lax.broadcasted_iota(jnp.int32, (16, 128), 0) == lax.broadcasted_iota(jnp.int32, (16, 128), 1)
        ).astype(F32).astype(BF)
        turned = lax.dot_general(pick, terms, nt_dims, preferred_element_type=F32).astype(BF)
        for i in range(per):
            gbs[g * per + i, :, :capp] = turned[:, i * capp : (i + 1) * capp]
        saved(g).start()
        for i in range(per):
            r = g * per + i
            if i == 0:

                @pl.when(g == 0)
                def _():
                    kept_copy.start()
                    g_kept.start()

                @pl.when(g > 0)
                def _():
                    each(back_copies(r), "start")
                    gate_copy(r).start()
            else:
                each(back_copies(r), "start")
                gate_copy(r).start()

        @pl.when(lax.rem(g, 2) == 1)
        def _():
            ring_step((g + 1) // 2)

    def weight_rows(at):
        for k in range(3):
            for c in range(0, width, 512):
                w[k, at, c : c + 512] = lax.dot_general(
                    eb[k, :, at],
                    (rgb if k == 2 else xb)[:, c : c + 512],
                    first_dims,
                    preferred_element_type=F32,
                ).astype(BF)

    @pl.loop(0, units // 256)
    def _(c):
        weight_rows(pl.ds(pl.multiple_of(c * 256, 256), 256))

    if units % 256:
        weight_rows(pl.ds(units // 256 * 256, units % 256))

    dw_core = remote(
        w.at[:, : 2 * quarter, :], dw_recv, dw_ss.at[0], dw_rs.at[0], "tp", core_peer
    )
    dw_core.start()
    ring_step(groups // 2 + 1)
    dw_core.wait()
    dw_in = pltpu.make_async_copy(dw_recv, w.at[:, : 2 * quarter, :], dw_sem.at[0])
    dw_in.start()
    dw_in.wait()
    for k in range(3):

        @pl.loop(0, quarter // 32)
        def _(c, k=k):
            far = pl.ds(pl.multiple_of(2 * quarter + c * 32, 32), 32)
            came = pl.ds(pl.multiple_of(quarter + c * 32, 32), 32)
            w[k, far, :] = (w[k, far, :].astype(F32) + w[k, came, :].astype(F32)).astype(BF)

    dw_far = remote(
        w.at[:, 2 * quarter : 3 * quarter, :], dw_y, dw_ss.at[1], dw_rs.at[1], "tp", y_peer
    )
    dw_far.start()
    for k in range(3):

        @pl.loop(0, quarter // 32)
        def _(c, k=k):
            far = pl.ds(pl.multiple_of(3 * quarter + c * 32, 32), 32)
            came = pl.ds(pl.multiple_of(c * 32, 32), 32)
            w[k, far, :] = (w[k, far, :].astype(F32) + w[k, came, :].astype(F32)).astype(BF)

    dw_keep = pltpu.make_async_copy(w.at[:, 3 * quarter :, :], dw_own, dw_sem.at[1])
    dw_keep.start()

    @pl.loop(groups // 2 + 2, n - 1)
    def _(step):
        ring_step(step)

    for ring in order:
        mine = term(ring, ep)
        ring_copy(ring, n % 2).wait_recv()
        done = mine + ring_recv[ring, n % 2, :, : wide_of[ring]].astype(F32)
        lo, hi = edges[ring], edges[ring + 1]
        for k, out in enumerate((gu_out.at[0], gu_out.at[1], dn_out)):
            a, b = max(lo, k * units), min(hi, (k + 1) * units)
            if a < b:
                out[:, a - k * units : b - k * units] = done[:, a - lo : b - lo].astype(BF)
    for ring in range(4):
        for slot in range(2):
            ring_copy(ring, slot).wait_send()
    g_kept.wait()
    kept_copy.wait()
    saved(groups - 1).wait()
    dw_keep.wait()
    dw_far.wait()

    @pl.loop(1, n)
    def _(r):
        each(back_copies(r), "wait")
        gate_copy(r).wait()


def routed_expert(n, n_tp, shape, x, u, weights, gates, nt, pg, og, sh):
    total, width = x.shape
    units = 4 * weights[-1].shape[0]
    gr = total // 4
    rows = width // n
    half = (3 * units // 128 + 3) // 4 * 128
    vmem = pl.BlockSpec(memory_space=pltpu.VMEM)
    hbm = pl.BlockSpec(memory_space=pl.ANY)
    dma = pltpu.SemaphoreType.DMA
    if rows % 128:
        nt, og = nt.T, og.T
    return pl.pallas_call(
        functools.partial(middle_kernel, n, n_tp, shape),
        out_shape=(
            jax.ShapeDtypeStruct((total, width), BF),
            jax.ShapeDtypeStruct((n, 16, 128), BF),
            jax.ShapeDtypeStruct((total, width), BF),
            jax.ShapeDtypeStruct((3, units // 2, width), BF),
            jax.ShapeDtypeStruct((3, units // 4, width), BF),
            jax.ShapeDtypeStruct((3, units // 4, width), BF),
            jax.ShapeDtypeStruct((2, rows, units), BF),
            jax.ShapeDtypeStruct((rows, units), BF),
        ),
        in_specs=[hbm] * 10 + [vmem] * 5,
        out_specs=[hbm] * 6 + [vmem] * 2,
        scratch_shapes=[
            pltpu.VMEM((max(shape[0] - shape[1], 16), width), BF),
            pltpu.VMEM((3, units, width), BF),
            pltpu.VMEM((total, width), BF),
            pltpu.VMEM((2, gr, width), BF),
            pltpu.VMEM((total, width), BF),
            pltpu.VMEM((3, total, units), BF),
            pltpu.VMEM((total, width), BF),
            pltpu.VMEM((n, 16, 128), BF),
            pltpu.VMEM((4, 2, rows, half), BF),
            pltpu.VMEM((4, 2, rows, half), BF),
            dma((8,)),
            dma,
            dma((2,)),
            dma((2,)),
            dma((4, 2)),
            dma((4, 2)),
            pltpu.SemaphoreType.REGULAR((4,)),
            dma((2, n)),
            dma((2, n)),
            dma((n,)),
            dma((n,)),
            dma((2,)),
            dma((2,)),
            dma((2,)),
        ],
        compiler_params=pltpu.CompilerParams(
            collective_id=1, has_side_effects=True, vmem_limit_bytes=63 * 2**20
        ),
        cost_estimate=pl.CostEstimate(
            flops=2 * total * width * 6 * units, bytes_accessed=40 * 2**20, transcendentals=0
        ),
    )(x, u, *weights, gates, nt, pg, og, sh)


def tp_total(
    project, between, tp, core_send, core_recv, y_send, y_recv, summed,
    core_ss, core_rs, y_ss, y_rs, g_ss, g_rs,
):
    core_peer, y_peer = flip(tp, 1), flip(tp, 2)
    pieces, size = core_send.shape[0], core_send.shape[2]
    half = pieces * size

    def core_copy(i):
        return remote(core_send.at[i], core_recv.at[i], core_ss.at[i], core_rs.at[i], "tp", core_peer)

    def y_copy(i):
        return remote(y_send.at[i], y_recv.at[i], y_ss.at[i], y_rs.at[i], "tp", y_peer)

    def gather_copy(i, slot):
        return remote(summed.at[slot, i], summed.at[slot, i], g_ss.at[i], g_rs.at[i], "tp", core_peer)

    me, other = tp % 2, core_peer % 2
    for i in range(pieces):
        core_send[i] = project(other * half, i, size).astype(BF)
        core_copy(i).start()
        own = project(me * half, i, size)
        core_copy(i).wait_recv()
        y_send[i] = (own + core_recv[i].astype(F32)).astype(BF)
        y_copy(i).start()
    between()
    for i in range(pieces):
        y_copy(i).wait_recv()
        summed[me, i] = (y_send[i].astype(F32) + y_recv[i].astype(F32)).astype(BF)
        gather_copy(i, me).start()
    for i in range(pieces):
        gather_copy(i, other).wait_recv()
    for i in range(pieces):
        core_copy(i).wait_send()
        y_copy(i).wait_send()
        gather_copy(i, me).wait_send()


def blocks_at_once(n, capp):
    per = 1
    while 2 * per * capp <= 128 and n % (2 * per) == 0:
        per *= 2
    return per


def block_copies(r, src, dst, ss, rs, to, shape, tp, zero):
    capp, base, extra = shape
    at = pl.ds(pl.multiple_of(r * capp, 16), base)
    out = [(None, remote(src.at[at, :], dst.at[at, :], ss.at[0, r], rs.at[0, r], "ep", to))]
    if base < capp:
        at = pl.ds(pl.multiple_of(r * capp + base, 16), capp - base)
        out.append((tp < extra, remote(src.at[at, :], dst.at[at, :], ss.at[1, r], rs.at[1, r], "ep", to)))
        out.append((tp >= extra, pltpu.make_async_copy(zero, dst.at[at, :], ss.at[1, r])))
    return out


def each(copies, verb):
    for condition, copy in copies:
        if condition is None:
            getattr(copy, verb)()
        else:
            pl.when(condition)(getattr(copy, verb))


def gate_column(tiles, r, capp):
    ones = jnp.ones((16, 128), BF)
    return lax.dot_general(
        tiles[r, :, :capp], ones, (((0,), (0,)), ((), ())), preferred_element_type=F32
    )[:, :1]


def front_kernel(
    n,
    n_tp,
    shape,
    hidden,
    gain1,
    gain2,
    w,
    bias,
    cosine,
    sine,
    prefix,
    ow,
    place,
    cot,
    gu_own,
    dn_own,
    up_rows,
    gu_a,
    dn_a,
    dn_b,
    n1,
    qkv,
    ctx,
    mid,
    nt,
    factor_one,
    zero,
    up_sent,
    core_send,
    core_recv,
    y_send,
    y_recv,
    summed,
    up_ss,
    up_rs,
    w_ss,
    w_rs,
    core_ss,
    core_rs,
    y_ss,
    y_rs,
    g_ss,
    g_rs,
):
    ep = lax.axis_index("ep")
    tp = lax.axis_index("tp")
    tokens, width = hidden.shape
    lw = ctx.shape[1]
    heads = lw // HEAD_DIM
    core_peer, y_peer = flip(tp, 1), flip(tp, 2)
    greet(n, n_tp, ep, tp)

    capp = shape[0]
    zero[...] = jnp.zeros_like(zero)

    def up_copies(r):
        return block_copies(r, up_sent, up_rows, up_ss, up_rs, lax.rem(ep + r, n), shape, tp, zero)

    kept = pltpu.make_async_copy(up_sent.at[:capp, :], up_rows.at[:capp, :], up_ss.at[0, 0])
    per = blocks_at_once(n, capp)
    size = per * capp

    @pl.loop(0, n // per)
    def _(b):
        at = pl.ds(pl.multiple_of(b * size, size), size)
        up_sent[at, :] = jnp.dot(place[at, :], cot[...], preferred_element_type=F32).astype(BF)
        for i in range(per):
            if i == 0:

                @pl.when(b == 0)
                def _():
                    kept.start()

                @pl.when(b > 0)
                def _():
                    each(up_copies(b * per), "start")
            else:
                each(up_copies(b * per + i), "start")

    w_copies = [
        remote(dn_own, dn_b, w_ss.at[0], w_rs.at[0], "tp", y_peer),
        remote(dn_own, dn_a, w_ss.at[1], w_rs.at[1], "tp", core_peer),
        remote(gu_own, gu_a, w_ss.at[2], w_rs.at[2], "tp", core_peer),
    ]
    for copy in w_copies:
        copy.start()

    @pl.loop(0, tokens // 64)
    def _(m):
        at = pl.ds(pl.multiple_of(m * 64, 64), 64)
        h = hidden[at, :].astype(F32)
        factor = lax.rsqrt(jnp.sum(h * h, axis=1, keepdims=True) * (1.0 / width) + EPSILON)
        factor_one[at, :] = factor
        n1[at, :] = (h * factor * gain1[...]).astype(BF)

    for k in range(3):

        @pl.loop(0, lw // 256)
        def _(c, k=k):
            at = pl.ds(pl.multiple_of(c * 256, 256), 256)
            x = jnp.dot(n1[...], w[k, :, at], preferred_element_type=F32) + bias[k : k + 1, at]
            if k < 2:
                x = jnp.concatenate(
                    [
                        x[:, i * HEAD_DIM : (i + 1) * HEAD_DIM] * cosine[...]
                        + pltpu.roll(x[:, i * HEAD_DIM : (i + 1) * HEAD_DIM], HEAD_DIM // 2, 1) * sine[...]
                        for i in range(256 // HEAD_DIM)
                    ],
                    axis=1,
                )
            qkv[k, :, at] = x.astype(BF)

    @pl.loop(0, tokens // 128)
    def _(m):
        at = pl.ds(pl.multiple_of(m * 128, 128), 128)
        row = lax.broadcasted_iota(jnp.int32, (128, tokens), 0) + m * 128
        col = lax.broadcasted_iota(jnp.int32, (128, tokens), 1)
        visible = (col <= row) | (col < prefix[...])
        for i in range(heads):
            lanes = slice(i * HEAD_DIM, (i + 1) * HEAD_DIM)
            s = lax.dot_general(
                qkv[0, at, lanes], qkv[1, :, lanes], (((1,), (1,)), ((), ())), preferred_element_type=F32
            )
            s = jnp.where(visible, s * HEAD_DIM ** (-0.5), -1e30)
            e = jnp.exp(s - jnp.max(s, axis=1, keepdims=True))
            e = e * (1.0 / jnp.sum(e, axis=1, keepdims=True))
            ctx[at, lanes] = jnp.dot(
                e.astype(BF), qkv[2, :, lanes], preferred_element_type=F32
            ).astype(BF)

    pieces, size = core_send.shape[0], core_send.shape[2]
    half = pieces * size

    def project(base, i, size):
        at = pl.ds(pl.multiple_of(base + i * size, size), size)
        return lax.dot_general(
            ctx[...], ow[at, :], (((1,), (1,)), ((), ())), preferred_element_type=F32
        )

    tp_total(
        project, lambda: None, tp, core_send, core_recv, y_send, y_recv, summed,
        core_ss, core_rs, y_ss, y_rs, g_ss, g_rs,
    )

    @pl.loop(0, tokens // 32)
    def _(m):
        at = pl.ds(pl.multiple_of(m * 32, 32), 32)
        total = jnp.zeros((32, 1), F32)
        for j in range(2):
            for i in range(pieces):
                lanes = slice(j * half + i * size, j * half + (i + 1) * size)
                x = hidden[at, lanes].astype(F32) + summed[j, i, at, :].astype(F32)
                mid[at, lanes] = x
                total = total + jnp.sum(x * x, axis=1, keepdims=True)
        factor = lax.rsqrt(total * (1.0 / width) + EPSILON)
        nt[at, :] = (mid[at, :] * factor * gain2[...]).astype(BF)

    for copy in w_copies:
        copy.wait()
    kept.wait()
    for r in range(1, n):
        each(up_copies(r), "wait")


def front(n, n_tp, shape, hidden, gain1, gain2, w, bias, cosine, sine, prefix, ow, place, cot, gu_own, dn_own):
    tokens, width = hidden.shape
    lw = ow.shape[1]
    quarter = dn_own.shape[0]
    vmem = pl.BlockSpec(memory_space=pltpu.VMEM)
    hbm = pl.BlockSpec(memory_space=pl.ANY)
    dma = pltpu.SemaphoreType.DMA
    return pl.pallas_call(
        functools.partial(front_kernel, n, n_tp, shape),
        out_shape=(
            jax.ShapeDtypeStruct((n * shape[0], width), BF),
            jax.ShapeDtypeStruct((2, quarter, width), BF),
            jax.ShapeDtypeStruct((quarter, width), BF),
            jax.ShapeDtypeStruct((quarter, width), BF),
            jax.ShapeDtypeStruct((tokens, width), BF),
            jax.ShapeDtypeStruct((3, tokens, lw), BF),
            jax.ShapeDtypeStruct((tokens, lw), BF),
            jax.ShapeDtypeStruct((tokens, width), F32),
            jax.ShapeDtypeStruct((tokens, width), BF),
            jax.ShapeDtypeStruct((tokens, 1), F32),
        ),
        in_specs=[vmem] * 11 + [hbm] * 2,
        out_specs=[hbm] * 4 + [vmem] * 6,
        scratch_shapes=[
            pltpu.VMEM((max(shape[0] - shape[1], 16), width), BF),
            pltpu.VMEM((n * shape[0], width), BF),
            pltpu.VMEM((4, tokens, width // 8), BF),
            pltpu.VMEM((4, tokens, width // 8), BF),
            pltpu.VMEM((4, tokens, width // 8), BF),
            pltpu.VMEM((4, tokens, width // 8), BF),
            pltpu.VMEM((2, 4, tokens, width // 8), BF),
            dma((2, n)),
            dma((2, n)),
            dma((3,)),
            dma((3,)),
            dma((4,)),
            dma((4,)),
            dma((4,)),
            dma((4,)),
            dma((4,)),
            dma((4,)),
        ],
        compiler_params=pltpu.CompilerParams(
            collective_id=2, has_side_effects=True, vmem_limit_bytes=56 * 2**20
        ),
        cost_estimate=pl.CostEstimate(
            flops=2 * tokens * width * 4 * lw, bytes_accessed=30 * 2**20, transcendentals=0
        ),
    )(hidden, gain1, gain2, w, bias, cosine, sine, prefix, ow, place, cot, gu_own, dn_own)


def dispatch_kernel(
    n,
    n_tp,
    shape,
    n_exp,
    nt,
    place,
    router,
    cot,
    sgu,
    sdn,
    gu_own,
    dn_b,
    dest_t,
    x_rows,
    g_rows,
    gu_b,
    gu_c,
    dn_c,
    probs,
    place_t,
    weighted,
    og,
    pg,
    sh,
    part,
    sback,
    sgrad,
    zero,
    gate,
    x_send,
    g_send,
    x_ss,
    x_rs,
    gate_ss,
    gate_rs,
    w_ss,
    w_rs,
):
    ep = lax.axis_index("ep")
    tp = lax.axis_index("tp")
    tokens, width = nt.shape
    units = sdn.shape[1]
    total = place.shape[0]
    core_peer, y_peer = flip(tp, 1), flip(tp, 2)
    greet(n, n_tp, ep, tp)
    w_y = remote(gu_own, gu_b, w_ss.at[0], w_rs.at[0], "tp", y_peer)
    w_y.start()
    w_on = remote(dn_b, dn_c, w_ss.at[1], w_rs.at[1], "tp", core_peer)
    w_on.start()

    capp = shape[0]
    zero[...] = jnp.zeros_like(zero)

    def x_copies(r):
        return block_copies(r, x_send, x_rows, x_ss, x_rs, lax.rem(ep + r, n), shape, tp, zero)

    def gate_copy(r, way):
        to = lax.rem(ep + r, n) if way == "out" else lax.rem(ep + n - r, n)
        return remote(g_send.at[r], g_rows.at[r], gate_ss.at[r], gate_rs.at[r], "ep", to)

    kept = pltpu.make_async_copy(x_send.at[:capp, :], x_rows.at[:capp, :], x_ss.at[0, 0])
    g_kept = pltpu.make_async_copy(g_send.at[0], g_rows.at[0], gate_ss.at[0])
    per = blocks_at_once(n, capp)
    size = per * capp

    @pl.loop(0, n // per)
    def _(b):
        at = pl.ds(pl.multiple_of(b * size, size), size)
        x_send[at, :] = jnp.dot(place[at, :], nt[...], preferred_element_type=F32).astype(BF)
        for i in range(per):
            if i == 0:

                @pl.when(b == 0)
                def _():
                    kept.start()

                @pl.when(b > 0)
                def _():
                    each(x_copies(b * per), "start")
            else:
                each(x_copies(b * per + i), "start")

    logits = jnp.dot(nt[...], router[...], preferred_element_type=F32)
    lane = lax.broadcasted_iota(jnp.int32, logits.shape, 1)
    chosen = jnp.where(lane < n_exp, logits, -1e30)
    e = jnp.exp(chosen - jnp.max(chosen, axis=1, keepdims=True))
    prob = e / jnp.sum(e, axis=1, keepdims=True)
    prob = jnp.where(lane == n_exp, jax.nn.sigmoid(logits), prob)
    probs[...] = prob
    hi = prob.astype(BF)
    lo = (prob - hi.astype(F32)).astype(BF)
    g_send[...] = jnp.zeros_like(g_send)
    across = (((0,), (1,)), ((), ()))

    for r in range(n):
        where = place[r * capp : (r + 1) * capp, :]
        pick = lax.broadcasted_iota(jnp.int32, (128, capp), 0) == lax.rem(r + ep, n)
        g_hi = jnp.sum(
            jnp.where(pick, lax.dot_general(hi, where, across, preferred_element_type=F32), 0.0),
            axis=0,
            keepdims=True,
        )
        g_lo = jnp.sum(
            jnp.where(pick, lax.dot_general(lo, where, across, preferred_element_type=F32), 0.0),
            axis=0,
            keepdims=True,
        )
        term = lax.broadcasted_iota(jnp.int32, (16, capp), 0)
        g_send[r, :, :capp] = jnp.where(term == 0, g_hi, jnp.where(term == 1, g_lo, 0.0)).astype(BF)
        gate[:, r * capp : (r + 1) * capp] = g_hi + g_lo
        if r == 0:
            g_kept.start()
        else:
            gate_copy(r, "out").start()

    @pl.loop(0, tokens // 64)
    def _(m):
        at = pl.ds(pl.multiple_of(m * 64, 64), 64)
        og[at, :] = (probs[at, n_exp : n_exp + 1] * cot[at, :].astype(F32)).astype(BF)

    def hidden(at, up_at):
        g_pre = jnp.dot(nt[...], sgu[0, :, at], preferred_element_type=F32)
        u_pre = jnp.dot(nt[...], sgu[1, :, at], preferred_element_type=F32)
        grad = jnp.dot(og[...], sdn[:, at], preferred_element_type=F32)
        sig = jax.nn.sigmoid(g_pre)
        sh[:, at] = (g_pre * sig * u_pre).astype(BF)
        pg[:, at] = (grad * u_pre * sig * (1.0 + g_pre * (1.0 - sig))).astype(BF)
        pg[:, up_at] = (grad * g_pre * sig).astype(BF)

    @pl.loop(0, units // 256)
    def _(c):
        hidden(
            pl.ds(pl.multiple_of(c * 256, 256), 256),
            pl.ds(pl.multiple_of(c * 256 + units, 128), 256),
        )

    if units % 256:
        rest = units // 256 * 256
        hidden(pl.ds(rest, units - rest), pl.ds(units + rest, units - rest))

    nt_dims = (((1,), (1,)), ((), ()))

    share = probs[:, n_exp : n_exp + 1]

    def columns(c, total):
        at = pl.ds(pl.multiple_of(c * 256, 256), 256)
        out = lax.dot_general(sh[...], sdn[at, :], nt_dims, preferred_element_type=F32)
        part[:, at] = (share * out).astype(BF)
        sback[:, at] = lax.dot_general(
            pg[:, :units], sgu[0, at, :], nt_dims, preferred_element_type=F32
        ) + lax.dot_general(pg[:, units:], sgu[1, at, :], nt_dims, preferred_element_type=F32)
        return total + jnp.sum(cot[:, at].astype(F32) * out, axis=1, keepdims=True)

    sgrad[...] = lax.fori_loop(0, width // 256, columns, jnp.zeros((tokens, 1), F32))

    @pl.loop(0, total // 128)
    def _(c):
        at = pl.ds(pl.multiple_of(c * 128, 128), 128)
        spot = lax.broadcasted_iota(jnp.int32, (tokens, 128), 1) + c * 128
        hit = dest_t[:, :1] == spot
        for k in range(1, dest_t.shape[1]):
            hit = hit | (dest_t[:, k : k + 1] == spot)
        place_t[:, at] = jnp.where(hit, 1.0, 0.0).astype(BF)
        weighted[:, at] = jnp.where(hit, gate[:, at], 0.0).astype(BF)

    w_y.wait()
    w_far = remote(gu_b, gu_c, w_ss.at[2], w_rs.at[2], "tp", core_peer)
    w_far.start()
    w_on.wait()
    w_far.wait()
    kept.wait()
    g_kept.wait()

    @pl.loop(1, n)
    def _(r):
        gate_copy(r, "in").wait()
        each(x_copies(r), "wait")


def dispatch(n, n_tp, shape, n_exp, nt, place, router, cot, sgu, sdn, gu_own, dn_b, dest_t):
    tokens, width = nt.shape
    units = sdn.shape[1]
    total = place.shape[0]
    vmem = pl.BlockSpec(memory_space=pltpu.VMEM)
    hbm = pl.BlockSpec(memory_space=pl.ANY)
    dma = pltpu.SemaphoreType.DMA
    return pl.pallas_call(
        functools.partial(dispatch_kernel, n, n_tp, shape, n_exp),
        out_shape=(
            jax.ShapeDtypeStruct((total, width), BF),
            jax.ShapeDtypeStruct((n, 16, 128), BF),
            jax.ShapeDtypeStruct(gu_own.shape, BF),
            jax.ShapeDtypeStruct(gu_own.shape, BF),
            jax.ShapeDtypeStruct(dn_b.shape, BF),
            jax.ShapeDtypeStruct((tokens, 128), F32),
            jax.ShapeDtypeStruct((tokens, total), BF),
            jax.ShapeDtypeStruct((tokens, total), BF),
            jax.ShapeDtypeStruct((tokens, width), BF),
            jax.ShapeDtypeStruct((tokens, 2 * units), BF),
            jax.ShapeDtypeStruct((tokens, units), BF),
            jax.ShapeDtypeStruct((tokens, width), BF),
            jax.ShapeDtypeStruct((tokens, width), F32),
            jax.ShapeDtypeStruct((tokens, 1), F32),
        ),
        in_specs=[vmem] * 6 + [hbm] * 2 + [vmem],
        out_specs=[hbm] * 5 + [vmem] * 9,
        scratch_shapes=[
            pltpu.VMEM((max(shape[0] - shape[1], 16), width), BF),
            pltpu.VMEM((1, total), F32),
            pltpu.VMEM((total, width), BF),
            pltpu.VMEM((n, 16, 128), BF),
            dma((2, n)),
            dma((2, n)),
            dma((n,)),
            dma((n,)),
            dma((3,)),
            dma((3,)),
        ],
        compiler_params=pltpu.CompilerParams(
            collective_id=3, has_side_effects=True, vmem_limit_bytes=60 * 2**20
        ),
        cost_estimate=pl.CostEstimate(
            flops=2 * tokens * width * 6 * units, bytes_accessed=40 * 2**20, transcendentals=0
        ),
    )(nt, place, router, cot, sgu, sdn, gu_own, dn_b, dest_t)

def backward_kernel(
    n,
    n_tp,
    shape,
    n_exp,
    back,
    g_back,
    place_t,
    sback,
    sgrad,
    probs,
    router,
    nt,
    mid,
    cot,
    gain2,
    qkv,
    ow,
    cosine,
    sine,
    prefix,
    o_sent,
    o_rows,
    ag,
    lg,
    bias,
    small,
    zero,
    core_send,
    core_recv,
    y_send,
    y_recv,
    summed,
    few_send,
    few_recv,
    ng,
    cg,
    dk,
    dv,
    o_ss,
    o_rs,
    core_ss,
    core_rs,
    y_ss,
    y_rs,
    g_ss,
    g_rs,
    few_ss,
    few_rs,
):
    ep = lax.axis_index("ep")
    tp = lax.axis_index("tp")
    tokens, width = nt.shape
    total = back.shape[0]
    lw = ow.shape[1]
    heads = lw // HEAD_DIM
    core_peer, y_peer = flip(tp, 1), flip(tp, 2)
    greet(n, n_tp, ep, tp)

    capp = shape[0]
    zero[...] = jnp.zeros_like(zero)

    def o_copies(r):
        return block_copies(r, o_sent, o_rows, o_ss, o_rs, lax.rem(ep + n - r, n), shape, tp, zero)

    kept = pltpu.make_async_copy(o_sent.at[:capp, :], o_rows.at[:capp, :], o_ss.at[0, 0])

    for r in range(1, n):
        each(o_copies(r), "start")
    kept.start()

    row = lax.broadcasted_iota(jnp.int32, (total, 128), 0)
    spot = lax.broadcasted_iota(jnp.int32, (total, 128), 1)
    expert = lax.rem(row // capp + ep * (n_exp // n), n_exp)
    gg = jnp.concatenate([gate_column(g_back, r, capp) for r in range(n)], axis=0)
    few = jnp.dot(
        place_t[...], jnp.where(spot == expert, gg, 0.0).astype(BF), preferred_element_type=F32
    )
    lane = lax.broadcasted_iota(jnp.int32, (tokens, 128), 1)
    few_send[0] = jnp.where(lane == n_exp, sgrad[...], few).astype(BF)
    few_core = remote(few_send.at[0], few_recv.at[0], few_ss.at[0], few_rs.at[0], "tp", core_peer)
    few_core.start()

    def project(base, i, size):
        at = pl.ds(pl.multiple_of(base + i * size, size), size)
        return sback[:, at] + jnp.dot(place_t[...], back[:, at], preferred_element_type=F32)

    def between():
        few_core.wait()
        few_send[1] = (few_send[0].astype(F32) + few_recv[0].astype(F32)).astype(BF)
        few_y = remote(few_send.at[1], few_recv.at[1], few_ss.at[1], few_rs.at[1], "tp", y_peer)
        few_y.start()
        few_y.wait()

    tp_total(
        project, between, tp, core_send, core_recv, y_send, y_recv, summed,
        core_ss, core_rs, y_ss, y_rs, g_ss, g_rs,
    )

    prob = jnp.where(lane < n_exp, probs[...], 0.0)
    share = probs[:, n_exp : n_exp + 1]
    grads = few_send[1].astype(F32) + few_recv[1].astype(F32)
    inner = jnp.sum(prob * grads, axis=1, keepdims=True)
    gate_in = grads * share * (1.0 - share)
    few_send[0] = jnp.where(
        lane < n_exp, prob * (grads - inner), jnp.where(lane == n_exp, gate_in, 0.0)
    ).astype(BF)
    pieces, size = summed.shape[1], summed.shape[3]
    for j in range(2):
        for i in range(pieces):
            at = slice((j * pieces + i) * size, (j * pieces + i + 1) * size)
            ng[:, at] = summed[j, i].astype(F32) + lax.dot_general(
                few_send[0], router[at, :], (((1,), (1,)), ((), ())), preferred_element_type=F32
            )

    step = 32

    def norm_rows(m, acc):
        at = pl.ds(pl.multiple_of(m * step, step), step)
        h = mid[at, :]
        grad = ng[at, :]
        factor = lax.rsqrt(jnp.sum(h * h, axis=1, keepdims=True) * (1.0 / width) + EPSILON)
        scaled = grad * gain2[...]
        mean = jnp.sum(scaled * h, axis=1, keepdims=True) * (1.0 / width)
        ag[at, :] = (
            cot[at, :].astype(F32) + factor * scaled - h * (factor * factor * factor) * mean
        ).astype(BF)
        return acc + jnp.sum((grad * h * factor).reshape(step // 8, 8, width), axis=0)

    acc = lax.fori_loop(0, tokens // step, norm_rows, jnp.zeros((8, width), F32))

    @pl.loop(0, lw // 256)
    def _(c):
        at = pl.ds(pl.multiple_of(c * 256, 256), 256)
        cg[:, at] = jnp.dot(ag[...], ow[:, at], preferred_element_type=F32).astype(BF)

    dk[...] = jnp.zeros_like(dk)
    dv[...] = jnp.zeros_like(dv)
    first_dims, last_dims = (((0,), (0,)), ((), ())), (((1,), (1,)), ((), ()))

    def attend(m, sums):
        at = pl.ds(pl.multiple_of(m * 128, 128), 128)
        row = lax.broadcasted_iota(jnp.int32, (128, tokens), 0) + m * 128
        col = lax.broadcasted_iota(jnp.int32, (128, tokens), 1)
        visible = (col <= row) | (col < prefix[...])
        parts = []
        for i in range(heads):
            lanes = slice(i * HEAD_DIM, (i + 1) * HEAD_DIM)
            q, grad = qkv[0, at, lanes], cg[at, lanes]
            s = lax.dot_general(q, qkv[1, :, lanes], last_dims, preferred_element_type=F32)
            s = jnp.where(visible, s * HEAD_DIM ** (-0.5), -1e30)
            e = jnp.exp(s - jnp.max(s, axis=1, keepdims=True))
            e = e * (1.0 / jnp.sum(e, axis=1, keepdims=True))
            dp = lax.dot_general(grad, qkv[2, :, lanes], last_dims, preferred_element_type=F32)
            delta = jnp.sum(e * dp, axis=1, keepdims=True)
            ds = (e * (dp - delta)).astype(BF)
            dv[:, lanes] += lax.dot_general(e.astype(BF), grad, first_dims, preferred_element_type=F32)
            dk[:, lanes] += lax.dot_general(ds, q, first_dims, preferred_element_type=F32)
            dq = jnp.dot(ds, qkv[1, :, lanes], preferred_element_type=F32) * HEAD_DIM ** (-0.5)
            dq = dq * cosine[at, :] - pltpu.roll(dq, HEAD_DIM // 2, 1) * sine[at, :]
            lg[at, lanes] = dq.astype(BF)
            parts.append(jnp.sum(dq.reshape(16, 8, HEAD_DIM), axis=0))
        return sums + jnp.concatenate(parts, axis=1)

    sums = lax.fori_loop(0, tokens // 128, attend, jnp.zeros((8, lw), F32))
    bias[:, :lw] = jnp.sum(sums, axis=0, keepdims=True)
    for i in range(heads):
        lanes = slice(i * HEAD_DIM, (i + 1) * HEAD_DIM)
        grad = dk[:, lanes] * HEAD_DIM ** (-0.5)
        grad = grad * cosine[...] - pltpu.roll(grad, HEAD_DIM // 2, 1) * sine[...]
        at = slice(lw + i * HEAD_DIM, lw + (i + 1) * HEAD_DIM)
        lg[:, at] = grad.astype(BF)
        bias[:, at] = jnp.sum(grad, axis=0, keepdims=True)
    lg[:, 2 * lw :] = dv[...].astype(BF)
    bias[:, 2 * lw :] = jnp.sum(dv[...], axis=0, keepdims=True)

    wide, span = small.shape[1:]
    gain_row = jnp.sum(acc, axis=0, keepdims=True)
    rows = lax.dot_general(few_send[0], nt[...], first_dims, preferred_element_type=F32)[:wide]
    index = lax.broadcasted_iota(jnp.int32, rows.shape, 0)
    rows = jnp.where(index == n_exp + 1, gain_row, rows).astype(BF)
    for r in range(n):
        small[r] = rows[:, r * span : (r + 1) * span]

    kept.wait()
    for r in range(1, n):
        each(o_copies(r), "wait")


def backward(n, n_tp, shape, n_exp, back, g_back, place_t, sback, sgrad, probs, router, nt, mid, cot, gain2, qkv, ow, cosine, sine, prefix, o_sent):
    tokens, width = nt.shape
    lw = ow.shape[1]
    wide = -(-(n_exp + 2) // 16) * 16
    vmem = pl.BlockSpec(memory_space=pltpu.VMEM)
    hbm = pl.BlockSpec(memory_space=pl.ANY)
    dma = pltpu.SemaphoreType.DMA
    piece = (4, tokens, width // 8)
    return pl.pallas_call(
        functools.partial(backward_kernel, n, n_tp, shape, n_exp),
        out_shape=(
            jax.ShapeDtypeStruct(o_sent.shape, BF),
            jax.ShapeDtypeStruct((tokens, width), BF),
            jax.ShapeDtypeStruct((tokens, 3 * lw), BF),
            jax.ShapeDtypeStruct((1, 3 * lw), F32),
            jax.ShapeDtypeStruct((n, wide, width // n), BF),
        ),
        in_specs=[vmem] * 16 + [hbm],
        out_specs=[hbm] + [vmem] * 4,
        scratch_shapes=[
            pltpu.VMEM((max(shape[0] - shape[1], 16), width), BF),
            pltpu.VMEM(piece, BF),
            pltpu.VMEM(piece, BF),
            pltpu.VMEM(piece, BF),
            pltpu.VMEM(piece, BF),
            pltpu.VMEM((2,) + piece, BF),
            pltpu.VMEM((2, tokens, 128), BF),
            pltpu.VMEM((2, tokens, 128), BF),
            pltpu.VMEM((tokens, width), F32),
            pltpu.VMEM((tokens, lw), BF),
            pltpu.VMEM((tokens, lw), F32),
            pltpu.VMEM((tokens, lw), F32),
            dma((2, n)),
            dma((2, n)),
            dma((4,)),
            dma((4,)),
            dma((4,)),
            dma((4,)),
            dma((4,)),
            dma((4,)),
            dma((2,)),
            dma((2,)),
        ],
        compiler_params=pltpu.CompilerParams(
            collective_id=4, has_side_effects=True, vmem_limit_bytes=60 * 2**20
        ),
        cost_estimate=pl.CostEstimate(
            flops=2 * tokens * width * 4 * lw, bytes_accessed=30 * 2**20, transcendentals=0
        ),
    )(back, g_back, place_t, sback, sgrad, probs, router, nt, mid, cot, gain2, qkv, ow, cosine, sine, prefix, o_sent)


def body(
    hidden,
    attn_gain,
    qkv_weight,
    qkv_bias,
    out_weight,
    mlp_gain,
    router_weight,
    share_gate,
    shared_gate_up,
    shared_down,
    expert_gate_up,
    expert_down,
    routes,
    priority,
    prefix,
    cotangent,
):
    tokens, width = hidden.shape
    n_ep = lax.axis_size("ep")
    n_tp = lax.axis_size("tp")
    tp_i = lax.axis_index("tp")
    local_width = qkv_weight.shape[2]
    expert_local = expert_gate_up.shape[0]
    n_exp = expert_local * n_ep
    top = routes.shape[1]
    capacity = (5 * tokens * top + 4 * n_exp - 1) // (4 * n_exp)
    tiles = -(-capacity // 16)
    least, extra = 16 * (tiles // n_tp), tiles % n_tp
    part_pad = least + (16 if extra else 0)
    shape = (part_pad, least, extra)
    rows = n_exp * part_pad

    flat_route = routes.T.reshape(-1)
    flat_order = priority.T.reshape(-1)
    hits = (flat_route[:, None] == jnp.arange(n_exp, dtype=jnp.int32)[None, :]).astype(BF)
    smaller = (flat_order[None, :] < flat_order[:, None]).astype(BF)
    counts = mm(smaller, hits, 1, 0)
    slot = jnp.sum(counts * hits.astype(F32), axis=1).astype(jnp.int32).reshape(top, tokens)
    kept = slot < capacity
    in_part = slot - (tp_i * least + 16 * jnp.minimum(tp_i, extra))
    mine = kept & (in_part >= 0) & (in_part < jnp.where(tp_i < extra, part_pad, least))
    ep_i = lax.axis_index("ep")
    hop = lax.rem(routes.T + n_exp - ep_i * expert_local, n_exp)
    dest = jnp.where(mine, hop * part_pad + in_part, -1)
    row_ids = jnp.arange(rows, dtype=jnp.int32)[:, None]
    place = (dest[0][None, :] == row_ids)
    for k in range(1, top):
        place = place | (dest[k][None, :] == row_ids)
    place = place.astype(BF)

    cos_all, sin_all = angle_tables(tokens, HEAD_DIM)
    w_t = jnp.transpose(qkv_weight, (1, 0, 2))
    sgu, hidden = lax.optimization_barrier((jnp.transpose(shared_gate_up, (1, 0, 2)), hidden))
    prefix_row = jnp.broadcast_to(prefix[None], (1, tokens))
    gu_own = jnp.transpose(expert_gate_up[0], (1, 2, 0))
    dn_own = jnp.transpose(expert_down[0], (1, 0))
    up_rows, gu_a, dn_a, dn_b, normed_one, qkv, context, middle, normed_two, factor_one = front(
        n_ep,
        n_tp,
        shape,
        hidden,
        attn_gain[None],
        mlp_gain[None],
        w_t,
        qkv_bias,
        cos_all,
        sin_all,
        prefix_row,
        out_weight,
        place,
        cotangent,
        gu_own,
        dn_own,
    )

    router_all = jnp.concatenate(
        [router_weight, share_gate[:, None], jnp.zeros((width, 127 - n_exp), BF)], axis=1
    )
    got, gates, gu_b, gu_c, dn_c, probs_all, place_t, weighted_place, shared_out_grad, pre_grad, shared_hidden, scaled_part, shared_back, scale_grad = (
        dispatch(
            n_ep,
            n_tp,
            shape,
            n_exp,
            normed_two,
            place,
            router_all,
            cotangent,
            sgu,
            shared_down,
            gu_own,
            dn_b,
            dest.T,
        )
    )
    back_rows, back_gates, e_out, _, dw_own, dw_y, gu_grad, shared_down_grad = routed_expert(
        n_ep,
        n_tp,
        shape,
        got,
        up_rows,
        (gu_a, gu_c, gu_b, gu_own, dn_a, dn_c, dn_b, dn_own),
        gates,
        normed_two,
        pre_grad,
        shared_out_grad,
        shared_hidden,
    )
    shared_gate_up_grad = jnp.transpose(gu_grad, (1, 0, 2)).astype(F32)
    shared_down_grad = shared_down_grad.astype(F32)
    expert_down_grad = jnp.transpose(dw_own[2].astype(F32) + dw_y[2].astype(F32), (1, 0))[None]
    expert_gate_up_grad = jnp.transpose(dw_own[:2].astype(F32) + dw_y[:2].astype(F32), (2, 0, 1))[None]

    out_rows, attn_grad, linear_grad, bias_grad, small = backward(
        n_ep,
        n_tp,
        shape,
        n_exp,
        back_rows,
        back_gates,
        place_t,
        shared_back,
        scale_grad,
        probs_all,
        router_all,
        normed_two,
        middle,
        cotangent,
        mlp_gain[None],
        qkv,
        out_weight,
        cos_all,
        sin_all,
        prefix_row,
        e_out,
    )
    qkv_grad, out_weight_grad, input_grad, output, gain_one, bias_sum, small_sum = tail(
        n_ep,
        n_tp,
        normed_one,
        linear_grad,
        attn_grad,
        context,
        w_t,
        hidden,
        factor_one,
        attn_gain[None],
        bias_grad,
        small,
        out_rows,
        weighted_place,
        scaled_part,
        middle,
    )
    small_sum = jnp.transpose(small_sum, (1, 0, 2)).reshape(-1, width)
    qkv_weight_grad = jnp.transpose(qkv_grad, (1, 0, 2))
    gain_one_sum = gain_one[0]
    bias_sum = bias_sum.reshape(3, local_width)
    router_sum = small_sum[:n_exp].T
    share_gate_sum = small_sum[n_exp]
    gain_two_sum = small_sum[n_exp + 1]
    return (
        output,
        input_grad,
        gain_one_sum,
        qkv_weight_grad,
        bias_sum,
        out_weight_grad,
        gain_two_sum,
        router_sum,
        share_gate_sum,
        shared_gate_up_grad,
        shared_down_grad,
        expert_gate_up_grad,
        expert_down_grad,
    )


def solution(mesh):
    return jax.shard_map(
        body,
        mesh=mesh,
        in_specs=(
            P("ep", None),
            P(),
            P(None, None, "tp"),
            P(None, "tp"),
            P(None, "tp"),
            P(),
            P(),
            P(),
            P(None, None, "tp"),
            P(None, "tp"),
            P("ep", None, None, "tp"),
            P("ep", None, "tp"),
            P("ep", None),
            P("ep", None),
            P("ep"),
            P("ep", None),
        ),
        out_specs=(
            P("ep", "tp"),
            P("ep", "tp"),
            P(),
            P("ep", None, "tp"),
            P(None, "tp"),
            P("ep", "tp"),
            P(),
            P(),
            P(),
            P("ep", None, "tp"),
            P("ep", "tp"),
            P("ep", None, None, "tp"),
            P("ep", None, "tp"),
        ),
        check_vma=False,
    )
```

```python
import functools

import jax
import jax.numpy as jnp
import numpy as np
from jax import lax
from jax.experimental import pallas as pl
from jax.experimental.pallas import tpu as pltpu
from jax.sharding import PartitionSpec as P

HEAD_DIM = 128
EPSILON = 1e-06
THETA = 1000000.0
BF = jnp.bfloat16
F32 = jnp.float32


def mm(a, b, ca, cb):
    return lax.dot_general(a, b, (((ca,), (cb,)), ((), ())), preferred_element_type=F32)


def angle_tables(length, head_size):
    half_size = head_size // 2
    frequency = (THETA ** (-np.arange(half_size, dtype=np.float32) * 2.0 / head_size)).astype(np.float32)
    angles = (np.arange(length, dtype=np.float32)[:, None] * frequency[None, :]).astype(np.float64)
    cosine, sine_val = np.cos(angles), np.sin(angles)
    return (
        np.concatenate([cosine, cosine], axis=1).astype(np.float32),
        np.concatenate([-sine_val, sine_val], axis=1).astype(np.float32),
    )


def ring_place(e, n):
    odd = e % 2
    return (1 - odd) * (e // 2) + odd * (n - 1 - e // 2)


def ring_member(p, n):
    second = p // (n // 2)
    return (1 - second) * 2 * p + second * (2 * (n - 1 - p) + 1)


def remote(src, dst, send_sem, recv_sem, axis, index):
    return pltpu.make_async_remote_copy(
        src_ref=src,
        dst_ref=dst,
        send_sem=send_sem,
        recv_sem=recv_sem,
        device_id={axis: index},
        device_id_type=pl.DeviceIdType.MESH,
    )


def greet(n, n_tp, ep, tp):
    barrier = pltpu.get_barrier_semaphore()
    for shift in range(1, n):
        pl.semaphore_signal(
            barrier, 1, device_id={"ep": lax.rem(ep + shift, n)}, device_id_type=pl.DeviceIdType.MESH
        )
    for shift in range(1, n_tp):
        pl.semaphore_signal(
            barrier, 1, device_id={"tp": lax.rem(tp + shift, n_tp)}, device_id_type=pl.DeviceIdType.MESH
        )
    pl.semaphore_wait(barrier, n - 1 + n_tp - 1)


def flip(index, bit):
    if bit == 1:
        return index + 1 - 2 * (index % 2)
    return index + 2 - 4 * ((index // 2) % 2)


def tail_kernel(
    n,
    n_tp,
    n1,
    lg,
    ag,
    ctx,
    w,
    hidden,
    r_one,
    gain_all,
    bias,
    small,
    o_rows,
    weighted,
    spart,
    mid,
    ag_hbm,
    qkv_out,
    o_out,
    in_out,
    out_out,
    gain_out,
    bias_out,
    small_out,
    h_cols,
    res_cols,
    ag_cols,
    in_sem,
    ring_recv,
    ring_send,
    part_own,
    part_send,
    part_recv,
    y_send,
    y_recv,
    mean_send,
    mean_recv,
    vec_send,
    vec_recv,
    small_recv,
    small_sum,
    gain_send,
    gain_recv,
    out_send,
    out_recv,
    oy_send,
    oy_recv,
    ring_ss,
    ring_rs,
    tp_ss,
    tp_rs,
    vec_ss,
    vec_rs,
    small_ss,
    small_rs,
    gain_ss,
    gain_rs,
):
    ep = lax.axis_index("ep")
    tp = lax.axis_index("tp")
    tokens, lw = ctx.shape
    columns = pl.ds(pl.multiple_of(tp * lw, lw), lw)
    col_in = [
        pltpu.make_async_copy(hidden.at[:, columns], h_cols, in_sem.at[0]),
        pltpu.make_async_copy(mid.at[:, columns], res_cols, in_sem.at[1]),
        pltpu.make_async_copy(ag_hbm.at[:, columns], ag_cols, in_sem.at[2]),
    ]
    for copy in col_in:
        copy.start()
    gain = gain_all[:, columns]
    rows = qkv_out.shape[1]
    width = rows * n
    p = ring_place(ep, n)
    nxt = ring_member(lax.rem(p + 1, n), n)
    prv = ring_member(lax.rem(p + n - 1, n), n)
    core_peer, y_peer = flip(tp, 1), flip(tp, 2)
    greet(n, n_tp, ep, tp)

    def small_copy(shift, turn, way):
        to, came = lax.rem(ep + shift, n), lax.rem(ep + n - shift, n)
        if turn == 0:
            src, dst, arrived = small.at[to], small_recv.at[ep], small_recv.at[came]
        else:
            src, dst, arrived = small_sum, small_out.at[ep], small_out.at[came]
        sems = small_ss.at[turn, shift], small_rs.at[turn, shift]
        if way == 0:
            return remote(src, dst, *sems, "ep", to)
        return remote(src, arrived, *sems, "ep", came)

    def block_of(ring, step):
        if ring < 2:
            return ring_member(lax.rem(p + 2 * n - 1 - step, n), n)
        return ring_member(lax.rem(p + 1 + step, n), n)

    def term(ring, owner):
        if ring == 1:
            return block_dot(ag, owner, rows, ctx[...])
        k = {0: 0, 2: 1, 3: 2}[ring]
        return block_dot(n1, owner, rows, lg[:, k * lw : (k + 1) * lw])

    def ring_copy(ring, step, slot):
        return remote(
            ring_send.at[ring, slot],
            ring_recv.at[ring, step],
            ring_ss.at[ring, slot],
            ring_rs.at[ring, step],
            "ep",
            nxt if ring < 2 else prv,
        )

    def ring_step(step, first):
        for ring in range(4):
            slot = lax.rem(step, 2)
            mine = term(ring, block_of(ring, step))
            ring_copy(ring, step - 1, slot).wait_recv()
            if not first:
                ring_copy(ring, step - 2, slot).wait_send()
            ring_send[ring, slot] = (mine + ring_recv[ring, step - 1].astype(F32)).astype(BF)
            ring_copy(ring, step, slot).start()

    for ring in range(4):
        ring_send[ring, 0] = term(ring, block_of(ring, 0)).astype(BF)
        ring_copy(ring, 0, 0).start()

    def part_block(column, store):
        for m in range(0, tokens, 128):
            total = None
            for k in range(3):
                d = lax.dot_general(
                    lg[m : m + 128, k * lw : (k + 1) * lw],
                    w[k, pl.ds(pl.multiple_of(column * lw, lw), lw), :],
                    (((1,), (1,)), ((), ())),
                    preferred_element_type=F32,
                )
                total = d if total is None else total + d
            store(m, total)

    def tp_copy(i, src, dst, peer):
        return remote(src, dst, tp_ss.at[i], tp_rs.at[i], "tp", peer)

    first = [tp_copy(i, part_send.at[i], part_recv.at[i], core_peer) for i in range(2)]
    for i in range(2):

        def put(m, total, i=i):
            part_send[i, m : m + 128, :] = total.astype(BF)

        part_block((core_peer % 2) + 2 * i, put)
        first[i].start()

    ring_step(1, True)

    small_recv[ep] = small[ep]
    for shift in range(1, n):
        small_copy(shift, 0, 0).start()
    for copy in col_in:
        copy.wait()

    def put_own(m, total):
        part_own[m : m + 128, :] = total

    other = (tp // 2) * -1 + 1
    part_block((tp % 2) + 2 * other, put_own)
    for i in range(2):
        first[i].wait()
    y_send[...] = (part_own[...] + part_recv[other].astype(F32)).astype(BF)
    second = tp_copy(2, y_send, y_recv, y_peer)
    second.start()

    ring_step(2, False)

    part_block(tp, put_own)
    second.wait()
    for m in range(0, tokens, 128):
        at = slice(m, m + 128)
        grad = (
            part_own[at, :]
            + part_recv[tp // 2, at, :].astype(F32)
            + y_recv[at, :].astype(F32)
        )
        part_own[at, :] = grad
        hid = h_cols[at, :].astype(F32)
        mean = jnp.sum(grad * gain * hid, axis=1, keepdims=True)
        mean_send[0, at, :] = jnp.broadcast_to(mean, (128, 128))
        col = jnp.sum(grad * hid * r_one[at, :], axis=0, keepdims=True)
        if m == 0:
            vec_send[:, :lw] = col
        else:
            vec_send[:, :lw] += col
    third = tp_copy(3, mean_send.at[0], mean_recv.at[0], core_peer)
    third.start()
    vec_send[:, lw:] = bias[...]
    vec_recv[ep] = vec_send[...]

    def vec_copy(shift, way):
        to = lax.rem(ep + shift, n)
        came = lax.rem(ep + n - shift, n)
        if way == "out":
            return remote(vec_send, vec_recv.at[ep], vec_ss.at[shift], vec_rs.at[shift], "ep", to)
        return remote(vec_send, vec_recv.at[came], vec_ss.at[shift], vec_rs.at[shift], "ep", came)

    for shift in range(1, n):
        vec_copy(shift, "out").start()

    ring_step(3, False)

    third.wait()
    mean_send[1] = mean_send[0] + mean_recv[0]
    fourth = tp_copy(4, mean_send.at[1], mean_recv.at[1], y_peer)
    fourth.start()

    def out_block(column):
        at = pl.ds(pl.multiple_of(column * lw, lw), lw)
        return spart[:, at].astype(F32) + jnp.dot(
            weighted[...], o_rows[:, at], preferred_element_type=F32
        )

    fifth = [tp_copy(5 + i, out_send.at[i], out_recv.at[i], core_peer) for i in range(2)]
    for i in range(2):
        out_send[i] = out_block((core_peer % 2) + 2 * i).astype(BF)
        fifth[i].start()

    ring_step(4, False)

    for shift in range(1, n):
        small_copy(shift, 0, 1).wait()
    total = small_recv[0].astype(F32)
    for e in range(1, n):
        total = total + small_recv[e].astype(F32)
    small_sum[...] = total
    small_out[ep] = total
    for shift in range(1, n):
        small_copy(shift, 1, 0).start()
    for copy in fifth:
        copy.wait()
    oy_send[...] = (out_block((tp % 2) + 2 * other) + out_recv[other].astype(F32)).astype(BF)
    sixth = tp_copy(7, oy_send, oy_recv, y_peer)
    sixth.start()
    fourth.wait()
    for m in range(0, tokens, 128):
        at = slice(m, m + 128)
        mean = (mean_send[1, at, :1] + mean_recv[1, at, :1]) * (1.0 / width)
        r = r_one[at, :]
        in_out[at, :] = (
            ag_cols[at, :].astype(F32)
            + r * part_own[at, :] * gain
            - h_cols[at, :].astype(F32) * (r * r * r) * mean
        ).astype(BF)
    for shift in range(1, n):
        vec_copy(shift, "in").wait()
    total = vec_recv[0]
    for e in range(1, n):
        total = total + vec_recv[e]
    bias_out[...] = total[:, lw:]
    gain_send[...] = total[:, :lw]
    gain_recv[tp] = total[:, :lw]

    def gain_copy(shift, way):
        to = lax.rem(tp + shift, n_tp)
        came = lax.rem(tp + n_tp - shift, n_tp)
        if way == "out":
            return remote(gain_send, gain_recv.at[tp], gain_ss.at[shift], gain_rs.at[shift], "tp", to)
        return remote(gain_send, gain_recv.at[came], gain_ss.at[shift], gain_rs.at[shift], "tp", came)

    for shift in range(1, n_tp):
        gain_copy(shift, "out").start()

    ring_step(5, False)

    own = out_block(tp) + res_cols[...] + out_recv[tp // 2].astype(F32)
    sixth.wait()
    out_out[...] = (own + oy_recv[...].astype(F32)).astype(BF)

    @pl.loop(6, n - 1)
    def _(step):
        ring_step(step, False)

    for shift in range(1, n):
        small_copy(shift, 1, 1).wait()
    for shift in range(1, n_tp):
        gain_copy(shift, "in").wait()
    for j in range(n_tp):
        gain_out[:, j * lw : (j + 1) * lw] = gain_recv[j]

    for ring in range(4):
        mine = term(ring, ep)
        ring_copy(ring, n - 2, 0).wait_recv()
        done = mine + ring_recv[ring, n - 2].astype(F32)
        if ring == 1:
            o_out[...] = done
        else:
            qkv_out[{0: 0, 2: 1, 3: 2}[ring]] = done
    for ring in range(4):
        for step in (n - 3, n - 2):
            ring_copy(ring, step, step % 2).wait_send()


def tail(n, n_tp, n1, lg, ag, ctx, w, hidden, r_one, gain, bias, small, o_rows, weighted, spart, mid):
    tokens, width = n1.shape
    lw = ctx.shape[1]
    rows = width // n
    ag_hbm = ag
    if rows % 128:
        n1, ag = n1.T, ag.T
    wide = small.shape[1]
    vmem = pl.BlockSpec(memory_space=pltpu.VMEM)
    hbm = pl.BlockSpec(memory_space=pl.ANY)
    dma = pltpu.SemaphoreType.DMA
    return pl.pallas_call(
        functools.partial(tail_kernel, n, n_tp),
        out_shape=(
            jax.ShapeDtypeStruct((3, rows, lw), F32),
            jax.ShapeDtypeStruct((rows, lw), F32),
            jax.ShapeDtypeStruct((tokens, lw), BF),
            jax.ShapeDtypeStruct((tokens, lw), BF),
            jax.ShapeDtypeStruct((1, width), F32),
            jax.ShapeDtypeStruct((1, 3 * lw), F32),
            jax.ShapeDtypeStruct((n, wide, rows), F32),
        ),
        in_specs=[vmem] * 5 + [hbm] + [vmem] * 7 + [hbm] * 2,
        out_specs=[vmem] * 7,
        scratch_shapes=[
            pltpu.VMEM((tokens, lw), BF),
            pltpu.VMEM((tokens, lw), F32),
            pltpu.VMEM((tokens, lw), BF),
            dma((3,)),
            pltpu.VMEM((4, n - 1, rows, lw), BF),
            pltpu.VMEM((4, 2, rows, lw), BF),
            pltpu.VMEM((tokens, lw), F32),
            pltpu.VMEM((2, tokens, lw), BF),
            pltpu.VMEM((2, tokens, lw), BF),
            pltpu.VMEM((tokens, lw), BF),
            pltpu.VMEM((tokens, lw), BF),
            pltpu.VMEM((2, tokens, 128), F32),
            pltpu.VMEM((2, tokens, 128), F32),
            pltpu.VMEM((1, 4 * lw), F32),
            pltpu.VMEM((n, 1, 4 * lw), F32),
            pltpu.VMEM((n, wide, rows), BF),
            pltpu.VMEM((wide, rows), F32),
            pltpu.VMEM((1, lw), F32),
            pltpu.VMEM((n_tp, 1, lw), F32),
            pltpu.VMEM((2, tokens, lw), BF),
            pltpu.VMEM((2, tokens, lw), BF),
            pltpu.VMEM((tokens, lw), BF),
            pltpu.VMEM((tokens, lw), BF),
            dma((4, 2)),
            dma((4, n - 1)),
            dma((8,)),
            dma((8,)),
            dma((n,)),
            dma((n,)),
            dma((2, n)),
            dma((2, n)),
            dma((n_tp,)),
            dma((n_tp,)),
        ],
        compiler_params=pltpu.CompilerParams(
            collective_id=0, has_side_effects=True, vmem_limit_bytes=60 * 2**20
        ),
        cost_estimate=pl.CostEstimate(
            flops=2 * tokens * width * 7 * lw, bytes_accessed=30 * 2**20, transcendentals=0
        ),
    )(n1, lg, ag, ctx, w, hidden, r_one, gain, bias, small, o_rows, weighted, spart, mid, ag_hbm)

def cols_of(ref, owner, rows):
    at = pl.ds(pl.multiple_of(owner * rows, rows), rows)
    return ref[:, at] if rows % 128 == 0 else ref[at, :]


def block_dot(ref, owner, rows, other):
    dims = (((0,), (0,)), ((), ())) if rows % 128 == 0 else (((1,), (0,)), ((), ()))
    return lax.dot_general(cols_of(ref, owner, rows), other, dims, preferred_element_type=F32)


def middle_kernel(
    n,
    n_tp,
    shape,
    x_hbm,
    u_hbm,
    gu_a,
    gu_c,
    gu_b,
    gu_own,
    dn_a,
    dn_c,
    dn_b,
    dn_own,
    gates,
    nt,
    pg,
    og,
    sh,
    back,
    g_back,
    o_hbm,
    dw_recv,
    dw_own,
    dw_y,
    gu_out,
    dn_out,
    zero,
    w,
    xb,
    ub,
    rgb,
    eb,
    rbs,
    gbs,
    ring_recv,
    ring_send,
    w_sem,
    x_sem,
    u_sem,
    out_sem,
    ring_ss,
    ring_rs,
    free,
    back_ss,
    back_rs,
    gate_ss,
    gate_rs,
    dw_ss,
    dw_rs,
    dw_sem,
):
    ep = lax.axis_index("ep")
    tp = lax.axis_index("tp")
    core_peer, y_peer = flip(tp, 1), flip(tp, 2)
    gr = ub.shape[1]
    capp = shape[0]
    zero[...] = jnp.zeros_like(zero)
    width = u_hbm.shape[1]
    units = w.shape[1]
    quarter = units // 4
    groups = x_hbm.shape[0] // gr
    per = n // groups
    rows = gu_out.shape[1]
    half = ring_recv.shape[3]
    p = ring_place(ep, n)
    nxt = ring_member(lax.rem(p + 1, n), n)
    prv = ring_member(lax.rem(p + n - 1, n), n)

    w_in = [
        pltpu.make_async_copy(ref, w.at[:2, i * quarter : (i + 1) * quarter, :], w_sem.at[i])
        for i, ref in enumerate((gu_a, gu_c, gu_b, gu_own))
    ] + [
        pltpu.make_async_copy(ref, w.at[2, i * quarter : (i + 1) * quarter, :], w_sem.at[4 + i])
        for i, ref in enumerate((dn_a, dn_c, dn_b, dn_own))
    ]
    for copy in w_in:
        copy.start()

    x_in = pltpu.make_async_copy(x_hbm, xb, x_sem)

    def u_copy(g):
        at = pl.ds(pl.multiple_of(g * gr, gr), gr)
        slot = lax.rem(g, 2)
        return pltpu.make_async_copy(u_hbm.at[at, :], ub.at[slot], u_sem.at[slot])

    x_in.start()
    u_copy(0).start()
    greet(n, n_tp, ep, tp)

    edges = [0]
    for ring in range(4):
        edges.append(edges[-1] + (3 * units // 128 + 3 - ring) // 4 * 128)
    wide_of = [edges[i + 1] - edges[i] for i in range(4)]

    def block_of(ring, step):
        if ring < 2:
            return ring_member(lax.rem(p + 2 * n - 1 - step, n), n)
        return ring_member(lax.rem(p + 1 + step, n), n)

    def term(ring, owner):
        lo, hi = edges[ring], edges[ring + 1]
        parts = []
        if lo < 2 * units:
            parts.append(block_dot(nt, owner, rows, pg[:, lo : min(hi, 2 * units)]))
        if hi > 2 * units:
            parts.append(block_dot(og, owner, rows, sh[:, max(lo - 2 * units, 0) : hi - 2 * units]))
        return parts[0] if len(parts) == 1 else jnp.concatenate(parts, axis=1)

    def ring_copy(ring, slot):
        return remote(
            ring_send.at[ring, slot, :, : wide_of[ring]],
            ring_recv.at[ring, slot, :, : wide_of[ring]],
            ring_ss.at[ring, slot],
            ring_rs.at[ring, slot],
            "ep",
            nxt if ring < 2 else prv,
        )

    order = (0, 2, 1, 3)

    def ring_step(step):
        slot, last = lax.rem(step, 2), lax.rem(step + 1, 2)
        for ring in order:
            size = wide_of[ring]
            mine = term(ring, block_of(ring, step))
            ring_copy(ring, last).wait_recv()

            @pl.when(step >= 2)
            def _():
                ring_copy(ring, slot).wait_send()

            ring_send[ring, slot, :, :size] = (
                mine + ring_recv[ring, last, :, :size].astype(F32)
            ).astype(BF)

            @pl.when(step <= n - 3)
            def _():
                pl.semaphore_signal(
                    free.at[ring],
                    1,
                    device_id={"ep": prv if ring < 2 else nxt},
                    device_id_type=pl.DeviceIdType.MESH,
                )

            @pl.when(step >= 2)
            def _():
                pl.semaphore_wait(free.at[ring], 1)

            ring_copy(ring, slot).start()

    for ring in order:
        ring_send[ring, 0, :, : wide_of[ring]] = term(ring, block_of(ring, 0)).astype(BF)
        ring_copy(ring, 0).start()

    for copy in w_in:
        copy.wait()
    x_in.wait()

    nt_dims, first_dims = (((1,), (1,)), ((), ())), (((0,), (0,)), ((), ()))

    def saved(g):
        at = pl.ds(pl.multiple_of(g * gr, gr), gr)
        slot = lax.rem(g, 2)
        return pltpu.make_async_copy(ub.at[slot], o_hbm.at[at, :], out_sem.at[slot])

    def back_copies(r):
        return block_copies(r, rbs, back, back_ss, back_rs, lax.rem(ep + n - r, n), shape, tp, zero)

    kept_copy = pltpu.make_async_copy(rbs.at[:capp, :], back.at[:capp, :], back_ss.at[0, 0])

    def gate_copy(r):
        return remote(
            gbs.at[r], g_back.at[r], gate_ss.at[r], gate_rs.at[r], "ep", lax.rem(ep + n - r, n)
        )

    g_kept = pltpu.make_async_copy(gbs.at[0], g_back.at[0], gate_ss.at[0])
    gbs[...] = jnp.zeros_like(gbs)

    @pl.loop(0, groups)
    def _(g):
        slot = lax.rem(g, 2)
        mine = pl.ds(pl.multiple_of(g * gr, gr), gr)
        u_copy(g).wait()

        @pl.when(g >= 1)
        def _():
            saved(g - 1).wait()

        @pl.when(g + 1 < groups)
        def _():
            u_copy(g + 1).start()

        gate = jnp.concatenate([gate_column(gates, g * per + i, capp) for i in range(per)], axis=0)
        rgb[mine, :] = (gate * ub[slot].astype(F32)).astype(BF)

        def hidden(at):
            x = xb[mine, :]
            g_pre = lax.dot_general(x, w[0, at, :], nt_dims, preferred_element_type=F32)
            u_pre = lax.dot_general(x, w[1, at, :], nt_dims, preferred_element_type=F32)
            grad = lax.dot_general(rgb[mine, :], w[2, at, :], nt_dims, preferred_element_type=F32)
            sig = jax.nn.sigmoid(g_pre)
            eb[2, mine, at] = (g_pre * sig * u_pre).astype(BF)
            eb[0, mine, at] = (grad * u_pre * sig * (1.0 + g_pre * (1.0 - sig))).astype(BF)
            eb[1, mine, at] = (grad * g_pre * sig).astype(BF)

        @pl.loop(0, units // 256)
        def _(c):
            hidden(pl.ds(pl.multiple_of(c * 256, 256), 256))

        if units % 256:
            hidden(pl.ds(units // 256 * 256, units % 256))

        def columns(c, total):
            at = pl.ds(pl.multiple_of(c * 256, 256), 256)
            out = jnp.dot(eb[2, mine, :], w[2, :, at], preferred_element_type=F32)
            grad = jnp.dot(eb[0, mine, :], w[0, :, at], preferred_element_type=F32) + jnp.dot(
                eb[1, mine, :], w[1, :, at], preferred_element_type=F32
            )
            rbs[mine, at] = grad.astype(BF)
            total = total + jnp.sum(out * ub[slot, :, at].astype(F32), axis=1, keepdims=True)
            ub[slot, :, at] = out.astype(BF)
            return total

        total = lax.fori_loop(0, width // 256, columns, jnp.zeros((gr, 1), F32))
        hi = total.astype(BF).astype(F32)
        lane = lax.broadcasted_iota(jnp.int32, (gr, 128), 1)
        terms = jnp.where(lane == 0, hi, jnp.where(lane == 1, total - hi, 0.0)).astype(BF)
        pick = (
            lax.broadcasted_iota(jnp.int32, (16, 128), 0) == lax.broadcasted_iota(jnp.int32, (16, 128), 1)
        ).astype(F32).astype(BF)
        turned = lax.dot_general(pick, terms, nt_dims, preferred_element_type=F32).astype(BF)
        for i in range(per):
            gbs[g * per + i, :, :capp] = turned[:, i * capp : (i + 1) * capp]
        saved(g).start()
        for i in range(per):
            r = g * per + i
            if i == 0:

                @pl.when(g == 0)
                def _():
                    kept_copy.start()
                    g_kept.start()

                @pl.when(g > 0)
                def _():
                    each(back_copies(r), "start")
                    gate_copy(r).start()
            else:
                each(back_copies(r), "start")
                gate_copy(r).start()

        @pl.when(lax.rem(g, 2) == 1)
        def _():
            ring_step((g + 1) // 2)

    def weight_rows(at):
        for k in range(3):
            for c in range(0, width, 512):
                w[k, at, c : c + 512] = lax.dot_general(
                    eb[k, :, at],
                    (rgb if k == 2 else xb)[:, c : c + 512],
                    first_dims,
                    preferred_element_type=F32,
                ).astype(BF)

    @pl.loop(0, units // 256)
    def _(c):
        weight_rows(pl.ds(pl.multiple_of(c * 256, 256), 256))

    if units % 256:
        weight_rows(pl.ds(units // 256 * 256, units % 256))

    dw_core = remote(
        w.at[:, : 2 * quarter, :], dw_recv, dw_ss.at[0], dw_rs.at[0], "tp", core_peer
    )
    dw_core.start()
    ring_step(groups // 2 + 1)
    dw_core.wait()
    dw_in = pltpu.make_async_copy(dw_recv, w.at[:, : 2 * quarter, :], dw_sem.at[0])
    dw_in.start()
    dw_in.wait()
    for k in range(3):

        @pl.loop(0, quarter // 32)
        def _(c, k=k):
            far = pl.ds(pl.multiple_of(2 * quarter + c * 32, 32), 32)
            came = pl.ds(pl.multiple_of(quarter + c * 32, 32), 32)
            w[k, far, :] = (w[k, far, :].astype(F32) + w[k, came, :].astype(F32)).astype(BF)

    dw_far = remote(
        w.at[:, 2 * quarter : 3 * quarter, :], dw_y, dw_ss.at[1], dw_rs.at[1], "tp", y_peer
    )
    dw_far.start()
    for k in range(3):

        @pl.loop(0, quarter // 32)
        def _(c, k=k):
            far = pl.ds(pl.multiple_of(3 * quarter + c * 32, 32), 32)
            came = pl.ds(pl.multiple_of(c * 32, 32), 32)
            w[k, far, :] = (w[k, far, :].astype(F32) + w[k, came, :].astype(F32)).astype(BF)

    dw_keep = pltpu.make_async_copy(w.at[:, 3 * quarter :, :], dw_own, dw_sem.at[1])
    dw_keep.start()

    @pl.loop(groups // 2 + 2, n - 1)
    def _(step):
        ring_step(step)

    for ring in order:
        mine = term(ring, ep)
        ring_copy(ring, n % 2).wait_recv()
        done = mine + ring_recv[ring, n % 2, :, : wide_of[ring]].astype(F32)
        lo, hi = edges[ring], edges[ring + 1]
        for k, out in enumerate((gu_out.at[0], gu_out.at[1], dn_out)):
            a, b = max(lo, k * units), min(hi, (k + 1) * units)
            if a < b:
                out[:, a - k * units : b - k * units] = done[:, a - lo : b - lo].astype(BF)
    for ring in range(4):
        for slot in range(2):
            ring_copy(ring, slot).wait_send()
    g_kept.wait()
    kept_copy.wait()
    saved(groups - 1).wait()
    dw_keep.wait()
    dw_far.wait()

    @pl.loop(1, n)
    def _(r):
        each(back_copies(r), "wait")
        gate_copy(r).wait()


def routed_expert(n, n_tp, shape, x, u, weights, gates, nt, pg, og, sh):
    total, width = x.shape
    units = 4 * weights[-1].shape[0]
    gr = total // 4
    rows = width // n
    half = (3 * units // 128 + 3) // 4 * 128
    vmem = pl.BlockSpec(memory_space=pltpu.VMEM)
    hbm = pl.BlockSpec(memory_space=pl.ANY)
    dma = pltpu.SemaphoreType.DMA
    if rows % 128:
        nt, og = nt.T, og.T
    return pl.pallas_call(
        functools.partial(middle_kernel, n, n_tp, shape),
        out_shape=(
            jax.ShapeDtypeStruct((total, width), BF),
            jax.ShapeDtypeStruct((n, 16, 128), BF),
            jax.ShapeDtypeStruct((total, width), BF),
            jax.ShapeDtypeStruct((3, units // 2, width), BF),
            jax.ShapeDtypeStruct((3, units // 4, width), BF),
            jax.ShapeDtypeStruct((3, units // 4, width), BF),
            jax.ShapeDtypeStruct((2, rows, units), BF),
            jax.ShapeDtypeStruct((rows, units), BF),
        ),
        in_specs=[hbm] * 10 + [vmem] * 5,
        out_specs=[hbm] * 6 + [vmem] * 2,
        scratch_shapes=[
            pltpu.VMEM((max(shape[0] - shape[1], 16), width), BF),
            pltpu.VMEM((3, units, width), BF),
            pltpu.VMEM((total, width), BF),
            pltpu.VMEM((2, gr, width), BF),
            pltpu.VMEM((total, width), BF),
            pltpu.VMEM((3, total, units), BF),
            pltpu.VMEM((total, width), BF),
            pltpu.VMEM((n, 16, 128), BF),
            pltpu.VMEM((4, 2, rows, half), BF),
            pltpu.VMEM((4, 2, rows, half), BF),
            dma((8,)),
            dma,
            dma((2,)),
            dma((2,)),
            dma((4, 2)),
            dma((4, 2)),
            pltpu.SemaphoreType.REGULAR((4,)),
            dma((2, n)),
            dma((2, n)),
            dma((n,)),
            dma((n,)),
            dma((2,)),
            dma((2,)),
            dma((2,)),
        ],
        compiler_params=pltpu.CompilerParams(
            collective_id=1, has_side_effects=True, vmem_limit_bytes=63 * 2**20
        ),
        cost_estimate=pl.CostEstimate(
            flops=2 * total * width * 6 * units, bytes_accessed=40 * 2**20, transcendentals=0
        ),
    )(x, u, *weights, gates, nt, pg, og, sh)


def tp_total(
    project, between, tp, core_send, core_recv, y_send, y_recv, summed,
    core_ss, core_rs, y_ss, y_rs, g_ss, g_rs,
):
    core_peer, y_peer = flip(tp, 1), flip(tp, 2)
    pieces, size = core_send.shape[0], core_send.shape[2]
    half = pieces * size

    def core_copy(i):
        return remote(core_send.at[i], core_recv.at[i], core_ss.at[i], core_rs.at[i], "tp", core_peer)

    def y_copy(i):
        return remote(y_send.at[i], y_recv.at[i], y_ss.at[i], y_rs.at[i], "tp", y_peer)

    def gather_copy(i, slot):
        return remote(summed.at[slot, i], summed.at[slot, i], g_ss.at[i], g_rs.at[i], "tp", core_peer)

    me, other = tp % 2, core_peer % 2
    for i in range(pieces):
        core_send[i] = project(other * half, i, size).astype(BF)
        core_copy(i).start()
        own = project(me * half, i, size)
        core_copy(i).wait_recv()
        y_send[i] = (own + core_recv[i].astype(F32)).astype(BF)
        y_copy(i).start()
    between()
    for i in range(pieces):
        y_copy(i).wait_recv()
        summed[me, i] = (y_send[i].astype(F32) + y_recv[i].astype(F32)).astype(BF)
        gather_copy(i, me).start()
    for i in range(pieces):
        gather_copy(i, other).wait_recv()
    for i in range(pieces):
        core_copy(i).wait_send()
        y_copy(i).wait_send()
        gather_copy(i, me).wait_send()


def blocks_at_once(n, capp):
    per = 1
    while 2 * per * capp <= 128 and n % (2 * per) == 0:
        per *= 2
    return per


def block_copies(r, src, dst, ss, rs, to, shape, tp, zero):
    capp, base, extra = shape
    at = pl.ds(pl.multiple_of(r * capp, 16), base)
    out = [(None, remote(src.at[at, :], dst.at[at, :], ss.at[0, r], rs.at[0, r], "ep", to))]
    if base < capp:
        at = pl.ds(pl.multiple_of(r * capp + base, 16), capp - base)
        out.append((tp < extra, remote(src.at[at, :], dst.at[at, :], ss.at[1, r], rs.at[1, r], "ep", to)))
        out.append((tp >= extra, pltpu.make_async_copy(zero, dst.at[at, :], ss.at[1, r])))
    return out


def each(copies, verb):
    for condition, copy in copies:
        if condition is None:
            getattr(copy, verb)()
        else:
            pl.when(condition)(getattr(copy, verb))


SEND_ORDER = (4, 5, 6, 7, 2, 3, 1, 0)


def send_order(i, n, ep):
    if n != len(SEND_ORDER):
        return (i + 1) % n
    to = ep
    for bit in (1, 2, 4):
        if SEND_ORDER[i] & bit:
            to = to + bit - 2 * bit * ((to // bit) % 2)
    return lax.rem(to + n - ep, n)


def gate_column(tiles, r, capp):
    ones = jnp.ones((16, 128), BF)
    return lax.dot_general(
        tiles[r, :, :capp], ones, (((0,), (0,)), ((), ())), preferred_element_type=F32
    )[:, :1]


def front_kernel(
    n,
    n_tp,
    shape,
    hidden,
    gain1,
    gain2,
    w,
    bias,
    cosine,
    sine,
    prefix,
    ow,
    place,
    cot,
    gu_own,
    dn_own,
    pairs,
    up_rows,
    gu_a,
    dn_a,
    dn_b,
    n1,
    qkv,
    ctx,
    mid,
    nt,
    factor_one,
    split,
    pair_in,
    pair_out,
    pair_si,
    pair_so,
    zero,
    up_sent,
    core_send,
    core_recv,
    y_send,
    y_recv,
    summed,
    up_ss,
    up_rs,
    w_ss,
    w_rs,
    core_ss,
    core_rs,
    y_ss,
    y_rs,
    g_ss,
    g_rs,
):
    ep = lax.axis_index("ep")
    tp = lax.axis_index("tp")
    tokens, width = hidden.shape
    lw = ctx.shape[1]
    heads = lw // HEAD_DIM
    core_peer, y_peer = flip(tp, 1), flip(tp, 2)
    greet(n, n_tp, ep, tp)

    capp = shape[0]
    zero[...] = jnp.zeros_like(zero)

    def up_copies(r):
        return block_copies(r, up_sent, up_rows, up_ss, up_rs, lax.rem(ep + r, n), shape, tp, zero)

    kept = pltpu.make_async_copy(up_sent.at[:capp, :], up_rows.at[:capp, :], up_ss.at[0, 0])
    per = blocks_at_once(n, capp)
    size = per * capp

    for i in range(n // per):
        b = send_order(i, n, ep) if per == 1 else i
        at = pl.ds(pl.multiple_of(b * size, size), size)
        up_sent[at, :] = jnp.dot(place[at, :], cot[...], preferred_element_type=F32).astype(BF)
        for j in range(per):
            if i == (n - 1 if per == 1 else 0) and j == 0:
                kept.start()
            else:
                each(up_copies(b * per + j), "start")

    w_copies = [
        remote(dn_own, dn_b, w_ss.at[0], w_rs.at[0], "tp", y_peer),
        remote(dn_own, dn_a, w_ss.at[1], w_rs.at[1], "tp", core_peer),
        remote(gu_own, gu_a, w_ss.at[2], w_rs.at[2], "tp", core_peer),
    ]
    for copy in w_copies:
        copy.start()

    chunk = pair_in.shape[1]
    chunks = pairs.shape[0] // chunk

    def pair_load(i):
        at, slot = pl.ds(pl.multiple_of(i * chunk, chunk), chunk), lax.rem(i, 2)
        return pltpu.make_async_copy(pairs.at[at], pair_in.at[slot], pair_si.at[slot])

    def pair_store(i):
        at, slot = pl.ds(pl.multiple_of(i * chunk, chunk), chunk), lax.rem(i, 2)
        return pltpu.make_async_copy(pair_out.at[slot], split.at[:, at, :], pair_so.at[slot])

    def set_apart(first, last):
        @pl.loop(first, last)
        def _(i):
            slot = lax.rem(i, 2)

            @pl.when(i + 1 < chunks)
            def _():
                pair_load(i + 1).start()

            pair_load(i).wait()

            @pl.when(i >= 2)
            def _():
                pair_store(i - 2).wait()

            pair_out[slot, 0] = pair_in[slot, :, 0, :]
            pair_out[slot, 1] = pair_in[slot, :, 1, :]
            pair_store(i).start()

    pair_load(0).start()

    @pl.loop(0, tokens // 64)
    def _(m):
        at = pl.ds(pl.multiple_of(m * 64, 64), 64)
        h = hidden[at, :].astype(F32)
        factor = lax.rsqrt(jnp.sum(h * h, axis=1, keepdims=True) * (1.0 / width) + EPSILON)
        factor_one[at, :] = factor
        n1[at, :] = (h * factor * gain1[...]).astype(BF)

    for k in range(3):

        @pl.loop(0, lw // 256)
        def _(c, k=k):
            at = pl.ds(pl.multiple_of(c * 256, 256), 256)
            x = jnp.dot(n1[...], w[k, :, at], preferred_element_type=F32) + bias[k : k + 1, at]
            if k < 2:
                x = jnp.concatenate(
                    [
                        x[:, i * HEAD_DIM : (i + 1) * HEAD_DIM] * cosine[...]
                        + pltpu.roll(x[:, i * HEAD_DIM : (i + 1) * HEAD_DIM], HEAD_DIM // 2, 1) * sine[...]
                        for i in range(256 // HEAD_DIM)
                    ],
                    axis=1,
                )
            qkv[k, :, at] = x.astype(BF)

    @pl.loop(0, tokens // 128)
    def _(m):
        at = pl.ds(pl.multiple_of(m * 128, 128), 128)
        row = lax.broadcasted_iota(jnp.int32, (128, tokens), 0) + m * 128
        col = lax.broadcasted_iota(jnp.int32, (128, tokens), 1)
        visible = (col <= row) | (col < prefix[...])
        for i in range(heads):
            lanes = slice(i * HEAD_DIM, (i + 1) * HEAD_DIM)
            s = lax.dot_general(
                qkv[0, at, lanes], qkv[1, :, lanes], (((1,), (1,)), ((), ())), preferred_element_type=F32
            )
            s = jnp.where(visible, s * HEAD_DIM ** (-0.5), -1e30)
            e = jnp.exp(s - jnp.max(s, axis=1, keepdims=True))
            e = e * (1.0 / jnp.sum(e, axis=1, keepdims=True))
            ctx[at, lanes] = jnp.dot(
                e.astype(BF), qkv[2, :, lanes], preferred_element_type=F32
            ).astype(BF)

    pieces, size = core_send.shape[0], core_send.shape[2]
    half = pieces * size

    def project(base, i, size):
        at = pl.ds(pl.multiple_of(base + i * size, size), size)
        return lax.dot_general(
            ctx[...], ow[at, :], (((1,), (1,)), ((), ())), preferred_element_type=F32
        )

    tp_total(
        project, lambda: set_apart(0, chunks * 11 // 16), tp, core_send, core_recv, y_send, y_recv, summed,
        core_ss, core_rs, y_ss, y_rs, g_ss, g_rs,
    )

    @pl.loop(0, tokens // 32)
    def _(m):
        at = pl.ds(pl.multiple_of(m * 32, 32), 32)
        total = jnp.zeros((32, 1), F32)
        for j in range(2):
            for i in range(pieces):
                lanes = slice(j * half + i * size, j * half + (i + 1) * size)
                x = hidden[at, lanes].astype(F32) + summed[j, i, at, :].astype(F32)
                mid[at, lanes] = x
                total = total + jnp.sum(x * x, axis=1, keepdims=True)
        factor = lax.rsqrt(total * (1.0 / width) + EPSILON)
        nt[at, :] = (mid[at, :] * factor * gain2[...]).astype(BF)

    set_apart(chunks * 11 // 16, chunks)
    pair_store(chunks - 2).wait()
    pair_store(chunks - 1).wait()
    for copy in w_copies:
        copy.wait()
    kept.wait()
    for r in range(1, n):
        each(up_copies(r), "wait")


def front(n, n_tp, shape, hidden, gain1, gain2, w, bias, cosine, sine, prefix, ow, place, cot, gu_own, dn_own, pairs):
    tokens, width = hidden.shape
    lw = ow.shape[1]
    quarter = dn_own.shape[0]
    vmem = pl.BlockSpec(memory_space=pltpu.VMEM)
    hbm = pl.BlockSpec(memory_space=pl.ANY)
    dma = pltpu.SemaphoreType.DMA
    return pl.pallas_call(
        functools.partial(front_kernel, n, n_tp, shape),
        out_shape=(
            jax.ShapeDtypeStruct((n * shape[0], width), BF),
            jax.ShapeDtypeStruct((2, quarter, width), BF),
            jax.ShapeDtypeStruct((quarter, width), BF),
            jax.ShapeDtypeStruct((quarter, width), BF),
            jax.ShapeDtypeStruct((tokens, width), BF),
            jax.ShapeDtypeStruct((3, tokens, lw), BF),
            jax.ShapeDtypeStruct((tokens, lw), BF),
            jax.ShapeDtypeStruct((tokens, width), F32),
            jax.ShapeDtypeStruct((tokens, width), BF),
            jax.ShapeDtypeStruct((tokens, 1), F32),
            jax.ShapeDtypeStruct((2, width, pairs.shape[2]), BF),
        ),
        in_specs=[vmem] * 11 + [hbm] * 3,
        out_specs=[hbm] * 4 + [vmem] * 6 + [hbm],
        scratch_shapes=[
            pltpu.VMEM((2, 128, 2, pairs.shape[2]), BF),
            pltpu.VMEM((2, 2, 128, pairs.shape[2]), BF),
            dma((2,)),
            dma((2,)),
            pltpu.VMEM((max(shape[0] - shape[1], 16), width), BF),
            pltpu.VMEM((n * shape[0], width), BF),
            pltpu.VMEM((4, tokens, width // 8), BF),
            pltpu.VMEM((4, tokens, width // 8), BF),
            pltpu.VMEM((4, tokens, width // 8), BF),
            pltpu.VMEM((4, tokens, width // 8), BF),
            pltpu.VMEM((2, 4, tokens, width // 8), BF),
            dma((2, n)),
            dma((2, n)),
            dma((3,)),
            dma((3,)),
            dma((4,)),
            dma((4,)),
            dma((4,)),
            dma((4,)),
            dma((4,)),
            dma((4,)),
        ],
        compiler_params=pltpu.CompilerParams(
            collective_id=2, has_side_effects=True, vmem_limit_bytes=56 * 2**20
        ),
        cost_estimate=pl.CostEstimate(
            flops=2 * tokens * width * 4 * lw, bytes_accessed=30 * 2**20, transcendentals=0
        ),
    )(hidden, gain1, gain2, w, bias, cosine, sine, prefix, ow, place, cot, gu_own, dn_own, pairs)


def dispatch_kernel(
    n,
    n_tp,
    shape,
    n_exp,
    nt,
    place,
    router,
    cot,
    sgu,
    sdn,
    gu_own,
    dn_b,
    dest_t,
    x_rows,
    g_rows,
    gu_b,
    gu_c,
    dn_c,
    probs,
    place_t,
    weighted,
    og,
    pg,
    sh,
    part,
    sback,
    sgrad,
    zero,
    gate,
    x_send,
    g_send,
    x_ss,
    x_rs,
    gate_ss,
    gate_rs,
    w_ss,
    w_rs,
):
    ep = lax.axis_index("ep")
    tp = lax.axis_index("tp")
    tokens, width = nt.shape
    units = sdn.shape[1]
    total = place.shape[0]
    core_peer, y_peer = flip(tp, 1), flip(tp, 2)
    greet(n, n_tp, ep, tp)
    w_y = remote(gu_own, gu_b, w_ss.at[0], w_rs.at[0], "tp", y_peer)
    w_y.start()
    w_on = remote(dn_b, dn_c, w_ss.at[1], w_rs.at[1], "tp", core_peer)
    w_on.start()

    capp = shape[0]
    zero[...] = jnp.zeros_like(zero)

    def x_copies(r):
        return block_copies(r, x_send, x_rows, x_ss, x_rs, lax.rem(ep + r, n), shape, tp, zero)

    def gate_copy(r, way):
        to = lax.rem(ep + r, n) if way == "out" else lax.rem(ep + n - r, n)
        return remote(g_send.at[r], g_rows.at[r], gate_ss.at[r], gate_rs.at[r], "ep", to)

    kept = pltpu.make_async_copy(x_send.at[:capp, :], x_rows.at[:capp, :], x_ss.at[0, 0])
    g_kept = pltpu.make_async_copy(g_send.at[0], g_rows.at[0], gate_ss.at[0])
    per = blocks_at_once(n, capp)
    size = per * capp

    for i in range(n // per):
        b = send_order(i, n, ep) if per == 1 else i
        at = pl.ds(pl.multiple_of(b * size, size), size)
        x_send[at, :] = jnp.dot(place[at, :], nt[...], preferred_element_type=F32).astype(BF)
        for j in range(per):
            if i == (n - 1 if per == 1 else 0) and j == 0:
                kept.start()
            else:
                each(x_copies(b * per + j), "start")

    logits = jnp.dot(nt[...], router[...], preferred_element_type=F32)
    lane = lax.broadcasted_iota(jnp.int32, logits.shape, 1)
    chosen = jnp.where(lane < n_exp, logits, -1e30)
    e = jnp.exp(chosen - jnp.max(chosen, axis=1, keepdims=True))
    prob = e / jnp.sum(e, axis=1, keepdims=True)
    prob = jnp.where(lane == n_exp, jax.nn.sigmoid(logits), prob)
    probs[...] = prob
    hi = prob.astype(BF)
    lo = (prob - hi.astype(F32)).astype(BF)
    g_send[...] = jnp.zeros_like(g_send)
    across = (((0,), (1,)), ((), ()))

    for r in range(n):
        where = place[r * capp : (r + 1) * capp, :]
        pick = lax.broadcasted_iota(jnp.int32, (128, capp), 0) == lax.rem(r + ep, n)
        g_hi = jnp.sum(
            jnp.where(pick, lax.dot_general(hi, where, across, preferred_element_type=F32), 0.0),
            axis=0,
            keepdims=True,
        )
        g_lo = jnp.sum(
            jnp.where(pick, lax.dot_general(lo, where, across, preferred_element_type=F32), 0.0),
            axis=0,
            keepdims=True,
        )
        term = lax.broadcasted_iota(jnp.int32, (16, capp), 0)
        g_send[r, :, :capp] = jnp.where(term == 0, g_hi, jnp.where(term == 1, g_lo, 0.0)).astype(BF)
        gate[:, r * capp : (r + 1) * capp] = g_hi + g_lo
        if r == 0:
            g_kept.start()
        else:
            gate_copy(r, "out").start()

    @pl.loop(0, tokens // 64)
    def _(m):
        at = pl.ds(pl.multiple_of(m * 64, 64), 64)
        og[at, :] = (probs[at, n_exp : n_exp + 1] * cot[at, :].astype(F32)).astype(BF)

    def hidden(at, up_at):
        g_pre = jnp.dot(nt[...], sgu[0, :, at], preferred_element_type=F32)
        u_pre = jnp.dot(nt[...], sgu[1, :, at], preferred_element_type=F32)
        grad = jnp.dot(og[...], sdn[:, at], preferred_element_type=F32)
        sig = jax.nn.sigmoid(g_pre)
        sh[:, at] = (g_pre * sig * u_pre).astype(BF)
        pg[:, at] = (grad * u_pre * sig * (1.0 + g_pre * (1.0 - sig))).astype(BF)
        pg[:, up_at] = (grad * g_pre * sig).astype(BF)

    @pl.loop(0, units // 256)
    def _(c):
        hidden(
            pl.ds(pl.multiple_of(c * 256, 256), 256),
            pl.ds(pl.multiple_of(c * 256 + units, 128), 256),
        )

    if units % 256:
        rest = units // 256 * 256
        hidden(pl.ds(rest, units - rest), pl.ds(units + rest, units - rest))

    nt_dims = (((1,), (1,)), ((), ()))

    share = probs[:, n_exp : n_exp + 1]

    def columns(c, total):
        at = pl.ds(pl.multiple_of(c * 256, 256), 256)
        out = lax.dot_general(sh[...], sdn[at, :], nt_dims, preferred_element_type=F32)
        part[:, at] = (share * out).astype(BF)
        sback[:, at] = lax.dot_general(
            pg[:, :units], sgu[0, at, :], nt_dims, preferred_element_type=F32
        ) + lax.dot_general(pg[:, units:], sgu[1, at, :], nt_dims, preferred_element_type=F32)
        return total + jnp.sum(cot[:, at].astype(F32) * out, axis=1, keepdims=True)

    sgrad[...] = lax.fori_loop(0, width // 256, columns, jnp.zeros((tokens, 1), F32))

    @pl.loop(0, total // 128)
    def _(c):
        at = pl.ds(pl.multiple_of(c * 128, 128), 128)
        spot = lax.broadcasted_iota(jnp.int32, (tokens, 128), 1) + c * 128
        hit = dest_t[:, :1] == spot
        for k in range(1, dest_t.shape[1]):
            hit = hit | (dest_t[:, k : k + 1] == spot)
        place_t[:, at] = jnp.where(hit, 1.0, 0.0).astype(BF)
        weighted[:, at] = jnp.where(hit, gate[:, at], 0.0).astype(BF)

    w_y.wait()
    w_far = remote(gu_b, gu_c, w_ss.at[2], w_rs.at[2], "tp", core_peer)
    w_far.start()
    w_on.wait()
    w_far.wait()
    kept.wait()
    g_kept.wait()

    @pl.loop(1, n)
    def _(r):
        gate_copy(r, "in").wait()
        each(x_copies(r), "wait")


def dispatch(n, n_tp, shape, n_exp, nt, place, router, cot, sgu, sdn, gu_own, dn_b, dest_t):
    tokens, width = nt.shape
    units = sdn.shape[1]
    total = place.shape[0]
    vmem = pl.BlockSpec(memory_space=pltpu.VMEM)
    hbm = pl.BlockSpec(memory_space=pl.ANY)
    dma = pltpu.SemaphoreType.DMA
    return pl.pallas_call(
        functools.partial(dispatch_kernel, n, n_tp, shape, n_exp),
        out_shape=(
            jax.ShapeDtypeStruct((total, width), BF),
            jax.ShapeDtypeStruct((n, 16, 128), BF),
            jax.ShapeDtypeStruct(gu_own.shape, BF),
            jax.ShapeDtypeStruct(gu_own.shape, BF),
            jax.ShapeDtypeStruct(dn_b.shape, BF),
            jax.ShapeDtypeStruct((tokens, 128), F32),
            jax.ShapeDtypeStruct((tokens, total), BF),
            jax.ShapeDtypeStruct((tokens, total), BF),
            jax.ShapeDtypeStruct((tokens, width), BF),
            jax.ShapeDtypeStruct((tokens, 2 * units), BF),
            jax.ShapeDtypeStruct((tokens, units), BF),
            jax.ShapeDtypeStruct((tokens, width), BF),
            jax.ShapeDtypeStruct((tokens, width), F32),
            jax.ShapeDtypeStruct((tokens, 1), F32),
        ),
        in_specs=[vmem] * 6 + [hbm] * 2 + [vmem],
        out_specs=[hbm] * 5 + [vmem] * 9,
        scratch_shapes=[
            pltpu.VMEM((max(shape[0] - shape[1], 16), width), BF),
            pltpu.VMEM((1, total), F32),
            pltpu.VMEM((total, width), BF),
            pltpu.VMEM((n, 16, 128), BF),
            dma((2, n)),
            dma((2, n)),
            dma((n,)),
            dma((n,)),
            dma((3,)),
            dma((3,)),
        ],
        compiler_params=pltpu.CompilerParams(
            collective_id=3, has_side_effects=True, vmem_limit_bytes=60 * 2**20
        ),
        cost_estimate=pl.CostEstimate(
            flops=2 * tokens * width * 6 * units, bytes_accessed=40 * 2**20, transcendentals=0
        ),
    )(nt, place, router, cot, sgu, sdn, gu_own, dn_b, dest_t)

def backward_kernel(
    n,
    n_tp,
    shape,
    n_exp,
    back,
    g_back,
    place_t,
    sback,
    sgrad,
    probs,
    router,
    nt,
    mid,
    cot,
    gain2,
    qkv,
    ow,
    cosine,
    sine,
    prefix,
    o_sent,
    o_rows,
    ag,
    lg,
    bias,
    small,
    zero,
    core_send,
    core_recv,
    y_send,
    y_recv,
    summed,
    few_send,
    few_recv,
    ng,
    cg,
    dk,
    dv,
    o_ss,
    o_rs,
    core_ss,
    core_rs,
    y_ss,
    y_rs,
    g_ss,
    g_rs,
    few_ss,
    few_rs,
):
    ep = lax.axis_index("ep")
    tp = lax.axis_index("tp")
    tokens, width = nt.shape
    total = back.shape[0]
    lw = ow.shape[1]
    heads = lw // HEAD_DIM
    core_peer, y_peer = flip(tp, 1), flip(tp, 2)
    greet(n, n_tp, ep, tp)

    capp = shape[0]
    zero[...] = jnp.zeros_like(zero)

    def o_copies(r):
        return block_copies(r, o_sent, o_rows, o_ss, o_rs, lax.rem(ep + n - r, n), shape, tp, zero)

    kept = pltpu.make_async_copy(o_sent.at[:capp, :], o_rows.at[:capp, :], o_ss.at[0, 0])

    for i in range(n - 1):
        each(o_copies(send_order(i, n, ep)), "start")
    kept.start()

    row = lax.broadcasted_iota(jnp.int32, (total, 128), 0)
    spot = lax.broadcasted_iota(jnp.int32, (total, 128), 1)
    expert = lax.rem(row // capp + ep * (n_exp // n), n_exp)
    gg = jnp.concatenate([gate_column(g_back, r, capp) for r in range(n)], axis=0)
    few = jnp.dot(
        place_t[...], jnp.where(spot == expert, gg, 0.0).astype(BF), preferred_element_type=F32
    )
    lane = lax.broadcasted_iota(jnp.int32, (tokens, 128), 1)
    few_send[0] = jnp.where(lane == n_exp, sgrad[...], few).astype(BF)
    few_core = remote(few_send.at[0], few_recv.at[0], few_ss.at[0], few_rs.at[0], "tp", core_peer)
    few_core.start()

    def project(base, i, size):
        at = pl.ds(pl.multiple_of(base + i * size, size), size)
        return sback[:, at] + jnp.dot(place_t[...], back[:, at], preferred_element_type=F32)

    def between():
        few_core.wait()
        few_send[1] = (few_send[0].astype(F32) + few_recv[0].astype(F32)).astype(BF)
        few_y = remote(few_send.at[1], few_recv.at[1], few_ss.at[1], few_rs.at[1], "tp", y_peer)
        few_y.start()
        few_y.wait()

    tp_total(
        project, between, tp, core_send, core_recv, y_send, y_recv, summed,
        core_ss, core_rs, y_ss, y_rs, g_ss, g_rs,
    )

    prob = jnp.where(lane < n_exp, probs[...], 0.0)
    share = probs[:, n_exp : n_exp + 1]
    grads = few_send[1].astype(F32) + few_recv[1].astype(F32)
    inner = jnp.sum(prob * grads, axis=1, keepdims=True)
    gate_in = grads * share * (1.0 - share)
    few_send[0] = jnp.where(
        lane < n_exp, prob * (grads - inner), jnp.where(lane == n_exp, gate_in, 0.0)
    ).astype(BF)
    pieces, size = summed.shape[1], summed.shape[3]
    for j in range(2):
        for i in range(pieces):
            at = slice((j * pieces + i) * size, (j * pieces + i + 1) * size)
            ng[:, at] = summed[j, i].astype(F32) + lax.dot_general(
                few_send[0], router[at, :], (((1,), (1,)), ((), ())), preferred_element_type=F32
            )

    step = 32

    def norm_rows(m, acc):
        at = pl.ds(pl.multiple_of(m * step, step), step)
        h = mid[at, :]
        grad = ng[at, :]
        factor = lax.rsqrt(jnp.sum(h * h, axis=1, keepdims=True) * (1.0 / width) + EPSILON)
        scaled = grad * gain2[...]
        mean = jnp.sum(scaled * h, axis=1, keepdims=True) * (1.0 / width)
        ag[at, :] = (
            cot[at, :].astype(F32) + factor * scaled - h * (factor * factor * factor) * mean
        ).astype(BF)
        return acc + jnp.sum((grad * h * factor).reshape(step // 8, 8, width), axis=0)

    acc = lax.fori_loop(0, tokens // step, norm_rows, jnp.zeros((8, width), F32))

    @pl.loop(0, lw // 256)
    def _(c):
        at = pl.ds(pl.multiple_of(c * 256, 256), 256)
        cg[:, at] = jnp.dot(ag[...], ow[:, at], preferred_element_type=F32).astype(BF)

    dk[...] = jnp.zeros_like(dk)
    dv[...] = jnp.zeros_like(dv)
    first_dims, last_dims = (((0,), (0,)), ((), ())), (((1,), (1,)), ((), ()))

    def attend(m, sums):
        at = pl.ds(pl.multiple_of(m * 128, 128), 128)
        row = lax.broadcasted_iota(jnp.int32, (128, tokens), 0) + m * 128
        col = lax.broadcasted_iota(jnp.int32, (128, tokens), 1)
        visible = (col <= row) | (col < prefix[...])
        parts = []
        for i in range(heads):
            lanes = slice(i * HEAD_DIM, (i + 1) * HEAD_DIM)
            q, grad = qkv[0, at, lanes], cg[at, lanes]
            s = lax.dot_general(q, qkv[1, :, lanes], last_dims, preferred_element_type=F32)
            s = jnp.where(visible, s * HEAD_DIM ** (-0.5), -1e30)
            e = jnp.exp(s - jnp.max(s, axis=1, keepdims=True))
            e = e * (1.0 / jnp.sum(e, axis=1, keepdims=True))
            dp = lax.dot_general(grad, qkv[2, :, lanes], last_dims, preferred_element_type=F32)
            delta = jnp.sum(e * dp, axis=1, keepdims=True)
            ds = (e * (dp - delta)).astype(BF)
            dv[:, lanes] += lax.dot_general(e.astype(BF), grad, first_dims, preferred_element_type=F32)
            dk[:, lanes] += lax.dot_general(ds, q, first_dims, preferred_element_type=F32)
            dq = jnp.dot(ds, qkv[1, :, lanes], preferred_element_type=F32) * HEAD_DIM ** (-0.5)
            dq = dq * cosine[at, :] - pltpu.roll(dq, HEAD_DIM // 2, 1) * sine[at, :]
            lg[at, lanes] = dq.astype(BF)
            parts.append(jnp.sum(dq.reshape(16, 8, HEAD_DIM), axis=0))
        return sums + jnp.concatenate(parts, axis=1)

    sums = lax.fori_loop(0, tokens // 128, attend, jnp.zeros((8, lw), F32))
    bias[:, :lw] = jnp.sum(sums, axis=0, keepdims=True)
    for i in range(heads):
        lanes = slice(i * HEAD_DIM, (i + 1) * HEAD_DIM)
        grad = dk[:, lanes] * HEAD_DIM ** (-0.5)
        grad = grad * cosine[...] - pltpu.roll(grad, HEAD_DIM // 2, 1) * sine[...]
        at = slice(lw + i * HEAD_DIM, lw + (i + 1) * HEAD_DIM)
        lg[:, at] = grad.astype(BF)
        bias[:, at] = jnp.sum(grad, axis=0, keepdims=True)
    lg[:, 2 * lw :] = dv[...].astype(BF)
    bias[:, 2 * lw :] = jnp.sum(dv[...], axis=0, keepdims=True)

    wide, span = small.shape[1:]
    gain_row = jnp.sum(acc, axis=0, keepdims=True)
    rows = lax.dot_general(few_send[0], nt[...], first_dims, preferred_element_type=F32)[:wide]
    index = lax.broadcasted_iota(jnp.int32, rows.shape, 0)
    rows = jnp.where(index == n_exp + 1, gain_row, rows).astype(BF)
    for r in range(n):
        small[r] = rows[:, r * span : (r + 1) * span]

    kept.wait()
    for r in range(1, n):
        each(o_copies(r), "wait")


def backward(n, n_tp, shape, n_exp, back, g_back, place_t, sback, sgrad, probs, router, nt, mid, cot, gain2, qkv, ow, cosine, sine, prefix, o_sent):
    tokens, width = nt.shape
    lw = ow.shape[1]
    wide = -(-(n_exp + 2) // 16) * 16
    vmem = pl.BlockSpec(memory_space=pltpu.VMEM)
    hbm = pl.BlockSpec(memory_space=pl.ANY)
    dma = pltpu.SemaphoreType.DMA
    piece = (4, tokens, width // 8)
    return pl.pallas_call(
        functools.partial(backward_kernel, n, n_tp, shape, n_exp),
        out_shape=(
            jax.ShapeDtypeStruct(o_sent.shape, BF),
            jax.ShapeDtypeStruct((tokens, width), BF),
            jax.ShapeDtypeStruct((tokens, 3 * lw), BF),
            jax.ShapeDtypeStruct((1, 3 * lw), F32),
            jax.ShapeDtypeStruct((n, wide, width // n), BF),
        ),
        in_specs=[vmem] * 16 + [hbm],
        out_specs=[hbm] + [vmem] * 4,
        scratch_shapes=[
            pltpu.VMEM((max(shape[0] - shape[1], 16), width), BF),
            pltpu.VMEM(piece, BF),
            pltpu.VMEM(piece, BF),
            pltpu.VMEM(piece, BF),
            pltpu.VMEM(piece, BF),
            pltpu.VMEM((2,) + piece, BF),
            pltpu.VMEM((2, tokens, 128), BF),
            pltpu.VMEM((2, tokens, 128), BF),
            pltpu.VMEM((tokens, width), F32),
            pltpu.VMEM((tokens, lw), BF),
            pltpu.VMEM((tokens, lw), F32),
            pltpu.VMEM((tokens, lw), F32),
            dma((2, n)),
            dma((2, n)),
            dma((4,)),
            dma((4,)),
            dma((4,)),
            dma((4,)),
            dma((4,)),
            dma((4,)),
            dma((2,)),
            dma((2,)),
        ],
        compiler_params=pltpu.CompilerParams(
            collective_id=4, has_side_effects=True, vmem_limit_bytes=60 * 2**20
        ),
        cost_estimate=pl.CostEstimate(
            flops=2 * tokens * width * 4 * lw, bytes_accessed=30 * 2**20, transcendentals=0
        ),
    )(back, g_back, place_t, sback, sgrad, probs, router, nt, mid, cot, gain2, qkv, ow, cosine, sine, prefix, o_sent)


def body(
    hidden,
    attn_gain,
    qkv_weight,
    qkv_bias,
    out_weight,
    mlp_gain,
    router_weight,
    share_gate,
    shared_gate_up,
    shared_down,
    expert_gate_up,
    expert_down,
    routes,
    priority,
    prefix,
    cotangent,
):
    tokens, width = hidden.shape
    n_ep = lax.axis_size("ep")
    n_tp = lax.axis_size("tp")
    tp_i = lax.axis_index("tp")
    local_width = qkv_weight.shape[2]
    expert_local = expert_gate_up.shape[0]
    n_exp = expert_local * n_ep
    top = routes.shape[1]
    capacity = (5 * tokens * top + 4 * n_exp - 1) // (4 * n_exp)
    tiles = -(-capacity // 16)
    least, extra = 16 * (tiles // n_tp), tiles % n_tp
    part_pad = least + (16 if extra else 0)
    shape = (part_pad, least, extra)
    rows = n_exp * part_pad

    flat_route = routes.T.reshape(-1)
    flat_order = priority.T.reshape(-1)
    hits = (flat_route[:, None] == jnp.arange(n_exp, dtype=jnp.int32)[None, :]).astype(BF)
    smaller = (flat_order[None, :] < flat_order[:, None]).astype(BF)
    counts = mm(smaller, hits, 1, 0)
    slot = jnp.sum(counts * hits.astype(F32), axis=1).astype(jnp.int32).reshape(top, tokens)
    kept = slot < capacity
    in_part = slot - (tp_i * least + 16 * jnp.minimum(tp_i, extra))
    mine = kept & (in_part >= 0) & (in_part < jnp.where(tp_i < extra, part_pad, least))
    ep_i = lax.axis_index("ep")
    hop = lax.rem(routes.T + n_exp - ep_i * expert_local, n_exp)
    dest = jnp.where(mine, hop * part_pad + in_part, -1)
    row_ids = jnp.arange(rows, dtype=jnp.int32)[:, None]
    place = (dest[0][None, :] == row_ids)
    for k in range(1, top):
        place = place | (dest[k][None, :] == row_ids)
    place = place.astype(BF)

    cos_all, sin_all = angle_tables(tokens, HEAD_DIM)
    w_t = jnp.transpose(qkv_weight, (1, 0, 2))
    prefix_row = jnp.broadcast_to(prefix[None], (1, tokens))
    gu_own = jnp.transpose(expert_gate_up[0], (1, 2, 0))
    dn_own = jnp.transpose(expert_down[0], (1, 0))
    up_rows, gu_a, dn_a, dn_b, normed_one, qkv, context, middle, normed_two, factor_one, sgu = front(
        n_ep,
        n_tp,
        shape,
        hidden,
        attn_gain[None],
        mlp_gain[None],
        w_t,
        qkv_bias,
        cos_all,
        sin_all,
        prefix_row,
        out_weight,
        place,
        cotangent,
        gu_own,
        dn_own,
        shared_gate_up,
    )

    router_all = jnp.concatenate(
        [router_weight, share_gate[:, None], jnp.zeros((width, 127 - n_exp), BF)], axis=1
    )
    got, gates, gu_b, gu_c, dn_c, probs_all, place_t, weighted_place, shared_out_grad, pre_grad, shared_hidden, scaled_part, shared_back, scale_grad = (
        dispatch(
            n_ep,
            n_tp,
            shape,
            n_exp,
            normed_two,
            place,
            router_all,
            cotangent,
            sgu,
            shared_down,
            gu_own,
            dn_b,
            dest.T,
        )
    )
    back_rows, back_gates, e_out, _, dw_own, dw_y, gu_grad, shared_down_grad = routed_expert(
        n_ep,
        n_tp,
        shape,
        got,
        up_rows,
        (gu_a, gu_c, gu_b, gu_own, dn_a, dn_c, dn_b, dn_own),
        gates,
        normed_two,
        pre_grad,
        shared_out_grad,
        shared_hidden,
    )
    shared_gate_up_grad = jnp.transpose(gu_grad, (1, 0, 2)).astype(F32)
    shared_down_grad = shared_down_grad.astype(F32)
    expert_down_grad = jnp.transpose(dw_own[2].astype(F32) + dw_y[2].astype(F32), (1, 0))[None]
    expert_gate_up_grad = jnp.transpose(dw_own[:2].astype(F32) + dw_y[:2].astype(F32), (2, 0, 1))[None]

    out_rows, attn_grad, linear_grad, bias_grad, small = backward(
        n_ep,
        n_tp,
        shape,
        n_exp,
        back_rows,
        back_gates,
        place_t,
        shared_back,
        scale_grad,
        probs_all,
        router_all,
        normed_two,
        middle,
        cotangent,
        mlp_gain[None],
        qkv,
        out_weight,
        cos_all,
        sin_all,
        prefix_row,
        e_out,
    )
    qkv_grad, out_weight_grad, input_grad, output, gain_one, bias_sum, small_sum = tail(
        n_ep,
        n_tp,
        normed_one,
        linear_grad,
        attn_grad,
        context,
        w_t,
        hidden,
        factor_one,
        attn_gain[None],
        bias_grad,
        small,
        out_rows,
        weighted_place,
        scaled_part,
        middle,
    )
    small_sum = jnp.transpose(small_sum, (1, 0, 2)).reshape(-1, width)
    qkv_weight_grad = jnp.transpose(qkv_grad, (1, 0, 2))
    gain_one_sum = gain_one[0]
    bias_sum = bias_sum.reshape(3, local_width)
    router_sum = small_sum[:n_exp].T
    share_gate_sum = small_sum[n_exp]
    gain_two_sum = small_sum[n_exp + 1]
    return (
        output,
        input_grad,
        gain_one_sum,
        qkv_weight_grad,
        bias_sum,
        out_weight_grad,
        gain_two_sum,
        router_sum,
        share_gate_sum,
        shared_gate_up_grad,
        shared_down_grad,
        expert_gate_up_grad,
        expert_down_grad,
    )


def solution(mesh):
    return jax.shard_map(
        body,
        mesh=mesh,
        in_specs=(
            P("ep", None),
            P(),
            P(None, None, "tp"),
            P(None, "tp"),
            P(None, "tp"),
            P(),
            P(),
            P(),
            P(None, None, "tp"),
            P(None, "tp"),
            P("ep", None, None, "tp"),
            P("ep", None, "tp"),
            P("ep", None),
            P("ep", None),
            P("ep"),
            P("ep", None),
        ),
        out_specs=(
            P("ep", "tp"),
            P("ep", "tp"),
            P(),
            P("ep", None, "tp"),
            P(None, "tp"),
            P("ep", "tp"),
            P(),
            P(),
            P(),
            P("ep", None, "tp"),
            P("ep", "tp"),
            P("ep", None, None, "tp"),
            P("ep", None, "tp"),
        ),
        check_vma=False,
    )
```

```python
import functools

import jax
import jax.numpy as jnp
import numpy as np
from jax import lax
from jax.experimental import pallas as pl
from jax.experimental.pallas import tpu as pltpu
from jax.sharding import PartitionSpec as P

HEAD_DIM = 128
EPSILON = 1e-06
THETA = 1000000.0
BF = jnp.bfloat16
F32 = jnp.float32


def mm(a, b, ca, cb):
    return lax.dot_general(a, b, (((ca,), (cb,)), ((), ())), preferred_element_type=F32)


def angle_tables(length, head_size):
    half_size = head_size // 2
    frequency = (THETA ** (-np.arange(half_size, dtype=np.float32) * 2.0 / head_size)).astype(np.float32)
    angles = (np.arange(length, dtype=np.float32)[:, None] * frequency[None, :]).astype(np.float64)
    cosine, sine_val = np.cos(angles), np.sin(angles)
    return (
        np.concatenate([cosine, cosine], axis=1).astype(np.float32),
        np.concatenate([-sine_val, sine_val], axis=1).astype(np.float32),
    )


def ring_place(e, n):
    odd = e % 2
    return (1 - odd) * (e // 2) + odd * (n - 1 - e // 2)


def ring_member(p, n):
    second = p // (n // 2)
    return (1 - second) * 2 * p + second * (2 * (n - 1 - p) + 1)


def remote(src, dst, send_sem, recv_sem, axis, index):
    return pltpu.make_async_remote_copy(
        src_ref=src,
        dst_ref=dst,
        send_sem=send_sem,
        recv_sem=recv_sem,
        device_id={axis: index},
        device_id_type=pl.DeviceIdType.MESH,
    )


def greet(n, n_tp, ep, tp):
    barrier = pltpu.get_barrier_semaphore()
    for shift in range(1, n):
        pl.semaphore_signal(
            barrier, 1, device_id={"ep": lax.rem(ep + shift, n)}, device_id_type=pl.DeviceIdType.MESH
        )
    for shift in range(1, n_tp):
        pl.semaphore_signal(
            barrier, 1, device_id={"tp": lax.rem(tp + shift, n_tp)}, device_id_type=pl.DeviceIdType.MESH
        )
    pl.semaphore_wait(barrier, n - 1 + n_tp - 1)


def flip(index, bit):
    if bit == 1:
        return index + 1 - 2 * (index % 2)
    return index + 2 - 4 * ((index // 2) % 2)


def tail_kernel(
    n,
    n_tp,
    n1,
    lg,
    ag,
    ctx,
    w,
    hidden,
    r_one,
    gain_all,
    bias,
    small,
    o_rows,
    weighted,
    spart,
    mid,
    ag_hbm,
    qkv_out,
    o_out,
    in_out,
    out_out,
    gain_out,
    bias_out,
    small_out,
    h_cols,
    res_cols,
    ag_cols,
    in_sem,
    ring_recv,
    ring_send,
    part_own,
    part_send,
    part_recv,
    y_send,
    y_recv,
    mean_send,
    mean_recv,
    vec_send,
    vec_recv,
    small_recv,
    small_sum,
    gain_send,
    gain_recv,
    out_send,
    out_recv,
    oy_send,
    oy_recv,
    ring_ss,
    ring_rs,
    tp_ss,
    tp_rs,
    vec_ss,
    vec_rs,
    small_ss,
    small_rs,
    gain_ss,
    gain_rs,
):
    ep = lax.axis_index("ep")
    tp = lax.axis_index("tp")
    tokens, lw = ctx.shape
    columns = pl.ds(pl.multiple_of(tp * lw, lw), lw)
    col_in = [
        pltpu.make_async_copy(hidden.at[:, columns], h_cols, in_sem.at[0]),
        pltpu.make_async_copy(mid.at[:, columns], res_cols, in_sem.at[1]),
        pltpu.make_async_copy(ag_hbm.at[:, columns], ag_cols, in_sem.at[2]),
    ]
    for copy in col_in:
        copy.start()
    gain = gain_all[:, columns]
    rows = qkv_out.shape[1]
    width = rows * n
    p = ring_place(ep, n)
    nxt = ring_member(lax.rem(p + 1, n), n)
    prv = ring_member(lax.rem(p + n - 1, n), n)
    core_peer, y_peer = flip(tp, 1), flip(tp, 2)
    greet(n, n_tp, ep, tp)

    def small_copy(shift, turn, way):
        to, came = lax.rem(ep + shift, n), lax.rem(ep + n - shift, n)
        if turn == 0:
            src, dst, arrived = small.at[to], small_recv.at[ep], small_recv.at[came]
        else:
            src, dst, arrived = small_sum, small_out.at[ep], small_out.at[came]
        sems = small_ss.at[turn, shift], small_rs.at[turn, shift]
        if way == 0:
            return remote(src, dst, *sems, "ep", to)
        return remote(src, arrived, *sems, "ep", came)

    def block_of(ring, step):
        if ring < 2:
            return ring_member(lax.rem(p + 2 * n - 1 - step, n), n)
        return ring_member(lax.rem(p + 1 + step, n), n)

    def term(ring, owner):
        if ring == 1:
            return block_dot(ag, owner, rows, ctx[...])
        k = {0: 0, 2: 1, 3: 2}[ring]
        return block_dot(n1, owner, rows, lg[:, k * lw : (k + 1) * lw])

    def ring_copy(ring, step, slot):
        return remote(
            ring_send.at[ring, slot],
            ring_recv.at[ring, step],
            ring_ss.at[ring, slot],
            ring_rs.at[ring, step],
            "ep",
            nxt if ring < 2 else prv,
        )

    def ring_step(step, first):
        for ring in range(4):
            slot = lax.rem(step, 2)
            mine = term(ring, block_of(ring, step))
            ring_copy(ring, step - 1, slot).wait_recv()
            if not first:
                ring_copy(ring, step - 2, slot).wait_send()
            ring_send[ring, slot] = (mine + ring_recv[ring, step - 1].astype(F32)).astype(BF)
            ring_copy(ring, step, slot).start()

    for ring in range(4):
        ring_send[ring, 0] = term(ring, block_of(ring, 0)).astype(BF)
        ring_copy(ring, 0, 0).start()

    def part_block(column, store):
        for m in range(0, tokens, 128):
            total = None
            for k in range(3):
                d = lax.dot_general(
                    lg[m : m + 128, k * lw : (k + 1) * lw],
                    w[k, pl.ds(pl.multiple_of(column * lw, lw), lw), :],
                    (((1,), (1,)), ((), ())),
                    preferred_element_type=F32,
                )
                total = d if total is None else total + d
            store(m, total)

    def tp_copy(i, src, dst, peer):
        return remote(src, dst, tp_ss.at[i], tp_rs.at[i], "tp", peer)

    first = [tp_copy(i, part_send.at[i], part_recv.at[i], core_peer) for i in range(2)]
    for i in range(2):

        def put(m, total, i=i):
            part_send[i, m : m + 128, :] = total.astype(BF)

        part_block((core_peer % 2) + 2 * i, put)
        first[i].start()

    ring_step(1, True)

    small_recv[ep] = small[ep]
    for shift in range(1, n):
        small_copy(shift, 0, 0).start()
    for copy in col_in:
        copy.wait()

    def put_own(m, total):
        part_own[m : m + 128, :] = total

    other = (tp // 2) * -1 + 1
    part_block((tp % 2) + 2 * other, put_own)
    for i in range(2):
        first[i].wait()
    y_send[...] = (part_own[...] + part_recv[other].astype(F32)).astype(BF)
    second = tp_copy(2, y_send, y_recv, y_peer)
    second.start()

    ring_step(2, False)

    part_block(tp, put_own)
    second.wait()
    for m in range(0, tokens, 128):
        at = slice(m, m + 128)
        grad = (
            part_own[at, :]
            + part_recv[tp // 2, at, :].astype(F32)
            + y_recv[at, :].astype(F32)
        )
        part_own[at, :] = grad
        hid = h_cols[at, :].astype(F32)
        mean = jnp.sum(grad * gain * hid, axis=1, keepdims=True)
        mean_send[0, at, :] = jnp.broadcast_to(mean, (128, 128))
        col = jnp.sum(grad * hid * r_one[at, :], axis=0, keepdims=True)
        if m == 0:
            vec_send[:, :lw] = col
        else:
            vec_send[:, :lw] += col
    third = tp_copy(3, mean_send.at[0], mean_recv.at[0], core_peer)
    third.start()
    vec_send[:, lw:] = bias[...]
    vec_recv[ep] = vec_send[...]

    def vec_copy(shift, way):
        to = lax.rem(ep + shift, n)
        came = lax.rem(ep + n - shift, n)
        if way == "out":
            return remote(vec_send, vec_recv.at[ep], vec_ss.at[shift], vec_rs.at[shift], "ep", to)
        return remote(vec_send, vec_recv.at[came], vec_ss.at[shift], vec_rs.at[shift], "ep", came)

    for shift in range(1, n):
        vec_copy(shift, "out").start()

    ring_step(3, False)

    third.wait()
    mean_send[1] = mean_send[0] + mean_recv[0]
    fourth = tp_copy(4, mean_send.at[1], mean_recv.at[1], y_peer)
    fourth.start()

    def out_block(column):
        at = pl.ds(pl.multiple_of(column * lw, lw), lw)
        return spart[:, at].astype(F32) + jnp.dot(
            weighted[...], o_rows[:, at], preferred_element_type=F32
        )

    fifth = [tp_copy(5 + i, out_send.at[i], out_recv.at[i], core_peer) for i in range(2)]
    for i in range(2):
        out_send[i] = out_block((core_peer % 2) + 2 * i).astype(BF)
        fifth[i].start()

    ring_step(4, False)

    for shift in range(1, n):
        small_copy(shift, 0, 1).wait()
    total = small_recv[0].astype(F32)
    for e in range(1, n):
        total = total + small_recv[e].astype(F32)
    small_sum[...] = total
    small_out[ep] = total
    for shift in range(1, n):
        small_copy(shift, 1, 0).start()
    for copy in fifth:
        copy.wait()
    oy_send[...] = (out_block((tp % 2) + 2 * other) + out_recv[other].astype(F32)).astype(BF)
    sixth = tp_copy(7, oy_send, oy_recv, y_peer)
    sixth.start()
    fourth.wait()
    for m in range(0, tokens, 128):
        at = slice(m, m + 128)
        mean = (mean_send[1, at, :1] + mean_recv[1, at, :1]) * (1.0 / width)
        r = r_one[at, :]
        in_out[at, :] = (
            ag_cols[at, :].astype(F32)
            + r * part_own[at, :] * gain
            - h_cols[at, :].astype(F32) * (r * r * r) * mean
        ).astype(BF)
    for shift in range(1, n):
        vec_copy(shift, "in").wait()
    total = vec_recv[0]
    for e in range(1, n):
        total = total + vec_recv[e]
    bias_out[...] = total[:, lw:]
    gain_send[...] = total[:, :lw]
    gain_recv[tp] = total[:, :lw]

    def gain_copy(shift, way):
        to = lax.rem(tp + shift, n_tp)
        came = lax.rem(tp + n_tp - shift, n_tp)
        if way == "out":
            return remote(gain_send, gain_recv.at[tp], gain_ss.at[shift], gain_rs.at[shift], "tp", to)
        return remote(gain_send, gain_recv.at[came], gain_ss.at[shift], gain_rs.at[shift], "tp", came)

    for shift in range(1, n_tp):
        gain_copy(shift, "out").start()

    ring_step(5, False)

    own = out_block(tp) + res_cols[...] + out_recv[tp // 2].astype(F32)
    sixth.wait()
    out_out[...] = (own + oy_recv[...].astype(F32)).astype(BF)

    @pl.loop(6, n - 1)
    def _(step):
        ring_step(step, False)

    for shift in range(1, n):
        small_copy(shift, 1, 1).wait()
    for shift in range(1, n_tp):
        gain_copy(shift, "in").wait()
    for j in range(n_tp):
        gain_out[:, j * lw : (j + 1) * lw] = gain_recv[j]

    for ring in range(4):
        mine = term(ring, ep)
        ring_copy(ring, n - 2, 0).wait_recv()
        done = mine + ring_recv[ring, n - 2].astype(F32)
        if ring == 1:
            o_out[...] = done
        else:
            qkv_out[{0: 0, 2: 1, 3: 2}[ring]] = done
    for ring in range(4):
        for step in (n - 3, n - 2):
            ring_copy(ring, step, step % 2).wait_send()


def tail(n, n_tp, n1, lg, ag, ctx, w, hidden, r_one, gain, bias, small, o_rows, weighted, spart, mid):
    tokens, width = n1.shape
    lw = ctx.shape[1]
    rows = width // n
    ag_hbm = ag
    if rows % 128:
        n1, ag = n1.T, ag.T
    wide = small.shape[1]
    vmem = pl.BlockSpec(memory_space=pltpu.VMEM)
    hbm = pl.BlockSpec(memory_space=pl.ANY)
    dma = pltpu.SemaphoreType.DMA
    return pl.pallas_call(
        functools.partial(tail_kernel, n, n_tp),
        out_shape=(
            jax.ShapeDtypeStruct((3, rows, lw), F32),
            jax.ShapeDtypeStruct((rows, lw), F32),
            jax.ShapeDtypeStruct((tokens, lw), BF),
            jax.ShapeDtypeStruct((tokens, lw), BF),
            jax.ShapeDtypeStruct((1, width), F32),
            jax.ShapeDtypeStruct((1, 3 * lw), F32),
            jax.ShapeDtypeStruct((n, wide, rows), F32),
        ),
        in_specs=[vmem] * 5 + [hbm] + [vmem] * 7 + [hbm] * 2,
        out_specs=[vmem] * 7,
        scratch_shapes=[
            pltpu.VMEM((tokens, lw), BF),
            pltpu.VMEM((tokens, lw), F32),
            pltpu.VMEM((tokens, lw), BF),
            dma((3,)),
            pltpu.VMEM((4, n - 1, rows, lw), BF),
            pltpu.VMEM((4, 2, rows, lw), BF),
            pltpu.VMEM((tokens, lw), F32),
            pltpu.VMEM((2, tokens, lw), BF),
            pltpu.VMEM((2, tokens, lw), BF),
            pltpu.VMEM((tokens, lw), BF),
            pltpu.VMEM((tokens, lw), BF),
            pltpu.VMEM((2, tokens, 128), F32),
            pltpu.VMEM((2, tokens, 128), F32),
            pltpu.VMEM((1, 4 * lw), F32),
            pltpu.VMEM((n, 1, 4 * lw), F32),
            pltpu.VMEM((n, wide, rows), BF),
            pltpu.VMEM((wide, rows), F32),
            pltpu.VMEM((1, lw), F32),
            pltpu.VMEM((n_tp, 1, lw), F32),
            pltpu.VMEM((2, tokens, lw), BF),
            pltpu.VMEM((2, tokens, lw), BF),
            pltpu.VMEM((tokens, lw), BF),
            pltpu.VMEM((tokens, lw), BF),
            dma((4, 2)),
            dma((4, n - 1)),
            dma((8,)),
            dma((8,)),
            dma((n,)),
            dma((n,)),
            dma((2, n)),
            dma((2, n)),
            dma((n_tp,)),
            dma((n_tp,)),
        ],
        compiler_params=pltpu.CompilerParams(
            collective_id=0, has_side_effects=True, vmem_limit_bytes=60 * 2**20
        ),
        cost_estimate=pl.CostEstimate(
            flops=2 * tokens * width * 7 * lw, bytes_accessed=30 * 2**20, transcendentals=0
        ),
    )(n1, lg, ag, ctx, w, hidden, r_one, gain, bias, small, o_rows, weighted, spart, mid, ag_hbm)

def cols_of(ref, owner, rows):
    at = pl.ds(pl.multiple_of(owner * rows, rows), rows)
    return ref[:, at] if rows % 128 == 0 else ref[at, :]


def block_dot(ref, owner, rows, other):
    dims = (((0,), (0,)), ((), ())) if rows % 128 == 0 else (((1,), (0,)), ((), ()))
    return lax.dot_general(cols_of(ref, owner, rows), other, dims, preferred_element_type=F32)


def middle_kernel(
    n,
    n_tp,
    shape,
    x_hbm,
    u_hbm,
    gu_a,
    gu_c,
    gu_b,
    gu_own,
    dn_a,
    dn_c,
    dn_b,
    dn_own,
    gates,
    nt,
    pg,
    og,
    sh,
    back,
    g_back,
    o_hbm,
    dw_recv,
    dw_own,
    dw_y,
    gu_out,
    dn_out,
    zero,
    w,
    xb,
    ub,
    rgb,
    eb,
    rbs,
    gbs,
    ring_recv,
    ring_send,
    w_sem,
    x_sem,
    u_sem,
    out_sem,
    ring_ss,
    ring_rs,
    free,
    back_ss,
    back_rs,
    gate_ss,
    gate_rs,
    dw_ss,
    dw_rs,
    dw_sem,
):
    ep = lax.axis_index("ep")
    tp = lax.axis_index("tp")
    core_peer, y_peer = flip(tp, 1), flip(tp, 2)
    gr = ub.shape[1]
    capp = shape[0]
    zero[...] = jnp.zeros_like(zero)
    width = u_hbm.shape[1]
    units = w.shape[1]
    quarter = units // 4
    groups = x_hbm.shape[0] // gr
    per = n // groups
    rows = gu_out.shape[1]
    half = ring_recv.shape[3]
    p = ring_place(ep, n)
    nxt = ring_member(lax.rem(p + 1, n), n)
    prv = ring_member(lax.rem(p + n - 1, n), n)

    w_in = [
        pltpu.make_async_copy(ref, w.at[:2, i * quarter : (i + 1) * quarter, :], w_sem.at[i])
        for i, ref in enumerate((gu_a, gu_c, gu_b, gu_own))
    ] + [
        pltpu.make_async_copy(ref, w.at[2, i * quarter : (i + 1) * quarter, :], w_sem.at[4 + i])
        for i, ref in enumerate((dn_a, dn_c, dn_b, dn_own))
    ]
    for copy in w_in:
        copy.start()

    x_in = pltpu.make_async_copy(x_hbm, xb, x_sem)

    def u_copy(g):
        at = pl.ds(pl.multiple_of(g * gr, gr), gr)
        slot = lax.rem(g, 2)
        return pltpu.make_async_copy(u_hbm.at[at, :], ub.at[slot], u_sem.at[slot])

    x_in.start()
    u_copy(0).start()
    greet(n, n_tp, ep, tp)

    edges = [0]
    for ring in range(4):
        edges.append(edges[-1] + (3 * units // 128 + 3 - ring) // 4 * 128)
    wide_of = [edges[i + 1] - edges[i] for i in range(4)]

    def block_of(ring, step):
        if ring < 2:
            return ring_member(lax.rem(p + 2 * n - 1 - step, n), n)
        return ring_member(lax.rem(p + 1 + step, n), n)

    def term(ring, owner):
        lo, hi = edges[ring], edges[ring + 1]
        parts = []
        if lo < 2 * units:
            parts.append(block_dot(nt, owner, rows, pg[:, lo : min(hi, 2 * units)]))
        if hi > 2 * units:
            parts.append(block_dot(og, owner, rows, sh[:, max(lo - 2 * units, 0) : hi - 2 * units]))
        return parts[0] if len(parts) == 1 else jnp.concatenate(parts, axis=1)

    def ring_copy(ring, slot):
        return remote(
            ring_send.at[ring, slot, :, : wide_of[ring]],
            ring_recv.at[ring, slot, :, : wide_of[ring]],
            ring_ss.at[ring, slot],
            ring_rs.at[ring, slot],
            "ep",
            nxt if ring < 2 else prv,
        )

    order = (0, 2, 1, 3)

    def ring_step(step):
        slot, last = lax.rem(step, 2), lax.rem(step + 1, 2)
        for ring in order:
            size = wide_of[ring]
            mine = term(ring, block_of(ring, step))
            ring_copy(ring, last).wait_recv()

            @pl.when(step >= 2)
            def _():
                ring_copy(ring, slot).wait_send()

            ring_send[ring, slot, :, :size] = (
                mine + ring_recv[ring, last, :, :size].astype(F32)
            ).astype(BF)

            @pl.when(step <= n - 3)
            def _():
                pl.semaphore_signal(
                    free.at[ring],
                    1,
                    device_id={"ep": prv if ring < 2 else nxt},
                    device_id_type=pl.DeviceIdType.MESH,
                )

            @pl.when(step >= 2)
            def _():
                pl.semaphore_wait(free.at[ring], 1)

            ring_copy(ring, slot).start()

    for ring in order:
        ring_send[ring, 0, :, : wide_of[ring]] = term(ring, block_of(ring, 0)).astype(BF)
        ring_copy(ring, 0).start()

    for copy in w_in:
        copy.wait()
    x_in.wait()

    nt_dims, first_dims = (((1,), (1,)), ((), ())), (((0,), (0,)), ((), ()))

    def saved(g):
        at = pl.ds(pl.multiple_of(g * gr, gr), gr)
        slot = lax.rem(g, 2)
        return pltpu.make_async_copy(ub.at[slot], o_hbm.at[at, :], out_sem.at[slot])

    def back_copies(r):
        return block_copies(r, rbs, back, back_ss, back_rs, ep, tp, n, shape, zero, True)

    kept_copy = pltpu.make_async_copy(rbs.at[:capp, :], back.at[:capp, :], back_ss.at[0, 0])

    def gate_copy(r):
        return remote(
            gbs.at[r], g_back.at[r], gate_ss.at[r], gate_rs.at[r], "ep", lax.rem(ep + n - r, n)
        )

    g_kept = pltpu.make_async_copy(gbs.at[0], g_back.at[0], gate_ss.at[0])
    gbs[...] = jnp.zeros_like(gbs)

    @pl.loop(0, groups)
    def _(g):
        slot = lax.rem(g, 2)
        mine = pl.ds(pl.multiple_of(g * gr, gr), gr)
        u_copy(g).wait()

        @pl.when(g >= 1)
        def _():
            saved(g - 1).wait()

        @pl.when(g + 1 < groups)
        def _():
            u_copy(g + 1).start()

        gate = jnp.concatenate([gate_column(gates, g * per + i, capp) for i in range(per)], axis=0)
        rgb[mine, :] = (gate * ub[slot].astype(F32)).astype(BF)

        def hidden(at):
            x = xb[mine, :]
            g_pre = lax.dot_general(x, w[0, at, :], nt_dims, preferred_element_type=F32)
            u_pre = lax.dot_general(x, w[1, at, :], nt_dims, preferred_element_type=F32)
            grad = lax.dot_general(rgb[mine, :], w[2, at, :], nt_dims, preferred_element_type=F32)
            sig = jax.nn.sigmoid(g_pre)
            eb[2, mine, at] = (g_pre * sig * u_pre).astype(BF)
            eb[0, mine, at] = (grad * u_pre * sig * (1.0 + g_pre * (1.0 - sig))).astype(BF)
            eb[1, mine, at] = (grad * g_pre * sig).astype(BF)

        @pl.loop(0, units // 256)
        def _(c):
            hidden(pl.ds(pl.multiple_of(c * 256, 256), 256))

        if units % 256:
            hidden(pl.ds(units // 256 * 256, units % 256))

        def columns(c, total):
            at = pl.ds(pl.multiple_of(c * 256, 256), 256)
            out = jnp.dot(eb[2, mine, :], w[2, :, at], preferred_element_type=F32)
            grad = jnp.dot(eb[0, mine, :], w[0, :, at], preferred_element_type=F32) + jnp.dot(
                eb[1, mine, :], w[1, :, at], preferred_element_type=F32
            )
            rbs[mine, at] = grad.astype(BF)
            total = total + jnp.sum(out * ub[slot, :, at].astype(F32), axis=1, keepdims=True)
            ub[slot, :, at] = out.astype(BF)
            return total

        total = lax.fori_loop(0, width // 256, columns, jnp.zeros((gr, 1), F32))
        hi = total.astype(BF).astype(F32)
        lane = lax.broadcasted_iota(jnp.int32, (gr, 128), 1)
        terms = jnp.where(lane == 0, hi, jnp.where(lane == 1, total - hi, 0.0)).astype(BF)
        pick = (
            lax.broadcasted_iota(jnp.int32, (16, 128), 0) == lax.broadcasted_iota(jnp.int32, (16, 128), 1)
        ).astype(F32).astype(BF)
        turned = lax.dot_general(pick, terms, nt_dims, preferred_element_type=F32).astype(BF)
        for i in range(per):
            gbs[g * per + i, :, :capp] = turned[:, i * capp : (i + 1) * capp]
        saved(g).start()
        for i in range(per):
            r = g * per + i
            if i == 0:

                @pl.when(g == 0)
                def _():
                    kept_copy.start()
                    g_kept.start()

                @pl.when(g > 0)
                def _():
                    each(back_copies(r), "start")
                    gate_copy(r).start()
            else:
                each(back_copies(r), "start")
                gate_copy(r).start()

        @pl.when(lax.rem(g, 2) == 1)
        def _():
            ring_step((g + 1) // 2)

    def weight_rows(at):
        for k in range(3):
            for c in range(0, width, 512):
                w[k, at, c : c + 512] = lax.dot_general(
                    eb[k, :, at],
                    (rgb if k == 2 else xb)[:, c : c + 512],
                    first_dims,
                    preferred_element_type=F32,
                ).astype(BF)

    @pl.loop(0, units // 256)
    def _(c):
        weight_rows(pl.ds(pl.multiple_of(c * 256, 256), 256))

    if units % 256:
        weight_rows(pl.ds(units // 256 * 256, units % 256))

    dw_core = remote(
        w.at[:, : 2 * quarter, :], dw_recv, dw_ss.at[0], dw_rs.at[0], "tp", core_peer
    )
    dw_core.start()
    ring_step(groups // 2 + 1)
    dw_core.wait()
    dw_in = pltpu.make_async_copy(dw_recv, w.at[:, : 2 * quarter, :], dw_sem.at[0])
    dw_in.start()
    dw_in.wait()
    for k in range(3):

        @pl.loop(0, quarter // 32)
        def _(c, k=k):
            far = pl.ds(pl.multiple_of(2 * quarter + c * 32, 32), 32)
            came = pl.ds(pl.multiple_of(quarter + c * 32, 32), 32)
            w[k, far, :] = (w[k, far, :].astype(F32) + w[k, came, :].astype(F32)).astype(BF)

    dw_far = remote(
        w.at[:, 2 * quarter : 3 * quarter, :], dw_y, dw_ss.at[1], dw_rs.at[1], "tp", y_peer
    )
    dw_far.start()
    for k in range(3):

        @pl.loop(0, quarter // 32)
        def _(c, k=k):
            far = pl.ds(pl.multiple_of(3 * quarter + c * 32, 32), 32)
            came = pl.ds(pl.multiple_of(c * 32, 32), 32)
            w[k, far, :] = (w[k, far, :].astype(F32) + w[k, came, :].astype(F32)).astype(BF)

    dw_keep = pltpu.make_async_copy(w.at[:, 3 * quarter :, :], dw_own, dw_sem.at[1])
    dw_keep.start()

    @pl.loop(groups // 2 + 2, n - 1)
    def _(step):
        ring_step(step)

    for ring in order:
        mine = term(ring, ep)
        ring_copy(ring, n % 2).wait_recv()
        done = mine + ring_recv[ring, n % 2, :, : wide_of[ring]].astype(F32)
        lo, hi = edges[ring], edges[ring + 1]
        for k, out in enumerate((gu_out.at[0], gu_out.at[1], dn_out)):
            a, b = max(lo, k * units), min(hi, (k + 1) * units)
            if a < b:
                out[:, a - k * units : b - k * units] = done[:, a - lo : b - lo].astype(BF)
    for ring in range(4):
        for slot in range(2):
            ring_copy(ring, slot).wait_send()
    g_kept.wait()
    kept_copy.wait()
    saved(groups - 1).wait()
    dw_keep.wait()
    dw_far.wait()

    @pl.loop(1, n)
    def _(r):
        each(back_copies(r), "wait")
        gate_copy(r).wait()


def routed_expert(n, n_tp, shape, x, u, weights, gates, nt, pg, og, sh):
    total, width = x.shape
    units = 4 * weights[-1].shape[0]
    gr = total // 4
    rows = width // n
    half = (3 * units // 128 + 3) // 4 * 128
    vmem = pl.BlockSpec(memory_space=pltpu.VMEM)
    hbm = pl.BlockSpec(memory_space=pl.ANY)
    dma = pltpu.SemaphoreType.DMA
    if rows % 128:
        nt, og = nt.T, og.T
    return pl.pallas_call(
        functools.partial(middle_kernel, n, n_tp, shape),
        out_shape=(
            jax.ShapeDtypeStruct((total, width), BF),
            jax.ShapeDtypeStruct((n, 16, 128), BF),
            jax.ShapeDtypeStruct((total, width), BF),
            jax.ShapeDtypeStruct((3, units // 2, width), BF),
            jax.ShapeDtypeStruct((3, units // 4, width), BF),
            jax.ShapeDtypeStruct((3, units // 4, width), BF),
            jax.ShapeDtypeStruct((2, rows, units), BF),
            jax.ShapeDtypeStruct((rows, units), BF),
        ),
        in_specs=[hbm] * 10 + [vmem] * 5,
        out_specs=[hbm] * 6 + [vmem] * 2,
        scratch_shapes=[
            pltpu.VMEM((max(shape[0] - shape[1], 16), width), BF),
            pltpu.VMEM((3, units, width), BF),
            pltpu.VMEM((total, width), BF),
            pltpu.VMEM((2, gr, width), BF),
            pltpu.VMEM((total, width), BF),
            pltpu.VMEM((3, total, units), BF),
            pltpu.VMEM((total, width), BF),
            pltpu.VMEM((n, 16, 128), BF),
            pltpu.VMEM((4, 2, rows, half), BF),
            pltpu.VMEM((4, 2, rows, half), BF),
            dma((8,)),
            dma,
            dma((2,)),
            dma((2,)),
            dma((4, 2)),
            dma((4, 2)),
            pltpu.SemaphoreType.REGULAR((4,)),
            dma((3, n)),
            dma((3, n)),
            dma((n,)),
            dma((n,)),
            dma((2,)),
            dma((2,)),
            dma((2,)),
        ],
        compiler_params=pltpu.CompilerParams(
            collective_id=1, has_side_effects=True, vmem_limit_bytes=63 * 2**20
        ),
        cost_estimate=pl.CostEstimate(
            flops=2 * total * width * 6 * units, bytes_accessed=40 * 2**20, transcendentals=0
        ),
    )(x, u, *weights, gates, nt, pg, og, sh)


def tp_total(
    project, between, tp, core_send, core_recv, y_send, y_recv, summed,
    core_ss, core_rs, y_ss, y_rs, g_ss, g_rs,
):
    core_peer, y_peer = flip(tp, 1), flip(tp, 2)
    pieces, size = core_send.shape[0], core_send.shape[2]
    half = pieces * size

    def core_copy(i):
        return remote(core_send.at[i], core_recv.at[i], core_ss.at[i], core_rs.at[i], "tp", core_peer)

    def y_copy(i):
        return remote(y_send.at[i], y_recv.at[i], y_ss.at[i], y_rs.at[i], "tp", y_peer)

    def gather_copy(i, slot):
        return remote(summed.at[slot, i], summed.at[slot, i], g_ss.at[i], g_rs.at[i], "tp", core_peer)

    me, other = tp % 2, core_peer % 2
    for i in range(pieces):
        core_send[i] = project(other * half, i, size).astype(BF)
        core_copy(i).start()
        own = project(me * half, i, size)
        core_copy(i).wait_recv()
        y_send[i] = (own + core_recv[i].astype(F32)).astype(BF)
        y_copy(i).start()
    between()
    for i in range(pieces):
        y_copy(i).wait_recv()
        summed[me, i] = (y_send[i].astype(F32) + y_recv[i].astype(F32)).astype(BF)
        gather_copy(i, me).start()
    for i in range(pieces):
        gather_copy(i, other).wait_recv()
    for i in range(pieces):
        core_copy(i).wait_send()
        y_copy(i).wait_send()
        gather_copy(i, me).wait_send()


def blocks_at_once(n, capp):
    per = 1
    while 2 * per * capp <= 128 and n % (2 * per) == 0:
        per *= 2
    return per


def has_more(tp, source, expert, n_tp, extra):
    return lax.rem(tp + 64 * n_tp - source - expert, n_tp) < extra


def block_copies(r, src, dst, ss, rs, ep, tp, n, shape, zero, home):
    capp, base, extra, n_tp = shape
    on, back = lax.rem(ep + r, n), lax.rem(ep + n - r, n)
    to, come = (back, on) if home else (on, back)
    at = pl.ds(pl.multiple_of(r * capp, 16), base)
    out = [(None, None, remote(src.at[at, :], dst.at[at, :], ss.at[0, r], rs.at[0, r], "ep", to))]
    if base < capp:
        at = pl.ds(pl.multiple_of(r * capp + base, 16), capp - base)
        sends, gets = has_more(tp, ep, to, n_tp, extra), has_more(tp, ep, come, n_tp, extra)
        out.append((sends, gets, remote(src.at[at, :], dst.at[at, :], ss.at[1, r], rs.at[1, r], "ep", to)))
        fill = jnp.logical_not(gets)
        out.append((fill, None, pltpu.make_async_copy(zero, dst.at[at, :], ss.at[2, r])))
    return out


def each(copies, verb):
    for sends, gets, copy in copies:
        if sends is None:
            getattr(copy, verb)()
        elif gets is None or verb == "start":
            pl.when(sends)(getattr(copy, verb))
        else:
            pl.when(sends)(copy.wait_send)
            pl.when(gets)(copy.wait_recv)


SEND_ORDER = (4, 5, 6, 7, 2, 3, 1, 0)


def send_order(i, n, ep):
    if n != len(SEND_ORDER):
        return (i + 1) % n
    to = ep
    for bit in (1, 2, 4):
        if SEND_ORDER[i] & bit:
            to = to + bit - 2 * bit * ((to // bit) % 2)
    return lax.rem(to + n - ep, n)


def gate_column(tiles, r, capp):
    ones = jnp.ones((16, 128), BF)
    return lax.dot_general(
        tiles[r, :, :capp], ones, (((0,), (0,)), ((), ())), preferred_element_type=F32
    )[:, :1]


def front_kernel(
    n,
    n_tp,
    shape,
    hidden,
    gain1,
    gain2,
    w,
    bias,
    cosine,
    sine,
    prefix,
    ow,
    place,
    cot,
    gu_own,
    dn_own,
    pairs,
    up_rows,
    gu_a,
    dn_a,
    dn_b,
    n1,
    qkv,
    ctx,
    mid,
    nt,
    factor_one,
    split,
    pair_in,
    pair_out,
    pair_si,
    pair_so,
    zero,
    up_sent,
    core_send,
    core_recv,
    y_send,
    y_recv,
    summed,
    up_ss,
    up_rs,
    w_ss,
    w_rs,
    core_ss,
    core_rs,
    y_ss,
    y_rs,
    g_ss,
    g_rs,
):
    ep = lax.axis_index("ep")
    tp = lax.axis_index("tp")
    tokens, width = hidden.shape
    lw = ctx.shape[1]
    heads = lw // HEAD_DIM
    core_peer, y_peer = flip(tp, 1), flip(tp, 2)
    greet(n, n_tp, ep, tp)

    capp = shape[0]
    zero[...] = jnp.zeros_like(zero)

    def up_copies(r):
        return block_copies(r, up_sent, up_rows, up_ss, up_rs, ep, tp, n, shape, zero, False)

    kept = pltpu.make_async_copy(up_sent.at[:capp, :], up_rows.at[:capp, :], up_ss.at[0, 0])
    per = blocks_at_once(n, capp)
    size = per * capp

    for i in range(n // per):
        b = send_order(i, n, ep) if per == 1 else i
        at = pl.ds(pl.multiple_of(b * size, size), size)
        up_sent[at, :] = jnp.dot(place[at, :], cot[...], preferred_element_type=F32).astype(BF)
        for j in range(per):
            if i == (n - 1 if per == 1 else 0) and j == 0:
                kept.start()
            else:
                each(up_copies(b * per + j), "start")

    w_copies = [
        remote(dn_own, dn_b, w_ss.at[0], w_rs.at[0], "tp", y_peer),
        remote(dn_own, dn_a, w_ss.at[1], w_rs.at[1], "tp", core_peer),
        remote(gu_own, gu_a, w_ss.at[2], w_rs.at[2], "tp", core_peer),
    ]
    for copy in w_copies:
        copy.start()

    chunk = pair_in.shape[1]
    chunks = pairs.shape[0] // chunk

    def pair_load(i):
        at, slot = pl.ds(pl.multiple_of(i * chunk, chunk), chunk), lax.rem(i, 2)
        return pltpu.make_async_copy(pairs.at[at], pair_in.at[slot], pair_si.at[slot])

    def pair_store(i):
        at, slot = pl.ds(pl.multiple_of(i * chunk, chunk), chunk), lax.rem(i, 2)
        return pltpu.make_async_copy(pair_out.at[slot], split.at[:, at, :], pair_so.at[slot])

    def set_apart(first, last):
        @pl.loop(first, last)
        def _(i):
            slot = lax.rem(i, 2)

            @pl.when(i + 1 < chunks)
            def _():
                pair_load(i + 1).start()

            pair_load(i).wait()

            @pl.when(i >= 2)
            def _():
                pair_store(i - 2).wait()

            pair_out[slot, 0] = pair_in[slot, :, 0, :]
            pair_out[slot, 1] = pair_in[slot, :, 1, :]
            pair_store(i).start()

    pair_load(0).start()

    @pl.loop(0, tokens // 64)
    def _(m):
        at = pl.ds(pl.multiple_of(m * 64, 64), 64)
        h = hidden[at, :].astype(F32)
        factor = lax.rsqrt(jnp.sum(h * h, axis=1, keepdims=True) * (1.0 / width) + EPSILON)
        factor_one[at, :] = factor
        n1[at, :] = (h * factor * gain1[...]).astype(BF)

    for k in range(3):

        @pl.loop(0, lw // 256)
        def _(c, k=k):
            at = pl.ds(pl.multiple_of(c * 256, 256), 256)
            x = jnp.dot(n1[...], w[k, :, at], preferred_element_type=F32) + bias[k : k + 1, at]
            if k < 2:
                x = jnp.concatenate(
                    [
                        x[:, i * HEAD_DIM : (i + 1) * HEAD_DIM] * cosine[...]
                        + pltpu.roll(x[:, i * HEAD_DIM : (i + 1) * HEAD_DIM], HEAD_DIM // 2, 1) * sine[...]
                        for i in range(256 // HEAD_DIM)
                    ],
                    axis=1,
                )
            qkv[k, :, at] = x.astype(BF)

    @pl.loop(0, tokens // 128)
    def _(m):
        at = pl.ds(pl.multiple_of(m * 128, 128), 128)
        row = lax.broadcasted_iota(jnp.int32, (128, tokens), 0) + m * 128
        col = lax.broadcasted_iota(jnp.int32, (128, tokens), 1)
        visible = (col <= row) | (col < prefix[...])
        for i in range(heads):
            lanes = slice(i * HEAD_DIM, (i + 1) * HEAD_DIM)
            s = lax.dot_general(
                qkv[0, at, lanes], qkv[1, :, lanes], (((1,), (1,)), ((), ())), preferred_element_type=F32
            )
            s = jnp.where(visible, s * HEAD_DIM ** (-0.5), -1e30)
            e = jnp.exp(s - jnp.max(s, axis=1, keepdims=True))
            e = e * (1.0 / jnp.sum(e, axis=1, keepdims=True))
            ctx[at, lanes] = jnp.dot(
                e.astype(BF), qkv[2, :, lanes], preferred_element_type=F32
            ).astype(BF)

    pieces, size = core_send.shape[0], core_send.shape[2]
    half = pieces * size

    def project(base, i, size):
        at = pl.ds(pl.multiple_of(base + i * size, size), size)
        return lax.dot_general(
            ctx[...], ow[at, :], (((1,), (1,)), ((), ())), preferred_element_type=F32
        )

    tp_total(
        project, lambda: set_apart(0, chunks * 11 // 16), tp, core_send, core_recv, y_send, y_recv, summed,
        core_ss, core_rs, y_ss, y_rs, g_ss, g_rs,
    )

    @pl.loop(0, tokens // 32)
    def _(m):
        at = pl.ds(pl.multiple_of(m * 32, 32), 32)
        total = jnp.zeros((32, 1), F32)
        for j in range(2):
            for i in range(pieces):
                lanes = slice(j * half + i * size, j * half + (i + 1) * size)
                x = hidden[at, lanes].astype(F32) + summed[j, i, at, :].astype(F32)
                mid[at, lanes] = x
                total = total + jnp.sum(x * x, axis=1, keepdims=True)
        factor = lax.rsqrt(total * (1.0 / width) + EPSILON)
        nt[at, :] = (mid[at, :] * factor * gain2[...]).astype(BF)

    set_apart(chunks * 11 // 16, chunks)
    pair_store(chunks - 2).wait()
    pair_store(chunks - 1).wait()
    for copy in w_copies:
        copy.wait()
    kept.wait()
    for r in range(1, n):
        each(up_copies(r), "wait")


def front(n, n_tp, shape, hidden, gain1, gain2, w, bias, cosine, sine, prefix, ow, place, cot, gu_own, dn_own, pairs):
    tokens, width = hidden.shape
    lw = ow.shape[1]
    quarter = dn_own.shape[0]
    vmem = pl.BlockSpec(memory_space=pltpu.VMEM)
    hbm = pl.BlockSpec(memory_space=pl.ANY)
    dma = pltpu.SemaphoreType.DMA
    return pl.pallas_call(
        functools.partial(front_kernel, n, n_tp, shape),
        out_shape=(
            jax.ShapeDtypeStruct((n * shape[0], width), BF),
            jax.ShapeDtypeStruct((2, quarter, width), BF),
            jax.ShapeDtypeStruct((quarter, width), BF),
            jax.ShapeDtypeStruct((quarter, width), BF),
            jax.ShapeDtypeStruct((tokens, width), BF),
            jax.ShapeDtypeStruct((3, tokens, lw), BF),
            jax.ShapeDtypeStruct((tokens, lw), BF),
            jax.ShapeDtypeStruct((tokens, width), F32),
            jax.ShapeDtypeStruct((tokens, width), BF),
            jax.ShapeDtypeStruct((tokens, 1), F32),
            jax.ShapeDtypeStruct((2, width, pairs.shape[2]), BF),
        ),
        in_specs=[vmem] * 11 + [hbm] * 3,
        out_specs=[hbm] * 4 + [vmem] * 6 + [hbm],
        scratch_shapes=[
            pltpu.VMEM((2, 128, 2, pairs.shape[2]), BF),
            pltpu.VMEM((2, 2, 128, pairs.shape[2]), BF),
            dma((2,)),
            dma((2,)),
            pltpu.VMEM((max(shape[0] - shape[1], 16), width), BF),
            pltpu.VMEM((n * shape[0], width), BF),
            pltpu.VMEM((4, tokens, width // 8), BF),
            pltpu.VMEM((4, tokens, width // 8), BF),
            pltpu.VMEM((4, tokens, width // 8), BF),
            pltpu.VMEM((4, tokens, width // 8), BF),
            pltpu.VMEM((2, 4, tokens, width // 8), BF),
            dma((3, n)),
            dma((3, n)),
            dma((3,)),
            dma((3,)),
            dma((4,)),
            dma((4,)),
            dma((4,)),
            dma((4,)),
            dma((4,)),
            dma((4,)),
        ],
        compiler_params=pltpu.CompilerParams(
            collective_id=2, has_side_effects=True, vmem_limit_bytes=56 * 2**20
        ),
        cost_estimate=pl.CostEstimate(
            flops=2 * tokens * width * 4 * lw, bytes_accessed=30 * 2**20, transcendentals=0
        ),
    )(hidden, gain1, gain2, w, bias, cosine, sine, prefix, ow, place, cot, gu_own, dn_own, pairs)


def dispatch_kernel(
    n,
    n_tp,
    shape,
    n_exp,
    nt,
    place,
    router,
    cot,
    sgu,
    sdn,
    gu_own,
    dn_b,
    dest_t,
    x_rows,
    g_rows,
    gu_b,
    gu_c,
    dn_c,
    probs,
    place_t,
    weighted,
    og,
    pg,
    sh,
    part,
    sback,
    sgrad,
    zero,
    gate,
    x_send,
    g_send,
    x_ss,
    x_rs,
    gate_ss,
    gate_rs,
    w_ss,
    w_rs,
):
    ep = lax.axis_index("ep")
    tp = lax.axis_index("tp")
    tokens, width = nt.shape
    units = sdn.shape[1]
    total = place.shape[0]
    core_peer, y_peer = flip(tp, 1), flip(tp, 2)
    greet(n, n_tp, ep, tp)
    w_y = remote(gu_own, gu_b, w_ss.at[0], w_rs.at[0], "tp", y_peer)
    w_y.start()
    w_on = remote(dn_b, dn_c, w_ss.at[1], w_rs.at[1], "tp", core_peer)
    w_on.start()

    capp = shape[0]
    zero[...] = jnp.zeros_like(zero)

    def x_copies(r):
        return block_copies(r, x_send, x_rows, x_ss, x_rs, ep, tp, n, shape, zero, False)

    def gate_copy(r, way):
        to = lax.rem(ep + r, n) if way == "out" else lax.rem(ep + n - r, n)
        return remote(g_send.at[r], g_rows.at[r], gate_ss.at[r], gate_rs.at[r], "ep", to)

    kept = pltpu.make_async_copy(x_send.at[:capp, :], x_rows.at[:capp, :], x_ss.at[0, 0])
    g_kept = pltpu.make_async_copy(g_send.at[0], g_rows.at[0], gate_ss.at[0])
    per = blocks_at_once(n, capp)
    size = per * capp

    for i in range(n // per):
        b = send_order(i, n, ep) if per == 1 else i
        at = pl.ds(pl.multiple_of(b * size, size), size)
        x_send[at, :] = jnp.dot(place[at, :], nt[...], preferred_element_type=F32).astype(BF)
        for j in range(per):
            if i == (n - 1 if per == 1 else 0) and j == 0:
                kept.start()
            else:
                each(x_copies(b * per + j), "start")

    logits = jnp.dot(nt[...], router[...], preferred_element_type=F32)
    lane = lax.broadcasted_iota(jnp.int32, logits.shape, 1)
    chosen = jnp.where(lane < n_exp, logits, -1e30)
    e = jnp.exp(chosen - jnp.max(chosen, axis=1, keepdims=True))
    prob = e / jnp.sum(e, axis=1, keepdims=True)
    prob = jnp.where(lane == n_exp, jax.nn.sigmoid(logits), prob)
    probs[...] = prob
    hi = prob.astype(BF)
    lo = (prob - hi.astype(F32)).astype(BF)
    g_send[...] = jnp.zeros_like(g_send)
    across = (((0,), (1,)), ((), ()))

    for r in range(n):
        where = place[r * capp : (r + 1) * capp, :]
        pick = lax.broadcasted_iota(jnp.int32, (128, capp), 0) == lax.rem(r + ep, n)
        g_hi = jnp.sum(
            jnp.where(pick, lax.dot_general(hi, where, across, preferred_element_type=F32), 0.0),
            axis=0,
            keepdims=True,
        )
        g_lo = jnp.sum(
            jnp.where(pick, lax.dot_general(lo, where, across, preferred_element_type=F32), 0.0),
            axis=0,
            keepdims=True,
        )
        term = lax.broadcasted_iota(jnp.int32, (16, capp), 0)
        g_send[r, :, :capp] = jnp.where(term == 0, g_hi, jnp.where(term == 1, g_lo, 0.0)).astype(BF)
        gate[:, r * capp : (r + 1) * capp] = g_hi + g_lo
        if r == 0:
            g_kept.start()
        else:
            gate_copy(r, "out").start()

    @pl.loop(0, tokens // 64)
    def _(m):
        at = pl.ds(pl.multiple_of(m * 64, 64), 64)
        og[at, :] = (probs[at, n_exp : n_exp + 1] * cot[at, :].astype(F32)).astype(BF)

    def hidden(at, up_at):
        g_pre = jnp.dot(nt[...], sgu[0, :, at], preferred_element_type=F32)
        u_pre = jnp.dot(nt[...], sgu[1, :, at], preferred_element_type=F32)
        grad = jnp.dot(og[...], sdn[:, at], preferred_element_type=F32)
        sig = jax.nn.sigmoid(g_pre)
        sh[:, at] = (g_pre * sig * u_pre).astype(BF)
        pg[:, at] = (grad * u_pre * sig * (1.0 + g_pre * (1.0 - sig))).astype(BF)
        pg[:, up_at] = (grad * g_pre * sig).astype(BF)

    @pl.loop(0, units // 256)
    def _(c):
        hidden(
            pl.ds(pl.multiple_of(c * 256, 256), 256),
            pl.ds(pl.multiple_of(c * 256 + units, 128), 256),
        )

    if units % 256:
        rest = units // 256 * 256
        hidden(pl.ds(rest, units - rest), pl.ds(units + rest, units - rest))

    nt_dims = (((1,), (1,)), ((), ()))

    share = probs[:, n_exp : n_exp + 1]

    def columns(c, total):
        at = pl.ds(pl.multiple_of(c * 256, 256), 256)
        out = lax.dot_general(sh[...], sdn[at, :], nt_dims, preferred_element_type=F32)
        part[:, at] = (share * out).astype(BF)
        sback[:, at] = lax.dot_general(
            pg[:, :units], sgu[0, at, :], nt_dims, preferred_element_type=F32
        ) + lax.dot_general(pg[:, units:], sgu[1, at, :], nt_dims, preferred_element_type=F32)
        return total + jnp.sum(cot[:, at].astype(F32) * out, axis=1, keepdims=True)

    sgrad[...] = lax.fori_loop(0, width // 256, columns, jnp.zeros((tokens, 1), F32))

    @pl.loop(0, total // 128)
    def _(c):
        at = pl.ds(pl.multiple_of(c * 128, 128), 128)
        spot = lax.broadcasted_iota(jnp.int32, (tokens, 128), 1) + c * 128
        hit = dest_t[:, :1] == spot
        for k in range(1, dest_t.shape[1]):
            hit = hit | (dest_t[:, k : k + 1] == spot)
        place_t[:, at] = jnp.where(hit, 1.0, 0.0).astype(BF)
        weighted[:, at] = jnp.where(hit, gate[:, at], 0.0).astype(BF)

    w_y.wait()
    w_far = remote(gu_b, gu_c, w_ss.at[2], w_rs.at[2], "tp", core_peer)
    w_far.start()
    w_on.wait()
    w_far.wait()
    kept.wait()
    g_kept.wait()

    @pl.loop(1, n)
    def _(r):
        gate_copy(r, "in").wait()
        each(x_copies(r), "wait")


def dispatch(n, n_tp, shape, n_exp, nt, place, router, cot, sgu, sdn, gu_own, dn_b, dest_t):
    tokens, width = nt.shape
    units = sdn.shape[1]
    total = place.shape[0]
    vmem = pl.BlockSpec(memory_space=pltpu.VMEM)
    hbm = pl.BlockSpec(memory_space=pl.ANY)
    dma = pltpu.SemaphoreType.DMA
    return pl.pallas_call(
        functools.partial(dispatch_kernel, n, n_tp, shape, n_exp),
        out_shape=(
            jax.ShapeDtypeStruct((total, width), BF),
            jax.ShapeDtypeStruct((n, 16, 128), BF),
            jax.ShapeDtypeStruct(gu_own.shape, BF),
            jax.ShapeDtypeStruct(gu_own.shape, BF),
            jax.ShapeDtypeStruct(dn_b.shape, BF),
            jax.ShapeDtypeStruct((tokens, 128), F32),
            jax.ShapeDtypeStruct((tokens, total), BF),
            jax.ShapeDtypeStruct((tokens, total), BF),
            jax.ShapeDtypeStruct((tokens, width), BF),
            jax.ShapeDtypeStruct((tokens, 2 * units), BF),
            jax.ShapeDtypeStruct((tokens, units), BF),
            jax.ShapeDtypeStruct((tokens, width), BF),
            jax.ShapeDtypeStruct((tokens, width), F32),
            jax.ShapeDtypeStruct((tokens, 1), F32),
        ),
        in_specs=[vmem] * 6 + [hbm] * 2 + [vmem],
        out_specs=[hbm] * 5 + [vmem] * 9,
        scratch_shapes=[
            pltpu.VMEM((max(shape[0] - shape[1], 16), width), BF),
            pltpu.VMEM((1, total), F32),
            pltpu.VMEM((total, width), BF),
            pltpu.VMEM((n, 16, 128), BF),
            dma((3, n)),
            dma((3, n)),
            dma((n,)),
            dma((n,)),
            dma((3,)),
            dma((3,)),
        ],
        compiler_params=pltpu.CompilerParams(
            collective_id=3, has_side_effects=True, vmem_limit_bytes=60 * 2**20
        ),
        cost_estimate=pl.CostEstimate(
            flops=2 * tokens * width * 6 * units, bytes_accessed=40 * 2**20, transcendentals=0
        ),
    )(nt, place, router, cot, sgu, sdn, gu_own, dn_b, dest_t)

def backward_kernel(
    n,
    n_tp,
    shape,
    n_exp,
    back,
    g_back,
    place_t,
    sback,
    sgrad,
    probs,
    router,
    nt,
    mid,
    cot,
    gain2,
    qkv,
    ow,
    cosine,
    sine,
    prefix,
    o_sent,
    o_rows,
    ag,
    lg,
    bias,
    small,
    zero,
    core_send,
    core_recv,
    y_send,
    y_recv,
    summed,
    few_send,
    few_recv,
    ng,
    cg,
    dk,
    dv,
    o_ss,
    o_rs,
    core_ss,
    core_rs,
    y_ss,
    y_rs,
    g_ss,
    g_rs,
    few_ss,
    few_rs,
):
    ep = lax.axis_index("ep")
    tp = lax.axis_index("tp")
    tokens, width = nt.shape
    total = back.shape[0]
    lw = ow.shape[1]
    heads = lw // HEAD_DIM
    core_peer, y_peer = flip(tp, 1), flip(tp, 2)
    greet(n, n_tp, ep, tp)

    capp = shape[0]
    zero[...] = jnp.zeros_like(zero)

    def o_copies(r):
        return block_copies(r, o_sent, o_rows, o_ss, o_rs, ep, tp, n, shape, zero, True)

    kept = pltpu.make_async_copy(o_sent.at[:capp, :], o_rows.at[:capp, :], o_ss.at[0, 0])

    for i in range(n - 1):
        each(o_copies(send_order(i, n, ep)), "start")
    kept.start()

    row = lax.broadcasted_iota(jnp.int32, (total, 128), 0)
    spot = lax.broadcasted_iota(jnp.int32, (total, 128), 1)
    expert = lax.rem(row // capp + ep * (n_exp // n), n_exp)
    gg = jnp.concatenate([gate_column(g_back, r, capp) for r in range(n)], axis=0)
    few = jnp.dot(
        place_t[...], jnp.where(spot == expert, gg, 0.0).astype(BF), preferred_element_type=F32
    )
    lane = lax.broadcasted_iota(jnp.int32, (tokens, 128), 1)
    few_send[0] = jnp.where(lane == n_exp, sgrad[...], few).astype(BF)
    few_core = remote(few_send.at[0], few_recv.at[0], few_ss.at[0], few_rs.at[0], "tp", core_peer)
    few_core.start()

    def project(base, i, size):
        at = pl.ds(pl.multiple_of(base + i * size, size), size)
        return sback[:, at] + jnp.dot(place_t[...], back[:, at], preferred_element_type=F32)

    def between():
        few_core.wait()
        few_send[1] = (few_send[0].astype(F32) + few_recv[0].astype(F32)).astype(BF)
        few_y = remote(few_send.at[1], few_recv.at[1], few_ss.at[1], few_rs.at[1], "tp", y_peer)
        few_y.start()
        few_y.wait()

    tp_total(
        project, between, tp, core_send, core_recv, y_send, y_recv, summed,
        core_ss, core_rs, y_ss, y_rs, g_ss, g_rs,
    )

    prob = jnp.where(lane < n_exp, probs[...], 0.0)
    share = probs[:, n_exp : n_exp + 1]
    grads = few_send[1].astype(F32) + few_recv[1].astype(F32)
    inner = jnp.sum(prob * grads, axis=1, keepdims=True)
    gate_in = grads * share * (1.0 - share)
    few_send[0] = jnp.where(
        lane < n_exp, prob * (grads - inner), jnp.where(lane == n_exp, gate_in, 0.0)
    ).astype(BF)
    pieces, size = summed.shape[1], summed.shape[3]
    for j in range(2):
        for i in range(pieces):
            at = slice((j * pieces + i) * size, (j * pieces + i + 1) * size)
            ng[:, at] = summed[j, i].astype(F32) + lax.dot_general(
                few_send[0], router[at, :], (((1,), (1,)), ((), ())), preferred_element_type=F32
            )

    step = 32

    def norm_rows(m, acc):
        at = pl.ds(pl.multiple_of(m * step, step), step)
        h = mid[at, :]
        grad = ng[at, :]
        factor = lax.rsqrt(jnp.sum(h * h, axis=1, keepdims=True) * (1.0 / width) + EPSILON)
        scaled = grad * gain2[...]
        mean = jnp.sum(scaled * h, axis=1, keepdims=True) * (1.0 / width)
        ag[at, :] = (
            cot[at, :].astype(F32) + factor * scaled - h * (factor * factor * factor) * mean
        ).astype(BF)
        return acc + jnp.sum((grad * h * factor).reshape(step // 8, 8, width), axis=0)

    acc = lax.fori_loop(0, tokens // step, norm_rows, jnp.zeros((8, width), F32))

    @pl.loop(0, lw // 256)
    def _(c):
        at = pl.ds(pl.multiple_of(c * 256, 256), 256)
        cg[:, at] = jnp.dot(ag[...], ow[:, at], preferred_element_type=F32).astype(BF)

    dk[...] = jnp.zeros_like(dk)
    dv[...] = jnp.zeros_like(dv)
    first_dims, last_dims = (((0,), (0,)), ((), ())), (((1,), (1,)), ((), ()))

    def attend(m, sums):
        at = pl.ds(pl.multiple_of(m * 128, 128), 128)
        row = lax.broadcasted_iota(jnp.int32, (128, tokens), 0) + m * 128
        col = lax.broadcasted_iota(jnp.int32, (128, tokens), 1)
        visible = (col <= row) | (col < prefix[...])
        parts = []
        for i in range(heads):
            lanes = slice(i * HEAD_DIM, (i + 1) * HEAD_DIM)
            q, grad = qkv[0, at, lanes], cg[at, lanes]
            s = lax.dot_general(q, qkv[1, :, lanes], last_dims, preferred_element_type=F32)
            s = jnp.where(visible, s * HEAD_DIM ** (-0.5), -1e30)
            e = jnp.exp(s - jnp.max(s, axis=1, keepdims=True))
            e = e * (1.0 / jnp.sum(e, axis=1, keepdims=True))
            dp = lax.dot_general(grad, qkv[2, :, lanes], last_dims, preferred_element_type=F32)
            delta = jnp.sum(e * dp, axis=1, keepdims=True)
            ds = (e * (dp - delta)).astype(BF)
            dv[:, lanes] += lax.dot_general(e.astype(BF), grad, first_dims, preferred_element_type=F32)
            dk[:, lanes] += lax.dot_general(ds, q, first_dims, preferred_element_type=F32)
            dq = jnp.dot(ds, qkv[1, :, lanes], preferred_element_type=F32) * HEAD_DIM ** (-0.5)
            dq = dq * cosine[at, :] - pltpu.roll(dq, HEAD_DIM // 2, 1) * sine[at, :]
            lg[at, lanes] = dq.astype(BF)
            parts.append(jnp.sum(dq.reshape(16, 8, HEAD_DIM), axis=0))
        return sums + jnp.concatenate(parts, axis=1)

    sums = lax.fori_loop(0, tokens // 128, attend, jnp.zeros((8, lw), F32))
    bias[:, :lw] = jnp.sum(sums, axis=0, keepdims=True)
    for i in range(heads):
        lanes = slice(i * HEAD_DIM, (i + 1) * HEAD_DIM)
        grad = dk[:, lanes] * HEAD_DIM ** (-0.5)
        grad = grad * cosine[...] - pltpu.roll(grad, HEAD_DIM // 2, 1) * sine[...]
        at = slice(lw + i * HEAD_DIM, lw + (i + 1) * HEAD_DIM)
        lg[:, at] = grad.astype(BF)
        bias[:, at] = jnp.sum(grad, axis=0, keepdims=True)
    lg[:, 2 * lw :] = dv[...].astype(BF)
    bias[:, 2 * lw :] = jnp.sum(dv[...], axis=0, keepdims=True)

    wide, span = small.shape[1:]
    gain_row = jnp.sum(acc, axis=0, keepdims=True)
    rows = lax.dot_general(few_send[0], nt[...], first_dims, preferred_element_type=F32)[:wide]
    index = lax.broadcasted_iota(jnp.int32, rows.shape, 0)
    rows = jnp.where(index == n_exp + 1, gain_row, rows).astype(BF)
    for r in range(n):
        small[r] = rows[:, r * span : (r + 1) * span]

    kept.wait()
    for r in range(1, n):
        each(o_copies(r), "wait")


def backward(n, n_tp, shape, n_exp, back, g_back, place_t, sback, sgrad, probs, router, nt, mid, cot, gain2, qkv, ow, cosine, sine, prefix, o_sent):
    tokens, width = nt.shape
    lw = ow.shape[1]
    wide = -(-(n_exp + 2) // 16) * 16
    vmem = pl.BlockSpec(memory_space=pltpu.VMEM)
    hbm = pl.BlockSpec(memory_space=pl.ANY)
    dma = pltpu.SemaphoreType.DMA
    piece = (4, tokens, width // 8)
    return pl.pallas_call(
        functools.partial(backward_kernel, n, n_tp, shape, n_exp),
        out_shape=(
            jax.ShapeDtypeStruct(o_sent.shape, BF),
            jax.ShapeDtypeStruct((tokens, width), BF),
            jax.ShapeDtypeStruct((tokens, 3 * lw), BF),
            jax.ShapeDtypeStruct((1, 3 * lw), F32),
            jax.ShapeDtypeStruct((n, wide, width // n), BF),
        ),
        in_specs=[vmem] * 16 + [hbm],
        out_specs=[hbm] + [vmem] * 4,
        scratch_shapes=[
            pltpu.VMEM((max(shape[0] - shape[1], 16), width), BF),
            pltpu.VMEM(piece, BF),
            pltpu.VMEM(piece, BF),
            pltpu.VMEM(piece, BF),
            pltpu.VMEM(piece, BF),
            pltpu.VMEM((2,) + piece, BF),
            pltpu.VMEM((2, tokens, 128), BF),
            pltpu.VMEM((2, tokens, 128), BF),
            pltpu.VMEM((tokens, width), F32),
            pltpu.VMEM((tokens, lw), BF),
            pltpu.VMEM((tokens, lw), F32),
            pltpu.VMEM((tokens, lw), F32),
            dma((3, n)),
            dma((3, n)),
            dma((4,)),
            dma((4,)),
            dma((4,)),
            dma((4,)),
            dma((4,)),
            dma((4,)),
            dma((2,)),
            dma((2,)),
        ],
        compiler_params=pltpu.CompilerParams(
            collective_id=4, has_side_effects=True, vmem_limit_bytes=60 * 2**20
        ),
        cost_estimate=pl.CostEstimate(
            flops=2 * tokens * width * 4 * lw, bytes_accessed=30 * 2**20, transcendentals=0
        ),
    )(back, g_back, place_t, sback, sgrad, probs, router, nt, mid, cot, gain2, qkv, ow, cosine, sine, prefix, o_sent)


def body(
    hidden,
    attn_gain,
    qkv_weight,
    qkv_bias,
    out_weight,
    mlp_gain,
    router_weight,
    share_gate,
    shared_gate_up,
    shared_down,
    expert_gate_up,
    expert_down,
    routes,
    priority,
    prefix,
    cotangent,
):
    tokens, width = hidden.shape
    n_ep = lax.axis_size("ep")
    n_tp = lax.axis_size("tp")
    tp_i = lax.axis_index("tp")
    local_width = qkv_weight.shape[2]
    expert_local = expert_gate_up.shape[0]
    n_exp = expert_local * n_ep
    top = routes.shape[1]
    capacity = (5 * tokens * top + 4 * n_exp - 1) // (4 * n_exp)
    tiles = -(-capacity // 16)
    least, extra = 16 * (tiles // n_tp), tiles % n_tp
    part_pad = least + (16 if extra else 0)
    shape = (part_pad, least, extra, n_tp)
    rows = n_exp * part_pad

    flat_route = routes.T.reshape(-1)
    flat_order = priority.T.reshape(-1)
    hits = (flat_route[:, None] == jnp.arange(n_exp, dtype=jnp.int32)[None, :]).astype(BF)
    smaller = (flat_order[None, :] < flat_order[:, None]).astype(BF)
    counts = mm(smaller, hits, 1, 0)
    slot = jnp.sum(counts * hits.astype(F32), axis=1).astype(jnp.int32).reshape(top, tokens)
    kept = slot < capacity
    ep_i = lax.axis_index("ep")
    more = [has_more(j, ep_i, routes.T // expert_local, n_tp, extra) for j in range(n_tp)]
    more.append(has_more(tp_i, ep_i, routes.T // expert_local, n_tp, extra))
    start = tp_i * least
    for j in range(n_tp):
        start = start + 16 * (more[j] & (j < tp_i)).astype(jnp.int32)
    in_part = slot - start
    mine = kept & (in_part >= 0) & (in_part < least + 16 * more[-1].astype(jnp.int32))
    hop = lax.rem(routes.T + n_exp - ep_i * expert_local, n_exp)
    dest = jnp.where(mine, hop * part_pad + in_part, -1)
    row_ids = jnp.arange(rows, dtype=jnp.int32)[:, None]
    place = (dest[0][None, :] == row_ids)
    for k in range(1, top):
        place = place | (dest[k][None, :] == row_ids)
    place = place.astype(BF)

    cos_all, sin_all = angle_tables(tokens, HEAD_DIM)
    w_t = jnp.transpose(qkv_weight, (1, 0, 2))
    prefix_row = jnp.broadcast_to(prefix[None], (1, tokens))
    gu_own = jnp.transpose(expert_gate_up[0], (1, 2, 0))
    dn_own = jnp.transpose(expert_down[0], (1, 0))
    up_rows, gu_a, dn_a, dn_b, normed_one, qkv, context, middle, normed_two, factor_one, sgu = front(
        n_ep,
        n_tp,
        shape,
        hidden,
        attn_gain[None],
        mlp_gain[None],
        w_t,
        qkv_bias,
        cos_all,
        sin_all,
        prefix_row,
        out_weight,
        place,
        cotangent,
        gu_own,
        dn_own,
        shared_gate_up,
    )

    router_all = jnp.concatenate(
        [router_weight, share_gate[:, None], jnp.zeros((width, 127 - n_exp), BF)], axis=1
    )
    got, gates, gu_b, gu_c, dn_c, probs_all, place_t, weighted_place, shared_out_grad, pre_grad, shared_hidden, scaled_part, shared_back, scale_grad = (
        dispatch(
            n_ep,
            n_tp,
            shape,
            n_exp,
            normed_two,
            place,
            router_all,
            cotangent,
            sgu,
            shared_down,
            gu_own,
            dn_b,
            dest.T,
        )
    )
    back_rows, back_gates, e_out, _, dw_own, dw_y, gu_grad, shared_down_grad = routed_expert(
        n_ep,
        n_tp,
        shape,
        got,
        up_rows,
        (gu_a, gu_c, gu_b, gu_own, dn_a, dn_c, dn_b, dn_own),
        gates,
        normed_two,
        pre_grad,
        shared_out_grad,
        shared_hidden,
    )
    shared_gate_up_grad = jnp.transpose(gu_grad, (1, 0, 2)).astype(F32)
    shared_down_grad = shared_down_grad.astype(F32)
    expert_down_grad = jnp.transpose(dw_own[2].astype(F32) + dw_y[2].astype(F32), (1, 0))[None]
    expert_gate_up_grad = jnp.transpose(dw_own[:2].astype(F32) + dw_y[:2].astype(F32), (2, 0, 1))[None]

    out_rows, attn_grad, linear_grad, bias_grad, small = backward(
        n_ep,
        n_tp,
        shape,
        n_exp,
        back_rows,
        back_gates,
        place_t,
        shared_back,
        scale_grad,
        probs_all,
        router_all,
        normed_two,
        middle,
        cotangent,
        mlp_gain[None],
        qkv,
        out_weight,
        cos_all,
        sin_all,
        prefix_row,
        e_out,
    )
    qkv_grad, out_weight_grad, input_grad, output, gain_one, bias_sum, small_sum = tail(
        n_ep,
        n_tp,
        normed_one,
        linear_grad,
        attn_grad,
        context,
        w_t,
        hidden,
        factor_one,
        attn_gain[None],
        bias_grad,
        small,
        out_rows,
        weighted_place,
        scaled_part,
        middle,
    )
    small_sum = jnp.transpose(small_sum, (1, 0, 2)).reshape(-1, width)
    qkv_weight_grad = jnp.transpose(qkv_grad, (1, 0, 2))
    gain_one_sum = gain_one[0]
    bias_sum = bias_sum.reshape(3, local_width)
    router_sum = small_sum[:n_exp].T
    share_gate_sum = small_sum[n_exp]
    gain_two_sum = small_sum[n_exp + 1]
    return (
        output,
        input_grad,
        gain_one_sum,
        qkv_weight_grad,
        bias_sum,
        out_weight_grad,
        gain_two_sum,
        router_sum,
        share_gate_sum,
        shared_gate_up_grad,
        shared_down_grad,
        expert_gate_up_grad,
        expert_down_grad,
    )


def solution(mesh):
    return jax.shard_map(
        body,
        mesh=mesh,
        in_specs=(
            P("ep", None),
            P(),
            P(None, None, "tp"),
            P(None, "tp"),
            P(None, "tp"),
            P(),
            P(),
            P(),
            P(None, None, "tp"),
            P(None, "tp"),
            P("ep", None, None, "tp"),
            P("ep", None, "tp"),
            P("ep", None),
            P("ep", None),
            P("ep"),
            P("ep", None),
        ),
        out_specs=(
            P("ep", "tp"),
            P("ep", "tp"),
            P(),
            P("ep", None, "tp"),
            P(None, "tp"),
            P("ep", "tp"),
            P(),
            P(),
            P(),
            P("ep", None, "tp"),
            P("ep", "tp"),
            P("ep", None, None, "tp"),
            P("ep", None, "tp"),
        ),
        check_vma=False,
    )
```

```python
import functools

import jax
import jax.numpy as jnp
import numpy as np
from jax import lax
from jax.experimental import pallas as pl
from jax.experimental.pallas import tpu as pltpu
from jax.sharding import PartitionSpec as P

HEAD_DIM = 128
EPSILON = 1e-06
THETA = 1000000.0
BF = jnp.bfloat16
F32 = jnp.float32


def mm(a, b, ca, cb):
    return lax.dot_general(a, b, (((ca,), (cb,)), ((), ())), preferred_element_type=F32)


def angle_tables(length, head_size):
    half_size = head_size // 2
    frequency = (THETA ** (-np.arange(half_size, dtype=np.float32) * 2.0 / head_size)).astype(np.float32)
    angles = (np.arange(length, dtype=np.float32)[:, None] * frequency[None, :]).astype(np.float64)
    cosine, sine_val = np.cos(angles), np.sin(angles)
    return (
        np.concatenate([cosine, cosine], axis=1).astype(np.float32),
        np.concatenate([-sine_val, sine_val], axis=1).astype(np.float32),
    )


def ring_place(e, n):
    odd = e % 2
    return (1 - odd) * (e // 2) + odd * (n - 1 - e // 2)


def ring_member(p, n):
    second = p // (n // 2)
    return (1 - second) * 2 * p + second * (2 * (n - 1 - p) + 1)


def remote(src, dst, send_sem, recv_sem, axis, index):
    return pltpu.make_async_remote_copy(
        src_ref=src,
        dst_ref=dst,
        send_sem=send_sem,
        recv_sem=recv_sem,
        device_id={axis: index},
        device_id_type=pl.DeviceIdType.MESH,
    )


def greet(n, n_tp, ep, tp):
    barrier = pltpu.get_barrier_semaphore()
    for shift in range(1, n):
        pl.semaphore_signal(
            barrier, 1, device_id={"ep": lax.rem(ep + shift, n)}, device_id_type=pl.DeviceIdType.MESH
        )
    for shift in range(1, n_tp):
        pl.semaphore_signal(
            barrier, 1, device_id={"tp": lax.rem(tp + shift, n_tp)}, device_id_type=pl.DeviceIdType.MESH
        )
    pl.semaphore_wait(barrier, n - 1 + n_tp - 1)


def flip(index, bit):
    if bit == 1:
        return index + 1 - 2 * (index % 2)
    return index + 2 - 4 * ((index // 2) % 2)


def tail_kernel(
    n,
    n_tp,
    ready,
    n1,
    lg,
    ag,
    ctx,
    w,
    hidden,
    r_one,
    gain_all,
    bias,
    small,
    o_rows,
    weighted,
    spart,
    mid,
    ag_hbm,
    qkv_out,
    o_out,
    in_out,
    out_out,
    gain_out,
    bias_out,
    small_out,
    h_cols,
    res_cols,
    ag_cols,
    in_sem,
    ring_recv,
    ring_send,
    part_own,
    part_send,
    part_recv,
    y_send,
    y_recv,
    mean_send,
    mean_recv,
    vec_send,
    vec_recv,
    small_recv,
    small_sum,
    gain_send,
    gain_recv,
    out_send,
    out_recv,
    oy_send,
    oy_recv,
    ring_ss,
    ring_rs,
    tp_ss,
    tp_rs,
    vec_ss,
    vec_rs,
    small_ss,
    small_rs,
    gain_ss,
    gain_rs,
):
    ep = lax.axis_index("ep")
    tp = lax.axis_index("tp")
    tokens, lw = ctx.shape
    columns = pl.ds(pl.multiple_of(tp * lw, lw), lw)
    col_in = [
        pltpu.make_async_copy(hidden.at[:, columns], h_cols, in_sem.at[0]),
        pltpu.make_async_copy(mid.at[:, columns], res_cols, in_sem.at[1]),
        pltpu.make_async_copy(ag_hbm.at[:, columns], ag_cols, in_sem.at[2]),
    ]
    for copy in col_in:
        copy.start()
    gain = gain_all[:, columns]
    rows = qkv_out.shape[1]
    width = rows * n
    p = ring_place(ep, n)
    nxt = ring_member(lax.rem(p + 1, n), n)
    prv = ring_member(lax.rem(p + n - 1, n), n)
    core_peer, y_peer = flip(tp, 1), flip(tp, 2)
    greet(n, n_tp, ep, tp)

    def small_copy(shift, turn, way):
        to, came = lax.rem(ep + shift, n), lax.rem(ep + n - shift, n)
        if turn == 0:
            src, dst, arrived = small.at[to], small_recv.at[ep], small_recv.at[came]
        else:
            src, dst, arrived = small_sum, small_out.at[ep], small_out.at[came]
        sems = small_ss.at[turn, shift], small_rs.at[turn, shift]
        if way == 0:
            return remote(src, dst, *sems, "ep", to)
        return remote(src, arrived, *sems, "ep", came)

    def block_of(ring, step):
        if ring < 2:
            return ring_member(lax.rem(p + 2 * n - 1 - step, n), n)
        return ring_member(lax.rem(p + 1 + step, n), n)

    def term(ring, owner):
        if ring == 1:
            return block_dot(ag, owner, rows, ctx[...])
        k = {0: 0, 2: 1, 3: 2}[ring]
        return block_dot(n1, owner, rows, lg[:, k * lw : (k + 1) * lw])

    def ring_copy(ring, step, slot):
        return remote(
            ring_send.at[ring, slot],
            ring_recv.at[ring, step],
            ring_ss.at[ring, slot],
            ring_rs.at[ring, step],
            "ep",
            nxt if ring < 2 else prv,
        )

    def ring_step(step, first):
        for ring in range(4):
            slot = lax.rem(step, 2)
            mine = term(ring, block_of(ring, step))
            ring_copy(ring, step - 1, slot).wait_recv()
            if not first:
                ring_copy(ring, step - 2, slot).wait_send()
            ring_send[ring, slot] = (mine + ring_recv[ring, step - 1].astype(F32)).astype(BF)
            ring_copy(ring, step, slot).start()

    for ring in range(4):
        ring_send[ring, 0] = term(ring, block_of(ring, 0)).astype(BF)
        ring_copy(ring, 0, 0).start()

    ready()

    def part_block(column, store):
        for m in range(0, tokens, 128):
            total = None
            for k in range(3):
                d = lax.dot_general(
                    lg[m : m + 128, k * lw : (k + 1) * lw],
                    w[k, pl.ds(pl.multiple_of(column * lw, lw), lw), :],
                    (((1,), (1,)), ((), ())),
                    preferred_element_type=F32,
                )
                total = d if total is None else total + d
            store(m, total)

    def tp_copy(i, src, dst, peer):
        return remote(src, dst, tp_ss.at[i], tp_rs.at[i], "tp", peer)

    first = [tp_copy(i, part_send.at[i], part_recv.at[i], core_peer) for i in range(2)]
    for i in range(2):

        def put(m, total, i=i):
            part_send[i, m : m + 128, :] = total.astype(BF)

        part_block((core_peer % 2) + 2 * i, put)
        first[i].start()

    ring_step(1, True)

    small_recv[ep] = small[ep]
    for shift in range(1, n):
        small_copy(shift, 0, 0).start()
    for copy in col_in:
        copy.wait()

    def put_own(m, total):
        part_own[m : m + 128, :] = total

    other = (tp // 2) * -1 + 1
    part_block((tp % 2) + 2 * other, put_own)
    for i in range(2):
        first[i].wait()
    y_send[...] = (part_own[...] + part_recv[other].astype(F32)).astype(BF)
    second = tp_copy(2, y_send, y_recv, y_peer)
    second.start()

    ring_step(2, False)

    part_block(tp, put_own)
    second.wait()
    for m in range(0, tokens, 128):
        at = slice(m, m + 128)
        grad = (
            part_own[at, :]
            + part_recv[tp // 2, at, :].astype(F32)
            + y_recv[at, :].astype(F32)
        )
        part_own[at, :] = grad
        hid = h_cols[at, :].astype(F32)
        mean = jnp.sum(grad * gain * hid, axis=1, keepdims=True)
        mean_send[0, at, :] = jnp.broadcast_to(mean, (128, 128))
        col = jnp.sum(grad * hid * r_one[at, :], axis=0, keepdims=True)
        if m == 0:
            vec_send[:, :lw] = col
        else:
            vec_send[:, :lw] += col
    third = tp_copy(3, mean_send.at[0], mean_recv.at[0], core_peer)
    third.start()
    vec_send[:, lw:] = bias[...]
    vec_recv[ep] = vec_send[...]

    def vec_copy(shift, way):
        to = lax.rem(ep + shift, n)
        came = lax.rem(ep + n - shift, n)
        if way == "out":
            return remote(vec_send, vec_recv.at[ep], vec_ss.at[shift], vec_rs.at[shift], "ep", to)
        return remote(vec_send, vec_recv.at[came], vec_ss.at[shift], vec_rs.at[shift], "ep", came)

    for shift in range(1, n):
        vec_copy(shift, "out").start()

    ring_step(3, False)

    third.wait()
    mean_send[1] = mean_send[0] + mean_recv[0]
    fourth = tp_copy(4, mean_send.at[1], mean_recv.at[1], y_peer)
    fourth.start()

    def out_block(column):
        at = pl.ds(pl.multiple_of(column * lw, lw), lw)
        return spart[:, at].astype(F32) + jnp.dot(
            weighted[...], o_rows[:, at], preferred_element_type=F32
        )

    fifth = [tp_copy(5 + i, out_send.at[i], out_recv.at[i], core_peer) for i in range(2)]
    for i in range(2):
        out_send[i] = out_block((core_peer % 2) + 2 * i).astype(BF)
        fifth[i].start()

    ring_step(4, False)

    for shift in range(1, n):
        small_copy(shift, 0, 1).wait()
    total = small_recv[0].astype(F32)
    for e in range(1, n):
        total = total + small_recv[e].astype(F32)
    small_sum[...] = total
    small_out[ep] = total
    for shift in range(1, n):
        small_copy(shift, 1, 0).start()
    for copy in fifth:
        copy.wait()
    oy_send[...] = (out_block((tp % 2) + 2 * other) + out_recv[other].astype(F32)).astype(BF)
    sixth = tp_copy(7, oy_send, oy_recv, y_peer)
    sixth.start()
    fourth.wait()
    for m in range(0, tokens, 128):
        at = slice(m, m + 128)
        mean = (mean_send[1, at, :1] + mean_recv[1, at, :1]) * (1.0 / width)
        r = r_one[at, :]
        in_out[at, :] = (
            ag_cols[at, :].astype(F32)
            + r * part_own[at, :] * gain
            - h_cols[at, :].astype(F32) * (r * r * r) * mean
        ).astype(BF)
    for shift in range(1, n):
        vec_copy(shift, "in").wait()
    total = vec_recv[0]
    for e in range(1, n):
        total = total + vec_recv[e]
    bias_out[...] = total[:, lw:]
    gain_send[...] = total[:, :lw]
    gain_recv[tp] = total[:, :lw]

    def gain_copy(shift, way):
        to = lax.rem(tp + shift, n_tp)
        came = lax.rem(tp + n_tp - shift, n_tp)
        if way == "out":
            return remote(gain_send, gain_recv.at[tp], gain_ss.at[shift], gain_rs.at[shift], "tp", to)
        return remote(gain_send, gain_recv.at[came], gain_ss.at[shift], gain_rs.at[shift], "tp", came)

    for shift in range(1, n_tp):
        gain_copy(shift, "out").start()

    ring_step(5, False)

    own = out_block(tp) + res_cols[...] + out_recv[tp // 2].astype(F32)
    sixth.wait()
    out_out[...] = (own + oy_recv[...].astype(F32)).astype(BF)

    @pl.loop(6, n - 1)
    def _(step):
        ring_step(step, False)

    for shift in range(1, n):
        small_copy(shift, 1, 1).wait()
    for shift in range(1, n_tp):
        gain_copy(shift, "in").wait()
    for j in range(n_tp):
        gain_out[:, j * lw : (j + 1) * lw] = gain_recv[j]

    for ring in range(4):
        mine = term(ring, ep)
        ring_copy(ring, n - 2, 0).wait_recv()
        done = mine + ring_recv[ring, n - 2].astype(F32)
        if ring == 1:
            o_out[...] = done
        else:
            qkv_out[{0: 0, 2: 1, 3: 2}[ring]] = done
    for ring in range(4):
        for step in (n - 3, n - 2):
            ring_copy(ring, step, step % 2).wait_send()


def tail(n, n_tp, n1, lg, ag, ctx, w, hidden, r_one, gain, bias, small, o_rows, weighted, spart, mid):
    tokens, width = n1.shape
    lw = ctx.shape[1]
    rows = width // n
    ag_hbm = ag
    if rows % 128:
        n1, ag = n1.T, ag.T
    wide = small.shape[1]
    vmem = pl.BlockSpec(memory_space=pltpu.VMEM)
    hbm = pl.BlockSpec(memory_space=pl.ANY)
    dma = pltpu.SemaphoreType.DMA
    operands = (n1, lg, ag, ctx, w, hidden, r_one, gain, bias, small, o_rows, weighted, spart, mid, ag_hbm)
    late = (4, 10, 11, 12)
    return pl.pallas_call(
        fetch_late(functools.partial(tail_kernel, n, n_tp), late),
        out_shape=(
            jax.ShapeDtypeStruct((3, rows, lw), F32),
            jax.ShapeDtypeStruct((rows, lw), F32),
            jax.ShapeDtypeStruct((tokens, lw), BF),
            jax.ShapeDtypeStruct((tokens, lw), BF),
            jax.ShapeDtypeStruct((1, width), F32),
            jax.ShapeDtypeStruct((1, 3 * lw), F32),
            jax.ShapeDtypeStruct((n, wide, rows), F32),
        ),
        in_specs=specs(15, (4, 5, 10, 11, 12, 13, 14)),
        out_specs=[vmem] * 7,
        scratch_shapes=[
            pltpu.VMEM((tokens, lw), BF),
            pltpu.VMEM((tokens, lw), F32),
            pltpu.VMEM((tokens, lw), BF),
            dma((3,)),
            pltpu.VMEM((4, n - 1, rows, lw), BF),
            pltpu.VMEM((4, 2, rows, lw), BF),
            pltpu.VMEM((tokens, lw), F32),
            pltpu.VMEM((2, tokens, lw), BF),
            pltpu.VMEM((2, tokens, lw), BF),
            pltpu.VMEM((tokens, lw), BF),
            pltpu.VMEM((tokens, lw), BF),
            pltpu.VMEM((2, tokens, 128), F32),
            pltpu.VMEM((2, tokens, 128), F32),
            pltpu.VMEM((1, 4 * lw), F32),
            pltpu.VMEM((n, 1, 4 * lw), F32),
            pltpu.VMEM((n, wide, rows), BF),
            pltpu.VMEM((wide, rows), F32),
            pltpu.VMEM((1, lw), F32),
            pltpu.VMEM((n_tp, 1, lw), F32),
            pltpu.VMEM((2, tokens, lw), BF),
            pltpu.VMEM((2, tokens, lw), BF),
            pltpu.VMEM((tokens, lw), BF),
            pltpu.VMEM((tokens, lw), BF),
            dma((4, 2)),
            dma((4, n - 1)),
            dma((8,)),
            dma((8,)),
            dma((n,)),
            dma((n,)),
            dma((2, n)),
            dma((2, n)),
            dma((n_tp,)),
            dma((n_tp,)),
        ]
        + late_scratch(operands, late),
        compiler_params=pltpu.CompilerParams(
            collective_id=0, has_side_effects=True, vmem_limit_bytes=60 * 2**20
        ),
        cost_estimate=pl.CostEstimate(
            flops=2 * tokens * width * 7 * lw, bytes_accessed=30 * 2**20, transcendentals=0
        ),
    )(*operands)


def cols_of(ref, owner, rows):
    at = pl.ds(pl.multiple_of(owner * rows, rows), rows)
    return ref[:, at] if rows % 128 == 0 else ref[at, :]


def block_dot(ref, owner, rows, other):
    dims = (((0,), (0,)), ((), ())) if rows % 128 == 0 else (((1,), (0,)), ((), ()))
    return lax.dot_general(cols_of(ref, owner, rows), other, dims, preferred_element_type=F32)


def middle_kernel(
    n,
    n_tp,
    shape,
    x_hbm,
    u_hbm,
    gu_a,
    gu_c,
    gu_b,
    gu_own,
    dn_a,
    dn_c,
    dn_b,
    dn_own,
    gates,
    nt,
    pg,
    og,
    sh,
    back,
    g_back,
    o_hbm,
    dw_recv,
    dw_own,
    dw_y,
    gu_out,
    dn_out,
    zero,
    w,
    xb,
    ub,
    rgb,
    eb,
    rbs,
    gbs,
    ring_recv,
    ring_send,
    w_sem,
    x_sem,
    u_sem,
    out_sem,
    ring_ss,
    ring_rs,
    free,
    back_ss,
    back_rs,
    gate_ss,
    gate_rs,
    dw_ss,
    dw_rs,
    dw_sem,
):
    ep = lax.axis_index("ep")
    tp = lax.axis_index("tp")
    core_peer, y_peer = flip(tp, 1), flip(tp, 2)
    gr = ub.shape[1]
    capp = shape[0]
    zero[...] = jnp.zeros_like(zero)
    width = u_hbm.shape[1]
    units = w.shape[1]
    quarter = units // 4
    groups = x_hbm.shape[0] // gr
    per = n // groups
    rows = gu_out.shape[1]
    half = ring_recv.shape[3]
    p = ring_place(ep, n)
    nxt = ring_member(lax.rem(p + 1, n), n)
    prv = ring_member(lax.rem(p + n - 1, n), n)

    w_in = [
        pltpu.make_async_copy(ref, w.at[:2, i * quarter : (i + 1) * quarter, :], w_sem.at[i])
        for i, ref in enumerate((gu_a, gu_c, gu_b, gu_own))
    ] + [
        pltpu.make_async_copy(ref, w.at[2, i * quarter : (i + 1) * quarter, :], w_sem.at[4 + i])
        for i, ref in enumerate((dn_a, dn_c, dn_b, dn_own))
    ]
    for copy in w_in:
        copy.start()

    x_in = pltpu.make_async_copy(x_hbm, xb, x_sem)

    def u_copy(g):
        at = pl.ds(pl.multiple_of(g * gr, gr), gr)
        slot = lax.rem(g, 2)
        return pltpu.make_async_copy(u_hbm.at[at, :], ub.at[slot], u_sem.at[slot])

    x_in.start()
    u_copy(0).start()
    greet(n, n_tp, ep, tp)

    edges = [0]
    for ring in range(4):
        edges.append(edges[-1] + (3 * units // 128 + 3 - ring) // 4 * 128)
    wide_of = [edges[i + 1] - edges[i] for i in range(4)]

    def block_of(ring, step):
        if ring < 2:
            return ring_member(lax.rem(p + 2 * n - 1 - step, n), n)
        return ring_member(lax.rem(p + 1 + step, n), n)

    def term(ring, owner):
        lo, hi = edges[ring], edges[ring + 1]
        parts = []
        if lo < 2 * units:
            parts.append(block_dot(nt, owner, rows, pg[:, lo : min(hi, 2 * units)]))
        if hi > 2 * units:
            parts.append(block_dot(og, owner, rows, sh[:, max(lo - 2 * units, 0) : hi - 2 * units]))
        return parts[0] if len(parts) == 1 else jnp.concatenate(parts, axis=1)

    def ring_copy(ring, slot):
        return remote(
            ring_send.at[ring, slot, :, : wide_of[ring]],
            ring_recv.at[ring, slot, :, : wide_of[ring]],
            ring_ss.at[ring, slot],
            ring_rs.at[ring, slot],
            "ep",
            nxt if ring < 2 else prv,
        )

    order = (0, 2, 1, 3)

    def ring_step(step):
        slot, last = lax.rem(step, 2), lax.rem(step + 1, 2)
        for ring in order:
            size = wide_of[ring]
            mine = term(ring, block_of(ring, step))
            ring_copy(ring, last).wait_recv()

            @pl.when(step >= 2)
            def _():
                ring_copy(ring, slot).wait_send()

            ring_send[ring, slot, :, :size] = (
                mine + ring_recv[ring, last, :, :size].astype(F32)
            ).astype(BF)

            @pl.when(step <= n - 3)
            def _():
                pl.semaphore_signal(
                    free.at[ring],
                    1,
                    device_id={"ep": prv if ring < 2 else nxt},
                    device_id_type=pl.DeviceIdType.MESH,
                )

            @pl.when(step >= 2)
            def _():
                pl.semaphore_wait(free.at[ring], 1)

            ring_copy(ring, slot).start()

    for ring in order:
        ring_send[ring, 0, :, : wide_of[ring]] = term(ring, block_of(ring, 0)).astype(BF)
        ring_copy(ring, 0).start()

    for copy in w_in:
        copy.wait()
    x_in.wait()

    nt_dims, first_dims = (((1,), (1,)), ((), ())), (((0,), (0,)), ((), ()))

    def saved(g):
        at = pl.ds(pl.multiple_of(g * gr, gr), gr)
        slot = lax.rem(g, 2)
        return pltpu.make_async_copy(ub.at[slot], o_hbm.at[at, :], out_sem.at[slot])

    def back_copies(r):
        return block_copies(r, rbs, back, back_ss, back_rs, ep, tp, n, shape, zero, True)

    kept_copy = pltpu.make_async_copy(rbs.at[:capp, :], back.at[:capp, :], back_ss.at[0, 0])

    def gate_copy(r):
        return remote(
            gbs.at[r], g_back.at[r], gate_ss.at[r], gate_rs.at[r], "ep", lax.rem(ep + n - r, n)
        )

    g_kept = pltpu.make_async_copy(gbs.at[0], g_back.at[0], gate_ss.at[0])
    gbs[...] = jnp.zeros_like(gbs)

    @pl.loop(0, groups)
    def _(g):
        slot = lax.rem(g, 2)
        mine = pl.ds(pl.multiple_of(g * gr, gr), gr)
        u_copy(g).wait()

        @pl.when(g >= 1)
        def _():
            saved(g - 1).wait()

        @pl.when(g + 1 < groups)
        def _():
            u_copy(g + 1).start()

        gate = jnp.concatenate([gate_column(gates, g * per + i, capp) for i in range(per)], axis=0)
        rgb[mine, :] = (gate * ub[slot].astype(F32)).astype(BF)

        def hidden(at):
            x = xb[mine, :]
            g_pre = lax.dot_general(x, w[0, at, :], nt_dims, preferred_element_type=F32)
            u_pre = lax.dot_general(x, w[1, at, :], nt_dims, preferred_element_type=F32)
            grad = lax.dot_general(rgb[mine, :], w[2, at, :], nt_dims, preferred_element_type=F32)
            sig = jax.nn.sigmoid(g_pre)
            eb[2, mine, at] = (g_pre * sig * u_pre).astype(BF)
            eb[0, mine, at] = (grad * u_pre * sig * (1.0 + g_pre * (1.0 - sig))).astype(BF)
            eb[1, mine, at] = (grad * g_pre * sig).astype(BF)

        @pl.loop(0, units // 256)
        def _(c):
            hidden(pl.ds(pl.multiple_of(c * 256, 256), 256))

        if units % 256:
            hidden(pl.ds(units // 256 * 256, units % 256))

        def columns(c, total):
            at = pl.ds(pl.multiple_of(c * 256, 256), 256)
            out = jnp.dot(eb[2, mine, :], w[2, :, at], preferred_element_type=F32)
            grad = jnp.dot(eb[0, mine, :], w[0, :, at], preferred_element_type=F32) + jnp.dot(
                eb[1, mine, :], w[1, :, at], preferred_element_type=F32
            )
            rbs[mine, at] = grad.astype(BF)
            total = total + jnp.sum(out * ub[slot, :, at].astype(F32), axis=1, keepdims=True)
            ub[slot, :, at] = out.astype(BF)
            return total

        total = lax.fori_loop(0, width // 256, columns, jnp.zeros((gr, 1), F32))
        hi = total.astype(BF).astype(F32)
        lane = lax.broadcasted_iota(jnp.int32, (gr, 128), 1)
        terms = jnp.where(lane == 0, hi, jnp.where(lane == 1, total - hi, 0.0)).astype(BF)
        pick = (
            lax.broadcasted_iota(jnp.int32, (16, 128), 0) == lax.broadcasted_iota(jnp.int32, (16, 128), 1)
        ).astype(F32).astype(BF)
        turned = lax.dot_general(pick, terms, nt_dims, preferred_element_type=F32).astype(BF)
        for i in range(per):
            gbs[g * per + i, :, :capp] = turned[:, i * capp : (i + 1) * capp]
        saved(g).start()
        for i in range(per):
            r = g * per + i
            if i == 0:

                @pl.when(g == 0)
                def _():
                    kept_copy.start()
                    g_kept.start()

                @pl.when(g > 0)
                def _():
                    each(back_copies(r), "start")
                    gate_copy(r).start()
            else:
                each(back_copies(r), "start")
                gate_copy(r).start()

        @pl.when(lax.rem(g, 2) == 1)
        def _():
            ring_step((g + 1) // 2)

    def weight_rows(at):
        for k in range(3):
            for c in range(0, width, 512):
                w[k, at, c : c + 512] = lax.dot_general(
                    eb[k, :, at],
                    (rgb if k == 2 else xb)[:, c : c + 512],
                    first_dims,
                    preferred_element_type=F32,
                ).astype(BF)

    @pl.loop(0, units // 256)
    def _(c):
        weight_rows(pl.ds(pl.multiple_of(c * 256, 256), 256))

    if units % 256:
        weight_rows(pl.ds(units // 256 * 256, units % 256))

    dw_core = remote(
        w.at[:, : 2 * quarter, :], dw_recv, dw_ss.at[0], dw_rs.at[0], "tp", core_peer
    )
    dw_core.start()
    ring_step(groups // 2 + 1)
    dw_core.wait()
    dw_in = pltpu.make_async_copy(dw_recv, w.at[:, : 2 * quarter, :], dw_sem.at[0])
    dw_in.start()
    dw_in.wait()
    for k in range(3):

        @pl.loop(0, quarter // 32)
        def _(c, k=k):
            far = pl.ds(pl.multiple_of(2 * quarter + c * 32, 32), 32)
            came = pl.ds(pl.multiple_of(quarter + c * 32, 32), 32)
            w[k, far, :] = (w[k, far, :].astype(F32) + w[k, came, :].astype(F32)).astype(BF)

    dw_far = remote(
        w.at[:, 2 * quarter : 3 * quarter, :], dw_y, dw_ss.at[1], dw_rs.at[1], "tp", y_peer
    )
    dw_far.start()
    for k in range(3):

        @pl.loop(0, quarter // 32)
        def _(c, k=k):
            far = pl.ds(pl.multiple_of(3 * quarter + c * 32, 32), 32)
            came = pl.ds(pl.multiple_of(c * 32, 32), 32)
            w[k, far, :] = (w[k, far, :].astype(F32) + w[k, came, :].astype(F32)).astype(BF)

    dw_keep = pltpu.make_async_copy(w.at[:, 3 * quarter :, :], dw_own, dw_sem.at[1])
    dw_keep.start()

    @pl.loop(groups // 2 + 2, n - 1)
    def _(step):
        ring_step(step)

    for ring in order:
        mine = term(ring, ep)
        ring_copy(ring, n % 2).wait_recv()
        done = mine + ring_recv[ring, n % 2, :, : wide_of[ring]].astype(F32)
        lo, hi = edges[ring], edges[ring + 1]
        for k, out in enumerate((gu_out.at[0], gu_out.at[1], dn_out)):
            a, b = max(lo, k * units), min(hi, (k + 1) * units)
            if a < b:
                out[:, a - k * units : b - k * units] = done[:, a - lo : b - lo].astype(BF)
    for ring in range(4):
        for slot in range(2):
            ring_copy(ring, slot).wait_send()
    g_kept.wait()
    kept_copy.wait()
    saved(groups - 1).wait()
    dw_keep.wait()
    dw_far.wait()

    @pl.loop(1, n)
    def _(r):
        each(back_copies(r), "wait")
        gate_copy(r).wait()


def routed_expert(n, n_tp, shape, x, u, weights, gates, nt, pg, og, sh):
    total, width = x.shape
    units = 4 * weights[-1].shape[0]
    gr = total // 4
    rows = width // n
    half = (3 * units // 128 + 3) // 4 * 128
    vmem = pl.BlockSpec(memory_space=pltpu.VMEM)
    hbm = pl.BlockSpec(memory_space=pl.ANY)
    dma = pltpu.SemaphoreType.DMA
    if rows % 128:
        nt, og = nt.T, og.T
    return pl.pallas_call(
        functools.partial(middle_kernel, n, n_tp, shape),
        out_shape=(
            jax.ShapeDtypeStruct((total, width), BF),
            jax.ShapeDtypeStruct((n, 16, 128), BF),
            jax.ShapeDtypeStruct((total, width), BF),
            jax.ShapeDtypeStruct((3, units // 2, width), BF),
            jax.ShapeDtypeStruct((3, units // 4, width), BF),
            jax.ShapeDtypeStruct((3, units // 4, width), BF),
            jax.ShapeDtypeStruct((2, rows, units), BF),
            jax.ShapeDtypeStruct((rows, units), BF),
        ),
        in_specs=[hbm] * 10 + [vmem] * 5,
        out_specs=[hbm] * 6 + [vmem] * 2,
        scratch_shapes=[
            pltpu.VMEM((max(shape[0] - shape[1], 16), width), BF),
            pltpu.VMEM((3, units, width), BF),
            pltpu.VMEM((total, width), BF),
            pltpu.VMEM((2, gr, width), BF),
            pltpu.VMEM((total, width), BF),
            pltpu.VMEM((3, total, units), BF),
            pltpu.VMEM((total, width), BF),
            pltpu.VMEM((n, 16, 128), BF),
            pltpu.VMEM((4, 2, rows, half), BF),
            pltpu.VMEM((4, 2, rows, half), BF),
            dma((8,)),
            dma,
            dma((2,)),
            dma((2,)),
            dma((4, 2)),
            dma((4, 2)),
            pltpu.SemaphoreType.REGULAR((4,)),
            dma((3, n)),
            dma((3, n)),
            dma((n,)),
            dma((n,)),
            dma((2,)),
            dma((2,)),
            dma((2,)),
        ],
        compiler_params=pltpu.CompilerParams(
            collective_id=1, has_side_effects=True, vmem_limit_bytes=63 * 2**20
        ),
        cost_estimate=pl.CostEstimate(
            flops=2 * total * width * 6 * units, bytes_accessed=40 * 2**20, transcendentals=0
        ),
    )(x, u, *weights, gates, nt, pg, og, sh)


def tp_total(
    project, between, tp, core_send, core_recv, y_send, y_recv, summed,
    core_ss, core_rs, y_ss, y_rs, g_ss, g_rs,
):
    core_peer, y_peer = flip(tp, 1), flip(tp, 2)
    pieces, size = core_send.shape[0], core_send.shape[2]
    half = pieces * size

    def core_copy(i):
        return remote(core_send.at[i], core_recv.at[i], core_ss.at[i], core_rs.at[i], "tp", core_peer)

    def y_copy(i):
        return remote(y_send.at[i], y_recv.at[i], y_ss.at[i], y_rs.at[i], "tp", y_peer)

    def gather_copy(i, slot):
        return remote(summed.at[slot, i], summed.at[slot, i], g_ss.at[i], g_rs.at[i], "tp", core_peer)

    me, other = tp % 2, core_peer % 2
    for i in range(pieces):
        core_send[i] = project(other * half, i, size).astype(BF)
        core_copy(i).start()
        own = project(me * half, i, size)
        core_copy(i).wait_recv()
        y_send[i] = (own + core_recv[i].astype(F32)).astype(BF)
        y_copy(i).start()
    between()
    for i in range(pieces):
        y_copy(i).wait_recv()
        summed[me, i] = (y_send[i].astype(F32) + y_recv[i].astype(F32)).astype(BF)
        gather_copy(i, me).start()
    for i in range(pieces):
        gather_copy(i, other).wait_recv()
    for i in range(pieces):
        core_copy(i).wait_send()
        y_copy(i).wait_send()
        gather_copy(i, me).wait_send()


def blocks_at_once(n, capp):
    per = 1
    while 2 * per * capp <= 128 and n % (2 * per) == 0:
        per *= 2
    return per


def has_more(tp, source, expert, n_tp, extra):
    return lax.rem(tp + 64 * n_tp - source - expert, n_tp) < extra


def block_copies(r, src, dst, ss, rs, ep, tp, n, shape, zero, home):
    capp, base, extra, n_tp = shape
    on, back = lax.rem(ep + r, n), lax.rem(ep + n - r, n)
    to, come = (back, on) if home else (on, back)
    at = pl.ds(pl.multiple_of(r * capp, 16), base)
    out = [(None, None, remote(src.at[at, :], dst.at[at, :], ss.at[0, r], rs.at[0, r], "ep", to))]
    if base < capp:
        at = pl.ds(pl.multiple_of(r * capp + base, 16), capp - base)
        sends, gets = has_more(tp, ep, to, n_tp, extra), has_more(tp, ep, come, n_tp, extra)
        out.append((sends, gets, remote(src.at[at, :], dst.at[at, :], ss.at[1, r], rs.at[1, r], "ep", to)))
        fill = jnp.logical_not(gets)
        out.append((fill, None, pltpu.make_async_copy(zero, dst.at[at, :], ss.at[2, r])))
    return out


def each(copies, verb):
    for sends, gets, copy in copies:
        if sends is None:
            getattr(copy, verb)()
        elif gets is None or verb == "start":
            pl.when(sends)(getattr(copy, verb))
        else:
            pl.when(sends)(copy.wait_send)
            pl.when(gets)(copy.wait_recv)


def fetch_late(kernel, late):
    def wrapped(*refs):
        refs, held, sems = refs[: -len(late) - 1], refs[-len(late) - 1 : -1], refs[-1]
        copies = [pltpu.make_async_copy(refs[at], held[i], sems.at[i]) for i, at in enumerate(late)]
        for copy in copies:
            copy.start()

        def ready():
            for copy in copies:
                copy.wait()

        refs = list(refs)
        for i, at in enumerate(late):
            refs[at] = held[i]
        kernel(ready, *refs)

    return wrapped


def late_scratch(operands, late):
    return [pltpu.VMEM(operands[at].shape, operands[at].dtype) for at in late] + [
        pltpu.SemaphoreType.DMA((len(late),))
    ]


def specs(count, apart):
    return [pl.BlockSpec(memory_space=pl.ANY if i in apart else pltpu.VMEM) for i in range(count)]


SEND_ORDER = (4, 5, 6, 7, 2, 3, 1, 0)


def send_order(i, n, ep):
    if n != len(SEND_ORDER):
        return (i + 1) % n
    to = ep
    for bit in (1, 2, 4):
        if SEND_ORDER[i] & bit:
            to = to + bit - 2 * bit * ((to // bit) % 2)
    return lax.rem(to + n - ep, n)


def gate_column(tiles, r, capp):
    ones = jnp.ones((16, 128), BF)
    return lax.dot_general(
        tiles[r, :, :capp], ones, (((0,), (0,)), ((), ())), preferred_element_type=F32
    )[:, :1]


def front_kernel(
    n,
    n_tp,
    shape,
    ready,
    hidden,
    gain1,
    gain2,
    w,
    bias,
    cosine,
    sine,
    prefix,
    ow,
    place,
    cot,
    gu_own,
    dn_own,
    pairs,
    up_rows,
    gu_a,
    dn_a,
    dn_b,
    n1,
    qkv,
    ctx,
    mid,
    nt,
    factor_one,
    split,
    pair_in,
    pair_out,
    pair_si,
    pair_so,
    zero,
    up_sent,
    core_send,
    core_recv,
    y_send,
    y_recv,
    summed,
    up_ss,
    up_rs,
    w_ss,
    w_rs,
    core_ss,
    core_rs,
    y_ss,
    y_rs,
    g_ss,
    g_rs,
):
    ep = lax.axis_index("ep")
    tp = lax.axis_index("tp")
    tokens, width = hidden.shape
    lw = ctx.shape[1]
    heads = lw // HEAD_DIM
    core_peer, y_peer = flip(tp, 1), flip(tp, 2)
    greet(n, n_tp, ep, tp)

    capp = shape[0]
    zero[...] = jnp.zeros_like(zero)

    def up_copies(r):
        return block_copies(r, up_sent, up_rows, up_ss, up_rs, ep, tp, n, shape, zero, False)

    kept = pltpu.make_async_copy(up_sent.at[:capp, :], up_rows.at[:capp, :], up_ss.at[0, 0])
    per = blocks_at_once(n, capp)
    size = per * capp

    for i in range(n // per):
        b = send_order(i, n, ep) if per == 1 else i
        at = pl.ds(pl.multiple_of(b * size, size), size)
        up_sent[at, :] = jnp.dot(place[at, :], cot[...], preferred_element_type=F32).astype(BF)
        for j in range(per):
            if i == (n - 1 if per == 1 else 0) and j == 0:
                kept.start()
            else:
                each(up_copies(b * per + j), "start")

    w_copies = [
        remote(dn_own, dn_b, w_ss.at[0], w_rs.at[0], "tp", y_peer),
        remote(dn_own, dn_a, w_ss.at[1], w_rs.at[1], "tp", core_peer),
        remote(gu_own, gu_a, w_ss.at[2], w_rs.at[2], "tp", core_peer),
    ]
    for copy in w_copies:
        copy.start()

    chunk = pair_in.shape[1]
    chunks = pairs.shape[0] // chunk

    def pair_load(i):
        at, slot = pl.ds(pl.multiple_of(i * chunk, chunk), chunk), lax.rem(i, 2)
        return pltpu.make_async_copy(pairs.at[at], pair_in.at[slot], pair_si.at[slot])

    def pair_store(i):
        at, slot = pl.ds(pl.multiple_of(i * chunk, chunk), chunk), lax.rem(i, 2)
        return pltpu.make_async_copy(pair_out.at[slot], split.at[:, at, :], pair_so.at[slot])

    def set_apart(first, last):
        @pl.loop(first, last)
        def _(i):
            slot = lax.rem(i, 2)

            @pl.when(i + 1 < chunks)
            def _():
                pair_load(i + 1).start()

            pair_load(i).wait()

            @pl.when(i >= 2)
            def _():
                pair_store(i - 2).wait()

            pair_out[slot, 0] = pair_in[slot, :, 0, :]
            pair_out[slot, 1] = pair_in[slot, :, 1, :]
            pair_store(i).start()

    pair_load(0).start()
    ready()

    @pl.loop(0, tokens // 64)
    def _(m):
        at = pl.ds(pl.multiple_of(m * 64, 64), 64)
        h = hidden[at, :].astype(F32)
        factor = lax.rsqrt(jnp.sum(h * h, axis=1, keepdims=True) * (1.0 / width) + EPSILON)
        factor_one[at, :] = factor
        n1[at, :] = (h * factor * gain1[...]).astype(BF)

    for k in range(3):

        @pl.loop(0, lw // 256)
        def _(c, k=k):
            at = pl.ds(pl.multiple_of(c * 256, 256), 256)
            x = jnp.dot(n1[...], w[k, :, at], preferred_element_type=F32) + bias[k : k + 1, at]
            if k < 2:
                x = jnp.concatenate(
                    [
                        x[:, i * HEAD_DIM : (i + 1) * HEAD_DIM] * cosine[...]
                        + pltpu.roll(x[:, i * HEAD_DIM : (i + 1) * HEAD_DIM], HEAD_DIM // 2, 1) * sine[...]
                        for i in range(256 // HEAD_DIM)
                    ],
                    axis=1,
                )
            qkv[k, :, at] = x.astype(BF)

    @pl.loop(0, tokens // 128)
    def _(m):
        at = pl.ds(pl.multiple_of(m * 128, 128), 128)
        row = lax.broadcasted_iota(jnp.int32, (128, tokens), 0) + m * 128
        col = lax.broadcasted_iota(jnp.int32, (128, tokens), 1)
        visible = (col <= row) | (col < prefix[...])
        for i in range(heads):
            lanes = slice(i * HEAD_DIM, (i + 1) * HEAD_DIM)
            s = lax.dot_general(
                qkv[0, at, lanes], qkv[1, :, lanes], (((1,), (1,)), ((), ())), preferred_element_type=F32
            )
            s = jnp.where(visible, s * HEAD_DIM ** (-0.5), -1e30)
            e = jnp.exp(s - jnp.max(s, axis=1, keepdims=True))
            e = e * (1.0 / jnp.sum(e, axis=1, keepdims=True))
            ctx[at, lanes] = jnp.dot(
                e.astype(BF), qkv[2, :, lanes], preferred_element_type=F32
            ).astype(BF)

    pieces, size = core_send.shape[0], core_send.shape[2]
    half = pieces * size

    def project(base, i, size):
        at = pl.ds(pl.multiple_of(base + i * size, size), size)
        return lax.dot_general(
            ctx[...], ow[at, :], (((1,), (1,)), ((), ())), preferred_element_type=F32
        )

    tp_total(
        project, lambda: set_apart(0, chunks * 11 // 16), tp, core_send, core_recv, y_send, y_recv, summed,
        core_ss, core_rs, y_ss, y_rs, g_ss, g_rs,
    )

    @pl.loop(0, tokens // 32)
    def _(m):
        at = pl.ds(pl.multiple_of(m * 32, 32), 32)
        total = jnp.zeros((32, 1), F32)
        for j in range(2):
            for i in range(pieces):
                lanes = slice(j * half + i * size, j * half + (i + 1) * size)
                x = hidden[at, lanes].astype(F32) + summed[j, i, at, :].astype(F32)
                mid[at, lanes] = x
                total = total + jnp.sum(x * x, axis=1, keepdims=True)
        factor = lax.rsqrt(total * (1.0 / width) + EPSILON)
        nt[at, :] = (mid[at, :] * factor * gain2[...]).astype(BF)

    set_apart(chunks * 11 // 16, chunks)
    pair_store(chunks - 2).wait()
    pair_store(chunks - 1).wait()
    for copy in w_copies:
        copy.wait()
    kept.wait()
    for r in range(1, n):
        each(up_copies(r), "wait")


def front(n, n_tp, shape, hidden, gain1, gain2, w, bias, cosine, sine, prefix, ow, place, cot, gu_own, dn_own, pairs):
    tokens, width = hidden.shape
    lw = ow.shape[1]
    quarter = dn_own.shape[0]
    vmem = pl.BlockSpec(memory_space=pltpu.VMEM)
    hbm = pl.BlockSpec(memory_space=pl.ANY)
    dma = pltpu.SemaphoreType.DMA
    operands = (hidden, gain1, gain2, w, bias, cosine, sine, prefix, ow, place, cot, gu_own, dn_own, pairs)
    late = (0, 3, 8)
    return pl.pallas_call(
        fetch_late(functools.partial(front_kernel, n, n_tp, shape), late),
        out_shape=(
            jax.ShapeDtypeStruct((n * shape[0], width), BF),
            jax.ShapeDtypeStruct((2, quarter, width), BF),
            jax.ShapeDtypeStruct((quarter, width), BF),
            jax.ShapeDtypeStruct((quarter, width), BF),
            jax.ShapeDtypeStruct((tokens, width), BF),
            jax.ShapeDtypeStruct((3, tokens, lw), BF),
            jax.ShapeDtypeStruct((tokens, lw), BF),
            jax.ShapeDtypeStruct((tokens, width), F32),
            jax.ShapeDtypeStruct((tokens, width), BF),
            jax.ShapeDtypeStruct((tokens, 1), F32),
            jax.ShapeDtypeStruct((2, width, pairs.shape[2]), BF),
        ),
        in_specs=specs(14, (0, 3, 8, 11, 12, 13)),
        out_specs=[hbm] * 4 + [vmem] * 6 + [hbm],
        scratch_shapes=[
            pltpu.VMEM((2, 128, 2, pairs.shape[2]), BF),
            pltpu.VMEM((2, 2, 128, pairs.shape[2]), BF),
            dma((2,)),
            dma((2,)),
            pltpu.VMEM((max(shape[0] - shape[1], 16), width), BF),
            pltpu.VMEM((n * shape[0], width), BF),
            pltpu.VMEM((4, tokens, width // 8), BF),
            pltpu.VMEM((4, tokens, width // 8), BF),
            pltpu.VMEM((4, tokens, width // 8), BF),
            pltpu.VMEM((4, tokens, width // 8), BF),
            pltpu.VMEM((2, 4, tokens, width // 8), BF),
            dma((3, n)),
            dma((3, n)),
            dma((3,)),
            dma((3,)),
            dma((4,)),
            dma((4,)),
            dma((4,)),
            dma((4,)),
            dma((4,)),
            dma((4,)),
        ]
        + late_scratch(operands, late),
        compiler_params=pltpu.CompilerParams(
            collective_id=2, has_side_effects=True, vmem_limit_bytes=56 * 2**20
        ),
        cost_estimate=pl.CostEstimate(
            flops=2 * tokens * width * 4 * lw, bytes_accessed=30 * 2**20, transcendentals=0
        ),
    )(*operands)


def dispatch_kernel(
    n,
    n_tp,
    shape,
    n_exp,
    ready,
    nt,
    place,
    router,
    cot,
    sgu,
    sdn,
    gu_own,
    dn_b,
    dest_t,
    x_rows,
    g_rows,
    gu_b,
    gu_c,
    dn_c,
    probs,
    place_t,
    weighted,
    og,
    pg,
    sh,
    part,
    sback,
    sgrad,
    zero,
    gate,
    x_send,
    g_send,
    x_ss,
    x_rs,
    gate_ss,
    gate_rs,
    w_ss,
    w_rs,
):
    ep = lax.axis_index("ep")
    tp = lax.axis_index("tp")
    tokens, width = nt.shape
    units = sdn.shape[1]
    total = place.shape[0]
    core_peer, y_peer = flip(tp, 1), flip(tp, 2)
    greet(n, n_tp, ep, tp)
    w_y = remote(gu_own, gu_b, w_ss.at[0], w_rs.at[0], "tp", y_peer)
    w_y.start()
    w_on = remote(dn_b, dn_c, w_ss.at[1], w_rs.at[1], "tp", core_peer)
    w_on.start()

    capp = shape[0]
    zero[...] = jnp.zeros_like(zero)

    def x_copies(r):
        return block_copies(r, x_send, x_rows, x_ss, x_rs, ep, tp, n, shape, zero, False)

    def gate_copy(r, way):
        to = lax.rem(ep + r, n) if way == "out" else lax.rem(ep + n - r, n)
        return remote(g_send.at[r], g_rows.at[r], gate_ss.at[r], gate_rs.at[r], "ep", to)

    kept = pltpu.make_async_copy(x_send.at[:capp, :], x_rows.at[:capp, :], x_ss.at[0, 0])
    g_kept = pltpu.make_async_copy(g_send.at[0], g_rows.at[0], gate_ss.at[0])
    per = blocks_at_once(n, capp)
    size = per * capp

    for i in range(n // per):
        b = send_order(i, n, ep) if per == 1 else i
        at = pl.ds(pl.multiple_of(b * size, size), size)
        x_send[at, :] = jnp.dot(place[at, :], nt[...], preferred_element_type=F32).astype(BF)
        for j in range(per):
            if i == (n - 1 if per == 1 else 0) and j == 0:
                kept.start()
            else:
                each(x_copies(b * per + j), "start")

    ready()

    logits = jnp.dot(nt[...], router[...], preferred_element_type=F32)
    lane = lax.broadcasted_iota(jnp.int32, logits.shape, 1)
    chosen = jnp.where(lane < n_exp, logits, -1e30)
    e = jnp.exp(chosen - jnp.max(chosen, axis=1, keepdims=True))
    prob = e / jnp.sum(e, axis=1, keepdims=True)
    prob = jnp.where(lane == n_exp, jax.nn.sigmoid(logits), prob)
    probs[...] = prob
    hi = prob.astype(BF)
    lo = (prob - hi.astype(F32)).astype(BF)
    g_send[...] = jnp.zeros_like(g_send)
    across = (((0,), (1,)), ((), ()))

    for r in range(n):
        where = place[r * capp : (r + 1) * capp, :]
        pick = lax.broadcasted_iota(jnp.int32, (128, capp), 0) == lax.rem(r + ep, n)
        g_hi = jnp.sum(
            jnp.where(pick, lax.dot_general(hi, where, across, preferred_element_type=F32), 0.0),
            axis=0,
            keepdims=True,
        )
        g_lo = jnp.sum(
            jnp.where(pick, lax.dot_general(lo, where, across, preferred_element_type=F32), 0.0),
            axis=0,
            keepdims=True,
        )
        term = lax.broadcasted_iota(jnp.int32, (16, capp), 0)
        g_send[r, :, :capp] = jnp.where(term == 0, g_hi, jnp.where(term == 1, g_lo, 0.0)).astype(BF)
        gate[:, r * capp : (r + 1) * capp] = g_hi + g_lo
        if r == 0:
            g_kept.start()
        else:
            gate_copy(r, "out").start()

    @pl.loop(0, tokens // 64)
    def _(m):
        at = pl.ds(pl.multiple_of(m * 64, 64), 64)
        og[at, :] = (probs[at, n_exp : n_exp + 1] * cot[at, :].astype(F32)).astype(BF)

    def hidden(at, up_at):
        g_pre = jnp.dot(nt[...], sgu[0, :, at], preferred_element_type=F32)
        u_pre = jnp.dot(nt[...], sgu[1, :, at], preferred_element_type=F32)
        grad = jnp.dot(og[...], sdn[:, at], preferred_element_type=F32)
        sig = jax.nn.sigmoid(g_pre)
        sh[:, at] = (g_pre * sig * u_pre).astype(BF)
        pg[:, at] = (grad * u_pre * sig * (1.0 + g_pre * (1.0 - sig))).astype(BF)
        pg[:, up_at] = (grad * g_pre * sig).astype(BF)

    @pl.loop(0, units // 256)
    def _(c):
        hidden(
            pl.ds(pl.multiple_of(c * 256, 256), 256),
            pl.ds(pl.multiple_of(c * 256 + units, 128), 256),
        )

    if units % 256:
        rest = units // 256 * 256
        hidden(pl.ds(rest, units - rest), pl.ds(units + rest, units - rest))

    nt_dims = (((1,), (1,)), ((), ()))

    share = probs[:, n_exp : n_exp + 1]

    def columns(c, total):
        at = pl.ds(pl.multiple_of(c * 256, 256), 256)
        out = lax.dot_general(sh[...], sdn[at, :], nt_dims, preferred_element_type=F32)
        part[:, at] = (share * out).astype(BF)
        sback[:, at] = lax.dot_general(
            pg[:, :units], sgu[0, at, :], nt_dims, preferred_element_type=F32
        ) + lax.dot_general(pg[:, units:], sgu[1, at, :], nt_dims, preferred_element_type=F32)
        return total + jnp.sum(cot[:, at].astype(F32) * out, axis=1, keepdims=True)

    sgrad[...] = lax.fori_loop(0, width // 256, columns, jnp.zeros((tokens, 1), F32))

    @pl.loop(0, total // 128)
    def _(c):
        at = pl.ds(pl.multiple_of(c * 128, 128), 128)
        spot = lax.broadcasted_iota(jnp.int32, (tokens, 128), 1) + c * 128
        hit = dest_t[:, :1] == spot
        for k in range(1, dest_t.shape[1]):
            hit = hit | (dest_t[:, k : k + 1] == spot)
        place_t[:, at] = jnp.where(hit, 1.0, 0.0).astype(BF)
        weighted[:, at] = jnp.where(hit, gate[:, at], 0.0).astype(BF)

    w_y.wait()
    w_far = remote(gu_b, gu_c, w_ss.at[2], w_rs.at[2], "tp", core_peer)
    w_far.start()
    w_on.wait()
    w_far.wait()
    kept.wait()
    g_kept.wait()

    @pl.loop(1, n)
    def _(r):
        gate_copy(r, "in").wait()
        each(x_copies(r), "wait")


def dispatch(n, n_tp, shape, n_exp, nt, place, router, cot, sgu, sdn, gu_own, dn_b, dest_t):
    tokens, width = nt.shape
    units = sdn.shape[1]
    total = place.shape[0]
    vmem = pl.BlockSpec(memory_space=pltpu.VMEM)
    hbm = pl.BlockSpec(memory_space=pl.ANY)
    dma = pltpu.SemaphoreType.DMA
    operands = (nt, place, router, cot, sgu, sdn, gu_own, dn_b, dest_t)
    late = (2, 3, 4, 5)
    return pl.pallas_call(
        fetch_late(functools.partial(dispatch_kernel, n, n_tp, shape, n_exp), late),
        out_shape=(
            jax.ShapeDtypeStruct((total, width), BF),
            jax.ShapeDtypeStruct((n, 16, 128), BF),
            jax.ShapeDtypeStruct(gu_own.shape, BF),
            jax.ShapeDtypeStruct(gu_own.shape, BF),
            jax.ShapeDtypeStruct(dn_b.shape, BF),
            jax.ShapeDtypeStruct((tokens, 128), F32),
            jax.ShapeDtypeStruct((tokens, total), BF),
            jax.ShapeDtypeStruct((tokens, total), BF),
            jax.ShapeDtypeStruct((tokens, width), BF),
            jax.ShapeDtypeStruct((tokens, 2 * units), BF),
            jax.ShapeDtypeStruct((tokens, units), BF),
            jax.ShapeDtypeStruct((tokens, width), BF),
            jax.ShapeDtypeStruct((tokens, width), F32),
            jax.ShapeDtypeStruct((tokens, 1), F32),
        ),
        in_specs=specs(9, (2, 3, 4, 5, 6, 7)),
        out_specs=[hbm] * 5 + [vmem] * 9,
        scratch_shapes=[
            pltpu.VMEM((max(shape[0] - shape[1], 16), width), BF),
            pltpu.VMEM((1, total), F32),
            pltpu.VMEM((total, width), BF),
            pltpu.VMEM((n, 16, 128), BF),
            dma((3, n)),
            dma((3, n)),
            dma((n,)),
            dma((n,)),
            dma((3,)),
            dma((3,)),
        ]
        + late_scratch(operands, late),
        compiler_params=pltpu.CompilerParams(
            collective_id=3, has_side_effects=True, vmem_limit_bytes=60 * 2**20
        ),
        cost_estimate=pl.CostEstimate(
            flops=2 * tokens * width * 6 * units, bytes_accessed=40 * 2**20, transcendentals=0
        ),
    )(*operands)


def backward_kernel(
    n,
    n_tp,
    shape,
    n_exp,
    ready,
    back,
    g_back,
    place_t,
    sback,
    sgrad,
    probs,
    router,
    nt,
    mid,
    cot,
    gain2,
    qkv,
    ow,
    cosine,
    sine,
    prefix,
    o_sent,
    o_rows,
    ag,
    lg,
    bias,
    small,
    zero,
    core_send,
    core_recv,
    y_send,
    y_recv,
    summed,
    few_send,
    few_recv,
    ng,
    cg,
    dk,
    dv,
    o_ss,
    o_rs,
    core_ss,
    core_rs,
    y_ss,
    y_rs,
    g_ss,
    g_rs,
    few_ss,
    few_rs,
):
    ep = lax.axis_index("ep")
    tp = lax.axis_index("tp")
    tokens, width = nt.shape
    total = back.shape[0]
    lw = ow.shape[1]
    heads = lw // HEAD_DIM
    core_peer, y_peer = flip(tp, 1), flip(tp, 2)
    greet(n, n_tp, ep, tp)

    capp = shape[0]
    zero[...] = jnp.zeros_like(zero)

    def o_copies(r):
        return block_copies(r, o_sent, o_rows, o_ss, o_rs, ep, tp, n, shape, zero, True)

    kept = pltpu.make_async_copy(o_sent.at[:capp, :], o_rows.at[:capp, :], o_ss.at[0, 0])

    for i in range(n - 1):
        each(o_copies(send_order(i, n, ep)), "start")
    kept.start()
    ready()

    row = lax.broadcasted_iota(jnp.int32, (total, 128), 0)
    spot = lax.broadcasted_iota(jnp.int32, (total, 128), 1)
    expert = lax.rem(row // capp + ep * (n_exp // n), n_exp)
    gg = jnp.concatenate([gate_column(g_back, r, capp) for r in range(n)], axis=0)
    few = jnp.dot(
        place_t[...], jnp.where(spot == expert, gg, 0.0).astype(BF), preferred_element_type=F32
    )
    lane = lax.broadcasted_iota(jnp.int32, (tokens, 128), 1)
    few_send[0] = jnp.where(lane == n_exp, sgrad[...], few).astype(BF)
    few_core = remote(few_send.at[0], few_recv.at[0], few_ss.at[0], few_rs.at[0], "tp", core_peer)
    few_core.start()

    def project(base, i, size):
        at = pl.ds(pl.multiple_of(base + i * size, size), size)
        return sback[:, at] + jnp.dot(place_t[...], back[:, at], preferred_element_type=F32)

    def between():
        few_core.wait()
        few_send[1] = (few_send[0].astype(F32) + few_recv[0].astype(F32)).astype(BF)
        few_y = remote(few_send.at[1], few_recv.at[1], few_ss.at[1], few_rs.at[1], "tp", y_peer)
        few_y.start()
        few_y.wait()

    tp_total(
        project, between, tp, core_send, core_recv, y_send, y_recv, summed,
        core_ss, core_rs, y_ss, y_rs, g_ss, g_rs,
    )

    prob = jnp.where(lane < n_exp, probs[...], 0.0)
    share = probs[:, n_exp : n_exp + 1]
    grads = few_send[1].astype(F32) + few_recv[1].astype(F32)
    inner = jnp.sum(prob * grads, axis=1, keepdims=True)
    gate_in = grads * share * (1.0 - share)
    few_send[0] = jnp.where(
        lane < n_exp, prob * (grads - inner), jnp.where(lane == n_exp, gate_in, 0.0)
    ).astype(BF)
    pieces, size = summed.shape[1], summed.shape[3]
    for j in range(2):
        for i in range(pieces):
            at = slice((j * pieces + i) * size, (j * pieces + i + 1) * size)
            ng[:, at] = summed[j, i].astype(F32) + lax.dot_general(
                few_send[0], router[at, :], (((1,), (1,)), ((), ())), preferred_element_type=F32
            )

    step = 32

    def norm_rows(m, acc):
        at = pl.ds(pl.multiple_of(m * step, step), step)
        h = mid[at, :]
        grad = ng[at, :]
        factor = lax.rsqrt(jnp.sum(h * h, axis=1, keepdims=True) * (1.0 / width) + EPSILON)
        scaled = grad * gain2[...]
        mean = jnp.sum(scaled * h, axis=1, keepdims=True) * (1.0 / width)
        ag[at, :] = (
            cot[at, :].astype(F32) + factor * scaled - h * (factor * factor * factor) * mean
        ).astype(BF)
        return acc + jnp.sum((grad * h * factor).reshape(step // 8, 8, width), axis=0)

    acc = lax.fori_loop(0, tokens // step, norm_rows, jnp.zeros((8, width), F32))

    @pl.loop(0, lw // 256)
    def _(c):
        at = pl.ds(pl.multiple_of(c * 256, 256), 256)
        cg[:, at] = jnp.dot(ag[...], ow[:, at], preferred_element_type=F32).astype(BF)

    dk[...] = jnp.zeros_like(dk)
    dv[...] = jnp.zeros_like(dv)
    first_dims, last_dims = (((0,), (0,)), ((), ())), (((1,), (1,)), ((), ()))

    def attend(m, sums):
        at = pl.ds(pl.multiple_of(m * 128, 128), 128)
        row = lax.broadcasted_iota(jnp.int32, (128, tokens), 0) + m * 128
        col = lax.broadcasted_iota(jnp.int32, (128, tokens), 1)
        visible = (col <= row) | (col < prefix[...])
        parts = []
        for i in range(heads):
            lanes = slice(i * HEAD_DIM, (i + 1) * HEAD_DIM)
            q, grad = qkv[0, at, lanes], cg[at, lanes]
            s = lax.dot_general(q, qkv[1, :, lanes], last_dims, preferred_element_type=F32)
            s = jnp.where(visible, s * HEAD_DIM ** (-0.5), -1e30)
            e = jnp.exp(s - jnp.max(s, axis=1, keepdims=True))
            e = e * (1.0 / jnp.sum(e, axis=1, keepdims=True))
            dp = lax.dot_general(grad, qkv[2, :, lanes], last_dims, preferred_element_type=F32)
            delta = jnp.sum(e * dp, axis=1, keepdims=True)
            ds = (e * (dp - delta)).astype(BF)
            dv[:, lanes] += lax.dot_general(e.astype(BF), grad, first_dims, preferred_element_type=F32)
            dk[:, lanes] += lax.dot_general(ds, q, first_dims, preferred_element_type=F32)
            dq = jnp.dot(ds, qkv[1, :, lanes], preferred_element_type=F32) * HEAD_DIM ** (-0.5)
            dq = dq * cosine[at, :] - pltpu.roll(dq, HEAD_DIM // 2, 1) * sine[at, :]
            lg[at, lanes] = dq.astype(BF)
            parts.append(jnp.sum(dq.reshape(16, 8, HEAD_DIM), axis=0))
        return sums + jnp.concatenate(parts, axis=1)

    sums = lax.fori_loop(0, tokens // 128, attend, jnp.zeros((8, lw), F32))
    bias[:, :lw] = jnp.sum(sums, axis=0, keepdims=True)
    for i in range(heads):
        lanes = slice(i * HEAD_DIM, (i + 1) * HEAD_DIM)
        grad = dk[:, lanes] * HEAD_DIM ** (-0.5)
        grad = grad * cosine[...] - pltpu.roll(grad, HEAD_DIM // 2, 1) * sine[...]
        at = slice(lw + i * HEAD_DIM, lw + (i + 1) * HEAD_DIM)
        lg[:, at] = grad.astype(BF)
        bias[:, at] = jnp.sum(grad, axis=0, keepdims=True)
    lg[:, 2 * lw :] = dv[...].astype(BF)
    bias[:, 2 * lw :] = jnp.sum(dv[...], axis=0, keepdims=True)

    wide, span = small.shape[1:]
    gain_row = jnp.sum(acc, axis=0, keepdims=True)
    rows = lax.dot_general(few_send[0], nt[...], first_dims, preferred_element_type=F32)[:wide]
    index = lax.broadcasted_iota(jnp.int32, rows.shape, 0)
    rows = jnp.where(index == n_exp + 1, gain_row, rows).astype(BF)
    for r in range(n):
        small[r] = rows[:, r * span : (r + 1) * span]

    kept.wait()
    for r in range(1, n):
        each(o_copies(r), "wait")


def backward(n, n_tp, shape, n_exp, back, g_back, place_t, sback, sgrad, probs, router, nt, mid, cot, gain2, qkv, ow, cosine, sine, prefix, o_sent):
    tokens, width = nt.shape
    lw = ow.shape[1]
    wide = -(-(n_exp + 2) // 16) * 16
    vmem = pl.BlockSpec(memory_space=pltpu.VMEM)
    hbm = pl.BlockSpec(memory_space=pl.ANY)
    dma = pltpu.SemaphoreType.DMA
    piece = (4, tokens, width // 8)
    operands = (back, g_back, place_t, sback, sgrad, probs, router, nt, mid, cot, gain2, qkv, ow, cosine, sine, prefix, o_sent)
    late = (0, 2, 3, 6, 7, 8, 9, 11, 12)
    return pl.pallas_call(
        fetch_late(functools.partial(backward_kernel, n, n_tp, shape, n_exp), late),
        out_shape=(
            jax.ShapeDtypeStruct(o_sent.shape, BF),
            jax.ShapeDtypeStruct((tokens, width), BF),
            jax.ShapeDtypeStruct((tokens, 3 * lw), BF),
            jax.ShapeDtypeStruct((1, 3 * lw), F32),
            jax.ShapeDtypeStruct((n, wide, width // n), BF),
        ),
        in_specs=specs(17, (0, 2, 3, 6, 7, 8, 9, 11, 12, 16)),
        out_specs=[hbm] + [vmem] * 4,
        scratch_shapes=[
            pltpu.VMEM((max(shape[0] - shape[1], 16), width), BF),
            pltpu.VMEM(piece, BF),
            pltpu.VMEM(piece, BF),
            pltpu.VMEM(piece, BF),
            pltpu.VMEM(piece, BF),
            pltpu.VMEM((2,) + piece, BF),
            pltpu.VMEM((2, tokens, 128), BF),
            pltpu.VMEM((2, tokens, 128), BF),
            pltpu.VMEM((tokens, width), F32),
            pltpu.VMEM((tokens, lw), BF),
            pltpu.VMEM((tokens, lw), F32),
            pltpu.VMEM((tokens, lw), F32),
            dma((3, n)),
            dma((3, n)),
            dma((4,)),
            dma((4,)),
            dma((4,)),
            dma((4,)),
            dma((4,)),
            dma((4,)),
            dma((2,)),
            dma((2,)),
        ]
        + late_scratch(operands, late),
        compiler_params=pltpu.CompilerParams(
            collective_id=4, has_side_effects=True, vmem_limit_bytes=60 * 2**20
        ),
        cost_estimate=pl.CostEstimate(
            flops=2 * tokens * width * 4 * lw, bytes_accessed=30 * 2**20, transcendentals=0
        ),
    )(*operands)


def body(
    hidden,
    attn_gain,
    qkv_weight,
    qkv_bias,
    out_weight,
    mlp_gain,
    router_weight,
    share_gate,
    shared_gate_up,
    shared_down,
    expert_gate_up,
    expert_down,
    routes,
    priority,
    prefix,
    cotangent,
):
    tokens, width = hidden.shape
    n_ep = lax.axis_size("ep")
    n_tp = lax.axis_size("tp")
    tp_i = lax.axis_index("tp")
    local_width = qkv_weight.shape[2]
    expert_local = expert_gate_up.shape[0]
    n_exp = expert_local * n_ep
    top = routes.shape[1]
    capacity = (5 * tokens * top + 4 * n_exp - 1) // (4 * n_exp)
    tiles = -(-capacity // 16)
    least, extra = 16 * (tiles // n_tp), tiles % n_tp
    part_pad = least + (16 if extra else 0)
    shape = (part_pad, least, extra, n_tp)
    rows = n_exp * part_pad

    flat_route = routes.T.reshape(-1)
    flat_order = priority.T.reshape(-1)
    hits = (flat_route[:, None] == jnp.arange(n_exp, dtype=jnp.int32)[None, :]).astype(BF)
    smaller = (flat_order[None, :] < flat_order[:, None]).astype(BF)
    counts = mm(smaller, hits, 1, 0)
    slot = jnp.sum(counts * hits.astype(F32), axis=1).astype(jnp.int32).reshape(top, tokens)
    kept = slot < capacity
    ep_i = lax.axis_index("ep")
    more = [has_more(j, ep_i, routes.T // expert_local, n_tp, extra) for j in range(n_tp)]
    more.append(has_more(tp_i, ep_i, routes.T // expert_local, n_tp, extra))
    start = tp_i * least
    for j in range(n_tp):
        start = start + 16 * (more[j] & (j < tp_i)).astype(jnp.int32)
    in_part = slot - start
    mine = kept & (in_part >= 0) & (in_part < least + 16 * more[-1].astype(jnp.int32))
    hop = lax.rem(routes.T + n_exp - ep_i * expert_local, n_exp)
    dest = jnp.where(mine, hop * part_pad + in_part, -1)
    row_ids = jnp.arange(rows, dtype=jnp.int32)[:, None]
    place = (dest[0][None, :] == row_ids)
    for k in range(1, top):
        place = place | (dest[k][None, :] == row_ids)
    place = place.astype(BF)

    cos_all, sin_all = angle_tables(tokens, HEAD_DIM)
    w_t = jnp.transpose(qkv_weight, (1, 0, 2))
    prefix_row = jnp.broadcast_to(prefix[None], (1, tokens))
    gu_own = jnp.transpose(expert_gate_up[0], (1, 2, 0))
    dn_own = jnp.transpose(expert_down[0], (1, 0))
    up_rows, gu_a, dn_a, dn_b, normed_one, qkv, context, middle, normed_two, factor_one, sgu = front(
        n_ep,
        n_tp,
        shape,
        hidden,
        attn_gain[None],
        mlp_gain[None],
        w_t,
        qkv_bias,
        cos_all,
        sin_all,
        prefix_row,
        out_weight,
        place,
        cotangent,
        gu_own,
        dn_own,
        shared_gate_up,
    )

    router_all = jnp.concatenate(
        [router_weight, share_gate[:, None], jnp.zeros((width, 127 - n_exp), BF)], axis=1
    )
    got, gates, gu_b, gu_c, dn_c, probs_all, place_t, weighted_place, shared_out_grad, pre_grad, shared_hidden, scaled_part, shared_back, scale_grad = (
        dispatch(
            n_ep,
            n_tp,
            shape,
            n_exp,
            normed_two,
            place,
            router_all,
            cotangent,
            sgu,
            shared_down,
            gu_own,
            dn_b,
            dest.T,
        )
    )
    back_rows, back_gates, e_out, _, dw_own, dw_y, gu_grad, shared_down_grad = routed_expert(
        n_ep,
        n_tp,
        shape,
        got,
        up_rows,
        (gu_a, gu_c, gu_b, gu_own, dn_a, dn_c, dn_b, dn_own),
        gates,
        normed_two,
        pre_grad,
        shared_out_grad,
        shared_hidden,
    )
    shared_gate_up_grad = jnp.transpose(gu_grad, (1, 0, 2)).astype(F32)
    shared_down_grad = shared_down_grad.astype(F32)
    expert_down_grad = jnp.transpose(dw_own[2].astype(F32) + dw_y[2].astype(F32), (1, 0))[None]
    expert_gate_up_grad = jnp.transpose(dw_own[:2].astype(F32) + dw_y[:2].astype(F32), (2, 0, 1))[None]

    out_rows, attn_grad, linear_grad, bias_grad, small = backward(
        n_ep,
        n_tp,
        shape,
        n_exp,
        back_rows,
        back_gates,
        place_t,
        shared_back,
        scale_grad,
        probs_all,
        router_all,
        normed_two,
        middle,
        cotangent,
        mlp_gain[None],
        qkv,
        out_weight,
        cos_all,
        sin_all,
        prefix_row,
        e_out,
    )
    qkv_grad, out_weight_grad, input_grad, output, gain_one, bias_sum, small_sum = tail(
        n_ep,
        n_tp,
        normed_one,
        linear_grad,
        attn_grad,
        context,
        w_t,
        hidden,
        factor_one,
        attn_gain[None],
        bias_grad,
        small,
        out_rows,
        weighted_place,
        scaled_part,
        middle,
    )
    small_sum = jnp.transpose(small_sum, (1, 0, 2)).reshape(-1, width)
    qkv_weight_grad = jnp.transpose(qkv_grad, (1, 0, 2))
    gain_one_sum = gain_one[0]
    bias_sum = bias_sum.reshape(3, local_width)
    router_sum = small_sum[:n_exp].T
    share_gate_sum = small_sum[n_exp]
    gain_two_sum = small_sum[n_exp + 1]
    return (
        output,
        input_grad,
        gain_one_sum,
        qkv_weight_grad,
        bias_sum,
        out_weight_grad,
        gain_two_sum,
        router_sum,
        share_gate_sum,
        shared_gate_up_grad,
        shared_down_grad,
        expert_gate_up_grad,
        expert_down_grad,
    )


def solution(mesh):
    return jax.shard_map(
        body,
        mesh=mesh,
        in_specs=(
            P("ep", None),
            P(),
            P(None, None, "tp"),
            P(None, "tp"),
            P(None, "tp"),
            P(),
            P(),
            P(),
            P(None, None, "tp"),
            P(None, "tp"),
            P("ep", None, None, "tp"),
            P("ep", None, "tp"),
            P("ep", None),
            P("ep", None),
            P("ep"),
            P("ep", None),
        ),
        out_specs=(
            P("ep", "tp"),
            P("ep", "tp"),
            P(),
            P("ep", None, "tp"),
            P(None, "tp"),
            P("ep", "tp"),
            P(),
            P(),
            P(),
            P("ep", None, "tp"),
            P("ep", "tp"),
            P("ep", None, None, "tp"),
            P("ep", None, "tp"),
        ),
        check_vma=False,
    )
```

```python
import functools

import jax
import jax.numpy as jnp
import numpy as np
from jax import lax
from jax.experimental import pallas as pl
from jax.experimental.pallas import tpu as pltpu
from jax.sharding import PartitionSpec as P

HEAD_DIM = 128
EPSILON = 1e-06
THETA = 1000000.0
BF = jnp.bfloat16
F32 = jnp.float32


def mm(a, b, ca, cb):
    return lax.dot_general(a, b, (((ca,), (cb,)), ((), ())), preferred_element_type=F32)


def angle_tables(length, head_size):
    half_size = head_size // 2
    frequency = (THETA ** (-np.arange(half_size, dtype=np.float32) * 2.0 / head_size)).astype(np.float32)
    angles = (np.arange(length, dtype=np.float32)[:, None] * frequency[None, :]).astype(np.float64)
    cosine, sine_val = np.cos(angles), np.sin(angles)
    return (
        np.concatenate([cosine, cosine], axis=1).astype(np.float32),
        np.concatenate([-sine_val, sine_val], axis=1).astype(np.float32),
    )


def ring_place(e, n):
    odd = e % 2
    return (1 - odd) * (e // 2) + odd * (n - 1 - e // 2)


def ring_member(p, n):
    second = p // (n // 2)
    return (1 - second) * 2 * p + second * (2 * (n - 1 - p) + 1)


def remote(src, dst, send_sem, recv_sem, axis, index):
    return pltpu.make_async_remote_copy(
        src_ref=src,
        dst_ref=dst,
        send_sem=send_sem,
        recv_sem=recv_sem,
        device_id={axis: index},
        device_id_type=pl.DeviceIdType.MESH,
    )


def greet(n, n_tp, ep, tp):
    barrier = pltpu.get_barrier_semaphore()
    for shift in range(1, n):
        pl.semaphore_signal(
            barrier, 1, device_id={"ep": lax.rem(ep + shift, n)}, device_id_type=pl.DeviceIdType.MESH
        )
    for shift in range(1, n_tp):
        pl.semaphore_signal(
            barrier, 1, device_id={"tp": lax.rem(tp + shift, n_tp)}, device_id_type=pl.DeviceIdType.MESH
        )
    pl.semaphore_wait(barrier, n - 1 + n_tp - 1)


def flip(index, bit):
    if bit == 1:
        return index + 1 - 2 * (index % 2)
    return index + 2 - 4 * ((index // 2) % 2)


def tail_kernel(
    n,
    n_tp,
    ready,
    n1,
    lg,
    ag,
    ctx,
    w,
    hidden,
    r_one,
    gain_all,
    bias,
    small,
    o_rows,
    weighted,
    spart,
    mid,
    ag_hbm,
    qkv_out,
    o_out,
    in_out,
    out_out,
    gain_out,
    bias_out,
    small_out,
    h_cols,
    res_cols,
    ag_cols,
    in_sem,
    ring_recv,
    ring_send,
    part_own,
    part_send,
    part_recv,
    y_send,
    y_recv,
    mean_send,
    mean_recv,
    vec_send,
    vec_recv,
    small_recv,
    small_sum,
    gain_send,
    gain_recv,
    out_send,
    out_recv,
    oy_send,
    oy_recv,
    ring_ss,
    ring_rs,
    tp_ss,
    tp_rs,
    vec_ss,
    vec_rs,
    small_ss,
    small_rs,
    gain_ss,
    gain_rs,
):
    ep = lax.axis_index("ep")
    tp = lax.axis_index("tp")
    tokens, lw = ctx.shape
    columns = pl.ds(pl.multiple_of(tp * lw, lw), lw)
    col_in = [
        pltpu.make_async_copy(hidden.at[:, columns], h_cols, in_sem.at[0]),
        pltpu.make_async_copy(mid.at[:, columns], res_cols, in_sem.at[1]),
        pltpu.make_async_copy(ag_hbm.at[:, columns], ag_cols, in_sem.at[2]),
    ]
    for copy in col_in:
        copy.start()
    gain = gain_all[:, columns]
    rows = qkv_out.shape[1]
    width = rows * n
    p = ring_place(ep, n)
    nxt = ring_member(lax.rem(p + 1, n), n)
    prv = ring_member(lax.rem(p + n - 1, n), n)
    core_peer, y_peer = flip(tp, 1), flip(tp, 2)
    greet(n, n_tp, ep, tp)

    def small_copy(shift, turn, way):
        to, came = lax.rem(ep + shift, n), lax.rem(ep + n - shift, n)
        if turn == 0:
            src, dst, arrived = small.at[to], small_recv.at[ep], small_recv.at[came]
        else:
            src, dst, arrived = small_sum, small_out.at[ep], small_out.at[came]
        sems = small_ss.at[turn, shift], small_rs.at[turn, shift]
        if way == 0:
            return remote(src, dst, *sems, "ep", to)
        return remote(src, arrived, *sems, "ep", came)

    def block_of(ring, step):
        if ring < 2:
            return ring_member(lax.rem(p + 2 * n - 1 - step, n), n)
        return ring_member(lax.rem(p + 1 + step, n), n)

    def term(ring, owner):
        if ring == 1:
            return block_dot(ag, owner, rows, ctx[...])
        k = {0: 0, 2: 1, 3: 2}[ring]
        return block_dot(n1, owner, rows, lg[:, k * lw : (k + 1) * lw])

    def ring_copy(ring, step, slot):
        return remote(
            ring_send.at[ring, slot],
            ring_recv.at[ring, step],
            ring_ss.at[ring, slot],
            ring_rs.at[ring, step],
            "ep",
            nxt if ring < 2 else prv,
        )

    def ring_step(step, first):
        for ring in range(4):
            slot = lax.rem(step, 2)
            mine = term(ring, block_of(ring, step))
            ring_copy(ring, step - 1, slot).wait_recv()
            if not first:
                ring_copy(ring, step - 2, slot).wait_send()
            ring_send[ring, slot] = (mine + ring_recv[ring, step - 1].astype(F32)).astype(BF)
            ring_copy(ring, step, slot).start()

    for ring in range(4):
        ring_send[ring, 0] = term(ring, block_of(ring, 0)).astype(BF)
        ring_copy(ring, 0, 0).start()

    ready()

    def part_block(column, store):
        for m in range(0, tokens, 128):
            total = None
            for k in range(3):
                d = lax.dot_general(
                    lg[m : m + 128, k * lw : (k + 1) * lw],
                    w[k, pl.ds(pl.multiple_of(column * lw, lw), lw), :],
                    (((1,), (1,)), ((), ())),
                    preferred_element_type=F32,
                )
                total = d if total is None else total + d
            store(m, total)

    def tp_copy(i, src, dst, peer):
        return remote(src, dst, tp_ss.at[i], tp_rs.at[i], "tp", peer)

    first = [tp_copy(i, part_send.at[i], part_recv.at[i], core_peer) for i in range(2)]
    for i in range(2):

        def put(m, total, i=i):
            part_send[i, m : m + 128, :] = total.astype(BF)

        part_block((core_peer % 2) + 2 * i, put)
        first[i].start()

    ring_step(1, True)

    small_recv[ep] = small[ep]
    for shift in range(1, n):
        small_copy(shift, 0, 0).start()
    for copy in col_in:
        copy.wait()

    def put_own(m, total):
        part_own[m : m + 128, :] = total

    other = (tp // 2) * -1 + 1
    part_block((tp % 2) + 2 * other, put_own)
    for i in range(2):
        first[i].wait()
    y_send[...] = (part_own[...] + part_recv[other].astype(F32)).astype(BF)
    second = tp_copy(2, y_send, y_recv, y_peer)
    second.start()

    ring_step(2, False)

    part_block(tp, put_own)
    second.wait()
    for m in range(0, tokens, 128):
        at = slice(m, m + 128)
        grad = (
            part_own[at, :]
            + part_recv[tp // 2, at, :].astype(F32)
            + y_recv[at, :].astype(F32)
        )
        part_own[at, :] = grad
        hid = h_cols[at, :].astype(F32)
        mean = jnp.sum(grad * gain * hid, axis=1, keepdims=True)
        mean_send[0, at, :] = jnp.broadcast_to(mean, (128, 128))
        col = jnp.sum(grad * hid * r_one[at, :], axis=0, keepdims=True)
        if m == 0:
            vec_send[:, :lw] = col
        else:
            vec_send[:, :lw] += col
    third = tp_copy(3, mean_send.at[0], mean_recv.at[0], core_peer)
    third.start()
    vec_send[:, lw:] = bias[...]
    vec_recv[ep] = vec_send[...]

    def vec_copy(shift, way):
        to = lax.rem(ep + shift, n)
        came = lax.rem(ep + n - shift, n)
        if way == "out":
            return remote(vec_send, vec_recv.at[ep], vec_ss.at[shift], vec_rs.at[shift], "ep", to)
        return remote(vec_send, vec_recv.at[came], vec_ss.at[shift], vec_rs.at[shift], "ep", came)

    for shift in range(1, n):
        vec_copy(shift, "out").start()

    ring_step(3, False)

    third.wait()
    mean_send[1] = mean_send[0] + mean_recv[0]
    fourth = tp_copy(4, mean_send.at[1], mean_recv.at[1], y_peer)
    fourth.start()

    def out_block(column):
        at = pl.ds(pl.multiple_of(column * lw, lw), lw)
        return spart[:, at].astype(F32) + jnp.dot(
            weighted[...], o_rows[:, at], preferred_element_type=F32
        )

    fifth = [tp_copy(5 + i, out_send.at[i], out_recv.at[i], core_peer) for i in range(2)]
    for i in range(2):
        out_send[i] = out_block((core_peer % 2) + 2 * i).astype(BF)
        fifth[i].start()

    ring_step(4, False)

    for shift in range(1, n):
        small_copy(shift, 0, 1).wait()
    total = small_recv[0].astype(F32)
    for e in range(1, n):
        total = total + small_recv[e].astype(F32)
    small_sum[...] = total
    small_out[ep] = total
    for shift in range(1, n):
        small_copy(shift, 1, 0).start()
    for copy in fifth:
        copy.wait()
    oy_send[...] = (out_block((tp % 2) + 2 * other) + out_recv[other].astype(F32)).astype(BF)
    sixth = tp_copy(7, oy_send, oy_recv, y_peer)
    sixth.start()
    fourth.wait()
    for m in range(0, tokens, 128):
        at = slice(m, m + 128)
        mean = (mean_send[1, at, :1] + mean_recv[1, at, :1]) * (1.0 / width)
        r = r_one[at, :]
        in_out[at, :] = (
            ag_cols[at, :].astype(F32)
            + r * part_own[at, :] * gain
            - h_cols[at, :].astype(F32) * (r * r * r) * mean
        ).astype(BF)
    for shift in range(1, n):
        vec_copy(shift, "in").wait()
    total = vec_recv[0]
    for e in range(1, n):
        total = total + vec_recv[e]
    bias_out[...] = total[:, lw:]
    gain_send[...] = total[:, :lw]
    gain_recv[tp] = total[:, :lw]

    def gain_copy(shift, way):
        to = lax.rem(tp + shift, n_tp)
        came = lax.rem(tp + n_tp - shift, n_tp)
        if way == "out":
            return remote(gain_send, gain_recv.at[tp], gain_ss.at[shift], gain_rs.at[shift], "tp", to)
        return remote(gain_send, gain_recv.at[came], gain_ss.at[shift], gain_rs.at[shift], "tp", came)

    for shift in range(1, n_tp):
        gain_copy(shift, "out").start()

    ring_step(5, False)

    own = out_block(tp) + res_cols[...] + out_recv[tp // 2].astype(F32)
    sixth.wait()
    out_out[...] = (own + oy_recv[...].astype(F32)).astype(BF)

    @pl.loop(6, n - 1)
    def _(step):
        ring_step(step, False)

    for shift in range(1, n):
        small_copy(shift, 1, 1).wait()
    for shift in range(1, n_tp):
        gain_copy(shift, "in").wait()
    for j in range(n_tp):
        gain_out[:, j * lw : (j + 1) * lw] = gain_recv[j]

    for ring in range(4):
        mine = term(ring, ep)
        ring_copy(ring, n - 2, 0).wait_recv()
        done = mine + ring_recv[ring, n - 2].astype(F32)
        if ring == 1:
            o_out[...] = done
        else:
            qkv_out[{0: 0, 2: 1, 3: 2}[ring]] = done
    for ring in range(4):
        for step in (n - 3, n - 2):
            ring_copy(ring, step, step % 2).wait_send()


def tail(n, n_tp, n1, lg, ag, ctx, w, hidden, r_one, gain, bias, small, o_rows, weighted, spart, mid):
    tokens, width = n1.shape
    lw = ctx.shape[1]
    rows = width // n
    ag_hbm = ag
    if rows % 128:
        n1, ag = n1.T, ag.T
    wide = small.shape[1]
    vmem = pl.BlockSpec(memory_space=pltpu.VMEM)
    hbm = pl.BlockSpec(memory_space=pl.ANY)
    dma = pltpu.SemaphoreType.DMA
    operands = (n1, lg, ag, ctx, w, hidden, r_one, gain, bias, small, o_rows, weighted, spart, mid, ag_hbm)
    late = (4, 10, 11, 12)
    return pl.pallas_call(
        fetch_late(functools.partial(tail_kernel, n, n_tp), late),
        out_shape=(
            jax.ShapeDtypeStruct((3, rows, lw), F32),
            jax.ShapeDtypeStruct((rows, lw), F32),
            jax.ShapeDtypeStruct((tokens, lw), BF),
            jax.ShapeDtypeStruct((tokens, lw), BF),
            jax.ShapeDtypeStruct((1, width), F32),
            jax.ShapeDtypeStruct((1, 3 * lw), F32),
            jax.ShapeDtypeStruct((n, wide, rows), F32),
        ),
        in_specs=specs(15, (4, 5, 10, 11, 12, 13, 14)),
        out_specs=[vmem] * 7,
        scratch_shapes=[
            pltpu.VMEM((tokens, lw), BF),
            pltpu.VMEM((tokens, lw), F32),
            pltpu.VMEM((tokens, lw), BF),
            dma((3,)),
            pltpu.VMEM((4, n - 1, rows, lw), BF),
            pltpu.VMEM((4, 2, rows, lw), BF),
            pltpu.VMEM((tokens, lw), F32),
            pltpu.VMEM((2, tokens, lw), BF),
            pltpu.VMEM((2, tokens, lw), BF),
            pltpu.VMEM((tokens, lw), BF),
            pltpu.VMEM((tokens, lw), BF),
            pltpu.VMEM((2, tokens, 128), F32),
            pltpu.VMEM((2, tokens, 128), F32),
            pltpu.VMEM((1, 4 * lw), F32),
            pltpu.VMEM((n, 1, 4 * lw), F32),
            pltpu.VMEM((n, wide, rows), BF),
            pltpu.VMEM((wide, rows), F32),
            pltpu.VMEM((1, lw), F32),
            pltpu.VMEM((n_tp, 1, lw), F32),
            pltpu.VMEM((2, tokens, lw), BF),
            pltpu.VMEM((2, tokens, lw), BF),
            pltpu.VMEM((tokens, lw), BF),
            pltpu.VMEM((tokens, lw), BF),
            dma((4, 2)),
            dma((4, n - 1)),
            dma((8,)),
            dma((8,)),
            dma((n,)),
            dma((n,)),
            dma((2, n)),
            dma((2, n)),
            dma((n_tp,)),
            dma((n_tp,)),
        ]
        + late_scratch(operands, late),
        compiler_params=pltpu.CompilerParams(
            collective_id=0, has_side_effects=True, vmem_limit_bytes=60 * 2**20
        ),
        cost_estimate=pl.CostEstimate(
            flops=2 * tokens * width * 7 * lw, bytes_accessed=30 * 2**20, transcendentals=0
        ),
    )(*operands)


def cols_of(ref, owner, rows):
    at = pl.ds(pl.multiple_of(owner * rows, rows), rows)
    return ref[:, at] if rows % 128 == 0 else ref[at, :]


def block_dot(ref, owner, rows, other):
    dims = (((0,), (0,)), ((), ())) if rows % 128 == 0 else (((1,), (0,)), ((), ()))
    return lax.dot_general(cols_of(ref, owner, rows), other, dims, preferred_element_type=F32)


def middle_kernel(
    n,
    n_tp,
    shape,
    ready,
    x_hbm,
    u_hbm,
    gu_a,
    gu_c,
    gu_b,
    gu_own,
    dn_a,
    dn_c,
    dn_b,
    dn_own,
    gates,
    nt,
    pg,
    og,
    sh,
    back,
    g_back,
    o_hbm,
    dw_recv,
    dw_own,
    dw_y,
    gu_out,
    dn_out,
    zero,
    w,
    xb,
    ub,
    rgb,
    eb,
    rbs,
    gbs,
    ring_recv,
    ring_send,
    w_sem,
    x_sem,
    u_sem,
    out_sem,
    ring_ss,
    ring_rs,
    free,
    back_ss,
    back_rs,
    gate_ss,
    gate_rs,
    dw_ss,
    dw_rs,
    dw_sem,
):
    ep = lax.axis_index("ep")
    tp = lax.axis_index("tp")
    core_peer, y_peer = flip(tp, 1), flip(tp, 2)
    gr = ub.shape[1]
    capp = shape[0]
    zero[...] = jnp.zeros_like(zero)
    width = u_hbm.shape[1]
    units = w.shape[1]
    quarter = units // 4
    groups = x_hbm.shape[0] // gr
    per = n // groups
    rows = gu_out.shape[1]
    half = ring_recv.shape[3]
    p = ring_place(ep, n)
    nxt = ring_member(lax.rem(p + 1, n), n)
    prv = ring_member(lax.rem(p + n - 1, n), n)

    w_in = [
        pltpu.make_async_copy(ref, w.at[:2, i * quarter : (i + 1) * quarter, :], w_sem.at[i])
        for i, ref in enumerate((gu_a, gu_c, gu_b, gu_own))
    ] + [
        pltpu.make_async_copy(ref, w.at[2, i * quarter : (i + 1) * quarter, :], w_sem.at[4 + i])
        for i, ref in enumerate((dn_a, dn_c, dn_b, dn_own))
    ]
    for copy in w_in:
        copy.start()

    x_in = pltpu.make_async_copy(x_hbm, xb, x_sem)

    def u_copy(g):
        at = pl.ds(pl.multiple_of(g * gr, gr), gr)
        slot = lax.rem(g, 2)
        return pltpu.make_async_copy(u_hbm.at[at, :], ub.at[slot], u_sem.at[slot])

    x_in.start()
    u_copy(0).start()
    greet(n, n_tp, ep, tp)

    ready()

    edges = [0]
    for ring in range(4):
        edges.append(edges[-1] + (3 * units // 128 + 3 - ring) // 4 * 128)
    wide_of = [edges[i + 1] - edges[i] for i in range(4)]

    def block_of(ring, step):
        if ring < 2:
            return ring_member(lax.rem(p + 2 * n - 1 - step, n), n)
        return ring_member(lax.rem(p + 1 + step, n), n)

    def term(ring, owner):
        lo, hi = edges[ring], edges[ring + 1]
        parts = []
        if lo < 2 * units:
            parts.append(block_dot(nt, owner, rows, pg[:, lo : min(hi, 2 * units)]))
        if hi > 2 * units:
            parts.append(block_dot(og, owner, rows, sh[:, max(lo - 2 * units, 0) : hi - 2 * units]))
        return parts[0] if len(parts) == 1 else jnp.concatenate(parts, axis=1)

    def ring_copy(ring, slot):
        return remote(
            ring_send.at[ring, slot, :, : wide_of[ring]],
            ring_recv.at[ring, slot, :, : wide_of[ring]],
            ring_ss.at[ring, slot],
            ring_rs.at[ring, slot],
            "ep",
            nxt if ring < 2 else prv,
        )

    order = (0, 2, 1, 3)

    def ring_step(step):
        slot, last = lax.rem(step, 2), lax.rem(step + 1, 2)
        for ring in order:
            size = wide_of[ring]
            mine = term(ring, block_of(ring, step))
            ring_copy(ring, last).wait_recv()

            @pl.when(step >= 2)
            def _():
                ring_copy(ring, slot).wait_send()

            ring_send[ring, slot, :, :size] = (
                mine + ring_recv[ring, last, :, :size].astype(F32)
            ).astype(BF)

            @pl.when(step <= n - 3)
            def _():
                pl.semaphore_signal(
                    free.at[ring],
                    1,
                    device_id={"ep": prv if ring < 2 else nxt},
                    device_id_type=pl.DeviceIdType.MESH,
                )

            @pl.when(step >= 2)
            def _():
                pl.semaphore_wait(free.at[ring], 1)

            ring_copy(ring, slot).start()

    for ring in order:
        ring_send[ring, 0, :, : wide_of[ring]] = term(ring, block_of(ring, 0)).astype(BF)
        ring_copy(ring, 0).start()

    for copy in w_in:
        copy.wait()
    x_in.wait()

    nt_dims, first_dims = (((1,), (1,)), ((), ())), (((0,), (0,)), ((), ()))

    def saved(g):
        at = pl.ds(pl.multiple_of(g * gr, gr), gr)
        slot = lax.rem(g, 2)
        return pltpu.make_async_copy(ub.at[slot], o_hbm.at[at, :], out_sem.at[slot])

    def back_copies(r):
        return block_copies(r, rbs, back, back_ss, back_rs, ep, tp, n, shape, zero, True)

    kept_copy = pltpu.make_async_copy(rbs.at[:capp, :], back.at[:capp, :], back_ss.at[0, 0])

    def gate_copy(r):
        return remote(
            gbs.at[r], g_back.at[r], gate_ss.at[r], gate_rs.at[r], "ep", lax.rem(ep + n - r, n)
        )

    g_kept = pltpu.make_async_copy(gbs.at[0], g_back.at[0], gate_ss.at[0])
    gbs[...] = jnp.zeros_like(gbs)

    @pl.loop(0, groups)
    def _(g):
        slot = lax.rem(g, 2)
        mine = pl.ds(pl.multiple_of(g * gr, gr), gr)
        u_copy(g).wait()

        @pl.when(g >= 1)
        def _():
            saved(g - 1).wait()

        @pl.when(g + 1 < groups)
        def _():
            u_copy(g + 1).start()

        gate = jnp.concatenate([gate_column(gates, g * per + i, capp) for i in range(per)], axis=0)
        rgb[mine, :] = (gate * ub[slot].astype(F32)).astype(BF)

        def hidden(at):
            x = xb[mine, :]
            g_pre = lax.dot_general(x, w[0, at, :], nt_dims, preferred_element_type=F32)
            u_pre = lax.dot_general(x, w[1, at, :], nt_dims, preferred_element_type=F32)
            grad = lax.dot_general(rgb[mine, :], w[2, at, :], nt_dims, preferred_element_type=F32)
            sig = jax.nn.sigmoid(g_pre)
            eb[2, mine, at] = (g_pre * sig * u_pre).astype(BF)
            eb[0, mine, at] = (grad * u_pre * sig * (1.0 + g_pre * (1.0 - sig))).astype(BF)
            eb[1, mine, at] = (grad * g_pre * sig).astype(BF)

        @pl.loop(0, units // 256)
        def _(c):
            hidden(pl.ds(pl.multiple_of(c * 256, 256), 256))

        if units % 256:
            hidden(pl.ds(units // 256 * 256, units % 256))

        def columns(c, total):
            at = pl.ds(pl.multiple_of(c * 256, 256), 256)
            out = jnp.dot(eb[2, mine, :], w[2, :, at], preferred_element_type=F32)
            grad = jnp.dot(eb[0, mine, :], w[0, :, at], preferred_element_type=F32) + jnp.dot(
                eb[1, mine, :], w[1, :, at], preferred_element_type=F32
            )
            rbs[mine, at] = grad.astype(BF)
            total = total + jnp.sum(out * ub[slot, :, at].astype(F32), axis=1, keepdims=True)
            ub[slot, :, at] = out.astype(BF)
            return total

        total = lax.fori_loop(0, width // 256, columns, jnp.zeros((gr, 1), F32))
        hi = total.astype(BF).astype(F32)
        lane = lax.broadcasted_iota(jnp.int32, (gr, 128), 1)
        terms = jnp.where(lane == 0, hi, jnp.where(lane == 1, total - hi, 0.0)).astype(BF)
        pick = (
            lax.broadcasted_iota(jnp.int32, (16, 128), 0) == lax.broadcasted_iota(jnp.int32, (16, 128), 1)
        ).astype(F32).astype(BF)
        turned = lax.dot_general(pick, terms, nt_dims, preferred_element_type=F32).astype(BF)
        for i in range(per):
            gbs[g * per + i, :, :capp] = turned[:, i * capp : (i + 1) * capp]
        saved(g).start()
        for i in range(per):
            r = g * per + i
            if i == 0:

                @pl.when(g == 0)
                def _():
                    kept_copy.start()
                    g_kept.start()

                @pl.when(g > 0)
                def _():
                    each(back_copies(r), "start")
                    gate_copy(r).start()
            else:
                each(back_copies(r), "start")
                gate_copy(r).start()

        @pl.when(lax.rem(g, 2) == 1)
        def _():
            ring_step((g + 1) // 2)

    def weight_rows(at):
        for k in range(3):
            for c in range(0, width, 512):
                w[k, at, c : c + 512] = lax.dot_general(
                    eb[k, :, at],
                    (rgb if k == 2 else xb)[:, c : c + 512],
                    first_dims,
                    preferred_element_type=F32,
                ).astype(BF)

    @pl.loop(0, units // 256)
    def _(c):
        weight_rows(pl.ds(pl.multiple_of(c * 256, 256), 256))

    if units % 256:
        weight_rows(pl.ds(units // 256 * 256, units % 256))

    dw_core = remote(
        w.at[:, : 2 * quarter, :], dw_recv, dw_ss.at[0], dw_rs.at[0], "tp", core_peer
    )
    dw_core.start()
    ring_step(groups // 2 + 1)
    dw_core.wait()
    dw_in = pltpu.make_async_copy(dw_recv, w.at[:, : 2 * quarter, :], dw_sem.at[0])
    dw_in.start()
    dw_in.wait()
    for k in range(3):

        @pl.loop(0, quarter // 32)
        def _(c, k=k):
            far = pl.ds(pl.multiple_of(2 * quarter + c * 32, 32), 32)
            came = pl.ds(pl.multiple_of(quarter + c * 32, 32), 32)
            w[k, far, :] = (w[k, far, :].astype(F32) + w[k, came, :].astype(F32)).astype(BF)

    dw_far = remote(
        w.at[:, 2 * quarter : 3 * quarter, :], dw_y, dw_ss.at[1], dw_rs.at[1], "tp", y_peer
    )
    dw_far.start()
    for k in range(3):

        @pl.loop(0, quarter // 32)
        def _(c, k=k):
            far = pl.ds(pl.multiple_of(3 * quarter + c * 32, 32), 32)
            came = pl.ds(pl.multiple_of(c * 32, 32), 32)
            w[k, far, :] = (w[k, far, :].astype(F32) + w[k, came, :].astype(F32)).astype(BF)

    dw_keep = pltpu.make_async_copy(w.at[:, 3 * quarter :, :], dw_own, dw_sem.at[1])
    dw_keep.start()

    @pl.loop(groups // 2 + 2, n - 1)
    def _(step):
        ring_step(step)

    for ring in order:
        mine = term(ring, ep)
        ring_copy(ring, n % 2).wait_recv()
        done = mine + ring_recv[ring, n % 2, :, : wide_of[ring]].astype(F32)
        lo, hi = edges[ring], edges[ring + 1]
        for k, out in enumerate((gu_out.at[0], gu_out.at[1], dn_out)):
            a, b = max(lo, k * units), min(hi, (k + 1) * units)
            if a < b:
                out[:, a - k * units : b - k * units] = done[:, a - lo : b - lo].astype(BF)
    for ring in range(4):
        for slot in range(2):
            ring_copy(ring, slot).wait_send()
    g_kept.wait()
    kept_copy.wait()
    saved(groups - 1).wait()
    dw_keep.wait()
    dw_far.wait()

    @pl.loop(1, n)
    def _(r):
        each(back_copies(r), "wait")
        gate_copy(r).wait()


def routed_expert(n, n_tp, shape, x, u, weights, gates, nt, pg, og, sh):
    total, width = x.shape
    units = 4 * weights[-1].shape[0]
    gr = total // 4
    rows = width // n
    half = (3 * units // 128 + 3) // 4 * 128
    vmem = pl.BlockSpec(memory_space=pltpu.VMEM)
    hbm = pl.BlockSpec(memory_space=pl.ANY)
    dma = pltpu.SemaphoreType.DMA
    if rows % 128:
        nt, og = nt.T, og.T
    operands = (x, u, *weights, gates, nt, pg, og, sh)
    late = (11, 12, 13, 14)
    return pl.pallas_call(
        fetch_late(functools.partial(middle_kernel, n, n_tp, shape), late),
        out_shape=(
            jax.ShapeDtypeStruct((total, width), BF),
            jax.ShapeDtypeStruct((n, 16, 128), BF),
            jax.ShapeDtypeStruct((total, width), BF),
            jax.ShapeDtypeStruct((3, units // 2, width), BF),
            jax.ShapeDtypeStruct((3, units // 4, width), BF),
            jax.ShapeDtypeStruct((3, units // 4, width), BF),
            jax.ShapeDtypeStruct((2, rows, units), BF),
            jax.ShapeDtypeStruct((rows, units), BF),
        ),
        in_specs=specs(15, (0, 1, 2, 3, 4, 5, 6, 7, 8, 9, 11, 12, 13, 14)),
        out_specs=[hbm] * 6 + [vmem] * 2,
        scratch_shapes=[
            pltpu.VMEM((max(shape[0] - shape[1], 16), width), BF),
            pltpu.VMEM((3, units, width), BF),
            pltpu.VMEM((total, width), BF),
            pltpu.VMEM((2, gr, width), BF),
            pltpu.VMEM((total, width), BF),
            pltpu.VMEM((3, total, units), BF),
            pltpu.VMEM((total, width), BF),
            pltpu.VMEM((n, 16, 128), BF),
            pltpu.VMEM((4, 2, rows, half), BF),
            pltpu.VMEM((4, 2, rows, half), BF),
            dma((8,)),
            dma,
            dma((2,)),
            dma((2,)),
            dma((4, 2)),
            dma((4, 2)),
            pltpu.SemaphoreType.REGULAR((4,)),
            dma((3, n)),
            dma((3, n)),
            dma((n,)),
            dma((n,)),
            dma((2,)),
            dma((2,)),
            dma((2,)),
        ]
        + late_scratch(operands, late),
        compiler_params=pltpu.CompilerParams(
            collective_id=1, has_side_effects=True, vmem_limit_bytes=63 * 2**20
        ),
        cost_estimate=pl.CostEstimate(
            flops=2 * total * width * 6 * units, bytes_accessed=40 * 2**20, transcendentals=0
        ),
    )(*operands)


def tp_total(
    project, between, tp, core_send, core_recv, y_send, y_recv, summed,
    core_ss, core_rs, y_ss, y_rs, g_ss, g_rs,
):
    core_peer, y_peer = flip(tp, 1), flip(tp, 2)
    pieces, size = core_send.shape[0], core_send.shape[2]
    half = pieces * size

    def core_copy(i):
        return remote(core_send.at[i], core_recv.at[i], core_ss.at[i], core_rs.at[i], "tp", core_peer)

    def y_copy(i):
        return remote(y_send.at[i], y_recv.at[i], y_ss.at[i], y_rs.at[i], "tp", y_peer)

    def gather_copy(i, slot):
        return remote(summed.at[slot, i], summed.at[slot, i], g_ss.at[i], g_rs.at[i], "tp", core_peer)

    me, other = tp % 2, core_peer % 2
    for i in range(pieces):
        core_send[i] = project(other * half, i, size).astype(BF)
        core_copy(i).start()
        own = project(me * half, i, size)
        core_copy(i).wait_recv()
        y_send[i] = (own + core_recv[i].astype(F32)).astype(BF)
        y_copy(i).start()
    between()
    for i in range(pieces):
        y_copy(i).wait_recv()
        summed[me, i] = (y_send[i].astype(F32) + y_recv[i].astype(F32)).astype(BF)
        gather_copy(i, me).start()
    for i in range(pieces):
        gather_copy(i, other).wait_recv()
    for i in range(pieces):
        core_copy(i).wait_send()
        y_copy(i).wait_send()
        gather_copy(i, me).wait_send()


def blocks_at_once(n, capp):
    per = 1
    while 2 * per * capp <= 128 and n % (2 * per) == 0:
        per *= 2
    return per


def has_more(tp, source, expert, n_tp, extra):
    return lax.rem(tp + 64 * n_tp - source - expert, n_tp) < extra


def block_copies(r, src, dst, ss, rs, ep, tp, n, shape, zero, home):
    capp, base, extra, n_tp = shape
    on, back = lax.rem(ep + r, n), lax.rem(ep + n - r, n)
    to, come = (back, on) if home else (on, back)
    at = pl.ds(pl.multiple_of(r * capp, 16), base)
    out = [(None, None, remote(src.at[at, :], dst.at[at, :], ss.at[0, r], rs.at[0, r], "ep", to))]
    if base < capp:
        at = pl.ds(pl.multiple_of(r * capp + base, 16), capp - base)
        sends, gets = has_more(tp, ep, to, n_tp, extra), has_more(tp, ep, come, n_tp, extra)
        out.append((sends, gets, remote(src.at[at, :], dst.at[at, :], ss.at[1, r], rs.at[1, r], "ep", to)))
        fill = jnp.logical_not(gets)
        out.append((fill, None, pltpu.make_async_copy(zero, dst.at[at, :], ss.at[2, r])))
    return out


def each(copies, verb):
    for sends, gets, copy in copies:
        if sends is None:
            getattr(copy, verb)()
        elif gets is None or verb == "start":
            pl.when(sends)(getattr(copy, verb))
        else:
            pl.when(sends)(copy.wait_send)
            pl.when(gets)(copy.wait_recv)


def fetch_late(kernel, late):
    def wrapped(*refs):
        refs, held, sems = refs[: -len(late) - 1], refs[-len(late) - 1 : -1], refs[-1]
        copies = [pltpu.make_async_copy(refs[at], held[i], sems.at[i]) for i, at in enumerate(late)]
        for copy in copies:
            copy.start()

        def ready():
            for copy in copies:
                copy.wait()

        refs = list(refs)
        for i, at in enumerate(late):
            refs[at] = held[i]
        kernel(ready, *refs)

    return wrapped


def late_scratch(operands, late):
    return [pltpu.VMEM(operands[at].shape, operands[at].dtype) for at in late] + [
        pltpu.SemaphoreType.DMA((len(late),))
    ]


def specs(count, apart):
    return [pl.BlockSpec(memory_space=pl.ANY if i in apart else pltpu.VMEM) for i in range(count)]


SEND_ORDER = (4, 5, 6, 7, 2, 3, 1, 0)


def send_order(i, n, ep):
    if n != len(SEND_ORDER):
        return (i + 1) % n
    to = ep
    for bit in (1, 2, 4):
        if SEND_ORDER[i] & bit:
            to = to + bit - 2 * bit * ((to // bit) % 2)
    return lax.rem(to + n - ep, n)


def gate_column(tiles, r, capp):
    ones = jnp.ones((16, 128), BF)
    return lax.dot_general(
        tiles[r, :, :capp], ones, (((0,), (0,)), ((), ())), preferred_element_type=F32
    )[:, :1]


def front_kernel(
    n,
    n_tp,
    shape,
    ready,
    hidden,
    gain1,
    gain2,
    w,
    bias,
    cosine,
    sine,
    prefix,
    ow,
    place,
    cot,
    gu_own,
    dn_own,
    pairs,
    up_rows,
    gu_a,
    dn_a,
    dn_b,
    n1,
    qkv,
    ctx,
    mid,
    nt,
    factor_one,
    split,
    pair_in,
    pair_out,
    pair_si,
    pair_so,
    zero,
    up_sent,
    core_send,
    core_recv,
    y_send,
    y_recv,
    summed,
    up_ss,
    up_rs,
    w_ss,
    w_rs,
    core_ss,
    core_rs,
    y_ss,
    y_rs,
    g_ss,
    g_rs,
):
    ep = lax.axis_index("ep")
    tp = lax.axis_index("tp")
    tokens, width = hidden.shape
    lw = ctx.shape[1]
    heads = lw // HEAD_DIM
    core_peer, y_peer = flip(tp, 1), flip(tp, 2)
    greet(n, n_tp, ep, tp)

    capp = shape[0]
    zero[...] = jnp.zeros_like(zero)

    def up_copies(r):
        return block_copies(r, up_sent, up_rows, up_ss, up_rs, ep, tp, n, shape, zero, False)

    kept = pltpu.make_async_copy(up_sent.at[:capp, :], up_rows.at[:capp, :], up_ss.at[0, 0])
    per = blocks_at_once(n, capp)
    size = per * capp

    for i in range(n // per):
        b = send_order(i, n, ep) if per == 1 else i
        at = pl.ds(pl.multiple_of(b * size, size), size)
        up_sent[at, :] = jnp.dot(place[at, :], cot[...], preferred_element_type=F32).astype(BF)
        for j in range(per):
            if i == (n - 1 if per == 1 else 0) and j == 0:
                kept.start()
            else:
                each(up_copies(b * per + j), "start")

    w_copies = [
        remote(dn_own, dn_b, w_ss.at[0], w_rs.at[0], "tp", y_peer),
        remote(dn_own, dn_a, w_ss.at[1], w_rs.at[1], "tp", core_peer),
        remote(gu_own, gu_a, w_ss.at[2], w_rs.at[2], "tp", core_peer),
    ]
    for copy in w_copies:
        copy.start()

    chunk = pair_in.shape[1]
    chunks = pairs.shape[0] // chunk

    def pair_load(i):
        at, slot = pl.ds(pl.multiple_of(i * chunk, chunk), chunk), lax.rem(i, 2)
        return pltpu.make_async_copy(pairs.at[at], pair_in.at[slot], pair_si.at[slot])

    def pair_store(i):
        at, slot = pl.ds(pl.multiple_of(i * chunk, chunk), chunk), lax.rem(i, 2)
        return pltpu.make_async_copy(pair_out.at[slot], split.at[:, at, :], pair_so.at[slot])

    def set_apart(first, last):
        @pl.loop(first, last)
        def _(i):
            slot = lax.rem(i, 2)

            @pl.when(i + 1 < chunks)
            def _():
                pair_load(i + 1).start()

            pair_load(i).wait()

            @pl.when(i >= 2)
            def _():
                pair_store(i - 2).wait()

            pair_out[slot, 0] = pair_in[slot, :, 0, :]
            pair_out[slot, 1] = pair_in[slot, :, 1, :]
            pair_store(i).start()

    pair_load(0).start()
    ready()

    @pl.loop(0, tokens // 64)
    def _(m):
        at = pl.ds(pl.multiple_of(m * 64, 64), 64)
        h = hidden[at, :].astype(F32)
        factor = lax.rsqrt(jnp.sum(h * h, axis=1, keepdims=True) * (1.0 / width) + EPSILON)
        factor_one[at, :] = factor
        n1[at, :] = (h * factor * gain1[...]).astype(BF)

    for k in range(3):

        @pl.loop(0, lw // 256)
        def _(c, k=k):
            at = pl.ds(pl.multiple_of(c * 256, 256), 256)
            x = jnp.dot(n1[...], w[k, :, at], preferred_element_type=F32) + bias[k : k + 1, at]
            if k < 2:
                x = jnp.concatenate(
                    [
                        x[:, i * HEAD_DIM : (i + 1) * HEAD_DIM] * cosine[...]
                        + pltpu.roll(x[:, i * HEAD_DIM : (i + 1) * HEAD_DIM], HEAD_DIM // 2, 1) * sine[...]
                        for i in range(256 // HEAD_DIM)
                    ],
                    axis=1,
                )
            qkv[k, :, at] = x.astype(BF)

    @pl.loop(0, tokens // 128)
    def _(m):
        at = pl.ds(pl.multiple_of(m * 128, 128), 128)
        row = lax.broadcasted_iota(jnp.int32, (128, tokens), 0) + m * 128
        col = lax.broadcasted_iota(jnp.int32, (128, tokens), 1)
        visible = (col <= row) | (col < prefix[...])
        for i in range(heads):
            lanes = slice(i * HEAD_DIM, (i + 1) * HEAD_DIM)
            s = lax.dot_general(
                qkv[0, at, lanes], qkv[1, :, lanes], (((1,), (1,)), ((), ())), preferred_element_type=F32
            )
            s = jnp.where(visible, s * HEAD_DIM ** (-0.5), -1e30)
            e = jnp.exp(s - jnp.max(s, axis=1, keepdims=True))
            e = e * (1.0 / jnp.sum(e, axis=1, keepdims=True))
            ctx[at, lanes] = jnp.dot(
                e.astype(BF), qkv[2, :, lanes], preferred_element_type=F32
            ).astype(BF)

    pieces, size = core_send.shape[0], core_send.shape[2]
    half = pieces * size

    def project(base, i, size):
        at = pl.ds(pl.multiple_of(base + i * size, size), size)
        return lax.dot_general(
            ctx[...], ow[at, :], (((1,), (1,)), ((), ())), preferred_element_type=F32
        )

    tp_total(
        project, lambda: set_apart(0, chunks * 12 // 16), tp, core_send, core_recv, y_send, y_recv, summed,
        core_ss, core_rs, y_ss, y_rs, g_ss, g_rs,
    )

    @pl.loop(0, tokens // 32)
    def _(m):
        at = pl.ds(pl.multiple_of(m * 32, 32), 32)
        total = jnp.zeros((32, 1), F32)
        for j in range(2):
            for i in range(pieces):
                lanes = slice(j * half + i * size, j * half + (i + 1) * size)
                x = hidden[at, lanes].astype(F32) + summed[j, i, at, :].astype(F32)
                mid[at, lanes] = x
                total = total + jnp.sum(x * x, axis=1, keepdims=True)
        factor = lax.rsqrt(total * (1.0 / width) + EPSILON)
        nt[at, :] = (mid[at, :] * factor * gain2[...]).astype(BF)

    set_apart(chunks * 12 // 16, chunks)
    pair_store(chunks - 2).wait()
    pair_store(chunks - 1).wait()
    for copy in w_copies:
        copy.wait()
    kept.wait()
    for r in range(1, n):
        each(up_copies(r), "wait")


def front(n, n_tp, shape, hidden, gain1, gain2, w, bias, cosine, sine, prefix, ow, place, cot, gu_own, dn_own, pairs):
    tokens, width = hidden.shape
    lw = ow.shape[1]
    quarter = dn_own.shape[0]
    vmem = pl.BlockSpec(memory_space=pltpu.VMEM)
    hbm = pl.BlockSpec(memory_space=pl.ANY)
    dma = pltpu.SemaphoreType.DMA
    operands = (hidden, gain1, gain2, w, bias, cosine, sine, prefix, ow, place, cot, gu_own, dn_own, pairs)
    late = (0, 3, 8)
    return pl.pallas_call(
        fetch_late(functools.partial(front_kernel, n, n_tp, shape), late),
        out_shape=(
            jax.ShapeDtypeStruct((n * shape[0], width), BF),
            jax.ShapeDtypeStruct((2, quarter, width), BF),
            jax.ShapeDtypeStruct((quarter, width), BF),
            jax.ShapeDtypeStruct((quarter, width), BF),
            jax.ShapeDtypeStruct((tokens, width), BF),
            jax.ShapeDtypeStruct((3, tokens, lw), BF),
            jax.ShapeDtypeStruct((tokens, lw), BF),
            jax.ShapeDtypeStruct((tokens, width), F32),
            jax.ShapeDtypeStruct((tokens, width), BF),
            jax.ShapeDtypeStruct((tokens, 1), F32),
            jax.ShapeDtypeStruct((2, width, pairs.shape[2]), BF),
        ),
        in_specs=specs(14, (0, 3, 8, 11, 12, 13)),
        out_specs=[hbm] * 4 + [vmem] * 6 + [hbm],
        scratch_shapes=[
            pltpu.VMEM((2, 128, 2, pairs.shape[2]), BF),
            pltpu.VMEM((2, 2, 128, pairs.shape[2]), BF),
            dma((2,)),
            dma((2,)),
            pltpu.VMEM((max(shape[0] - shape[1], 16), width), BF),
            pltpu.VMEM((n * shape[0], width), BF),
            pltpu.VMEM((4, tokens, width // 8), BF),
            pltpu.VMEM((4, tokens, width // 8), BF),
            pltpu.VMEM((4, tokens, width // 8), BF),
            pltpu.VMEM((4, tokens, width // 8), BF),
            pltpu.VMEM((2, 4, tokens, width // 8), BF),
            dma((3, n)),
            dma((3, n)),
            dma((3,)),
            dma((3,)),
            dma((4,)),
            dma((4,)),
            dma((4,)),
            dma((4,)),
            dma((4,)),
            dma((4,)),
        ]
        + late_scratch(operands, late),
        compiler_params=pltpu.CompilerParams(
            collective_id=2, has_side_effects=True, vmem_limit_bytes=56 * 2**20
        ),
        cost_estimate=pl.CostEstimate(
            flops=2 * tokens * width * 4 * lw, bytes_accessed=30 * 2**20, transcendentals=0
        ),
    )(*operands)


def dispatch_kernel(
    n,
    n_tp,
    shape,
    n_exp,
    ready,
    nt,
    place,
    router,
    cot,
    sgu,
    sdn,
    gu_own,
    dn_b,
    dest_t,
    x_rows,
    g_rows,
    gu_b,
    gu_c,
    dn_c,
    probs,
    place_t,
    weighted,
    og,
    pg,
    sh,
    part,
    sback,
    sgrad,
    zero,
    gate,
    x_send,
    g_send,
    x_ss,
    x_rs,
    gate_ss,
    gate_rs,
    w_ss,
    w_rs,
):
    ep = lax.axis_index("ep")
    tp = lax.axis_index("tp")
    tokens, width = nt.shape
    units = sdn.shape[1]
    total = place.shape[0]
    core_peer, y_peer = flip(tp, 1), flip(tp, 2)
    greet(n, n_tp, ep, tp)
    w_y = remote(gu_own, gu_b, w_ss.at[0], w_rs.at[0], "tp", y_peer)
    w_y.start()
    w_on = remote(dn_b, dn_c, w_ss.at[1], w_rs.at[1], "tp", core_peer)
    w_on.start()

    capp = shape[0]
    zero[...] = jnp.zeros_like(zero)

    def x_copies(r):
        return block_copies(r, x_send, x_rows, x_ss, x_rs, ep, tp, n, shape, zero, False)

    def gate_copy(r, way):
        to = lax.rem(ep + r, n) if way == "out" else lax.rem(ep + n - r, n)
        return remote(g_send.at[r], g_rows.at[r], gate_ss.at[r], gate_rs.at[r], "ep", to)

    kept = pltpu.make_async_copy(x_send.at[:capp, :], x_rows.at[:capp, :], x_ss.at[0, 0])
    g_kept = pltpu.make_async_copy(g_send.at[0], g_rows.at[0], gate_ss.at[0])
    per = blocks_at_once(n, capp)
    size = per * capp

    for i in range(n // per):
        b = send_order(i, n, ep) if per == 1 else i
        at = pl.ds(pl.multiple_of(b * size, size), size)
        x_send[at, :] = jnp.dot(place[at, :], nt[...], preferred_element_type=F32).astype(BF)
        for j in range(per):
            if i == (n - 1 if per == 1 else 0) and j == 0:
                kept.start()
            else:
                each(x_copies(b * per + j), "start")

    ready()

    logits = jnp.dot(nt[...], router[...], preferred_element_type=F32)
    lane = lax.broadcasted_iota(jnp.int32, logits.shape, 1)
    chosen = jnp.where(lane < n_exp, logits, -1e30)
    e = jnp.exp(chosen - jnp.max(chosen, axis=1, keepdims=True))
    prob = e / jnp.sum(e, axis=1, keepdims=True)
    prob = jnp.where(lane == n_exp, jax.nn.sigmoid(logits), prob)
    probs[...] = prob
    hi = prob.astype(BF)
    lo = (prob - hi.astype(F32)).astype(BF)
    g_send[...] = jnp.zeros_like(g_send)
    across = (((0,), (1,)), ((), ()))

    for r in range(n):
        where = place[r * capp : (r + 1) * capp, :]
        pick = lax.broadcasted_iota(jnp.int32, (128, capp), 0) == lax.rem(r + ep, n)
        g_hi = jnp.sum(
            jnp.where(pick, lax.dot_general(hi, where, across, preferred_element_type=F32), 0.0),
            axis=0,
            keepdims=True,
        )
        g_lo = jnp.sum(
            jnp.where(pick, lax.dot_general(lo, where, across, preferred_element_type=F32), 0.0),
            axis=0,
            keepdims=True,
        )
        term = lax.broadcasted_iota(jnp.int32, (16, capp), 0)
        g_send[r, :, :capp] = jnp.where(term == 0, g_hi, jnp.where(term == 1, g_lo, 0.0)).astype(BF)
        gate[:, r * capp : (r + 1) * capp] = g_hi + g_lo
        if r == 0:
            g_kept.start()
        else:
            gate_copy(r, "out").start()

    @pl.loop(0, tokens // 64)
    def _(m):
        at = pl.ds(pl.multiple_of(m * 64, 64), 64)
        og[at, :] = (probs[at, n_exp : n_exp + 1] * cot[at, :].astype(F32)).astype(BF)

    def hidden(at, up_at):
        g_pre = jnp.dot(nt[...], sgu[0, :, at], preferred_element_type=F32)
        u_pre = jnp.dot(nt[...], sgu[1, :, at], preferred_element_type=F32)
        grad = jnp.dot(og[...], sdn[:, at], preferred_element_type=F32)
        sig = jax.nn.sigmoid(g_pre)
        sh[:, at] = (g_pre * sig * u_pre).astype(BF)
        pg[:, at] = (grad * u_pre * sig * (1.0 + g_pre * (1.0 - sig))).astype(BF)
        pg[:, up_at] = (grad * g_pre * sig).astype(BF)

    @pl.loop(0, units // 256)
    def _(c):
        hidden(
            pl.ds(pl.multiple_of(c * 256, 256), 256),
            pl.ds(pl.multiple_of(c * 256 + units, 128), 256),
        )

    if units % 256:
        rest = units // 256 * 256
        hidden(pl.ds(rest, units - rest), pl.ds(units + rest, units - rest))

    nt_dims = (((1,), (1,)), ((), ()))

    share = probs[:, n_exp : n_exp + 1]

    def columns(c, total):
        at = pl.ds(pl.multiple_of(c * 256, 256), 256)
        out = lax.dot_general(sh[...], sdn[at, :], nt_dims, preferred_element_type=F32)
        part[:, at] = (share * out).astype(BF)
        sback[:, at] = lax.dot_general(
            pg[:, :units], sgu[0, at, :], nt_dims, preferred_element_type=F32
        ) + lax.dot_general(pg[:, units:], sgu[1, at, :], nt_dims, preferred_element_type=F32)
        return total + jnp.sum(cot[:, at].astype(F32) * out, axis=1, keepdims=True)

    sgrad[...] = lax.fori_loop(0, width // 256, columns, jnp.zeros((tokens, 1), F32))

    @pl.loop(0, total // 128)
    def _(c):
        at = pl.ds(pl.multiple_of(c * 128, 128), 128)
        spot = lax.broadcasted_iota(jnp.int32, (tokens, 128), 1) + c * 128
        hit = dest_t[:, :1] == spot
        for k in range(1, dest_t.shape[1]):
            hit = hit | (dest_t[:, k : k + 1] == spot)
        place_t[:, at] = jnp.where(hit, 1.0, 0.0).astype(BF)
        weighted[:, at] = jnp.where(hit, gate[:, at], 0.0).astype(BF)

    w_y.wait()
    w_far = remote(gu_b, gu_c, w_ss.at[2], w_rs.at[2], "tp", core_peer)
    w_far.start()
    w_on.wait()
    w_far.wait()
    kept.wait()
    g_kept.wait()

    @pl.loop(1, n)
    def _(r):
        gate_copy(r, "in").wait()
        each(x_copies(r), "wait")


def dispatch(n, n_tp, shape, n_exp, nt, place, router, cot, sgu, sdn, gu_own, dn_b, dest_t):
    tokens, width = nt.shape
    units = sdn.shape[1]
    total = place.shape[0]
    vmem = pl.BlockSpec(memory_space=pltpu.VMEM)
    hbm = pl.BlockSpec(memory_space=pl.ANY)
    dma = pltpu.SemaphoreType.DMA
    operands = (nt, place, router, cot, sgu, sdn, gu_own, dn_b, dest_t)
    late = (2, 3, 4, 5)
    return pl.pallas_call(
        fetch_late(functools.partial(dispatch_kernel, n, n_tp, shape, n_exp), late),
        out_shape=(
            jax.ShapeDtypeStruct((total, width), BF),
            jax.ShapeDtypeStruct((n, 16, 128), BF),
            jax.ShapeDtypeStruct(gu_own.shape, BF),
            jax.ShapeDtypeStruct(gu_own.shape, BF),
            jax.ShapeDtypeStruct(dn_b.shape, BF),
            jax.ShapeDtypeStruct((tokens, 128), F32),
            jax.ShapeDtypeStruct((tokens, total), BF),
            jax.ShapeDtypeStruct((tokens, total), BF),
            jax.ShapeDtypeStruct((tokens, width), BF),
            jax.ShapeDtypeStruct((tokens, 2 * units), BF),
            jax.ShapeDtypeStruct((tokens, units), BF),
            jax.ShapeDtypeStruct((tokens, width), BF),
            jax.ShapeDtypeStruct((tokens, width), F32),
            jax.ShapeDtypeStruct((tokens, 1), F32),
        ),
        in_specs=specs(9, (2, 3, 4, 5, 6, 7)),
        out_specs=[hbm] * 5 + [vmem] * 9,
        scratch_shapes=[
            pltpu.VMEM((max(shape[0] - shape[1], 16), width), BF),
            pltpu.VMEM((1, total), F32),
            pltpu.VMEM((total, width), BF),
            pltpu.VMEM((n, 16, 128), BF),
            dma((3, n)),
            dma((3, n)),
            dma((n,)),
            dma((n,)),
            dma((3,)),
            dma((3,)),
        ]
        + late_scratch(operands, late),
        compiler_params=pltpu.CompilerParams(
            collective_id=3, has_side_effects=True, vmem_limit_bytes=60 * 2**20
        ),
        cost_estimate=pl.CostEstimate(
            flops=2 * tokens * width * 6 * units, bytes_accessed=40 * 2**20, transcendentals=0
        ),
    )(*operands)


def backward_kernel(
    n,
    n_tp,
    shape,
    n_exp,
    ready,
    back,
    g_back,
    place_t,
    sback,
    sgrad,
    probs,
    router,
    nt,
    mid,
    cot,
    gain2,
    qkv,
    ow,
    cosine,
    sine,
    prefix,
    o_sent,
    o_rows,
    ag,
    lg,
    bias,
    small,
    zero,
    core_send,
    core_recv,
    y_send,
    y_recv,
    summed,
    few_send,
    few_recv,
    ng,
    cg,
    dk,
    dv,
    o_ss,
    o_rs,
    core_ss,
    core_rs,
    y_ss,
    y_rs,
    g_ss,
    g_rs,
    few_ss,
    few_rs,
):
    ep = lax.axis_index("ep")
    tp = lax.axis_index("tp")
    tokens, width = nt.shape
    total = back.shape[0]
    lw = ow.shape[1]
    heads = lw // HEAD_DIM
    core_peer, y_peer = flip(tp, 1), flip(tp, 2)
    greet(n, n_tp, ep, tp)

    capp = shape[0]
    zero[...] = jnp.zeros_like(zero)

    def o_copies(r):
        return block_copies(r, o_sent, o_rows, o_ss, o_rs, ep, tp, n, shape, zero, True)

    kept = pltpu.make_async_copy(o_sent.at[:capp, :], o_rows.at[:capp, :], o_ss.at[0, 0])

    for i in range(n - 1):
        each(o_copies(send_order(i, n, ep)), "start")
    kept.start()
    ready()

    row = lax.broadcasted_iota(jnp.int32, (total, 128), 0)
    spot = lax.broadcasted_iota(jnp.int32, (total, 128), 1)
    expert = lax.rem(row // capp + ep * (n_exp // n), n_exp)
    gg = jnp.concatenate([gate_column(g_back, r, capp) for r in range(n)], axis=0)
    few = jnp.dot(
        place_t[...], jnp.where(spot == expert, gg, 0.0).astype(BF), preferred_element_type=F32
    )
    lane = lax.broadcasted_iota(jnp.int32, (tokens, 128), 1)
    few_send[0] = jnp.where(lane == n_exp, sgrad[...], few).astype(BF)
    few_core = remote(few_send.at[0], few_recv.at[0], few_ss.at[0], few_rs.at[0], "tp", core_peer)
    few_core.start()

    def project(base, i, size):
        at = pl.ds(pl.multiple_of(base + i * size, size), size)
        return sback[:, at] + jnp.dot(place_t[...], back[:, at], preferred_element_type=F32)

    def between():
        few_core.wait()
        few_send[1] = (few_send[0].astype(F32) + few_recv[0].astype(F32)).astype(BF)
        few_y = remote(few_send.at[1], few_recv.at[1], few_ss.at[1], few_rs.at[1], "tp", y_peer)
        few_y.start()
        few_y.wait()

    tp_total(
        project, between, tp, core_send, core_recv, y_send, y_recv, summed,
        core_ss, core_rs, y_ss, y_rs, g_ss, g_rs,
    )

    prob = jnp.where(lane < n_exp, probs[...], 0.0)
    share = probs[:, n_exp : n_exp + 1]
    grads = few_send[1].astype(F32) + few_recv[1].astype(F32)
    inner = jnp.sum(prob * grads, axis=1, keepdims=True)
    gate_in = grads * share * (1.0 - share)
    few_send[0] = jnp.where(
        lane < n_exp, prob * (grads - inner), jnp.where(lane == n_exp, gate_in, 0.0)
    ).astype(BF)
    pieces, size = summed.shape[1], summed.shape[3]
    for j in range(2):
        for i in range(pieces):
            at = slice((j * pieces + i) * size, (j * pieces + i + 1) * size)
            ng[:, at] = summed[j, i].astype(F32) + lax.dot_general(
                few_send[0], router[at, :], (((1,), (1,)), ((), ())), preferred_element_type=F32
            )

    step = 32

    def norm_rows(m, acc):
        at = pl.ds(pl.multiple_of(m * step, step), step)
        h = mid[at, :]
        grad = ng[at, :]
        factor = lax.rsqrt(jnp.sum(h * h, axis=1, keepdims=True) * (1.0 / width) + EPSILON)
        scaled = grad * gain2[...]
        mean = jnp.sum(scaled * h, axis=1, keepdims=True) * (1.0 / width)
        ag[at, :] = (
            cot[at, :].astype(F32) + factor * scaled - h * (factor * factor * factor) * mean
        ).astype(BF)
        return acc + jnp.sum((grad * h * factor).reshape(step // 8, 8, width), axis=0)

    acc = lax.fori_loop(0, tokens // step, norm_rows, jnp.zeros((8, width), F32))

    @pl.loop(0, lw // 256)
    def _(c):
        at = pl.ds(pl.multiple_of(c * 256, 256), 256)
        cg[:, at] = jnp.dot(ag[...], ow[:, at], preferred_element_type=F32).astype(BF)

    dk[...] = jnp.zeros_like(dk)
    dv[...] = jnp.zeros_like(dv)
    first_dims, last_dims = (((0,), (0,)), ((), ())), (((1,), (1,)), ((), ()))

    def attend(m, sums):
        at = pl.ds(pl.multiple_of(m * 128, 128), 128)
        row = lax.broadcasted_iota(jnp.int32, (128, tokens), 0) + m * 128
        col = lax.broadcasted_iota(jnp.int32, (128, tokens), 1)
        visible = (col <= row) | (col < prefix[...])
        parts = []
        for i in range(heads):
            lanes = slice(i * HEAD_DIM, (i + 1) * HEAD_DIM)
            q, grad = qkv[0, at, lanes], cg[at, lanes]
            s = lax.dot_general(q, qkv[1, :, lanes], last_dims, preferred_element_type=F32)
            s = jnp.where(visible, s * HEAD_DIM ** (-0.5), -1e30)
            e = jnp.exp(s - jnp.max(s, axis=1, keepdims=True))
            e = e * (1.0 / jnp.sum(e, axis=1, keepdims=True))
            dp = lax.dot_general(grad, qkv[2, :, lanes], last_dims, preferred_element_type=F32)
            delta = jnp.sum(e * dp, axis=1, keepdims=True)
            ds = (e * (dp - delta)).astype(BF)
            dv[:, lanes] += lax.dot_general(e.astype(BF), grad, first_dims, preferred_element_type=F32)
            dk[:, lanes] += lax.dot_general(ds, q, first_dims, preferred_element_type=F32)
            dq = jnp.dot(ds, qkv[1, :, lanes], preferred_element_type=F32) * HEAD_DIM ** (-0.5)
            dq = dq * cosine[at, :] - pltpu.roll(dq, HEAD_DIM // 2, 1) * sine[at, :]
            lg[at, lanes] = dq.astype(BF)
            parts.append(jnp.sum(dq.reshape(16, 8, HEAD_DIM), axis=0))
        return sums + jnp.concatenate(parts, axis=1)

    sums = lax.fori_loop(0, tokens // 128, attend, jnp.zeros((8, lw), F32))
    bias[:, :lw] = jnp.sum(sums, axis=0, keepdims=True)
    for i in range(heads):
        lanes = slice(i * HEAD_DIM, (i + 1) * HEAD_DIM)
        grad = dk[:, lanes] * HEAD_DIM ** (-0.5)
        grad = grad * cosine[...] - pltpu.roll(grad, HEAD_DIM // 2, 1) * sine[...]
        at = slice(lw + i * HEAD_DIM, lw + (i + 1) * HEAD_DIM)
        lg[:, at] = grad.astype(BF)
        bias[:, at] = jnp.sum(grad, axis=0, keepdims=True)
    lg[:, 2 * lw :] = dv[...].astype(BF)
    bias[:, 2 * lw :] = jnp.sum(dv[...], axis=0, keepdims=True)

    wide, span = small.shape[1:]
    gain_row = jnp.sum(acc, axis=0, keepdims=True)
    rows = lax.dot_general(few_send[0], nt[...], first_dims, preferred_element_type=F32)[:wide]
    index = lax.broadcasted_iota(jnp.int32, rows.shape, 0)
    rows = jnp.where(index == n_exp + 1, gain_row, rows).astype(BF)
    for r in range(n):
        small[r] = rows[:, r * span : (r + 1) * span]

    kept.wait()
    for r in range(1, n):
        each(o_copies(r), "wait")


def backward(n, n_tp, shape, n_exp, back, g_back, place_t, sback, sgrad, probs, router, nt, mid, cot, gain2, qkv, ow, cosine, sine, prefix, o_sent):
    tokens, width = nt.shape
    lw = ow.shape[1]
    wide = -(-(n_exp + 2) // 16) * 16
    vmem = pl.BlockSpec(memory_space=pltpu.VMEM)
    hbm = pl.BlockSpec(memory_space=pl.ANY)
    dma = pltpu.SemaphoreType.DMA
    piece = (4, tokens, width // 8)
    operands = (back, g_back, place_t, sback, sgrad, probs, router, nt, mid, cot, gain2, qkv, ow, cosine, sine, prefix, o_sent)
    late = (0, 2, 3, 6, 7, 8, 9, 11, 12)
    return pl.pallas_call(
        fetch_late(functools.partial(backward_kernel, n, n_tp, shape, n_exp), late),
        out_shape=(
            jax.ShapeDtypeStruct(o_sent.shape, BF),
            jax.ShapeDtypeStruct((tokens, width), BF),
            jax.ShapeDtypeStruct((tokens, 3 * lw), BF),
            jax.ShapeDtypeStruct((1, 3 * lw), F32),
            jax.ShapeDtypeStruct((n, wide, width // n), BF),
        ),
        in_specs=specs(17, (0, 2, 3, 6, 7, 8, 9, 11, 12, 16)),
        out_specs=[hbm] + [vmem] * 4,
        scratch_shapes=[
            pltpu.VMEM((max(shape[0] - shape[1], 16), width), BF),
            pltpu.VMEM(piece, BF),
            pltpu.VMEM(piece, BF),
            pltpu.VMEM(piece, BF),
            pltpu.VMEM(piece, BF),
            pltpu.VMEM((2,) + piece, BF),
            pltpu.VMEM((2, tokens, 128), BF),
            pltpu.VMEM((2, tokens, 128), BF),
            pltpu.VMEM((tokens, width), F32),
            pltpu.VMEM((tokens, lw), BF),
            pltpu.VMEM((tokens, lw), F32),
            pltpu.VMEM((tokens, lw), F32),
            dma((3, n)),
            dma((3, n)),
            dma((4,)),
            dma((4,)),
            dma((4,)),
            dma((4,)),
            dma((4,)),
            dma((4,)),
            dma((2,)),
            dma((2,)),
        ]
        + late_scratch(operands, late),
        compiler_params=pltpu.CompilerParams(
            collective_id=4, has_side_effects=True, vmem_limit_bytes=60 * 2**20
        ),
        cost_estimate=pl.CostEstimate(
            flops=2 * tokens * width * 4 * lw, bytes_accessed=30 * 2**20, transcendentals=0
        ),
    )(*operands)


def body(
    hidden,
    attn_gain,
    qkv_weight,
    qkv_bias,
    out_weight,
    mlp_gain,
    router_weight,
    share_gate,
    shared_gate_up,
    shared_down,
    expert_gate_up,
    expert_down,
    routes,
    priority,
    prefix,
    cotangent,
):
    tokens, width = hidden.shape
    n_ep = lax.axis_size("ep")
    n_tp = lax.axis_size("tp")
    tp_i = lax.axis_index("tp")
    local_width = qkv_weight.shape[2]
    expert_local = expert_gate_up.shape[0]
    n_exp = expert_local * n_ep
    top = routes.shape[1]
    capacity = (5 * tokens * top + 4 * n_exp - 1) // (4 * n_exp)
    tiles = -(-capacity // 16)
    least, extra = 16 * (tiles // n_tp), tiles % n_tp
    part_pad = least + (16 if extra else 0)
    shape = (part_pad, least, extra, n_tp)
    rows = n_exp * part_pad

    flat_route = routes.T.reshape(-1)
    flat_order = priority.T.reshape(-1)
    hits = (flat_route[:, None] == jnp.arange(n_exp, dtype=jnp.int32)[None, :]).astype(BF)
    smaller = (flat_order[None, :] < flat_order[:, None]).astype(BF)
    counts = mm(smaller, hits, 1, 0)
    slot = jnp.sum(counts * hits.astype(F32), axis=1).astype(jnp.int32).reshape(top, tokens)
    kept = slot < capacity
    ep_i = lax.axis_index("ep")
    more = [has_more(j, ep_i, routes.T // expert_local, n_tp, extra) for j in range(n_tp)]
    more.append(has_more(tp_i, ep_i, routes.T // expert_local, n_tp, extra))
    start = tp_i * least
    for j in range(n_tp):
        start = start + 16 * (more[j] & (j < tp_i)).astype(jnp.int32)
    in_part = slot - start
    mine = kept & (in_part >= 0) & (in_part < least + 16 * more[-1].astype(jnp.int32))
    hop = lax.rem(routes.T + n_exp - ep_i * expert_local, n_exp)
    dest = jnp.where(mine, hop * part_pad + in_part, -1)
    row_ids = jnp.arange(rows, dtype=jnp.int32)[:, None]
    place = (dest[0][None, :] == row_ids)
    for k in range(1, top):
        place = place | (dest[k][None, :] == row_ids)
    place = place.astype(BF)

    cos_all, sin_all = angle_tables(tokens, HEAD_DIM)
    w_t = jnp.transpose(qkv_weight, (1, 0, 2))
    prefix_row = jnp.broadcast_to(prefix[None], (1, tokens))
    gu_own = jnp.transpose(expert_gate_up[0], (1, 2, 0))
    dn_own = jnp.transpose(expert_down[0], (1, 0))
    up_rows, gu_a, dn_a, dn_b, normed_one, qkv, context, middle, normed_two, factor_one, sgu = front(
        n_ep,
        n_tp,
        shape,
        hidden,
        attn_gain[None],
        mlp_gain[None],
        w_t,
        qkv_bias,
        cos_all,
        sin_all,
        prefix_row,
        out_weight,
        place,
        cotangent,
        gu_own,
        dn_own,
        shared_gate_up,
    )

    router_all = jnp.concatenate(
        [router_weight, share_gate[:, None], jnp.zeros((width, 127 - n_exp), BF)], axis=1
    )
    got, gates, gu_b, gu_c, dn_c, probs_all, place_t, weighted_place, shared_out_grad, pre_grad, shared_hidden, scaled_part, shared_back, scale_grad = (
        dispatch(
            n_ep,
            n_tp,
            shape,
            n_exp,
            normed_two,
            place,
            router_all,
            cotangent,
            sgu,
            shared_down,
            gu_own,
            dn_b,
            dest.T,
        )
    )
    back_rows, back_gates, e_out, _, dw_own, dw_y, gu_grad, shared_down_grad = routed_expert(
        n_ep,
        n_tp,
        shape,
        got,
        up_rows,
        (gu_a, gu_c, gu_b, gu_own, dn_a, dn_c, dn_b, dn_own),
        gates,
        normed_two,
        pre_grad,
        shared_out_grad,
        shared_hidden,
    )
    shared_gate_up_grad = jnp.transpose(gu_grad, (1, 0, 2)).astype(F32)
    shared_down_grad = shared_down_grad.astype(F32)
    expert_down_grad = jnp.transpose(dw_own[2].astype(F32) + dw_y[2].astype(F32), (1, 0))[None]
    expert_gate_up_grad = jnp.transpose(dw_own[:2].astype(F32) + dw_y[:2].astype(F32), (2, 0, 1))[None]

    out_rows, attn_grad, linear_grad, bias_grad, small = backward(
        n_ep,
        n_tp,
        shape,
        n_exp,
        back_rows,
        back_gates,
        place_t,
        shared_back,
        scale_grad,
        probs_all,
        router_all,
        normed_two,
        middle,
        cotangent,
        mlp_gain[None],
        qkv,
        out_weight,
        cos_all,
        sin_all,
        prefix_row,
        e_out,
    )
    qkv_grad, out_weight_grad, input_grad, output, gain_one, bias_sum, small_sum = tail(
        n_ep,
        n_tp,
        normed_one,
        linear_grad,
        attn_grad,
        context,
        w_t,
        hidden,
        factor_one,
        attn_gain[None],
        bias_grad,
        small,
        out_rows,
        weighted_place,
        scaled_part,
        middle,
    )
    small_sum = jnp.transpose(small_sum, (1, 0, 2)).reshape(-1, width)
    qkv_weight_grad = jnp.transpose(qkv_grad, (1, 0, 2))
    gain_one_sum = gain_one[0]
    bias_sum = bias_sum.reshape(3, local_width)
    router_sum = small_sum[:n_exp].T
    share_gate_sum = small_sum[n_exp]
    gain_two_sum = small_sum[n_exp + 1]
    return (
        output,
        input_grad,
        gain_one_sum,
        qkv_weight_grad,
        bias_sum,
        out_weight_grad,
        gain_two_sum,
        router_sum,
        share_gate_sum,
        shared_gate_up_grad,
        shared_down_grad,
        expert_gate_up_grad,
        expert_down_grad,
    )


def solution(mesh):
    return jax.shard_map(
        body,
        mesh=mesh,
        in_specs=(
            P("ep", None),
            P(),
            P(None, None, "tp"),
            P(None, "tp"),
            P(None, "tp"),
            P(),
            P(),
            P(),
            P(None, None, "tp"),
            P(None, "tp"),
            P("ep", None, None, "tp"),
            P("ep", None, "tp"),
            P("ep", None),
            P("ep", None),
            P("ep"),
            P("ep", None),
        ),
        out_specs=(
            P("ep", "tp"),
            P("ep", "tp"),
            P(),
            P("ep", None, "tp"),
            P(None, "tp"),
            P("ep", "tp"),
            P(),
            P(),
            P(),
            P("ep", None, "tp"),
            P("ep", "tp"),
            P("ep", None, None, "tp"),
            P("ep", None, "tp"),
        ),
        check_vma=False,
    )
```
